32 devices in a mesh: dp: 8 (over z, x), mp: 4 (over y, core).
Axes of the slice: x: 2, y: 2, z: 4, core: 2. Of those that a mesh axis runs over, the one named last changes fastest.
Arguments:
- teacher_in: bfloat16 [16384, 1024], P('dp'), may hold values from -6 to 6
- segment_ids: int32 [8, 2048], replicated, may hold values from 0 to 7, never falling along the last dimension, each value on 1 to 1568 neighbouring positions
- keep_mask: int32 [8, 2048], replicated, may hold values from 0 to 1, as said below
- block_owner: int32 [8, 12], replicated, may hold values from -1 to 7, as said below
- student_in: bfloat16 [96, 128, 768], P('dp'), may hold values from -6 to 6
- t_norm1_gain: bfloat16 [1024], replicated, may hold values from 0.25 to 1.75
- t_norm1_shift: bfloat16 [1024], replicated, may hold values from -1.75 to 1.75
- t_qkv: bfloat16 [3, 1024, 1024], P(None, None, 'mp'), may hold values from -0.1875 to 0.1875
- t_qv_bias: bfloat16 [2, 1024], P(None, 'mp'), may hold values from -0.3125 to 0.3125
- t_out: bfloat16 [1024, 1024], P('mp'), may hold values from -3 to 3
- t_out_bias: bfloat16 [1024], replicated, may hold values from -1.75 to 1.75
- t_norm2_gain: bfloat16 [1024], replicated, may hold values from 0.25 to 1.75
- t_norm2_shift: bfloat16 [1024], replicated, may hold values from -1.75 to 1.75
- t_fc1: bfloat16 [1024, 4096], P(None, 'mp'), may hold values from -0.1875 to 0.1875
- t_fc1_bias: bfloat16 [4096], P('mp'), may hold values from -1.75 to 1.75
- t_fc2: bfloat16 [4096, 1024], P('mp'), may hold values from -0.09375 to 0.09375
- t_fc2_bias: bfloat16 [1024], replicated, may hold values from -1.75 to 1.75
- s_norm1_gain: bfloat16 [768], replicated, may hold values from 0.25 to 1.75
- s_norm1_shift: bfloat16 [768], replicated, may hold values from -1.75 to 1.75
- s_qkv: bfloat16 [3, 768, 768], P(None, None, 'mp'), may hold values from -0.21875 to 0.21875
- s_qv_bias: bfloat16 [2, 768], P(None, 'mp'), may hold values from -0.3125 to 0.3125
- s_out: bfloat16 [768, 768], P('mp'), may hold values from -3.5 to 3.5
- s_out_bias: bfloat16 [768], replicated, may hold values from -1.75 to 1.75
- s_norm2_gain: bfloat16 [768], replicated, may hold values from 0.25 to 1.75
- s_norm2_shift: bfloat16 [768], replicated, may hold values from -1.75 to 1.75
- s_fc1: bfloat16 [768, 3072], P(None, 'mp'), may hold values from -0.21875 to 0.21875
- s_fc1_bias: bfloat16 [3072], P('mp'), may hold values from -1.75 to 1.75
- s_fc2: bfloat16 [3072, 768], P('mp'), may hold values from -0.109375 to 0.109375
- s_fc2_bias: bfloat16 [768], replicated, may hold values from -1.75 to 1.75
- head_weight: bfloat16 [768, 1024], replicated, may hold values from -0.21875 to 0.21875
- head_bias: bfloat16 [1024], replicated, may hold values from -1.75 to 1.75
Outputs:
- loss: float32 [], replicated
- student_out: bfloat16 [64, 128, 768], P('dp', 'mp')
- grad_student_in: float32 [96, 128, 768], P('dp', 'mp')
- grad_s_norm1_gain: float32 [768], replicated
- grad_s_norm1_shift: float32 [768], replicated
- grad_s_qkv: float32 [3, 768, 768], P(None, None, 'mp')
- grad_s_qv_bias: float32 [2, 768], P(None, 'mp')
- grad_s_out: float32 [768, 768], P('mp')
- grad_s_out_bias: float32 [768], replicated
- grad_s_norm2_gain: float32 [768], replicated
- grad_s_norm2_shift: float32 [768], replicated
- grad_s_fc1: float32 [768, 3072], P(None, 'mp')
- grad_s_fc1_bias: float32 [3072], P('mp')
- grad_s_fc2: float32 [3072, 768], P('mp')
- grad_s_fc2_bias: float32 [768], replicated
- grad_head: float32 [768, 1024], replicated
- grad_head_bias: float32 [1024], replicated
The draws below stay inside these ranges and needn't reach their ends.
Inputs may be any that keep to these rules, and one draw needn't show every extreme that they name: `keep_mask`: the ones of each row fill at least 4 and at most 12 blocks of 128 (rounded up); some row fills exactly 12. `block_owner`: entry (i, b) names the index of dp that processes block b of home i's kept slots; it is -1 exactly for the blocks that hold no kept token of row i of keep_mask. Every index of dp is named exactly 8 times; no row names one index more than 2 times, and some row names some index exactly 2 times. `segment_ids`: row i numbers the clips of home i, never falling; each clip has 1 to 1568 tokens and one has exactly 1568.
All inputs are finite; a program needn't handle non-finite values.
Results may differ from the reference program's by a relative error of at most 0.015.
The reference program's roundings to bfloat16 on the way count: a program that leaves them out, or rounds other values in their place, can miss the bound.
Values may be sent and summed in bfloat16 or wider, within the bound.
No kernel may reach another device: no remote copies, remote signals or barrier semaphores. Data moves between devices by JAX's collectives and lax.ppermute only.
A program may use at most 128 MiB of HBM per device.

```python
import math
import jax
import jax.numpy as jnp
import numpy as np
from jax import lax

DS = 768
HD = 64
FS = 3072
DT = 1024
FT = 4096
BLK = 128
OWN = 8
CLIPS = 8
CLIP_MAX = 1568
KB = 12
TOK_HOME = 2048
N_DP = 8
N_MP = 4


def make_plan(key):
    half = N_DP // 2
    key_spread, key_order, key_tail, key_mask, key_place, key_names = jax.random.split(key, 6)
    spread = jax.random.randint(key_spread, (half,), 0, OWN // 2 + 1)
    spread = spread.at[0].set(OWN // 2)
    counts = jnp.concatenate([OWN + spread, OWN - spread])
    counts = counts[jax.random.permutation(key_order, N_DP)]
    tails = jax.random.randint(key_tail, (N_DP,), 1, BLK + 1)
    kept = (counts - 1) * BLK + tails
    ranks = jax.vmap(lambda k: jax.random.permutation(k, TOK_HOME))(jax.random.split(key_mask, N_DP))
    mask = (ranks < kept[:, None]).astype(jnp.int32)
    listing = jax.random.permutation(key_place, N_DP)
    earlier = (listing[None, :] < listing[:, None]).astype(jnp.int32)
    starts = jnp.sum(earlier * counts[None, :], axis=1)
    shift = jax.random.randint(key_names, (), 0, N_DP)
    names = jax.random.permutation(jax.random.fold_in(key_names, 1), N_DP)
    slots = jnp.arange(KB, dtype=jnp.int32)
    places = (starts[:, None] + slots[None, :] + shift) % N_DP
    owner = jnp.where(slots[None, :] < counts[:, None], names[places], -1)
    return (mask, owner.astype(jnp.int32))


def draw_keep_mask(key, part):
    mask, owner = make_plan(key)
    return mask


def draw_block_owner(key, part):
    mask, owner = make_plan(key)
    return owner


def block_scale(key, dims, pieces, least, high):
    factor_of = 1.0
    for position, shards_of in pieces:
        draws = jax.random.uniform(jax.random.fold_in(jax.random.fold_in(key, 6), position), (shards_of,), jnp.float32, least / len(pieces), high / len(pieces))
        factor_of = factor_of * jnp.repeat(jnp.exp(draws), dims[position] // shards_of).reshape((-1,) + (1,) * (len(dims) - 1 - position))
    return factor_of


def length_profile(number_of, total, bound, skew):
    weights = [(1 << 20) // math.isqrt(standing ** skew) + 1 for standing in range(2, number_of + 1)]
    rest, given = total - bound - (number_of - 1), [1] * (number_of - 1)
    while rest > 0:
        movable = [i for i in range(number_of - 1) if given[i] < bound]
        mass, budget = sum([weights[i] for i in movable]), rest
        for i in movable:
            extra = min(bound - given[i], max(1, budget * weights[i] // mass), rest)
            given[i] = given[i] + extra
            rest = rest - extra
    return np.array([bound] + given)


def ragged(own_key, number_of, total, limit, skew):
    if number_of == 2:
        one = jax.random.randint(own_key, (), max(1, total - limit), min(limit, total - 1) + 1)
        return jnp.stack([one, total - one])
    lengths = jnp.asarray(length_profile(number_of, total, limit, skew), jnp.int32)
    pairs = (number_of - 1) // 2
    source_of, receiver = lengths[1:1 + 2 * pairs:2], lengths[2:2 + 2 * pairs:2]
    room = jnp.minimum(source_of - 1, limit - receiver)
    passed = jax.random.randint(jax.random.fold_in(own_key, 1), (pairs,), 0, 1 << 20) % (room + 1)
    lengths = lengths.at[1:1 + 2 * pairs:2].set(source_of - passed).at[2:2 + 2 * pairs:2].set(receiver + passed)
    return lengths[jax.random.permutation(jax.random.fold_in(own_key, 2), number_of)]


def scatter_about(own_key, shape, scale, most, cuts=(), held_as=jnp.bfloat16):
    entries = scale * jax.random.normal(own_key, shape, jnp.float32)
    if cuts:
        entries = entries * block_scale(own_key, shape, cuts, -0.22, 0.18)
    return jnp.clip(entries, -most, most).astype(held_as)


def setup_inputs(seed: int = 0) -> dict:
    streams_of = jax.random.split(jax.random.key(seed), 32)
    return {
        "teacher_in": scatter_about(streams_of[0], (N_DP * TOK_HOME, DT), 1.0, 6.0, ((0, 8),)),
        "segment_ids": jax.vmap(lambda own: jnp.searchsorted(jnp.cumsum(ragged(own, CLIPS, TOK_HOME, CLIP_MAX, 1)), jnp.arange(TOK_HOME), side="right"))(jax.random.split(streams_of[1], N_DP)).reshape((N_DP, TOK_HOME)).astype(jnp.int32),
        "keep_mask": draw_keep_mask(jax.random.fold_in(streams_of[31], 71), 0),
        "block_owner": draw_block_owner(jax.random.fold_in(streams_of[31], 71), 0),
        "student_in": scatter_about(streams_of[4], (N_DP * KB, BLK, DS), 1.0, 6.0, ((0, 8),)),
        "t_norm1_gain": jnp.clip(1.0 + 0.15 * jax.random.normal(streams_of[5], (DT,), jnp.float32), 0.25, 1.75).astype(jnp.bfloat16),
        "t_norm1_shift": scatter_about(streams_of[6], (DT,), 0.3, 1.75),
        "t_qkv": scatter_about(streams_of[7], (3, DT, DT), DT ** -0.5, 0.1875, ((2, 4),)),
        "t_qv_bias": scatter_about(streams_of[8], (2, DT), 0.05, 0.3125, ((1, 4),)),
        "t_out": scatter_about(streams_of[9], (DT, DT), (max(1, DT // 256)) ** -0.5, 3.0, ((0, 4),)),
        "t_out_bias": scatter_about(streams_of[10], (DT,), 0.3, 1.75),
        "t_norm2_gain": jnp.clip(1.0 + 0.15 * jax.random.normal(streams_of[11], (DT,), jnp.float32), 0.25, 1.75).astype(jnp.bfloat16),
        "t_norm2_shift": scatter_about(streams_of[12], (DT,), 0.3, 1.75),
        "t_fc1": scatter_about(streams_of[13], (DT, FT), DT ** -0.5, 0.1875, ((1, 4),)),
        "t_fc1_bias": scatter_about(streams_of[14], (FT,), 0.3, 1.75, ((0, 4),)),
        "t_fc2": scatter_about(streams_of[15], (FT, DT), FT ** -0.5, 0.09375, ((0, 4),)),
        "t_fc2_bias": scatter_about(streams_of[16], (DT,), 0.3, 1.75),
        "s_norm1_gain": jnp.clip(1.0 + 0.15 * jax.random.normal(streams_of[17], (DS,), jnp.float32), 0.25, 1.75).astype(jnp.bfloat16),
        "s_norm1_shift": scatter_about(streams_of[18], (DS,), 0.3, 1.75),
        "s_qkv": scatter_about(streams_of[19], (3, DS, DS), DS ** -0.5, 0.21875, ((2, 4),)),
        "s_qv_bias": scatter_about(streams_of[20], (2, DS), 0.05, 0.3125, ((1, 4),)),
        "s_out": scatter_about(streams_of[21], (DS, DS), (max(1, DS // 256)) ** -0.5, 3.5, ((0, 4),)),
        "s_out_bias": scatter_about(streams_of[22], (DS,), 0.3, 1.75),
        "s_norm2_gain": jnp.clip(1.0 + 0.15 * jax.random.normal(streams_of[23], (DS,), jnp.float32), 0.25, 1.75).astype(jnp.bfloat16),
        "s_norm2_shift": scatter_about(streams_of[24], (DS,), 0.3, 1.75),
        "s_fc1": scatter_about(streams_of[25], (DS, FS), DS ** -0.5, 0.21875, ((1, 4),)),
        "s_fc1_bias": scatter_about(streams_of[26], (FS,), 0.3, 1.75, ((0, 4),)),
        "s_fc2": scatter_about(streams_of[27], (FS, DS), FS ** -0.5, 0.109375, ((0, 4),)),
        "s_fc2_bias": scatter_about(streams_of[28], (DS,), 0.3, 1.75),
        "head_weight": scatter_about(streams_of[29], (DS, DT), DS ** -0.5, 0.21875),
        "head_bias": scatter_about(streams_of[30], (DT,), 0.3, 1.75),
    }


highest = lax.Precision.HIGHEST
eps = 1e-05
minus_big = -1e+30

@jax.custom_vjp
def low(v):
    return lax.optimization_barrier(v.astype(jnp.bfloat16)).astype(jnp.float32)

@jax.custom_vjp
def low_back(v):
    return v

def low_keep(v):
    return (low(v), None)

def low_pass(kept, grad):
    return (grad,)

def back_keep(v):
    return (v, None)

def back_low(kept, grad):
    return (low(grad),)
low.defvjp(low_keep, low_pass)
low_back.defvjp(back_keep, back_low)

def layer_norm(values, gain, shift):
    mean = lax.optimization_barrier(jnp.mean(values, axis=-1, keepdims=True))
    centred = values - mean
    spread = lax.optimization_barrier(jnp.mean(centred * centred, axis=-1, keepdims=True))
    return centred * lax.rsqrt(spread + eps) * gain + shift

def row_block(count):
    return 512 if count % 512 == 0 else count

def kept_layout(mask_row, seg_row, slots, clips):
    total = mask_row.shape[0]
    places = jnp.arange(total, dtype=jnp.int32)
    rank = (jnp.cumsum(mask_row) - 1).astype(jnp.int32)
    target = jnp.where(mask_row == 1, rank, slots).astype(jnp.int32)
    source = jnp.zeros((slots,), jnp.int32).at[target].set(places, mode='drop')
    kept_total = jnp.sum(mask_row).astype(jnp.int32)
    live = jnp.arange(slots, dtype=jnp.int32) < kept_total
    seg_kept = jnp.where(live, seg_row[source], clips).astype(jnp.int32)
    labels = jnp.arange(clips, dtype=jnp.int32)
    member = (seg_row[None, :] == labels[:, None]).astype(jnp.int32)
    counts = lax.optimization_barrier(jnp.sum(member * mask_row[None, :], axis=1)).astype(jnp.int32)
    inverse = 1.0 / jnp.maximum(counts, 1).astype(jnp.float32)
    pick = (seg_kept[:, None] == labels[None, :]).astype(jnp.float32)
    weight = lax.optimization_barrier(jnp.sum(pick * inverse[None, :], axis=1))
    return (source, live, seg_kept, weight)

def attention(queries, keys, values, seg_rows):
    count = queries.shape[0]
    step = row_block(count)
    scale = queries.shape[2] ** (-0.5)

    def one_block(start):
        q_part = lax.dynamic_slice_in_dim(queries, start, step, 0)
        s_part = lax.dynamic_slice_in_dim(seg_rows, start, step, 0)
        scores = low_back(jnp.einsum('qhd,khd->hqk', q_part, keys, precision=highest) * scale)
        same = s_part[:, None] == seg_rows[None, :]
        probs = jax.nn.softmax(jnp.where(same[None], scores, minus_big), axis=-1)
        return jnp.einsum('hqk,khd->qhd', low(probs), values, precision=highest)
    starts = jnp.arange(count // step, dtype=jnp.int32) * step
    mixed = lax.map(jax.checkpoint(one_block), starts)
    return mixed.reshape(queries.shape)

def teacher_home(x_rows, seg_row, params):
    gain1, shift1, qkv, qv_bias, out_w, out_b, gain2, shift2, fc1, fc1_b, fc2, fc2_b = params
    count = x_rows.shape[0]
    heads_all = qkv.shape[2] // HD
    normed = low(layer_norm(x_rows, gain1, shift1))
    proj = jnp.einsum('td,pdc->ptc', normed, qkv, precision=highest)
    query = low(proj[0] + qv_bias[0]).reshape(count, heads_all, HD)
    key_rows = low(proj[1]).reshape(count, heads_all, HD)
    value = low(proj[2] + qv_bias[1]).reshape(count, heads_all, HD)
    ctx = low(attention(query, key_rows, value, seg_row).reshape(count, -1))
    group = out_w.shape[0] // N_MP
    parts = jnp.einsum('tgc,gcd->gtd', ctx.reshape(count, N_MP, group), out_w.reshape(N_MP, group, -1), precision=highest)
    resid = x_rows + lax.optimization_barrier(jnp.sum(low(parts), axis=0)) + out_b
    normed2 = low(layer_norm(resid, gain2, shift2))
    hidden = low(jax.nn.gelu(jnp.dot(normed2, fc1, precision=highest) + fc1_b, approximate=False))
    return resid + jnp.dot(hidden, fc2, precision=highest) + fc2_b

def student_forward(params, inputs, segs, targets, row_weights):
    gain1, shift1, qkv, qv_bias, out_w, out_b, gain2, shift2, fc1, fc1_b, fc2, fc2_b, head_w, head_b = params
    homes, count, width = inputs.shape
    heads_all = qkv.shape[2] // HD

    def home_attend(pair):
        x_rows, seg_rows = pair
        normed = low(layer_norm(x_rows, gain1, shift1))
        proj = jnp.einsum('td,pdc->ptc', normed, qkv, precision=highest)
        query = low(low_back(proj[0] + qv_bias[0])).reshape(count, heads_all, HD)
        key_rows = low(low_back(proj[1])).reshape(count, heads_all, HD)
        value = low(low_back(proj[2] + qv_bias[1])).reshape(count, heads_all, HD)
        ctx = low(low_back(attention(query, key_rows, value, seg_rows).reshape(count, -1)))
        return x_rows + jnp.dot(ctx, out_w, precision=highest) + out_b
    resid = lax.map(home_attend, (inputs, segs))
    sent = low(low_back(resid.reshape(-1, width)))
    normed2 = low(layer_norm(sent, gain2, shift2))
    pre = low_back(jnp.dot(normed2, fc1, precision=highest) + fc1_b)
    hidden = low(jax.nn.gelu(pre, approximate=False))
    out = low(low_back(sent + jnp.dot(hidden, fc2, precision=highest) + fc2_b))
    guess = low_back(jnp.dot(out, head_w, precision=highest) + head_b)
    miss = guess - targets
    loss = 0.5 * jnp.sum(row_weights[:, None] * miss * miss)
    return (loss, out)

def reference(teacher_in, segment_ids, keep_mask, block_owner, student_in, t_norm1_gain, t_norm1_shift, t_qkv, t_qv_bias, t_out, t_out_bias, t_norm2_gain, t_norm2_shift, t_fc1, t_fc1_bias, t_fc2, t_fc2_bias, s_norm1_gain, s_norm1_shift, s_qkv, s_qv_bias, s_out, s_out_bias, s_norm2_gain, s_norm2_shift, s_fc1, s_fc1_bias, s_fc2, s_fc2_bias, head_weight, head_bias):
    rows = KB * BLK
    sources, lives, segs, weights = jax.vmap(lambda m, s: kept_layout(m, s, rows, CLIPS))(keep_mask, segment_ids)
    teach = tuple((w.astype(jnp.float32) for w in (t_norm1_gain, t_norm1_shift, t_qkv, t_qv_bias, t_out, t_out_bias, t_norm2_gain, t_norm2_shift, t_fc1, t_fc1_bias, t_fc2, t_fc2_bias)))
    homes_in = teacher_in.astype(jnp.float32).reshape(N_DP, TOK_HOME, DT)
    params = tuple((w.astype(jnp.float32) for w in (s_norm1_gain, s_norm1_shift, s_qkv, s_qv_bias, s_out, s_out_bias, s_norm2_gain, s_norm2_shift, s_fc1, s_fc1_bias, s_fc2, s_fc2_bias, head_weight, head_bias)))
    inputs = student_in.astype(jnp.float32).reshape(N_DP, rows, DS)
    flat_weights = weights.reshape(-1)

    def one_home(pack):
        x_rows, seg_row, source, live = pack
        final = teacher_home(x_rows, seg_row, teach)
        return low(jnp.where(live[:, None], final[source], 0.0))

    def forward(values_params, values_in):
        targets = lax.map(one_home, (homes_in, segment_ids, sources, lives)).reshape(-1, DT)
        return student_forward(values_params, values_in, segs, targets, flat_weights)
    (loss, out), pullback = jax.vjp(forward, params, inputs)
    grads, grad_inputs = pullback((jnp.ones((), jnp.float32), jnp.zeros_like(out)))
    flat = block_owner.reshape(-1)
    names = jnp.arange(N_DP, dtype=jnp.int32)
    hits = (flat[:, None] == names[None, :]).astype(jnp.int32)
    rank = lax.optimization_barrier(jnp.sum((jnp.cumsum(hits, axis=0) - hits) * hits, axis=1)).astype(jnp.int32)
    dest = jnp.where(flat >= 0, flat * OWN + rank, N_DP * OWN).astype(jnp.int32)
    table = jnp.zeros((N_DP * OWN,), jnp.int32).at[dest].set(jnp.arange(N_DP * KB, dtype=jnp.int32), mode='drop')
    student_out = out.reshape(N_DP * KB, BLK, DS)[table].astype(jnp.bfloat16)
    return (loss, student_out, grad_inputs.reshape(N_DP * KB, BLK, DS), grads[0], grads[1], grads[2], grads[3], grads[4], grads[5], grads[6], grads[7], grads[8], grads[9], grads[10], grads[11], grads[12], grads[13])
```

```python
import functools

import jax
import jax.numpy as jnp
from jax import lax
from jax.experimental import pallas as pl
from jax.experimental.pallas import tpu as pltpu
from jax.sharding import PartitionSpec as P

HD = 64
OWN = 8
CLIPS = 8
EPS = 1e-05
BIG = -1e30
F32 = jnp.float32
BF = jnp.bfloat16
LIMIT = 52 * 2**20

ORD, CUM, END, LOW = 0, 4, 12, 20


def dot_nn(a, b):
    return lax.dot_general(a, b, (((1,), (0,)), ((), ())), preferred_element_type=F32)


def dot_nt(a, b):
    return lax.dot_general(a, b, (((1,), (1,)), ((), ())), preferred_element_type=F32)


def dot_tn(a, b):
    return lax.dot_general(a, b, (((0,), (0,)), ((), ())), preferred_element_type=F32)


def unit(values):
    mean = jnp.mean(values, axis=-1, keepdims=True)
    centred = values - mean
    spread = jnp.mean(centred * centred, axis=-1, keepdims=True)
    inverse = lax.rsqrt(spread + EPS)
    return centred * inverse, inverse


def norm_low(values, gain_ref, shift_ref):
    u, _ = unit(values)
    return (u * gain_ref[...].astype(F32) + shift_ref[...].astype(F32)).astype(BF)


def whole(shape):
    return pl.BlockSpec(shape, lambda *_: (0,) * len(shape))


def call(kernel, name, grid, in_specs, out_specs, out_shape, args, scratch=(), flops=0, scalars=None):
    moved = sum(a.size * a.dtype.itemsize for a in args)
    moved += sum(s.size * jnp.dtype(s.dtype).itemsize for s in jax.tree.leaves(out_shape))
    params = pltpu.CompilerParams(
        dimension_semantics=("arbitrary",) * len(grid), vmem_limit_bytes=LIMIT
    )
    cost = pl.CostEstimate(flops=int(flops), bytes_accessed=int(moved), transcendentals=0)
    lead = 0 if scalars is None else 1
    spec = pltpu.PrefetchScalarGridSpec(
        num_scalar_prefetch=lead,
        grid=grid,
        in_specs=in_specs,
        out_specs=out_specs,
        scratch_shapes=list(scratch),
    )
    run = pl.pallas_call(
        kernel,
        grid_spec=spec,
        out_shape=out_shape,
        compiler_params=params,
        cost_estimate=cost,
        name=name,
    )
    return run(*([scalars] if lead else []), *args)


def sds(shape, dtype):
    return jax.ShapeDtypeStruct(shape, dtype)


def group_of(index, sc, base):
    group = jnp.zeros(index.shape, jnp.int32)
    for c in range(CLIPS):
        group = group + (index >= sc[base + c]).astype(jnp.int32)
    return group


def teacher_kv_kernel(x_ref, g_ref, s_ref, w_ref, b_ref, k_ref, v_ref):
    a = norm_low(x_ref[...].astype(F32), g_ref, s_ref)
    k_ref[...] = dot_nn(a, w_ref[1]).astype(BF)
    v_ref[...] = (dot_nn(a, w_ref[2]) + b_ref[1:2, :].astype(F32)).astype(BF)


def teacher_q_kernel(slots, block, step, sc, x_ref, rank_ref, g_ref, s_ref, w_ref, b_ref, xk_ref, q_ref, acc):
    j = pl.program_id(0)
    pieces, nb, piece, width = xk_ref.shape
    rows = pieces * nb * piece

    def slot_of(lanes):
        row = lax.broadcasted_iota(jnp.int32, (rows, lanes), 0)
        part = row // (nb * piece)
        inner = row % (nb * piece)
        order = jnp.zeros((rows, lanes), jnp.int32)
        for p in range(pieces):
            order = jnp.where(part == p, sc[ORD + p], order)
        return (j * nb + inner // piece) * block + order * piece + inner % piece

    slot = slot_of(step)
    acc[...] = jnp.zeros_like(acc)

    def one(t, _):
        hit = jnp.where(slot == rank_ref[pl.ds(t, 1), :], 1.0, 0.0).astype(BF)
        acc[...] += dot_nn(hit, x_ref[pl.ds(pl.multiple_of(t * step, step), step), :])
        return 0

    steps = slots // nb
    lax.fori_loop(sc[LOW + j], sc[LOW + steps + j], one, 0)
    kept = acc[...]
    xk_ref[...] = kept.astype(BF).reshape(xk_ref.shape)
    a = norm_low(kept, g_ref, s_ref)
    q = (dot_nn(a, w_ref[0]) + b_ref[0:1, :].astype(F32)).astype(BF)
    slot128 = slot_of(128)
    lane = lax.broadcasted_iota(jnp.int32, (rows, 128), 1)
    other = (lane != group_of(slot128, sc, CUM)) & (lane <= CLIPS)
    mask = jnp.where(other, BIG, 0.0).astype(BF)
    pairs = q.shape[1] // 128
    out = []
    for p in range(pairs):
        out += [q[:, 128 * p : 128 * (p + 1)], mask]
    q_ref[...] = jnp.concatenate(out, axis=1).reshape(q_ref.shape)


def teacher_attend_kernel(sc, q_ref, k_ref, v_ref, ctx_ref, kaug, vaug):
    keys, width = k_ref.shape
    heads = width // HD

    @pl.when(pl.program_id(0) == 0)
    def _():
        token = lax.broadcasted_iota(jnp.int32, (keys, 128), 0)
        lane = lax.broadcasted_iota(jnp.int32, (keys, 128), 1)
        hot = jnp.where(lane == group_of(token, sc, END), 1.0, 0.0).astype(BF)
        for h in range(heads):
            pair = h // 2
            mine = (lane // HD) == (h % 2)
            k = k_ref[:, 128 * pair : 128 * (pair + 1)].astype(F32)
            v = v_ref[:, 128 * pair : 128 * (pair + 1)].astype(F32)
            kaug[h, :, :128] = jnp.where(mine, k * (HD**-0.5), 0.0).astype(BF)
            kaug[h, :, 128:] = hot
            vaug[h] = jnp.where(mine, v, 0.0).astype(BF)

    pieces, nb, piece, both = q_ref.shape
    rows = pieces * nb * piece
    q = q_ref[...].reshape(rows, both)
    for pair in range(heads // 2):
        part = q[:, 256 * pair : 256 * (pair + 1)]
        total = jnp.zeros((rows, 128), F32)
        for h in (2 * pair, 2 * pair + 1):
            s = dot_nt(part, kaug[h])
            top = jnp.max(s, axis=1, keepdims=True)
            e = jnp.exp(s - top)
            under = 1.0 / jnp.sum(e, axis=1, keepdims=True)
            total += dot_nn(e.astype(BF), vaug[h]) * under
        ctx_ref[:, :, :, 128 * pair : 128 * (pair + 1)] = total.astype(BF).reshape(pieces, nb, piece, 128)


def student_qkv_kernel(block, used, sc, x_ref, g_ref, s_ref, w_ref, b_ref, xo_ref, a_ref, q_ref, k_ref, v_ref):
    slots, _, piece, width = x_ref.shape
    rows = slots * piece
    x = x_ref[...].reshape(rows, width)
    xo_ref[...] = x
    a = norm_low(x.astype(F32), g_ref, s_ref)
    a_ref[...] = a
    wide = q_ref.shape[1]
    row = lax.broadcasted_iota(jnp.int32, (rows, wide), 0)
    lane = lax.broadcasted_iota(jnp.int32, (rows, wide), 1)
    slot = (row // piece) * block + sc[ORD + pl.program_id(0)] * piece + row % piece
    same = (lane - used) == group_of(slot, sc, CUM)
    other = jnp.logical_not(same) & (lane >= used) & (lane <= used + CLIPS)
    q = (dot_nn(a, w_ref[0]) + b_ref[0:1, :].astype(F32)).astype(BF)
    q_ref[...] = jnp.where(other, BIG, q.astype(F32)).astype(BF)
    k = dot_nn(a, w_ref[1]).astype(BF).astype(F32) * (HD**-0.5)
    k_ref[...] = jnp.where(same, 1.0, k).astype(BF)
    v_ref[...] = (dot_nn(a, w_ref[2]) + b_ref[1:2, :].astype(F32)).astype(BF)


def three(value):
    high = value.astype(BF).astype(F32)
    middle = (value - high).astype(BF).astype(F32)
    return high, middle, value - high - middle


def put_three(base, lane, used, values):
    for h, value in enumerate(values):
        for i, part in enumerate(three(value)):
            base = jnp.where(lane == used + 16 + 8 * i + h, -part, base)
    return base


def one_lanes(lane, used, h):
    hit = lane == used + 16 + h
    return hit | (lane == used + 24 + h) | (lane == used + 32 + h)


def student_attend_kernel(used, q_ref, k_ref, v_ref, ctx_ref, mixed_ref, qb_ref, kaug, vaug):
    keys, wide = k_ref.shape
    heads = used // HD

    @pl.when(pl.program_id(0) == 0)
    def _():
        lane = lax.broadcasted_iota(jnp.int32, (keys, wide), 1)
        k = k_ref[...].astype(F32)
        v = v_ref[...].astype(F32)
        for h in range(heads):
            mine = (lane // HD) == h
            kaug[h] = jnp.where(mine | (lane >= used), k, 0.0).astype(BF)
            vaug[h] = jnp.where(mine, v, 0.0).astype(BF)

    q = q_ref[...]
    rows = q.shape[0]
    total = jnp.zeros((rows, wide), F32)
    logs = []
    for h in range(heads):
        s = dot_nt(q, kaug[h])
        top = jnp.max(s, axis=1, keepdims=True)
        e = jnp.exp(s - top)
        mass = jnp.sum(e, axis=1, keepdims=True)
        total += dot_nn(e.astype(BF), vaug[h]) * (1.0 / mass)
        logs.append(top + jnp.log(mass))
    mixed_ref[...] = total
    ctx_ref[...] = total[:, :used].astype(BF)
    lane = lax.broadcasted_iota(jnp.int32, (rows, wide), 1)
    qb_ref[...] = put_three(q.astype(F32), lane, used, logs).astype(BF)


def student_back_kernel(used, ds_ref, w_ref, mixed_ref, qb_ref, k_ref, v_ref, kt_ref, out_ref, sums_ref, kaug, vaug, dk, dv, dqs):
    keys, wide = k_ref.shape
    heads = used // HD
    j = pl.program_id(0)
    steps = pl.num_programs(0)

    @pl.when(j == 0)
    def _():
        lane = lax.broadcasted_iota(jnp.int32, (keys, wide), 1)
        k = k_ref[...].astype(F32)
        v = v_ref[...].astype(F32)
        for h in range(heads):
            mine = (lane // HD) == h
            ones = one_lanes(lane, used, h)
            keep = mine | ((lane >= used) & (lane <= used + CLIPS))
            kaug[h] = jnp.where(ones, 1.0, jnp.where(keep, k, 0.0)).astype(BF)
            vaug[h] = jnp.where(ones, 1.0, jnp.where(mine, v, 0.0)).astype(BF)
        dk[...] = jnp.zeros_like(dk)
        dv[...] = jnp.zeros_like(dv)
        dqs[...] = jnp.zeros_like(dqs)

    qb = qb_ref[...]
    rows = qb.shape[0]
    lane = lax.broadcasted_iota(jnp.int32, (rows, wide), 1)
    da = dot_nt(ds_ref[...], w_ref[...]).astype(BF).astype(F32)
    product = da * mixed_ref[...]
    deltas = [
        jnp.sum(jnp.where((lane // HD) == h, product, 0.0), axis=1, keepdims=True)
        for h in range(heads)
    ]
    daug = put_three(da, lane, used, deltas).astype(BF)
    qf = qb.astype(F32)
    grads_q = []
    for h in range(heads):
        mine = (lane // HD) == h
        pt = jnp.exp(dot_nt(kaug[h], qb))
        dpt = dot_nt(vaug[h], daug)
        dst = (pt * dpt).astype(BF)
        dv[...] += dot_nn(pt.astype(BF), jnp.where(mine, da, 0.0).astype(BF))
        dk[...] += dot_nn(dst, jnp.where(mine, qf, 0.0).astype(BF))
        grads_q.append(dot_nn(kt_ref[HD * h : HD * (h + 1), :], dst))
    grads_q.append(jnp.zeros((wide - used, rows), F32))
    dq = jnp.concatenate(grads_q, axis=0).T.astype(BF)
    out_ref[pl.ds(pl.multiple_of(j * rows, rows), rows), 0:wide] = dq
    dqs[...] += jnp.sum(dq.astype(F32), axis=0, keepdims=True)

    @pl.when(j == steps - 1)
    def _():
        out_ref[:, wide : 2 * wide] = (dk[...] * (HD**-0.5)).astype(BF)
        low = dv[...].astype(BF)
        out_ref[:, 2 * wide : 3 * wide] = low
        sums_ref[...] = jnp.concatenate(
            [dqs[...], jnp.sum(low.astype(F32), axis=0, keepdims=True)], axis=0
        )


def gelu_both(pre):
    phi = 0.5 * (1.0 + lax.erf(pre * 0.7071067811865476))
    return pre * phi, phi + pre * (0.3989422804014327 * jnp.exp(-0.5 * pre * pre))


def flipped(ref, lo, hi):
    half = ref.shape[0] // 2
    return jnp.concatenate([ref[half:, lo:hi], ref[:half, lo:hi]], axis=0)


def forward_kernel(
    student, half_steps,
    near_ref, far_ref, w0, w1, w2, w3, x_ref, ob_ref, g_ref, s_ref,
    f1a, f1b, b1a, b1b, f2a, f2b, b2_ref, *rest,
):
    if student:
        send_ref, own_ref, sent_ref, a2_ref, act_ref, slope_ref, a2, acc, base = rest
    else:
        send_ref, own_ref, a2, acc, base = rest
    j = pl.program_id(0)
    rows = x_ref.shape[0]

    @pl.when(j == 0)
    def _():
        c = w0.shape[0]
        parts = [
            dot_nn(near_ref[:, :c], w0[...]),
            dot_nn(near_ref[:, c : 2 * c], w1[...]),
            dot_nn(flipped(far_ref, 0, c), w2[...]),
            dot_nn(flipped(far_ref, c, 2 * c), w3[...]),
        ]
        if not student:
            parts = [p.astype(BF).astype(F32) for p in parts]
        resid = x_ref[...].astype(F32) + (parts[0] + parts[1] + parts[2] + parts[3])
        resid = resid + ob_ref[...].astype(F32)
        if student:
            low = resid.astype(BF)
            sent_ref[...] = low
            resid = low.astype(F32)
        a2[...] = norm_low(resid, g_ref, s_ref)
        if student:
            a2_ref[...] = a2[...]
        base[...] = resid[: rows // 2] + b2_ref[...].astype(F32)
        acc[...] = jnp.zeros_like(acc)

    def half(f1, b1, f2):
        pre = dot_nn(a2[...], f1[...]) + b1[...].astype(F32)
        if student:
            act, slope = gelu_both(pre)
            slope_ref[...] = slope
        else:
            act = pre * (0.5 * (1.0 + lax.erf(pre * 0.7071067811865476)))
        act = act.astype(BF)
        if student:
            act_ref[...] = act
        acc[...] += dot_nn(act, f2[...])

    @pl.when(j < half_steps)
    def _():
        half(f1a, b1a, f2a)

    @pl.when(j >= half_steps)
    def _():
        half(f1b, b1b, f2b)

    @pl.when(j == 2 * half_steps - 1)
    def _():
        own_ref[...] = acc[: rows // 2] + base[...]
        send_ref[...] = acc[rows // 2 :].astype(BF)


def forward(student, near, far, w_out, x, out_b, gain, shift, f1, b1, f2, b2, chunk):
    rows, width = near.shape[0], x.shape[1]
    hidden = f1[0].shape[1]
    n = hidden // chunk
    first = lambda j: jnp.minimum(j, n - 1)
    second = lambda j: jnp.maximum(j - n, 0)
    specs = [whole(near.shape), whole(far.shape)] + [whole(w.shape) for w in w_out]
    specs += [pl.BlockSpec((rows, width), lambda j: (0, 0))] + [whole((1, width))] * 3
    specs += [pl.BlockSpec((width, chunk), lambda j, f=f: (0, f(j))) for f in (first, second)]
    specs += [pl.BlockSpec((1, chunk), lambda j, f=f: (0, f(j))) for f in (first, second)]
    specs += [pl.BlockSpec((chunk, width), lambda j, f=f: (f(j), 0)) for f in (first, second)]
    specs += [whole((1, width))]
    half = rows // 2
    outs = [sds((half, width), BF), sds((half, width), F32)]
    out_specs = [whole((half, width))] * 2
    if student:
        outs += [sds((rows, width), BF)] * 2 + [sds((rows, 2 * hidden), BF), sds((rows, 2 * hidden), F32)]
        out_specs += [whole((rows, width))] * 2 + [pl.BlockSpec((rows, chunk), lambda j: (0, j))] * 2
    return call(
        functools.partial(forward_kernel, student, n),
        "student_forward" if student else "teacher_forward",
        (2 * n,),
        specs,
        out_specs,
        outs,
        (near, far, *w_out, x, out_b, gain, shift, *f1, *b1, *f2, b2),
        scratch=[pltpu.VMEM((rows, width), BF), pltpu.VMEM((rows, width), F32), pltpu.VMEM((half, width), F32)],
        flops=2 * rows * width * (4 * w_out[0].shape[0] + 4 * hidden),
    )


def head_kernel(block, sc, own_ref, recv_ref, out_ref, w_ref, b_ref, inv_ref, dg_ref, do_ref, loss_ref, hb_ref, ob_ref):
    rows, width = own_ref.shape
    target = (own_ref[...] + recv_ref[...].astype(F32)).astype(BF).astype(F32)
    row = lax.broadcasted_iota(jnp.int32, (rows, 1), 0)
    piece = block // 4
    slot = (row // piece) * block + sc[ORD] * piece + row % piece
    live = slot < sc[CUM + CLIPS - 1]
    group = group_of(slot, sc, CUM)
    weight = jnp.zeros((rows, 1), F32)
    for c in range(CLIPS):
        weight = jnp.where(group == c, inv_ref[0, c], weight)
    weight = jnp.where(live, weight, 0.0)
    target = jnp.where(live, target, 0.0)
    miss = dot_nn(out_ref[...], w_ref[...]) + b_ref[...].astype(F32) - target
    dg = (weight * miss).astype(BF)
    dg_ref[...] = dg
    loss_ref[...] = 0.5 * jnp.sum(weight * miss * miss, axis=0, keepdims=True)
    hb_ref[...] = jnp.sum(dg.astype(F32), axis=0, keepdims=True)
    do = dot_nt(dg, w_ref[...]).astype(BF)
    do_ref[...] = do
    ob_ref[...] = jnp.sum(do.astype(F32), axis=0, keepdims=True)


def feed_back_kernel(d0, d1, act_ref, slope_ref, a2_ref, f1a, f1b, f2a, f2b,
                     g1_ref, g1s_ref, g2_ref, g2s_ref, own_ref, send_ref, gb_ref, d, acc):
    j = pl.program_id(0)
    half = d0.shape[0]

    @pl.when(j == 0)
    def _():
        d[:half] = d0[...]
        d[half:] = d1[...]
        acc[...] = jnp.zeros_like(acc)

    def part(f1, f2, g1, g2):
        grad = d[...]
        dpre = (dot_nt(grad, f2[...]) * slope_ref[...]).astype(BF)
        gb_ref[...] = jnp.sum(dpre.astype(F32), axis=0, keepdims=True)
        acc[...] += dot_nt(dpre, f1[...])
        g2[...] = dot_tn(act_ref[...], grad).astype(g2.dtype)
        g1[...] = dot_tn(a2_ref[...], dpre).astype(g1.dtype)

    @pl.when(j == 0)
    def _():
        part(f1a, f2a, g1_ref, g2_ref)

    @pl.when(j == 1)
    def _():
        part(f1b, f2b, g1s_ref, g2s_ref)
        own_ref[...] = acc[:half]
        send_ref[...] = acc[half:].astype(BF)


def norm_back_kernel(own_ref, recv_ref, base_ref, x_ref, g_ref, dx_ref, sums_ref):
    d = own_ref[...].astype(F32) + recv_ref[...].astype(F32)
    u, inverse = unit(x_ref[...].astype(F32))
    e = g_ref[...].astype(F32) * d
    mean_e = jnp.mean(e, axis=-1, keepdims=True)
    mean_eu = jnp.mean(e * u, axis=-1, keepdims=True)
    dx = base_ref[...].astype(F32) + (e - mean_e - u * mean_eu) * inverse
    dx = dx.astype(dx_ref.dtype)
    dx_ref[...] = dx
    sums_ref[...] = jnp.concatenate(
        [
            jnp.sum(d * u, axis=0, keepdims=True),
            jnp.sum(d, axis=0, keepdims=True),
            jnp.sum(dx.astype(F32), axis=0, keepdims=True),
        ],
        axis=0,
    )


def norm_back(name, own, recv, base, x, gain, dtype):
    rows, width = own.shape
    half = pl.BlockSpec((rows, width), lambda *_: (0, 0))
    return call(
        norm_back_kernel, name, (1,),
        [half] * 4 + [whole((1, width))],
        [half, whole((3, width))],
        [sds((rows, width), dtype), sds((3, width), F32)],
        (own, recv, base, x, gain),
    )


def swap(x, bit, count):
    return lax.ppermute(x, "mp", [(i, i ^ bit) for i in range(count)])


def row(vector):
    return vector.reshape(1, -1)


def layout(mask_row, seg_row, order, steps, span):
    tokens = mask_row.shape[0]
    grid = mask_row.reshape(tokens // 128, 128).astype(BF)
    upper = (jnp.arange(128)[:, None] <= jnp.arange(128)[None, :]).astype(BF)
    within = jnp.dot(grid, upper, preferred_element_type=F32)
    lines = tokens // 128
    lower = (jnp.arange(lines)[:, None] > jnp.arange(lines)[None, :]).astype(BF)
    ahead = jnp.dot(lower, within[:, 127:].astype(BF), preferred_element_type=F32)
    count = (within + ahead).astype(jnp.int32).reshape(tokens)
    rank = jnp.where(mask_row == 1, count - 1, -1)
    labels = jnp.arange(CLIPS, dtype=jnp.int32)
    upto = (seg_row[None, :] <= labels[:, None]).astype(jnp.int32)
    ends = jnp.sum(upto, axis=1)
    cum = jnp.sum(upto * mask_row[None, :], axis=1)
    edge = jnp.arange(steps, dtype=jnp.int32) * span
    low = jnp.sum((count[None, :] <= edge[:, None]).astype(jnp.int32), axis=1)
    high = jnp.sum((count[None, :] < edge[:, None] + span).astype(jnp.int32), axis=1)
    low = low // span
    high = jnp.minimum(high, tokens - 1) // span + 1
    each = cum - jnp.concatenate([jnp.zeros((1,), jnp.int32), cum[:-1]])
    inverse = 1.0 / jnp.maximum(each, 1).astype(F32)
    scalars = jnp.concatenate([order, cum, ends, low, high])
    return rank.reshape(tokens // span, span), scalars, inverse.reshape(1, CLIPS)


def body(
    teacher_in, segment_ids, keep_mask, block_owner, student_in,
    t_norm1_gain, t_norm1_shift, t_qkv, t_qv_bias, t_out, t_out_bias,
    t_norm2_gain, t_norm2_shift, t_fc1, t_fc1_bias, t_fc2, t_fc2_bias,
    s_norm1_gain, s_norm1_shift, s_qkv, s_qv_bias, s_out, s_out_bias,
    s_norm2_gain, s_norm2_shift, s_fc1, s_fc1_bias, s_fc2, s_fc2_bias,
    head_weight, head_bias,
):
    mp = lax.axis_size("mp")
    me = lax.axis_index("mp")
    homes = lax.axis_size("dp")
    home = lax.axis_index("dp")
    slots, block, width = student_in.shape
    piece = block // mp
    rows = slots * block
    mine = rows // mp
    near = 2 * mine
    tokens, t_width = teacher_in.shape
    used = s_qkv.shape[2]
    wide = 256
    nb = 2
    span = nb * block
    steps = slots // nb
    core = lambda x: swap(x, 1, mp)
    across = lambda x: swap(x, 2, mp)

    order = jnp.stack([me, me ^ 2, me ^ 1, me ^ 3]).astype(jnp.int32)
    mask_row = lax.dynamic_index_in_dim(keep_mask, home, 0, keepdims=False)
    seg_row = lax.dynamic_index_in_dim(segment_ids, home, 0, keepdims=False)
    rank, scalars, inverse = layout(mask_row, seg_row, order, steps, span)

    t_w2 = across(t_out)
    s_w2 = across(s_out)
    t_f1 = (t_fc1, core(t_fc1))
    t_f2 = (t_fc2, core(t_fc2))
    s_f1 = (s_fc1, core(s_fc1))
    s_f2 = (s_fc2, core(s_fc2))
    biases = core(jnp.concatenate([t_fc1_bias, s_fc1_bias]))
    t_b1 = (row(t_fc1_bias), row(biases[: t_fc1_bias.shape[0]]))
    s_b1 = (row(s_fc1_bias), row(biases[t_fc1_bias.shape[0] :]))
    t_w = (t_out, core(t_out), t_w2, core(t_w2))
    s_w = (s_out, core(s_out), s_w2, core(s_w2))

    w_pad = jnp.pad(s_qkv, ((0, 0), (0, 0), (0, wide - used)))
    b_pad = jnp.pad(s_qv_bias, ((0, 0), (0, wide - used)))
    x4 = student_in.reshape(slots, mp, piece, width)
    by_piece = lambda w: pl.BlockSpec((mine, w), lambda k, sc: (k, 0))
    x_stud, a_stud, sq, sk, sv = call(
        functools.partial(student_qkv_kernel, block, used), "student_qkv", (mp,),
        [
            pl.BlockSpec((slots, 1, piece, width), lambda k, sc: (0, sc[ORD + k], 0, 0)),
            whole((1, width)), whole((1, width)), whole(w_pad.shape), whole(b_pad.shape),
        ],
        [by_piece(width)] * 2 + [by_piece(wide)] * 3,
        [sds((rows, width), BF)] * 2 + [sds((rows, wide), BF)] * 3,
        (x4, row(s_norm1_gain), row(s_norm1_shift), w_pad, b_pad),
        flops=2 * rows * width * 3 * wide, scalars=scalars,
    )
    heads = used // HD
    qrows = 256
    by_rows = lambda w: pl.BlockSpec((qrows, w), lambda j: (j, 0))
    ctx, mixed, qb = call(
        functools.partial(student_attend_kernel, used), "student_attend", (rows // qrows,),
        [by_rows(wide), whole((rows, wide)), whole((rows, wide))],
        [by_rows(used), by_rows(wide), by_rows(wide)],
        [sds((rows, used), BF), sds((rows, wide), F32), sds((rows, wide), BF)],
        (sq, sk, sv),
        scratch=[pltpu.VMEM((heads, rows, wide), BF)] * 2,
        flops=heads * rows * rows * wide * 4,
    )
    s_near = jnp.concatenate([ctx[:near], core(ctx[near:])], axis=1)
    s_far = across(s_near)

    by_512 = lambda w: pl.BlockSpec((512, w), lambda j: (j, 0))
    cols = t_qkv.shape[2]
    tk, tv = call(
        teacher_kv_kernel, "teacher_kv", (tokens // 512,),
        [by_512(t_width), whole((1, t_width)), whole((1, t_width)), whole(t_qkv.shape), whole(t_qv_bias.shape)],
        [by_512(cols)] * 2,
        [sds((tokens, cols), BF)] * 2,
        (teacher_in, row(t_norm1_gain), row(t_norm1_shift), t_qkv, t_qv_bias),
        flops=2 * tokens * t_width * 2 * cols,
    )
    by_slot = lambda w: pl.BlockSpec((mp, nb, piece, w), lambda j, sc: (0, j, 0, 0))
    x_kept, tq = call(
        functools.partial(teacher_q_kernel, slots, block, span), "teacher_q", (steps,),
        [
            whole(teacher_in.shape), whole(rank.shape), whole((1, t_width)), whole((1, t_width)),
            whole(t_qkv.shape), whole(t_qv_bias.shape),
        ],
        [by_slot(t_width), by_slot(2 * cols)],
        [sds((mp, slots, piece, t_width), BF), sds((mp, slots, piece, 2 * cols), BF)],
        (teacher_in, rank, row(t_norm1_gain), row(t_norm1_shift), t_qkv, t_qv_bias),
        scratch=[pltpu.VMEM((span, t_width), F32)],
        flops=2 * rows * t_width * (cols + 512), scalars=scalars,
    )
    t_ctx = call(
        teacher_attend_kernel, "teacher_attend", (steps,),
        [by_slot(2 * cols), whole((tokens, cols)), whole((tokens, cols))],
        by_slot(cols),
        sds((mp, slots, piece, cols), BF),
        (tq, tk, tv),
        scratch=[pltpu.VMEM((cols // HD, tokens, 256), BF), pltpu.VMEM((cols // HD, tokens, 128), BF)],
        flops=(cols // HD) * rows * tokens * (512 + 256), scalars=scalars,
    ).reshape(rows, cols)
    t_near = jnp.concatenate([t_ctx[:near], core(t_ctx[near:])], axis=1)
    t_far = across(t_near)

    s_send, s_own, sent, a2, act, slope = forward(
        True, s_near, s_far, s_w, x_stud, row(s_out_bias), row(s_norm2_gain), row(s_norm2_shift),
        s_f1, s_b1, s_f2, row(s_fc2_bias), s_fc1.shape[1],
    )
    out_rows = (s_own + across(s_send).astype(F32)).astype(BF)

    t_send, t_own = forward(
        False, t_near, t_far, t_w, x_kept.reshape(rows, t_width), row(t_out_bias), row(t_norm2_gain),
        row(t_norm2_shift), t_f1, t_b1, t_f2, row(t_fc2_bias), 512,
    )
    t_recv = across(t_send)

    owners = lax.dynamic_index_in_dim(block_owner, home, 0, keepdims=False)
    capacity = (slots + homes - 1) // homes
    labels = jnp.arange(homes, dtype=jnp.int32)
    hits = (owners[:, None] == labels[None, :]).astype(jnp.int32)
    order_in = jnp.sum((jnp.cumsum(hits, axis=0) - hits) * hits, axis=1)
    place = jnp.where(owners >= 0, owners * capacity + order_in, homes * capacity)
    pick = (jnp.arange(homes * capacity, dtype=jnp.int32)[:, None] == place[None, :]).astype(BF)
    outbound = jnp.dot(pick, out_rows.reshape(slots, piece * width), preferred_element_type=BF)
    inbound = lax.all_to_all(
        outbound.reshape(homes * capacity, piece, width), "dp", split_axis=0, concat_axis=0, tiled=True
    )
    per_source = jnp.sum((block_owner == home).astype(jnp.int32), axis=1)
    before = jnp.cumsum(per_source) - per_source
    lane = jnp.arange(capacity, dtype=jnp.int32)
    target_slot = jnp.where(lane[None, :] < per_source[:, None], before[:, None] + lane[None, :], OWN).reshape(-1)
    choose = (jnp.arange(OWN, dtype=jnp.int32)[:, None] == target_slot[None, :]).astype(BF)
    student_out = jnp.dot(
        choose, inbound.reshape(homes * capacity, piece * width), preferred_element_type=BF
    ).reshape(OWN, piece, width)

    d_guess, d_out, loss_row, head_b_row, fc2_b_row = call(
        functools.partial(head_kernel, block), "head", (1,),
        [
            whole((mine, t_width)), whole((mine, t_width)), whole((mine, width)), whole((width, t_width)),
            whole((1, t_width)), pl.BlockSpec(memory_space=pltpu.SMEM),
        ],
        [whole((mine, t_width)), whole((mine, width)), whole((1, t_width)), whole((1, t_width)), whole((1, width))],
        [sds((mine, t_width), BF), sds((mine, width), BF), sds((1, t_width), F32), sds((1, t_width), F32), sds((1, width), F32)],
        (t_own, t_recv, out_rows, head_weight, row(head_bias), inverse),
        flops=4 * mine * width * t_width, scalars=scalars,
    )
    d_out_far = across(d_out)
    g_head = dot_tn(out_rows, d_guess)

    hidden = s_fc1.shape[1]
    cut = pl.BlockSpec((near, hidden), lambda j: (0, j))
    g1, g1_send, g2, g2_send, da2_own, da2_send, b1_row = call(
        feed_back_kernel, "feed_back", (2,),
        [whole((mine, width))] * 2 + [cut, cut, whole((near, width))]
        + [whole((width, hidden))] * 2 + [whole((hidden, width))] * 2,
        [whole((width, hidden))] * 2 + [whole((hidden, width))] * 2 + [whole((mine, width))] * 2
        + [pl.BlockSpec((1, hidden), lambda j: (0, j))],
        [
            sds((width, hidden), F32), sds((width, hidden), BF), sds((hidden, width), F32), sds((hidden, width), BF),
            sds((mine, width), F32), sds((mine, width), BF), sds((1, 2 * hidden), F32),
        ],
        (d_out, d_out_far, act, slope, a2, *s_f1, *s_f2),
        scratch=[pltpu.VMEM((near, width), BF), pltpu.VMEM((near, width), F32)],
        flops=2 * near * width * hidden * 8,
    )
    da2_far = across(da2_send)
    d_sent, sums2 = norm_back("norm2_back", da2_own, da2_far, d_out, sent[:mine], row(s_norm2_gain), BF)

    side = me % 2
    level = me // 2
    half_rows = width // 2
    quarter = width // 4
    low_head = g_head.astype(BF)
    head_send = lax.dynamic_slice_in_dim(low_head, (1 - side) * half_rows, half_rows, 0)
    head_half = lax.dynamic_slice_in_dim(g_head, side * half_rows, half_rows, 0) + core(head_send).astype(F32)
    low_half = head_half.astype(BF)
    head_send2 = lax.dynamic_slice_in_dim(low_half, (1 - level) * quarter, quarter, 0)
    head_quarter = lax.dynamic_slice_in_dim(head_half, level * quarter, quarter, 0) + across(head_send2).astype(F32)

    g2_sum = (g2 + core(g2_send).astype(F32)).astype(BF)
    g1_sum = (g1 + core(g1_send).astype(F32)).astype(BF)
    head_all = lax.psum(head_quarter.astype(BF), "dp")
    g2_all = lax.psum(g2_sum, "dp")
    g1_all = lax.psum(g1_sum, "dp")

    ds_near = jnp.concatenate([d_sent, across(d_sent)], axis=0)
    ds = jnp.concatenate([ds_near, core(ds_near)], axis=0)
    so_pad = jnp.pad(s_out, ((0, wide - used), (0, 0)))
    k_turned = sk[:, :used].T
    d_qkv, qv_sums = call(
        functools.partial(student_back_kernel, used), "student_back", (rows // qrows,),
        [
            by_rows(width), whole((wide, width)), by_rows(wide), by_rows(wide), whole((rows, wide)),
            whole((rows, wide)), whole((used, rows)),
        ],
        [whole((rows, 3 * wide)), whole((2, wide))],
        [sds((rows, 3 * wide), BF), sds((2, wide), F32)],
        (ds, so_pad, mixed, qb, sk, sv, k_turned),
        scratch=[pltpu.VMEM((heads, rows, wide), BF)] * 2 + [pltpu.VMEM((rows, wide), F32)] * 2
        + [pltpu.VMEM((1, wide), F32)],
        flops=heads * rows * rows * wide * 9,
    )
    g_out = dot_tn(ctx, ds)
    w_line = jnp.transpose(w_pad, (0, 2, 1)).reshape(3 * wide, width)
    da1 = dot_nn(d_qkv, w_line)
    da1_near = da1[:near] + core(da1[near:].astype(BF)).astype(F32)
    da1_far = across(da1_near[mine:].astype(BF))
    g_qkv = dot_tn(a_stud, d_qkv).reshape(width, 3, wide)[:, :, :used]
    grad_in, sums1 = norm_back("norm1_back", da1_near[:mine], da1_far, d_sent, x_stud[:mine], row(s_norm1_gain), F32)

    fit = lambda v: jnp.pad(v, ((0, 0), (0, t_width - v.shape[1])))
    short = jnp.concatenate(
        [fit(sums1[:2]), fit(sums2), fit(fc2_b_row), head_b_row, loss_row, fit(b1_row[:, hidden:])], axis=0
    )
    short_in = core(short)
    short_own = jnp.concatenate([short[:8], fit(b1_row[:, :hidden])], axis=0) + short_in
    short_sum = short_own[:8] + across(short_own[:8])
    short_dp = jnp.concatenate([short_sum, short_own[8:], fit(qv_sums)], axis=0)
    qkv_all, out_all, short_all = lax.psum((g_qkv.astype(BF), g_out.astype(BF), short_dp.astype(BF)), "dp")

    head_other = across(head_all)
    head_pair = jnp.where(
        level == 0,
        jnp.concatenate([head_all, head_other], axis=0),
        jnp.concatenate([head_other, head_all], axis=0),
    )
    head_peer = core(head_pair)
    grad_head = jnp.where(
        side == 0,
        jnp.concatenate([head_pair, head_peer], axis=0),
        jnp.concatenate([head_peer, head_pair], axis=0),
    ).astype(F32)
    vec = short_all.astype(F32)
    return (
        jnp.sum(vec[7]),
        student_out,
        grad_in.reshape(slots, piece, width),
        vec[0, :width],
        vec[1, :width],
        jnp.transpose(qkv_all.astype(F32), (1, 0, 2)),
        vec[9:11, :used],
        out_all.astype(F32),
        vec[4, :width],
        vec[2, :width],
        vec[3, :width],
        g1_all.astype(F32),
        vec[8, :hidden],
        g2_all.astype(F32),
        vec[5, :width],
        grad_head,
        vec[6, :t_width],
    )


def solution(mesh):
    rep = P()
    in_specs = (
        P("dp", None), rep, rep, rep, P("dp", None, None), rep, rep, P(None, None, "mp"), P(None, "mp"),
        P("mp", None), rep, rep, rep, P(None, "mp"), P("mp"), P("mp", None), rep, rep, rep,
        P(None, None, "mp"), P(None, "mp"), P("mp", None), rep, rep, rep, P(None, "mp"), P("mp"),
        P("mp", None), rep, rep, rep,
    )
    out_specs = (
        rep, P("dp", "mp", None), P("dp", "mp", None), rep, rep, P(None, None, "mp"), P(None, "mp"),
        P("mp", None), rep, rep, rep, P(None, "mp"), P("mp"), P("mp", None), rep, rep, rep,
    )
    return jax.shard_map(body, mesh=mesh, in_specs=in_specs, out_specs=out_specs, check_vma=False)
```

```python
import functools

import jax
import jax.numpy as jnp
from jax import lax
from jax.experimental import pallas as pl
from jax.experimental.pallas import tpu as pltpu
from jax.sharding import PartitionSpec as P

HD = 64
OWN = 8
CLIPS = 8
EPS = 1e-05
BIG = -1e30
F32 = jnp.float32
BF = jnp.bfloat16
LIMIT = 52 * 2**20

ORD, CUM, END, LOW = 0, 4, 12, 20


def dot_nn(a, b):
    return lax.dot_general(a, b, (((1,), (0,)), ((), ())), preferred_element_type=F32)


def dot_nt(a, b):
    return lax.dot_general(a, b, (((1,), (1,)), ((), ())), preferred_element_type=F32)


def dot_tn(a, b):
    return lax.dot_general(a, b, (((0,), (0,)), ((), ())), preferred_element_type=F32)


def unit(values):
    mean = jnp.mean(values, axis=-1, keepdims=True)
    centred = values - mean
    spread = jnp.mean(centred * centred, axis=-1, keepdims=True)
    inverse = lax.rsqrt(spread + EPS)
    return centred * inverse, inverse


def norm_low(values, gain_ref, shift_ref):
    u, _ = unit(values)
    return (u * gain_ref[...].astype(F32) + shift_ref[...].astype(F32)).astype(BF)


def log2(size):
    return size.bit_length() - 1


def whole(shape):
    return pl.BlockSpec(shape, lambda *_: (0,) * len(shape))


def call(kernel, name, grid, in_specs, out_specs, out_shape, args, scratch=(), flops=0, scalars=None):
    moved = sum(a.size * a.dtype.itemsize for a in args)
    moved += sum(s.size * jnp.dtype(s.dtype).itemsize for s in jax.tree.leaves(out_shape))
    params = pltpu.CompilerParams(
        dimension_semantics=("arbitrary",) * len(grid), vmem_limit_bytes=LIMIT
    )
    cost = pl.CostEstimate(flops=int(flops), bytes_accessed=int(moved), transcendentals=0)
    lead = 0 if scalars is None else 1
    spec = pltpu.PrefetchScalarGridSpec(
        num_scalar_prefetch=lead,
        grid=grid,
        in_specs=in_specs,
        out_specs=out_specs,
        scratch_shapes=list(scratch),
    )
    run = pl.pallas_call(
        kernel,
        grid_spec=spec,
        out_shape=out_shape,
        compiler_params=params,
        cost_estimate=cost,
        name=name,
    )
    return run(*([scalars] if lead else []), *args)


def sds(shape, dtype):
    return jax.ShapeDtypeStruct(shape, dtype)


def group_of(index, sc, base):
    group = jnp.zeros(index.shape, jnp.int32)
    for c in range(CLIPS):
        group = group + (index >= sc[base + c]).astype(jnp.int32)
    return group


def teacher_kv_kernel(x_ref, g_ref, s_ref, w_ref, b_ref, k_ref, v_ref):
    a = norm_low(x_ref[...].astype(F32), g_ref, s_ref)
    k_ref[...] = dot_nn(a, w_ref[1]).astype(BF)
    v_ref[...] = (dot_nn(a, w_ref[2]) + b_ref[1:2, :].astype(F32)).astype(BF)


def teacher_q_kernel(slots, block, step, sc, x_ref, rank_ref, g_ref, s_ref, w_ref, b_ref, xk_ref, q_ref, acc):
    j = pl.program_id(0)
    pieces, nb, piece, width = xk_ref.shape
    rows = pieces * nb * piece

    line = lax.broadcasted_iota(jnp.int32, (rows, 1), 0)
    part = line >> log2(nb * piece)
    inner = line & (nb * piece - 1)
    order = jnp.zeros((rows, 1), jnp.int32)
    for p in range(pieces):
        order = jnp.where(part == p, sc[ORD + p], order)
    slot = (j * nb + (inner >> log2(piece))) * block + order * piece + (inner & (piece - 1))
    group = group_of(slot, sc, CUM)
    acc[...] = jnp.zeros_like(acc)

    def one(t, _):
        hit = jnp.where(slot == rank_ref[pl.ds(t, 1), :], 1.0, 0.0).astype(BF)
        acc[...] += dot_nn(hit, x_ref[pl.ds(pl.multiple_of(t * step, step), step), :])
        return 0

    steps = slots // nb
    lax.fori_loop(sc[LOW + j], sc[LOW + steps + j], one, 0)
    kept = acc[...]
    xk_ref[...] = kept.astype(BF).reshape(xk_ref.shape)
    a = norm_low(kept, g_ref, s_ref)
    q = (dot_nn(a, w_ref[0]) + b_ref[0:1, :].astype(F32)).astype(BF)
    lane = lax.broadcasted_iota(jnp.int32, (rows, 128), 1)
    other = (lane != group) & (lane <= CLIPS)
    mask = jnp.where(other, BIG, 0.0).astype(BF)
    pairs = q.shape[1] // 128
    out = []
    for p in range(pairs):
        out += [q[:, 128 * p : 128 * (p + 1)], mask]
    q_ref[...] = jnp.concatenate(out, axis=1).reshape(q_ref.shape)


def teacher_attend_kernel(sc, q_ref, k_ref, v_ref, ctx_ref, kaug, vaug):
    keys, width = k_ref.shape
    heads = width // HD

    @pl.when(pl.program_id(0) == 0)
    def _():
        token = lax.broadcasted_iota(jnp.int32, (keys, 1), 0)
        lane = lax.broadcasted_iota(jnp.int32, (keys, 128), 1)
        hot = jnp.where(lane == group_of(token, sc, END), 1.0, 0.0).astype(BF)
        for h in range(heads):
            pair = h // 2
            mine = (lane >> 6) == (h % 2)
            k = k_ref[:, 128 * pair : 128 * (pair + 1)].astype(F32)
            v = v_ref[:, 128 * pair : 128 * (pair + 1)].astype(F32)
            kaug[h, :, :128] = jnp.where(mine, k * (HD**-0.5), 0.0).astype(BF)
            kaug[h, :, 128:] = hot
            vaug[h] = jnp.where(mine, v, 0.0).astype(BF)

    pieces, nb, piece, both = q_ref.shape
    rows = pieces * nb * piece
    q = q_ref[...].reshape(rows, both)
    for pair in range(heads // 2):
        part = q[:, 256 * pair : 256 * (pair + 1)]
        total = jnp.zeros((rows, 128), F32)
        for h in (2 * pair, 2 * pair + 1):
            s = dot_nt(part, kaug[h])
            top = jnp.max(s, axis=1, keepdims=True)
            e = jnp.exp(s - top)
            under = 1.0 / jnp.sum(e, axis=1, keepdims=True)
            total += dot_nn(e.astype(BF), vaug[h]) * under
        ctx_ref[:, :, :, 128 * pair : 128 * (pair + 1)] = total.astype(BF).reshape(pieces, nb, piece, 128)


def student_qkv_kernel(block, used, sc, x_ref, g_ref, s_ref, w_ref, b_ref, xo_ref, a_ref, q_ref, k_ref, v_ref):
    slots, _, piece, width = x_ref.shape
    rows = slots * piece
    x = x_ref[...].reshape(rows, width)
    xo_ref[...] = x
    a = norm_low(x.astype(F32), g_ref, s_ref)
    a_ref[...] = a
    wide = q_ref.shape[1]
    line = lax.broadcasted_iota(jnp.int32, (rows, 1), 0)
    lane = lax.broadcasted_iota(jnp.int32, (rows, wide), 1)
    slot = (line >> log2(piece)) * block + sc[ORD + pl.program_id(0)] * piece + (line & (piece - 1))
    same = lane == group_of(slot, sc, CUM) + used
    other = jnp.logical_not(same) & (lane >= used) & (lane <= used + CLIPS)
    q = (dot_nn(a, w_ref[0]) + b_ref[0:1, :].astype(F32)).astype(BF)
    q_ref[...] = jnp.where(other, BIG, q.astype(F32)).astype(BF)
    k = dot_nn(a, w_ref[1]).astype(BF).astype(F32) * (HD**-0.5)
    k_ref[...] = jnp.where(same, 1.0, k).astype(BF)
    v_ref[...] = (dot_nn(a, w_ref[2]) + b_ref[1:2, :].astype(F32)).astype(BF)


def three(value):
    high = value.astype(BF).astype(F32)
    middle = (value - high).astype(BF).astype(F32)
    return high, middle, value - high - middle


def put_three(base, lane, used, values):
    for h, value in enumerate(values):
        for i, part in enumerate(three(value)):
            base = jnp.where(lane == used + 16 + 8 * i + h, -part, base)
    return base


def one_lanes(lane, used, h):
    hit = lane == used + 16 + h
    return hit | (lane == used + 24 + h) | (lane == used + 32 + h)


def student_attend_kernel(used, q_ref, k_ref, v_ref, ctx_ref, mixed_ref, qb_ref, kaug, vaug):
    keys, wide = k_ref.shape
    heads = used // HD

    @pl.when(pl.program_id(0) == 0)
    def _():
        lane = lax.broadcasted_iota(jnp.int32, (keys, wide), 1)
        k = k_ref[...].astype(F32)
        v = v_ref[...].astype(F32)
        for h in range(heads):
            mine = (lane >> 6) == h
            kaug[h] = jnp.where(mine | (lane >= used), k, 0.0).astype(BF)
            vaug[h] = jnp.where(mine, v, 0.0).astype(BF)

    q = q_ref[...]
    rows = q.shape[0]
    total = jnp.zeros((rows, wide), F32)
    logs = []
    for h in range(heads):
        s = dot_nt(q, kaug[h])
        top = jnp.max(s, axis=1, keepdims=True)
        e = jnp.exp(s - top)
        mass = jnp.sum(e, axis=1, keepdims=True)
        total += dot_nn(e.astype(BF), vaug[h]) * (1.0 / mass)
        logs.append(top + jnp.log(mass))
    mixed_ref[...] = total
    ctx_ref[...] = total[:, :used].astype(BF)
    lane = lax.broadcasted_iota(jnp.int32, (rows, wide), 1)
    qb_ref[...] = put_three(q.astype(F32), lane, used, logs).astype(BF)


def student_back_kernel(used, picked, ds_ref, w_ref, mixed_ref, qb_ref, k_ref, v_ref, kt_ref, out_ref, sums_ref, kaug, vaug, dk, dv, dqs):
    keys, wide = k_ref.shape
    j = pl.program_id(0)
    steps = pl.num_programs(0)
    lo, size = HD * picked[0], HD * len(picked)

    @pl.when(j == 0)
    def _():
        lane = lax.broadcasted_iota(jnp.int32, (keys, wide), 1)
        k = k_ref[...].astype(F32)
        v = v_ref[...].astype(F32)
        for i, h in enumerate(picked):
            mine = (lane >> 6) == h
            ones = one_lanes(lane, used, h)
            keep = mine | ((lane >= used) & (lane <= used + CLIPS))
            kaug[i] = jnp.where(ones, 1.0, jnp.where(keep, k, 0.0)).astype(BF)
            vaug[i] = jnp.where(ones, 1.0, jnp.where(mine, v, 0.0)).astype(BF)
        dk[...] = jnp.zeros_like(dk)
        dv[...] = jnp.zeros_like(dv)
        dqs[...] = jnp.zeros_like(dqs)

    qb = qb_ref[...]
    rows = qb.shape[0]
    lane = lax.broadcasted_iota(jnp.int32, (rows, wide), 1)
    da = dot_nt(ds_ref[...], w_ref[...]).astype(BF).astype(F32)
    product = da * mixed_ref[...]
    deltas = [
        jnp.sum(jnp.where((lane >> 6) == h, product, 0.0), axis=1, keepdims=True)
        if h in picked
        else jnp.zeros((rows, 1), F32)
        for h in range(used // HD)
    ]
    daug = put_three(da, lane, used, deltas).astype(BF)
    qf = qb.astype(F32)
    grads_q = []
    for i, h in enumerate(picked):
        mine = (lane >> 6) == h
        pt = jnp.exp(dot_nt(kaug[i], qb))
        dpt = dot_nt(vaug[i], daug)
        dst = (pt * dpt).astype(BF)
        dv[...] += dot_nn(pt.astype(BF), jnp.where(mine, da, 0.0).astype(BF))
        dk[...] += dot_nn(dst, jnp.where(mine, qf, 0.0).astype(BF))
        grads_q.append(dot_nn(kt_ref[HD * h : HD * (h + 1), :], dst))
    dq = jnp.concatenate(grads_q, axis=0).T.astype(BF)
    out_ref[pl.ds(pl.multiple_of(j * rows, rows), rows), 0:size] = dq
    dqs[...] += jnp.sum(dq.astype(F32), axis=0, keepdims=True)

    @pl.when(j == steps - 1)
    def _():
        out_ref[:, size : 2 * size] = (dk[:, lo : lo + size] * (HD**-0.5)).astype(BF)
        low = dv[:, lo : lo + size].astype(BF)
        out_ref[:, 2 * size : 3 * size] = low
        sums_ref[...] = jnp.concatenate(
            [dqs[...], jnp.sum(low.astype(F32), axis=0, keepdims=True)], axis=0
        )


def gelu_both(pre):
    phi = 0.5 * (1.0 + lax.erf(pre * 0.7071067811865476))
    return pre * phi, phi + pre * (0.3989422804014327 * jnp.exp(-0.5 * pre * pre))


def flipped(ref):
    half = ref.shape[0] // 2
    return jnp.concatenate([ref[half:], ref[:half]], axis=0)


def forward_kernel(
    mode, half_steps,
    c0, c1, c2, c3, w0, w1, w2, w3, x_ref, ob_ref, g_ref, s_ref,
    f1a, f1b, b1a, b1b, f2a, f2b, b2_ref, *rest,
):
    both = mode == "both"
    if both:
        send_ref, own_ref, sent_ref, a2_ref, act_ref, slope_ref, a2, acc, base = rest
    elif mode == "own":
        own_ref, a2, acc, base = rest
    else:
        send_ref, a2, acc = rest
    j = pl.program_id(0)
    rows = x_ref.shape[0]

    @pl.when(j == 0)
    def _():
        far = (flipped(c2), flipped(c3)) if both else (c2[...], c3[...])
        parts = [
            dot_nn(c0[...], w0[...]),
            dot_nn(c1[...], w1[...]),
            dot_nn(far[0], w2[...]),
            dot_nn(far[1], w3[...]),
        ]
        if not both:
            parts = [p.astype(BF).astype(F32) for p in parts]
        resid = x_ref[...].astype(F32) + (parts[0] + parts[1] + parts[2] + parts[3])
        resid = resid + ob_ref[...].astype(F32)
        if both:
            low = resid.astype(BF)
            sent_ref[...] = low
            resid = low.astype(F32)
        a2[...] = norm_low(resid, g_ref, s_ref)
        if both:
            a2_ref[...] = a2[...]
            base[...] = resid[: rows // 2] + b2_ref[...].astype(F32)
        elif mode == "own":
            base[...] = resid + b2_ref[...].astype(F32)
        acc[...] = jnp.zeros_like(acc)

    def half(f1, b1, f2):
        pre = dot_nn(a2[...], f1[...]) + b1[...].astype(F32)
        if both:
            act, slope = gelu_both(pre)
            slope_ref[...] = slope
        else:
            act = pre * (0.5 * (1.0 + lax.erf(pre * 0.7071067811865476)))
        act = act.astype(BF)
        if both:
            act_ref[...] = act
        acc[...] += dot_nn(act, f2[...])

    @pl.when(j < half_steps)
    def _():
        half(f1a, b1a, f2a)

    @pl.when(j >= half_steps)
    def _():
        half(f1b, b1b, f2b)

    @pl.when(j == 2 * half_steps - 1)
    def _():
        if both:
            own_ref[...] = acc[: rows // 2] + base[...]
            send_ref[...] = acc[rows // 2 :].astype(BF)
        elif mode == "own":
            own_ref[...] = acc[...] + base[...]
        else:
            send_ref[...] = acc[...].astype(BF)


def forward(mode, name, rows, ctx, w_out, x, out_b, gain, shift, f1, b1, f2, b2, chunk):
    width = x.shape[1]
    heads_wide, hidden = w_out[0].shape[0], f1[0].shape[1]
    n = hidden // chunk
    both = mode == "both"
    near_at = 1 if mode == "send" else 0
    far_at = 1 if mode == "own" else 0
    first = lambda j: jnp.minimum(j, n - 1)
    second = lambda j: jnp.maximum(j - n, 0)
    at = lambda i, w: pl.BlockSpec((rows, w), lambda j: (i, 0))
    specs = [at(near_at, heads_wide)] * 2 + [at(far_at, heads_wide)] * 2
    specs += [whole(w.shape) for w in w_out]
    specs += [at(near_at, width)] + [whole((1, width))] * 3
    specs += [pl.BlockSpec((width, chunk), lambda j, f=f: (0, f(j))) for f in (first, second)]
    specs += [pl.BlockSpec((1, chunk), lambda j, f=f: (0, f(j))) for f in (first, second)]
    specs += [pl.BlockSpec((chunk, width), lambda j, f=f: (f(j), 0)) for f in (first, second)]
    specs += [whole((1, width))]
    half = rows // 2
    scratch = [pltpu.VMEM((rows, width), BF), pltpu.VMEM((rows, width), F32)]
    if both:
        outs = [sds((half, width), BF), sds((half, width), F32)] + [sds((rows, width), BF)] * 2
        outs += [sds((rows, 2 * hidden), BF), sds((rows, 2 * hidden), F32)]
        out_specs = [whole((half, width))] * 2 + [whole((rows, width))] * 2
        out_specs += [pl.BlockSpec((rows, chunk), lambda j: (0, j))] * 2
        scratch += [pltpu.VMEM((half, width), F32)]
    elif mode == "own":
        outs, out_specs = sds((rows, width), F32), whole((rows, width))
        scratch += [pltpu.VMEM((rows, width), F32)]
    else:
        outs, out_specs = sds((rows, width), BF), whole((rows, width))
    return call(
        functools.partial(forward_kernel, mode, n), name, (2 * n,), specs, out_specs, outs,
        (*ctx, *w_out, x, out_b, gain, shift, *f1, *b1, *f2, b2),
        scratch=scratch,
        flops=2 * rows * width * (4 * heads_wide + 4 * hidden),
    )


def head_kernel(block, piece, sc, own_ref, recv_ref, out_ref, w_ref, b_ref, inv_ref, dg_ref, do_ref, loss_ref, hb_ref, ob_ref):
    rows, width = own_ref.shape
    target = (own_ref[...] + recv_ref[...].astype(F32)).astype(BF).astype(F32)
    line = lax.broadcasted_iota(jnp.int32, (rows, 1), 0)
    slot = (line >> log2(piece)) * block + sc[ORD] * piece + (line & (piece - 1))
    live = slot < sc[CUM + CLIPS - 1]
    group = group_of(slot, sc, CUM)
    weight = jnp.zeros((rows, 1), F32)
    for c in range(CLIPS):
        weight = jnp.where(group == c, inv_ref[0, c], weight)
    weight = jnp.where(live, weight, 0.0)
    target = jnp.where(live, target, 0.0)
    miss = dot_nn(out_ref[...], w_ref[...]) + b_ref[...].astype(F32) - target
    dg = (weight * miss).astype(BF)
    dg_ref[...] = dg
    loss_ref[...] = 0.5 * jnp.sum(weight * miss * miss, axis=0, keepdims=True)
    hb_ref[...] = jnp.sum(dg.astype(F32), axis=0, keepdims=True)
    do = dot_nt(dg, w_ref[...]).astype(BF)
    do_ref[...] = do
    ob_ref[...] = jnp.sum(do.astype(F32), axis=0, keepdims=True)


def feed_back_kernel(d0, d1, act_ref, slope_ref, a2_ref, f1, f2, *rest):
    last = len(rest) == 7
    if last:
        before, g1_ref, g2_ref, gb_ref, own_ref, send_ref, d = rest
    else:
        g1_ref, g2_ref, gb_ref, acc_ref, d = rest
    half = d0.shape[0]
    d[:half] = d0[...]
    d[half:] = d1[...]
    grad = d[...]
    dpre = (dot_nt(grad, f2[...]) * slope_ref[...]).astype(BF)
    gb_ref[...] = jnp.sum(dpre.astype(F32), axis=0, keepdims=True)
    part = dot_nt(dpre, f1[...])
    if last:
        part += before[...]
        own_ref[...] = part[:half]
        send_ref[...] = part[half:].astype(BF)
    else:
        acc_ref[...] = part
    g2_ref[...] = dot_tn(act_ref[...], grad).astype(g2_ref.dtype)
    g1_ref[...] = dot_tn(a2_ref[...], dpre).astype(g1_ref.dtype)


def norm_back_kernel(own_ref, recv_ref, base_ref, x_ref, g_ref, dx_ref, sums_ref):
    d = own_ref[...].astype(F32) + recv_ref[...].astype(F32)
    u, inverse = unit(x_ref[...].astype(F32))
    e = g_ref[...].astype(F32) * d
    mean_e = jnp.mean(e, axis=-1, keepdims=True)
    mean_eu = jnp.mean(e * u, axis=-1, keepdims=True)
    dx = base_ref[...].astype(F32) + (e - mean_e - u * mean_eu) * inverse
    dx = dx.astype(dx_ref.dtype)
    dx_ref[...] = dx
    sums_ref[...] = jnp.concatenate(
        [
            jnp.sum(d * u, axis=0, keepdims=True),
            jnp.sum(d, axis=0, keepdims=True),
            jnp.sum(dx.astype(F32), axis=0, keepdims=True),
        ],
        axis=0,
    )


def norm_back(name, own, recv, base, x, gain, dtype):
    rows, width = own.shape
    half = pl.BlockSpec((rows, width), lambda *_: (0, 0))
    return call(
        norm_back_kernel, name, (1,),
        [half] * 4 + [whole((1, width))],
        [half, whole((3, width))],
        [sds((rows, width), dtype), sds((3, width), F32)],
        (own, recv, base, x, gain),
    )


def swap(x, bit, count):
    return lax.ppermute(x, "mp", [(i, i ^ bit) for i in range(count)])


def row(vector):
    return vector.reshape(1, -1)


def layout(mask_row, seg_row, order, steps, span):
    tokens = mask_row.shape[0]
    grid = mask_row.reshape(tokens // 128, 128).astype(BF)
    upper = (jnp.arange(128)[:, None] <= jnp.arange(128)[None, :]).astype(BF)
    within = jnp.dot(grid, upper, preferred_element_type=F32)
    lines = tokens // 128
    lower = (jnp.arange(lines)[:, None] > jnp.arange(lines)[None, :]).astype(BF)
    ahead = jnp.dot(lower, within[:, 127:].astype(BF), preferred_element_type=F32)
    count = (within + ahead).astype(jnp.int32).reshape(tokens)
    rank = jnp.where(mask_row == 1, count - 1, -1)
    labels = jnp.arange(CLIPS, dtype=jnp.int32)
    upto = (seg_row[None, :] <= labels[:, None]).astype(jnp.int32)
    ends = jnp.sum(upto, axis=1)
    cum = jnp.sum(upto * mask_row[None, :], axis=1)
    edge = jnp.arange(steps, dtype=jnp.int32) * span
    low = jnp.sum((count[None, :] <= edge[:, None]).astype(jnp.int32), axis=1)
    high = jnp.sum((count[None, :] < edge[:, None] + span).astype(jnp.int32), axis=1)
    low = low // span
    high = jnp.minimum(high, tokens - 1) // span + 1
    each = cum - jnp.concatenate([jnp.zeros((1,), jnp.int32), cum[:-1]])
    inverse = 1.0 / jnp.maximum(each, 1).astype(F32)
    scalars = jnp.concatenate([order, cum, ends, low, high])
    return rank.reshape(tokens // span, span), scalars, inverse.reshape(1, CLIPS)


def body(
    teacher_in, segment_ids, keep_mask, block_owner, student_in,
    t_norm1_gain, t_norm1_shift, t_qkv, t_qv_bias, t_out, t_out_bias,
    t_norm2_gain, t_norm2_shift, t_fc1, t_fc1_bias, t_fc2, t_fc2_bias,
    s_norm1_gain, s_norm1_shift, s_qkv, s_qv_bias, s_out, s_out_bias,
    s_norm2_gain, s_norm2_shift, s_fc1, s_fc1_bias, s_fc2, s_fc2_bias,
    head_weight, head_bias,
):
    mp = lax.axis_size("mp")
    me = lax.axis_index("mp")
    homes = lax.axis_size("dp")
    home = lax.axis_index("dp")
    slots, block, width = student_in.shape
    piece = block // mp
    rows = slots * block
    mine = rows // mp
    near = 2 * mine
    tokens, t_width = teacher_in.shape
    used = s_qkv.shape[2]
    wide = 256
    nb = 2
    span = nb * block
    steps = slots // nb
    core = lambda x: swap(x, 1, mp)
    across = lambda x: swap(x, 2, mp)

    order = jnp.stack([me, me ^ 2, me ^ 1, me ^ 3]).astype(jnp.int32)
    mask_row = lax.dynamic_index_in_dim(keep_mask, home, 0, keepdims=False)
    seg_row = lax.dynamic_index_in_dim(segment_ids, home, 0, keepdims=False)
    rank, scalars, inverse = layout(mask_row, seg_row, order, steps, span)

    t_w2 = across(t_out)
    s_w2 = across(s_out)
    t_f1 = (t_fc1, core(t_fc1))
    t_f2 = (t_fc2, core(t_fc2))
    s_f1 = (s_fc1, core(s_fc1))
    s_f2 = (s_fc2, core(s_fc2))
    biases = core(jnp.concatenate([t_fc1_bias, s_fc1_bias]))
    t_w1 = core(t_out)
    s_w1 = core(s_out)

    w_pad = jnp.pad(s_qkv, ((0, 0), (0, 0), (0, wide - used)))
    b_pad = jnp.pad(s_qv_bias, ((0, 0), (0, wide - used)))
    x4 = student_in.reshape(slots, mp, piece, width)
    by_piece = lambda w: pl.BlockSpec((mine, w), lambda k, sc: (k, 0))
    x_stud, a_stud, sq, sk, sv = call(
        functools.partial(student_qkv_kernel, block, used), "student_qkv", (mp,),
        [
            pl.BlockSpec((slots, 1, piece, width), lambda k, sc: (0, sc[ORD + k], 0, 0)),
            whole((1, width)), whole((1, width)), whole(w_pad.shape), whole(b_pad.shape),
        ],
        [by_piece(width)] * 2 + [by_piece(wide)] * 3,
        [sds((rows, width), BF)] * 2 + [sds((rows, wide), BF)] * 3,
        (x4, row(s_norm1_gain), row(s_norm1_shift), w_pad, b_pad),
        flops=2 * rows * width * 3 * wide, scalars=scalars,
    )
    heads = used // HD
    qrows = 256
    by_rows = lambda w: pl.BlockSpec((qrows, w), lambda j: (j, 0))
    ctx, mixed, qb = call(
        functools.partial(student_attend_kernel, used), "student_attend", (rows // qrows,),
        [by_rows(wide), whole((rows, wide)), whole((rows, wide))],
        [by_rows(used), by_rows(wide), by_rows(wide)],
        [sds((rows, used), BF), sds((rows, wide), F32), sds((rows, wide), BF)],
        (sq, sk, sv),
        scratch=[pltpu.VMEM((heads, rows, wide), BF)] * 2,
        flops=heads * rows * rows * wide * 4,
    )

    ctx, teacher_rows, t_w2, s_w2, t_f1, t_f2, s_f1, s_f2, t_w1, s_w1, biases = lax.optimization_barrier(
        (ctx, teacher_in, t_w2, s_w2, t_f1, t_f2, s_f1, s_f2, t_w1, s_w1, biases)
    )
    t_b1 = (row(t_fc1_bias), row(biases[: t_fc1_bias.shape[0]]))
    s_b1 = (row(s_fc1_bias), row(biases[t_fc1_bias.shape[0] :]))
    s_c0 = ctx[:near]
    s_c1 = core(ctx[near:])
    s_c2 = across(s_c0)
    t_w3 = core(t_w2)
    s_w3 = core(s_w2)

    by_512 = lambda w: pl.BlockSpec((512, w), lambda j: (j, 0))
    cols = t_qkv.shape[2]
    tk, tv = call(
        teacher_kv_kernel, "teacher_kv", (tokens // 512,),
        [by_512(t_width), whole((1, t_width)), whole((1, t_width)), whole(t_qkv.shape), whole(t_qv_bias.shape)],
        [by_512(cols)] * 2,
        [sds((tokens, cols), BF)] * 2,
        (teacher_rows, row(t_norm1_gain), row(t_norm1_shift), t_qkv, t_qv_bias),
        flops=2 * tokens * t_width * 2 * cols,
    )
    tk, teacher_rows, s_c1, t_w3, s_w3 = lax.optimization_barrier((tk, teacher_rows, s_c1, t_w3, s_w3))
    s_c3 = across(s_c1)
    by_slot = lambda w: pl.BlockSpec((mp, nb, piece, w), lambda j, sc: (0, j, 0, 0))
    x_kept, tq = call(
        functools.partial(teacher_q_kernel, slots, block, span), "teacher_q", (steps,),
        [
            whole(teacher_in.shape), whole(rank.shape), whole((1, t_width)), whole((1, t_width)),
            whole(t_qkv.shape), whole(t_qv_bias.shape),
        ],
        [by_slot(t_width), by_slot(2 * cols)],
        [sds((mp, slots, piece, t_width), BF), sds((mp, slots, piece, 2 * cols), BF)],
        (teacher_rows, rank, row(t_norm1_gain), row(t_norm1_shift), t_qkv, t_qv_bias),
        scratch=[pltpu.VMEM((span, t_width), F32)],
        flops=2 * rows * t_width * (cols + 512), scalars=scalars,
    )
    t_ctx = call(
        teacher_attend_kernel, "teacher_attend", (steps,),
        [by_slot(2 * cols), whole((tokens, cols)), whole((tokens, cols))],
        by_slot(cols),
        sds((mp, slots, piece, cols), BF),
        (tq, tk, tv),
        scratch=[pltpu.VMEM((cols // HD, tokens, 256), BF), pltpu.VMEM((cols // HD, tokens, 128), BF)],
        flops=(cols // HD) * rows * tokens * (512 + 256), scalars=scalars,
    ).reshape(rows, cols)

    t_ctx, s_c2, s_c3 = lax.optimization_barrier((t_ctx, s_c2, s_c3))
    t_c0 = t_ctx[:near]
    t_c2 = across(t_c0)
    t_c1 = core(t_ctx[near:])
    t_c3 = across(t_c1)
    s_send, s_own, sent, a2, act, slope = forward(
        "both", "student_forward", near, (s_c0, s_c1, s_c2, s_c3), (s_out, s_w1, s_w2, s_w3), x_stud,
        row(s_out_bias), row(s_norm2_gain), row(s_norm2_shift), s_f1, s_b1, s_f2, row(s_fc2_bias), s_fc1.shape[1],
    )
    s_send, t_c2, t_c3 = lax.optimization_barrier((s_send, t_c2, t_c3))
    s_recv = across(s_send)
    t_args = (
        (t_ctx, t_c1, t_c2, t_c3), (t_out, t_w1, t_w2, t_w3), x_kept.reshape(rows, t_width), row(t_out_bias),
        row(t_norm2_gain), row(t_norm2_shift), t_f1, t_b1, t_f2, row(t_fc2_bias),
    )
    t_send = forward("send", "teacher_forward_far", mine, *t_args, 512)
    s_recv, t_args, t_send = lax.optimization_barrier((s_recv, t_args, t_send))
    t_recv = across(t_send)
    t_own = forward("own", "teacher_forward_own", mine, *t_args, 512)
    t_own, t_recv = lax.optimization_barrier((t_own, t_recv))
    out_rows = (s_own + s_recv.astype(F32)).astype(BF)

    owners = lax.dynamic_index_in_dim(block_owner, home, 0, keepdims=False)
    capacity = (slots + homes - 1) // homes
    labels = jnp.arange(homes, dtype=jnp.int32)
    hits = (owners[:, None] == labels[None, :]).astype(jnp.int32)
    order_in = jnp.sum((jnp.cumsum(hits, axis=0) - hits) * hits, axis=1)
    place = jnp.where(owners >= 0, owners * capacity + order_in, homes * capacity)
    pick = (jnp.arange(homes * capacity, dtype=jnp.int32)[:, None] == place[None, :]).astype(BF)
    outbound = jnp.dot(pick, out_rows.reshape(slots, piece * width), preferred_element_type=BF)
    inbound = lax.all_to_all(
        outbound.reshape(homes * capacity, piece, width), "dp", split_axis=0, concat_axis=0, tiled=True
    )
    per_source = jnp.sum((block_owner == home).astype(jnp.int32), axis=1)
    before = jnp.cumsum(per_source) - per_source
    lane = jnp.arange(capacity, dtype=jnp.int32)
    target_slot = jnp.where(lane[None, :] < per_source[:, None], before[:, None] + lane[None, :], OWN).reshape(-1)
    choose = (jnp.arange(OWN, dtype=jnp.int32)[:, None] == target_slot[None, :]).astype(BF)

    d_guess, d_out, loss_row, head_b_row, fc2_b_row = call(
        functools.partial(head_kernel, block, piece), "head", (1,),
        [
            whole((mine, t_width)), whole((mine, t_width)), whole((mine, width)), whole((width, t_width)),
            whole((1, t_width)), pl.BlockSpec(memory_space=pltpu.SMEM),
        ],
        [whole((mine, t_width)), whole((mine, width)), whole((1, t_width)), whole((1, t_width)), whole((1, width))],
        [sds((mine, t_width), BF), sds((mine, width), BF), sds((1, t_width), F32), sds((1, t_width), F32), sds((1, width), F32)],
        (t_own, t_recv, out_rows, head_weight, row(head_bias), inverse),
        flops=4 * mine * width * t_width, scalars=scalars,
    )
    d_out_far = across(d_out)
    g_head = dot_tn(out_rows, d_guess)
    side = me % 2
    level = me // 2
    half_rows = width // 2
    quarter = width // 4
    head_send = lax.dynamic_slice_in_dim(g_head, (1 - side) * half_rows, half_rows, 0).astype(BF)
    head_recv = core(head_send)
    d_out_far, inbound, head_recv = lax.optimization_barrier((d_out_far, inbound, head_recv))
    student_out = jnp.dot(
        choose, inbound.reshape(homes * capacity, piece * width), preferred_element_type=BF
    ).reshape(OWN, piece, width)

    hidden = s_fc1.shape[1]
    cut = lambda i: pl.BlockSpec((near, hidden), lambda j: (0, i))
    square, line = whole((width, hidden)), whole((1, hidden))
    feed_specs = lambda i: [whole((mine, width))] * 2 + [cut(i), cut(i), whole((near, width)), square, whole((hidden, width))]
    feed_flops = 2 * near * width * hidden * 4
    g1_send, g2_send, b1_send, da2_part = call(
        feed_back_kernel, "feed_back_far", (1,), feed_specs(1),
        [square, whole((hidden, width)), line, whole((near, width))],
        [sds((width, hidden), BF), sds((hidden, width), BF), sds((1, hidden), F32), sds((near, width), F32)],
        (d_out, d_out_far, act, slope, a2, s_f1[1], s_f2[1]),
        scratch=[pltpu.VMEM((near, width), BF)], flops=feed_flops,
    )
    g1_recv, g2_recv = core(g1_send), core(g2_send)
    g1, g2, b1_own, da2_own, da2_send = call(
        feed_back_kernel, "feed_back_own", (1,), feed_specs(0) + [whole((near, width))],
        [square, whole((hidden, width)), line, whole((mine, width)), whole((mine, width))],
        [
            sds((width, hidden), F32), sds((hidden, width), F32), sds((1, hidden), F32),
            sds((mine, width), F32), sds((mine, width), BF),
        ],
        (d_out, d_out_far, act, slope, a2, s_f1[0], s_f2[0], da2_part),
        scratch=[pltpu.VMEM((near, width), BF)], flops=feed_flops,
    )

    head_half = lax.dynamic_slice_in_dim(g_head, side * half_rows, half_rows, 0) + head_recv.astype(F32)
    head_send2 = lax.dynamic_slice_in_dim(head_half, (1 - level) * quarter, quarter, 0).astype(BF)
    head_own = lax.dynamic_slice_in_dim(head_half, level * quarter, quarter, 0)
    head_recv2 = across(head_send2)
    g1_recv, g2_recv, head_recv2, g1, g2, da2_own, da2_send = lax.optimization_barrier(
        (g1_recv, g2_recv, head_recv2, g1, g2, da2_own, da2_send)
    )
    da2_far = across(da2_send)

    bits = log2(homes)
    x_first = list(range(bits))
    z_first = x_first[1:] + x_first[:1]

    def partner(value, bit):
        return lax.ppermute(value, "dp", [(i, i ^ (1 << bit)) for i in range(homes)])

    def cut_half(value, bit):
        size = value.shape[0] // 2
        mark = (home >> bit) & 1
        send = lax.dynamic_slice_in_dim(value, (1 - mark) * size, size, 0).astype(BF)
        keep = lax.dynamic_slice_in_dim(value, mark * size, size, 0)
        return keep, partner(send, bit)

    def join_half(value, other, bit):
        mark = (home >> bit) & 1
        return jnp.where(
            mark == 0, jnp.concatenate([value, other], axis=0), jnp.concatenate([other, value], axis=0)
        )

    def add(pair):
        return (pair[0].astype(F32) + pair[1].astype(F32)).astype(BF)

    head_quarter = (head_own + head_recv2.astype(F32)).reshape(-1, width)
    head_rows = head_quarter.shape[0]
    one = (jnp.concatenate([g1 + g1_recv.astype(F32), head_quarter], axis=0)).astype(BF)
    two = (g2 + g2_recv.astype(F32)).astype(BF)

    def halve(values, orders, step):
        return [cut_half(v, o[step]) for v, o in zip(values, orders)]

    def double(values, orders, step):
        return [partner(v, o[step]) for v, o in zip(values, orders)]

    def join(values, others, orders, step):
        return [join_half(v, w, o[step]) for v, w, o in zip(values, others, orders)]

    orders = (x_first, z_first)
    sums = [one, two]
    flight = halve(sums, orders, 0)

    d_sent, sums2 = norm_back("norm2_back", da2_own, da2_far, d_out, sent[:mine], row(s_norm2_gain), BF)
    ds_near = jnp.concatenate([d_sent, across(d_sent)], axis=0)
    ds = jnp.concatenate([ds_near, core(ds_near)], axis=0)
    ds, flight = lax.optimization_barrier((ds, flight))
    sums = [add(p) for p in flight]
    flight = halve(sums, orders, 1)
    so_pad = jnp.pad(s_out, ((0, wide - used), (0, 0)))
    k_turned = sk[:, :used].T

    def back(name, picked):
        size = HD * len(picked)
        return call(
            functools.partial(student_back_kernel, used, picked), name, (rows // qrows,),
            [
                by_rows(width), whole((wide, width)), by_rows(wide), by_rows(wide), whole((rows, wide)),
                whole((rows, wide)), whole((used, rows)),
            ],
            [whole((rows, 3 * size)), whole((2, size))],
            [sds((rows, 3 * size), BF), sds((2, size), F32)],
            (ds, so_pad, mixed, qb, sk, sv, k_turned),
            scratch=[pltpu.VMEM((len(picked), rows, wide), BF)] * 2 + [pltpu.VMEM((rows, wide), F32)] * 2
            + [pltpu.VMEM((1, size), F32)],
            flops=len(picked) * rows * rows * wide * 9,
        )

    pair, odd = tuple(range(heads - 1)), (heads - 1,)
    d_pair, pair_sums = back("student_back_pair", pair)
    g_out = dot_tn(ctx, ds)
    d_pair, ds, flight = lax.optimization_barrier((d_pair, ds, flight))
    sums = [add(p) for p in flight]
    for step in range(2, bits):
        flight = halve(sums, orders, step)
        if step < bits - 1:
            sums = [add(p) for p in flight]
    d_odd, odd_sums = back("student_back_odd", odd)
    d_odd, flight = lax.optimization_barrier((d_odd, flight))
    sums = [add(p) for p in flight]
    flight = double(sums, orders, bits - 1)

    mixed_size = HD * (heads - 1)
    w_turn = jnp.transpose(s_qkv, (0, 2, 1))
    w_pair = w_turn[:, :mixed_size].reshape(3 * mixed_size, width)
    w_odd = w_turn[:, mixed_size:].reshape(3 * HD, width)
    da1 = dot_nn(d_pair, w_pair) + dot_nn(d_odd, w_odd)
    da1_recv = core(da1[near:].astype(BF))
    g_pair = dot_tn(d_pair, a_stud).astype(BF)
    g_odd = dot_tn(d_odd, a_stud).astype(BF)
    last = [g_pair, jnp.concatenate([g_odd, g_out.astype(BF)], axis=0)]
    last, da1_recv, flight = lax.optimization_barrier((last, da1_recv, flight))
    last_flight = halve(last, orders, 0)
    da1_near = da1[:near] + da1_recv.astype(F32)
    da1_far = across(da1_near[mine:].astype(BF))
    sums = join(sums, flight, orders, bits - 1)
    for step in range(bits - 2, 0, -1):
        flight = double(sums, orders, step)
        sums = join(sums, flight, orders, step)
    grad_in, sums1 = norm_back("norm1_back", da1_near[:mine], da1_far, d_sent, x_stud[:mine], row(s_norm1_gain), F32)
    last = [add(p) for p in last_flight]

    fit = lambda v: jnp.pad(v, ((0, 0), (0, width - v.shape[1])))
    loss_fit = jnp.sum(loss_row.reshape(-1, t_width // 4), axis=0, keepdims=True)
    short = jnp.concatenate(
        [sums1[:2], sums2, fc2_b_row, head_b_row[:, :width], fit(head_b_row[:, width:]), fit(loss_fit), b1_send],
        axis=0,
    )
    short_own = jnp.concatenate([short[:9], b1_own], axis=0) + core(short)
    short_sum = short_own[:9] + across(short_own[:9])
    qv = jnp.concatenate([pair_sums, odd_sums], axis=1)
    short_all = jnp.concatenate([short_sum, short_own[9:], fit(qv), jnp.zeros((4, width), F32)], axis=0)

    flight = double(sums, orders, 0)
    for step in range(1, bits):
        last = [add(p) for p in halve(last, orders, step)]
        short_all = short_all + partner(short_all, step - 1)
    short_all = short_all + partner(short_all, bits - 1)
    for step in range(bits - 1, -1, -1):
        last = join(last, double(last, orders, step), orders, step)
    sums = join(sums, flight, orders, 0)

    g1_all, head_all = sums[0][:width], sums[0][width:].reshape(quarter, t_width)
    head_other = across(head_all)
    head_pair = jnp.where(
        level == 0,
        jnp.concatenate([head_all, head_other], axis=0),
        jnp.concatenate([head_other, head_all], axis=0),
    )
    head_peer = core(head_pair)
    grad_head = jnp.where(
        side == 0,
        jnp.concatenate([head_pair, head_peer], axis=0),
        jnp.concatenate([head_peer, head_pair], axis=0),
    ).astype(F32)
    vec = short_all
    qkv_turned = jnp.concatenate(
        [last[0].reshape(3, mixed_size, width), last[1][: 3 * HD].reshape(3, HD, width)], axis=1
    )
    return (
        jnp.sum(vec[8]),
        student_out,
        grad_in.reshape(slots, piece, width),
        vec[0],
        vec[1],
        jnp.transpose(qkv_turned, (0, 2, 1)).astype(F32),
        vec[10:12, :used],
        last[1][3 * HD :].astype(F32),
        vec[4],
        vec[2],
        vec[3],
        g1_all.astype(F32),
        vec[9],
        sums[1].astype(F32),
        vec[5],
        grad_head,
        jnp.concatenate([vec[6], vec[7, : t_width - width]]),
    )


def solution(mesh):
    rep = P()
    in_specs = (
        P("dp", None), rep, rep, rep, P("dp", None, None), rep, rep, P(None, None, "mp"), P(None, "mp"),
        P("mp", None), rep, rep, rep, P(None, "mp"), P("mp"), P("mp", None), rep, rep, rep,
        P(None, None, "mp"), P(None, "mp"), P("mp", None), rep, rep, rep, P(None, "mp"), P("mp"),
        P("mp", None), rep, rep, rep,
    )
    out_specs = (
        rep, P("dp", "mp", None), P("dp", "mp", None), rep, rep, P(None, None, "mp"), P(None, "mp"),
        P("mp", None), rep, rep, rep, P(None, "mp"), P("mp"), P("mp", None), rep, rep, rep,
    )
    return jax.shard_map(body, mesh=mesh, in_specs=in_specs, out_specs=out_specs, check_vma=False)
```

```python
import functools

import jax
import jax.numpy as jnp
from jax import lax
from jax.experimental import pallas as pl
from jax.experimental.pallas import tpu as pltpu
from jax.sharding import PartitionSpec as P

HD = 64
OWN = 8
CLIPS = 8
EPS = 1e-05
BIG = -1e30
F32 = jnp.float32
BF = jnp.bfloat16
LIMIT = 24 * 2**20
COST = 1

ORD, CUM, END, HOME, LOW = 0, 4, 12, 20, 21


def dot_nn(a, b):
    return lax.dot_general(a, b, (((1,), (0,)), ((), ())), preferred_element_type=F32)


def dot_nt(a, b):
    return lax.dot_general(a, b, (((1,), (1,)), ((), ())), preferred_element_type=F32)


def dot_tn(a, b):
    return lax.dot_general(a, b, (((0,), (0,)), ((), ())), preferred_element_type=F32)


def unit(values):
    mean = jnp.mean(values, axis=-1, keepdims=True)
    centred = values - mean
    spread = jnp.mean(centred * centred, axis=-1, keepdims=True)
    inverse = lax.rsqrt(spread + EPS)
    return centred * inverse, inverse


def norm_low(values, gain_ref, shift_ref):
    u, _ = unit(values)
    return (u * gain_ref[...].astype(F32) + shift_ref[...].astype(F32)).astype(BF)


def log2(size):
    return size.bit_length() - 1


def whole(shape):
    return pl.BlockSpec(shape, lambda *_: (0,) * len(shape))


def call(kernel, name, grid, in_specs, out_specs, out_shape, args, scratch=(), flops=0, scalars=None):
    moved = sum(a.size * a.dtype.itemsize for a in args)
    moved += sum(s.size * jnp.dtype(s.dtype).itemsize for s in jax.tree.leaves(out_shape))
    params = pltpu.CompilerParams(
        dimension_semantics=("arbitrary",) * len(grid), vmem_limit_bytes=LIMIT
    )
    cost = pl.CostEstimate(flops=int(flops) // COST, bytes_accessed=int(moved) // COST, transcendentals=0)
    lead = 0 if scalars is None else 1
    spec = pltpu.PrefetchScalarGridSpec(
        num_scalar_prefetch=lead,
        grid=grid,
        in_specs=in_specs,
        out_specs=out_specs,
        scratch_shapes=list(scratch),
    )
    run = pl.pallas_call(
        kernel,
        grid_spec=spec,
        out_shape=out_shape,
        compiler_params=params,
        cost_estimate=cost,
        name=name,
    )
    return run(*([scalars] if lead else []), *args)


def sds(shape, dtype):
    return jax.ShapeDtypeStruct(shape, dtype)


def group_of(index, sc, base):
    group = jnp.zeros(index.shape, jnp.int32)
    for c in range(CLIPS):
        group = group + (index >= sc[base + c]).astype(jnp.int32)
    return group


def teacher_kv_kernel(sc, x_ref, g_ref, s_ref, w_ref, b_ref, k_ref, v_ref):
    rows = x_ref.shape[0]
    a = norm_low(x_ref[...].astype(F32), g_ref, s_ref)
    token = pl.program_id(0) * rows + lax.broadcasted_iota(jnp.int32, (rows, 1), 0)
    lane = lax.broadcasted_iota(jnp.int32, (rows, 128), 1)
    hot = jnp.where(lane == group_of(token, sc, END), 1.0, 0.0).astype(BF)
    k = (dot_nn(a, w_ref[1]).astype(BF).astype(F32) * (HD**-0.5)).astype(BF)
    for p in range(k.shape[1] // 128):
        k_ref[:, 256 * p : 256 * p + 128] = k[:, 128 * p : 128 * (p + 1)]
        k_ref[:, 256 * p + 128 : 256 * (p + 1)] = hot
    v_ref[...] = (dot_nn(a, w_ref[2]) + b_ref[1:2, :].astype(F32)).T.astype(BF)


def teacher_q_kernel(slots, block, step, sc, x_ref, rank_ref, g_ref, s_ref, w_ref, b_ref, xk_ref, q_ref, acc):
    j = pl.program_id(0)
    pieces, nb, piece, width = xk_ref.shape
    rows = pieces * nb * piece

    line = lax.broadcasted_iota(jnp.int32, (rows, 1), 0)
    part = line >> log2(nb * piece)
    inner = line & (nb * piece - 1)
    order = jnp.zeros((rows, 1), jnp.int32)
    for p in range(pieces):
        order = jnp.where(part == p, sc[ORD + p], order)
    slot = (j * nb + (inner >> log2(piece))) * block + order * piece + (inner & (piece - 1))
    group = group_of(slot, sc, CUM)
    acc[...] = jnp.zeros_like(acc)

    def one(t, _):
        hit = jnp.where(slot == rank_ref[pl.ds(t, 1), :], 1.0, 0.0).astype(BF)
        acc[...] += dot_nn(hit, x_ref[pl.ds(pl.multiple_of(t * step, step), step), :])
        return 0

    steps = slots // nb
    lax.fori_loop(sc[LOW + j], sc[LOW + steps + j], one, 0)
    kept = acc[...]
    xk_ref[...] = kept.astype(BF).reshape(xk_ref.shape)
    a = norm_low(kept, g_ref, s_ref)
    q = (dot_nn(a, w_ref[0]) + b_ref[0:1, :].astype(F32)).astype(BF)
    lane = lax.broadcasted_iota(jnp.int32, (rows, 128), 1)
    other = (lane != group) & (lane <= CLIPS)
    mask = jnp.where(other, BIG, 0.0).astype(BF)
    pairs = q.shape[1] // 128
    out = []
    for p in range(pairs):
        out += [q[:, 128 * p : 128 * (p + 1)], mask]
    q_ref[...] = jnp.concatenate(out, axis=1).reshape(q_ref.shape)


def softmax_mix(keys, query, values):
    scores = dot_nt(keys, query)
    top = jnp.max(scores, axis=0, keepdims=True)
    e = jnp.exp(scores - top)
    mass = jnp.sum(e, axis=0, keepdims=True)
    return dot_nn(values, e.astype(BF)) * (1.0 / mass), top + jnp.log(mass)


def teacher_attend_kernel(q_ref, k_ref, v_ref, ctx_ref):
    pieces, nb, piece, both = q_ref.shape
    rows = pieces * nb * piece
    q = q_ref[...].reshape(rows, both)
    lane = lax.broadcasted_iota(jnp.int32, (rows, 256), 1)
    mixed = []
    for p in range(both // 256):
        part = q[:, 256 * p : 256 * (p + 1)].astype(F32)
        for h in range(2):
            mine = ((lane >> 6) == h) | (lane >= 128)
            query = jnp.where(mine, part, 0.0).astype(BF)
            at = HD * (2 * p + h)
            mixed.append(softmax_mix(k_ref[:, 256 * p : 256 * (p + 1)], query, v_ref[at : at + HD, :])[0])
    ctx_ref[...] = jnp.concatenate(mixed, axis=0).T.astype(BF).reshape(ctx_ref.shape)


def student_qkv_kernel(block, sc, x_ref, g_ref, s_ref, w_ref, b_ref, xo_ref, a_ref, q_ref, k_ref, v_ref, kt_ref, vt_ref):
    slots, _, piece, width = x_ref.shape
    rows = slots * piece
    used, wide = w_ref.shape[2], q_ref.shape[1]
    x = x_ref[...].reshape(rows, width)
    xo_ref[...] = x
    a = norm_low(x.astype(F32), g_ref, s_ref)
    a_ref[...] = a
    line = lax.broadcasted_iota(jnp.int32, (rows, 1), 0)
    lane = lax.broadcasted_iota(jnp.int32, (rows, wide - used), 1)
    slot = (line >> log2(piece)) * block + sc[ORD + pl.program_id(0)] * piece + (line & (piece - 1))
    same = lane == group_of(slot, sc, CUM)
    q_ref[:, :used] = (dot_nn(a, w_ref[0]) + b_ref[0:1, :].astype(F32)).astype(BF)
    q_ref[:, used:] = jnp.where(same | (lane > CLIPS), 0.0, BIG).astype(BF)
    k = dot_nn(a, w_ref[1]).astype(BF).astype(F32) * (HD**-0.5)
    k_ref[:, :used] = k.astype(BF)
    k_ref[:, used:] = jnp.where(same, 1.0, 0.0).astype(BF)
    kt_ref[...] = k.T.astype(BF)
    v = dot_nn(a, w_ref[2]) + b_ref[1:2, :].astype(F32)
    v_ref[:, :used] = v.astype(BF)
    v_ref[:, used:] = jnp.zeros((rows, wide - used), BF)
    vt_ref[...] = v.T.astype(BF)


def student_attend_kernel(used, q_ref, k_ref, vt_ref, ctx_ref, mixed_ref, log_ref):
    q = q_ref[...].astype(F32)
    rows, wide = q.shape
    lane = lax.broadcasted_iota(jnp.int32, (rows, wide), 1)
    mixed, logs = [], []
    for h in range(used // HD):
        query = jnp.where(((lane >> 6) == h) | (lane >= used), q, 0.0).astype(BF)
        part, log = softmax_mix(k_ref[...], query, vt_ref[HD * h : HD * (h + 1), :])
        mixed.append(part)
        logs.append(log)
    total = jnp.concatenate(mixed, axis=0)
    mixed_ref[...] = total
    ctx_ref[...] = total.T.astype(BF)
    log_ref[...] = jnp.concatenate(logs + [jnp.zeros((8 - len(logs), rows), F32)], axis=0)


def student_back_kernel(used, picked, with_out, p0, p1, w_ref, mixed_ref, log_ref, q_ref, k_ref, v_ref, kt_ref, *rest):
    if with_out:
        out_ref, sums_ref, w_grad_ref, ds, da, dk, dv, dqs, dw = rest
    else:
        out_ref, sums_ref, ds, da, dk, dv, dqs = rest
    j = pl.program_id(0)
    steps = pl.num_programs(0)
    lo, size = HD * picked[0], HD * len(picked)
    rows, wide = q_ref.shape

    @pl.when(j == 0)
    def _():
        dk[...] = jnp.zeros_like(dk)
        dv[...] = jnp.zeros_like(dv)
        dqs[...] = jnp.zeros_like(dqs)
        ds[...] = p0[...]
        if with_out:
            dw[...] = jnp.zeros_like(dw)

    @pl.when(j == 1)
    def _():
        ds[...] = p1[...]

    grad = ds[...]
    da[:, :used] = dot_nt(grad, w_ref[...])
    da[:, used:] = jnp.zeros((rows, wide - used), F32)
    low = da[...].astype(BF).astype(F32)
    mixed = mixed_ref[...]
    turned = dot_nt(w_ref[lo : lo + size, :], grad).astype(BF).astype(F32)
    product = turned * mixed[lo : lo + size, :]
    if with_out:
        dw[...] += dot_nn(mixed.astype(BF), grad)
    lane = lax.broadcasted_iota(jnp.int32, (rows, wide), 1)
    q = q_ref[...].astype(F32)
    grads_q = []
    for i, h in enumerate(picked):
        mine = (lane >> 6) == h
        query = jnp.where(mine | (lane >= used), q, 0.0).astype(BF)
        outer = jnp.where(mine, low, 0.0).astype(BF)
        delta = jnp.sum(product[HD * i : HD * (i + 1), :], axis=0, keepdims=True)
        pt = jnp.exp(dot_nt(k_ref[...], query) - log_ref[h : h + 1, :])
        dst = (pt * (dot_nt(v_ref[...], outer) - delta)).astype(BF)
        dv[...] += dot_nn(pt.astype(BF), outer)
        dk[...] += dot_nn(dst, query)
        grads_q.append(dot_nn(kt_ref[HD * h : HD * (h + 1), :], dst))
    dq = jnp.concatenate(grads_q, axis=0).T.astype(BF)
    out_ref[pl.ds(pl.multiple_of(j * rows, rows), rows), 0:size] = dq
    dqs[...] += jnp.sum(dq.astype(F32), axis=0, keepdims=True)

    @pl.when(j == steps - 1)
    def _():
        out_ref[:, size : 2 * size] = (dk[:, lo : lo + size] * (HD**-0.5)).astype(BF)
        dv_low = dv[:, lo : lo + size].astype(BF)
        out_ref[:, 2 * size : 3 * size] = dv_low
        sums_ref[...] = jnp.concatenate(
            [dqs[...], jnp.sum(dv_low.astype(F32), axis=0, keepdims=True)], axis=0
        )
        if with_out:
            w_grad_ref[...] = dw[...]


def gelu_both(pre):
    phi = 0.5 * (1.0 + lax.erf(pre * 0.7071067811865476))
    return pre * phi, phi + pre * (0.3989422804014327 * jnp.exp(-0.5 * pre * pre))


def flipped(ref):
    half = ref.shape[0] // 2
    return jnp.concatenate([ref[half:], ref[:half]], axis=0)


def forward_kernel(
    mode, half_steps,
    c0, c1, c2, c3, w0, w1, w2, w3, x_ref, ob_ref, g_ref, s_ref,
    f1a, f1b, b1a, b1b, f2a, f2b, b2_ref, *rest,
):
    both = mode == "both"
    if both:
        send_ref, own_ref, sent_ref, a2_ref, act_ref, slope_ref, a2, acc, base = rest
    elif mode == "own":
        own_ref, a2, acc, base = rest
    else:
        send_ref, a2, acc = rest
    j = pl.program_id(0)
    rows = x_ref.shape[0]

    @pl.when(j == 0)
    def _():
        far = (flipped(c2), flipped(c3)) if both else (c2[...], c3[...])
        parts = [
            dot_nn(c0[...], w0[...]),
            dot_nn(c1[...], w1[...]),
            dot_nn(far[0], w2[...]),
            dot_nn(far[1], w3[...]),
        ]
        if not both:
            parts = [p.astype(BF).astype(F32) for p in parts]
        resid = x_ref[...].astype(F32) + (parts[0] + parts[1] + parts[2] + parts[3])
        resid = resid + ob_ref[...].astype(F32)
        if both:
            low = resid.astype(BF)
            sent_ref[...] = low
            resid = low.astype(F32)
        a2[...] = norm_low(resid, g_ref, s_ref)
        if both:
            a2_ref[...] = a2[...]
            base[...] = resid[: rows // 2] + b2_ref[...].astype(F32)
        elif mode == "own":
            base[...] = resid + b2_ref[...].astype(F32)
        acc[...] = jnp.zeros_like(acc)

    def half(f1, b1, f2):
        pre = dot_nn(a2[...], f1[...]) + b1[...].astype(F32)
        if both:
            act, slope = gelu_both(pre)
            slope_ref[...] = slope
        else:
            act = pre * (0.5 * (1.0 + lax.erf(pre * 0.7071067811865476)))
        act = act.astype(BF)
        if both:
            act_ref[...] = act
        acc[...] += dot_nn(act, f2[...])

    @pl.when(j < half_steps)
    def _():
        half(f1a, b1a, f2a)

    @pl.when(j >= half_steps)
    def _():
        half(f1b, b1b, f2b)

    @pl.when(j == 2 * half_steps - 1)
    def _():
        if both:
            own_ref[...] = acc[: rows // 2] + base[...]
            send_ref[...] = acc[rows // 2 :].astype(BF)
        elif mode == "own":
            own_ref[...] = acc[...] + base[...]
        else:
            send_ref[...] = acc[...].astype(BF)


def forward(mode, name, rows, ctx, w_out, x, out_b, gain, shift, f1, b1, f2, b2, chunk):
    width = x.shape[1]
    heads_wide, hidden = w_out[0].shape[0], f1[0].shape[1]
    n = hidden // chunk
    both = mode == "both"
    near_at = 1 if mode == "send" else 0
    far_at = 1 if mode == "own" else 0
    first = lambda j: jnp.minimum(j, n - 1)
    second = lambda j: jnp.maximum(j - n, 0)
    at = lambda i, w: pl.BlockSpec((rows, w), lambda j: (i, 0))
    specs = [at(near_at, heads_wide)] * 2 + [at(far_at, heads_wide)] * 2
    specs += [whole(w.shape) for w in w_out]
    specs += [at(near_at, width)] + [whole((1, width))] * 3
    specs += [pl.BlockSpec((width, chunk), lambda j, f=f: (0, f(j))) for f in (first, second)]
    specs += [pl.BlockSpec((1, chunk), lambda j, f=f: (0, f(j))) for f in (first, second)]
    specs += [pl.BlockSpec((chunk, width), lambda j, f=f: (f(j), 0)) for f in (first, second)]
    specs += [whole((1, width))]
    half = rows // 2
    scratch = [pltpu.VMEM((rows, width), BF), pltpu.VMEM((rows, width), F32)]
    if both:
        outs = [sds((half, width), BF), sds((half, width), F32)] + [sds((rows, width), BF)] * 2
        outs += [sds((rows, 2 * hidden), BF), sds((rows, 2 * hidden), F32)]
        out_specs = [whole((half, width))] * 2 + [whole((rows, width))] * 2
        out_specs += [pl.BlockSpec((rows, chunk), lambda j: (0, j))] * 2
        scratch += [pltpu.VMEM((half, width), F32)]
    elif mode == "own":
        outs, out_specs = sds((rows, width), F32), whole((rows, width))
        scratch += [pltpu.VMEM((rows, width), F32)]
    else:
        outs, out_specs = sds((rows, width), BF), whole((rows, width))
    return call(
        functools.partial(forward_kernel, mode, n), name, (2 * n,), specs, out_specs, outs,
        (*ctx, *w_out, x, out_b, gain, shift, *f1, *b1, *f2, b2),
        scratch=scratch,
        flops=2 * rows * width * (4 * heads_wide + 4 * hidden),
    )


def head_kernel(block, piece, sc, own_ref, recv_ref, out_ref, w_ref, b_ref, inv_ref, dg_ref, do_ref, loss_ref, hb_ref, ob_ref):
    rows, width = own_ref.shape
    target = (own_ref[...] + recv_ref[...].astype(F32)).astype(BF).astype(F32)
    line = lax.broadcasted_iota(jnp.int32, (rows, 1), 0)
    slot = (line >> log2(piece)) * block + sc[ORD] * piece + (line & (piece - 1))
    live = slot < sc[CUM + CLIPS - 1]
    group = group_of(slot, sc, CUM)
    weight = jnp.zeros((rows, 1), F32)
    for c in range(CLIPS):
        weight = jnp.where(group == c, inv_ref[0, c], weight)
    weight = jnp.where(live, weight, 0.0)
    target = jnp.where(live, target, 0.0)
    miss = dot_nn(out_ref[...], w_ref[...]) + b_ref[...].astype(F32) - target
    dg = (weight * miss).astype(BF)
    dg_ref[...] = dg
    loss_ref[...] = 0.5 * jnp.sum(weight * miss * miss, axis=0, keepdims=True)
    hb_ref[...] = jnp.sum(dg.astype(F32), axis=0, keepdims=True)
    do = dot_nt(dg, w_ref[...]).astype(BF)
    do_ref[...] = do
    ob_ref[...] = jnp.sum(do.astype(F32), axis=0, keepdims=True)


def head_grad_kernel(sc, out_ref, own_ref, other_ref, keep_ref, send_ref):
    keep_ref[...] = dot_tn(out_ref[...], own_ref[...])
    send_ref[...] = dot_tn(out_ref[...], other_ref[...]).astype(BF)


def head_add_kernel(sc, keep_a, recv_a, keep_b, recv_b, keep_ref, send_ref):
    keep_ref[...] = keep_a[...] + recv_a[...].astype(F32)
    send_ref[...] = (keep_b[...] + recv_b[...].astype(F32)).astype(BF)


def feed_far_kernel(d0, d1, act_ref, slope_ref, a2_ref, f1, f2, g1_ref, g2_ref, gb_ref, acc_ref, d):
    half = d0.shape[0]
    d[:half] = d0[...]
    d[half:] = d1[...]
    grad = d[...]
    dpre = (dot_nt(grad, f2[...]) * slope_ref[...]).astype(BF)
    gb_ref[...] = jnp.sum(dpre.astype(F32), axis=0, keepdims=True)
    acc_ref[...] = dot_nt(dpre, f1[...])
    g2_ref[...] = dot_tn(act_ref[...], grad).astype(BF)
    g1_ref[...] = dot_tn(a2_ref[...], dpre).astype(BF)


def feed_own_kernel(d0, d1, slope_ref, f1, f2, before, dpre_ref, gb_ref, own_ref, send_ref, d):
    half = d0.shape[0]
    d[:half] = d0[...]
    d[half:] = d1[...]
    dpre = (dot_nt(d[...], f2[...]) * slope_ref[...]).astype(BF)
    dpre_ref[...] = dpre
    gb_ref[...] = jnp.sum(dpre.astype(F32), axis=0, keepdims=True)
    part = dot_nt(dpre, f1[...]) + before[...]
    own_ref[...] = part
    send_ref[:half] = part[half:].astype(BF)
    send_ref[half:] = part[:half].astype(BF)


def keep_and_send(value, mark, keep_ref, send_ref):
    half = value.shape[0] // 2
    top, bottom = value[:half], value[half:]
    first = mark == 0
    keep_ref[...] = jnp.where(first, top, bottom).astype(keep_ref.dtype)
    send_ref[...] = jnp.where(first, bottom, top).astype(send_ref.dtype)


def feed_grad_kernel(bit_a, bit_b, sc, d0, d1, act_ref, a2_ref, dpre_ref, r1, r2, hk, hr,
                     keep_a, send_a, keep_b, send_b, d):
    half = d0.shape[0]
    d[:half] = d0[...]
    d[half:] = d1[...]
    g1 = dot_tn(a2_ref[...], dpre_ref[...]) + r1[...].astype(F32)
    head = hk[...] + hr[...].astype(F32)
    keep_and_send(jnp.concatenate([g1, head], axis=1), (sc[HOME] >> bit_a) & 1, keep_a, send_a)
    g2 = dot_tn(act_ref[...], d[...]) + r2[...].astype(F32)
    keep_and_send(g2, (sc[HOME] >> bit_b) & 1, keep_b, send_b)


def project_grad_kernel(bit, more, sc, d_ref, a_ref, *rest):
    value = dot_tn(d_ref[...], a_ref[...])
    if more:
        value = jnp.concatenate([value, rest[0][...]], axis=0)
    keep_and_send(value, (sc[HOME] >> bit) & 1, rest[-2], rest[-1])


def input_grad_kernel(da_ref, db_ref, wa_ref, wb_ref, near_ref, send_ref):
    value = dot_nn(da_ref[...], wa_ref[...]) + dot_nn(db_ref[...], wb_ref[...])

    @pl.when(pl.program_id(0) == 0)
    def _():
        send_ref[...] = value.astype(BF)

    @pl.when(pl.program_id(0) == 1)
    def _():
        near_ref[...] = value


def stage_kernel(ops, sc, *refs):
    ins, outs = refs[: 2 * len(ops)], refs[2 * len(ops) :]
    at = 0
    for i, (kind, bit, parts) in enumerate(ops):
        a, b = ins[2 * i][...].astype(F32), ins[2 * i + 1][...].astype(F32)
        mark = (sc[HOME] >> bit) & 1
        if kind == "split":
            keep_and_send(a + b, mark, outs[at], outs[at + 1])
            at += 2
        elif kind == "add":
            outs[at][...] = (a + b).astype(BF)
            at += 1
        else:
            rows = a.shape[0]
            for lo, hi, dtype in parts:
                outs[at][:rows] = jnp.where(mark == 0, a[:, lo:hi], b[:, lo:hi]).astype(dtype)
                outs[at][rows:] = jnp.where(mark == 0, b[:, lo:hi], a[:, lo:hi]).astype(dtype)
                at += 1


def stage(name, ops, pairs, scalars):
    shapes = []
    for (kind, bit, parts), (a, b) in zip(ops, pairs):
        rows, width = a.shape
        if kind == "split":
            shapes.append([sds((rows // 2, width), BF)] * 2)
        elif kind == "add":
            shapes.append([sds((rows, width), BF)])
        else:
            shapes.append([sds((2 * rows, hi - lo), dtype) for lo, hi, dtype in parts])
    sizes = [a.shape[0] for a, _ in pairs] + [s.shape[0] for group in shapes for s in group]
    if all(size % 16 == 0 for size in sizes):
        flat = [x for pair in pairs for x in pair]
        outs = [s for group in shapes for s in group]
        found = call(
            functools.partial(stage_kernel, ops), name, (1,), [whole(x.shape) for x in flat],
            [whole(s.shape) for s in outs], outs, flat, scalars=scalars,
        )
    else:
        found = []
        for (kind, bit, parts), (a, b) in zip(ops, pairs):
            first = ((scalars[HOME] >> bit) & 1) == 0
            if kind == "join":
                for lo, hi, dtype in parts:
                    a1, b1 = a[:, lo:hi].astype(dtype), b[:, lo:hi].astype(dtype)
                    found.append(
                        jnp.where(first, jnp.concatenate([a1, b1], 0), jnp.concatenate([b1, a1], 0))
                    )
                continue
            total = (a.astype(F32) + b.astype(F32)).astype(BF)
            if kind == "add":
                found.append(total)
            else:
                half = total.shape[0] // 2
                found.append(jnp.where(first, total[:half], total[half:]))
                found.append(jnp.where(first, total[half:], total[:half]))
    result, at = [], 0
    for group in shapes:
        result.append(found[at : at + len(group)])
        at += len(group)
    return result


class Bundle:
    def __init__(self, bits, keep, recv, parts):
        self.bits, self.step, self.phase, self.parts = bits, 0, "split", parts
        self.flight = (keep, recv)
        self.result = None

    def op(self):
        if self.phase == "split":
            last = self.step == len(self.bits) - 1
            return ("add", 0, None) if last else ("split", self.bits[self.step + 1], None)
        width = self.flight[0].shape[1]
        parts = self.parts if self.step == 0 else ((0, width, BF),)
        return ("join", self.bits[self.step], parts)


def advance(name, bundles, partner, scalars):
    ops = [b.op() for b in bundles]
    done = stage(name, ops, [b.flight for b in bundles], scalars)
    for b, (kind, bit, _), got in zip(bundles, ops, done):
        if kind == "split":
            b.step += 1
            b.flight = (got[0], partner(got[1], bit))
        elif kind == "add":
            b.phase = "join"
            b.flight = (got[0], partner(got[0], b.bits[b.step]))
        elif b.step == 0:
            b.flight, b.result = None, got
        else:
            b.step -= 1
            b.flight = (got[0], partner(got[0], b.bits[b.step]))


def pick_kernel(places, in_ref, out_ref):
    for i in range(out_ref.shape[0]):
        out_ref[i] = in_ref[places[i]]


def place_kernel(sc, h0, h1, h2, h3, out_ref):
    for i, ref in enumerate((h0, h1, h2, h3)):

        @pl.when(pl.program_id(0) == i)
        def _(ref=ref):
            out_ref[...] = ref[...].astype(F32)


def norm_back_kernel(count, own_ref, recv_ref, *rest):
    base_refs, (x_ref, g_ref, dx_ref, sums_ref) = rest[:count], rest[count:]
    rows = own_ref.shape[0]
    mine = rows // count
    d = own_ref[...].astype(F32) + recv_ref[...].astype(F32)
    u, inverse = unit(x_ref[...].astype(F32))
    e = g_ref[...].astype(F32) * d
    mean_e = jnp.mean(e, axis=-1, keepdims=True)
    mean_eu = jnp.mean(e * u, axis=-1, keepdims=True)
    change = (e - mean_e - u * mean_eu) * inverse
    for i, base in enumerate(base_refs):
        at = slice(mine * i, mine * (i + 1))
        dx_ref[at] = (base[...].astype(F32) + change[at]).astype(dx_ref.dtype)
    sums_ref[...] = jnp.concatenate(
        [
            jnp.sum((d * u)[:mine], axis=0, keepdims=True),
            jnp.sum(d[:mine], axis=0, keepdims=True),
            jnp.sum(dx_ref[:mine].astype(F32), axis=0, keepdims=True),
        ],
        axis=0,
    )


def norm_back(name, own, recv, bases, x, gain, dtype):
    rows, width = own.shape
    block = pl.BlockSpec((rows, width), lambda *_: (0, 0))
    piece = pl.BlockSpec((rows // len(bases), width), lambda *_: (0, 0))
    return call(
        functools.partial(norm_back_kernel, len(bases)), name, (1,),
        [block] * 2 + [piece] * len(bases) + [block, whole((1, width))],
        [block, whole((3, width))],
        [sds((rows, width), dtype), sds((3, width), F32)],
        (own, recv, *bases, x, gain),
    )


def swap(x, bit, count):
    return lax.ppermute(x, "mp", [(i, i ^ bit) for i in range(count)])


def row(vector):
    return vector.reshape(1, -1)


def layout(mask_row, seg_row, order, home, steps, span):
    tokens = mask_row.shape[0]
    grid = mask_row.reshape(tokens // 128, 128).astype(BF)
    upper = (jnp.arange(128)[:, None] <= jnp.arange(128)[None, :]).astype(BF)
    within = jnp.dot(grid, upper, preferred_element_type=F32)
    lines = tokens // 128
    lower = (jnp.arange(lines)[:, None] > jnp.arange(lines)[None, :]).astype(BF)
    ahead = jnp.dot(lower, within[:, 127:].astype(BF), preferred_element_type=F32)
    count = (within + ahead).astype(jnp.int32).reshape(tokens)
    rank = jnp.where(mask_row == 1, count - 1, -1)
    labels = jnp.arange(CLIPS, dtype=jnp.int32)
    upto = (seg_row[None, :] <= labels[:, None]).astype(jnp.int32)
    ends = jnp.sum(upto, axis=1)
    cum = jnp.sum(upto * mask_row[None, :], axis=1)
    edge = jnp.arange(steps, dtype=jnp.int32) * span
    low = jnp.sum((count[None, :] <= edge[:, None]).astype(jnp.int32), axis=1)
    high = jnp.sum((count[None, :] < edge[:, None] + span).astype(jnp.int32), axis=1)
    low = low // span
    high = jnp.minimum(high, tokens - 1) // span + 1
    each = cum - jnp.concatenate([jnp.zeros((1,), jnp.int32), cum[:-1]])
    inverse = 1.0 / jnp.maximum(each, 1).astype(F32)
    scalars = jnp.concatenate([order, cum, ends, home[None].astype(jnp.int32), low, high])
    return rank.reshape(tokens // span, span), scalars, inverse.reshape(1, CLIPS)


def body(
    teacher_in, segment_ids, keep_mask, block_owner, student_in,
    t_norm1_gain, t_norm1_shift, t_qkv, t_qv_bias, t_out, t_out_bias,
    t_norm2_gain, t_norm2_shift, t_fc1, t_fc1_bias, t_fc2, t_fc2_bias,
    s_norm1_gain, s_norm1_shift, s_qkv, s_qv_bias, s_out, s_out_bias,
    s_norm2_gain, s_norm2_shift, s_fc1, s_fc1_bias, s_fc2, s_fc2_bias,
    head_weight, head_bias,
):
    mp = lax.axis_size("mp")
    me = lax.axis_index("mp")
    homes = lax.axis_size("dp")
    home = lax.axis_index("dp")
    slots, block, width = student_in.shape
    piece = block // mp
    rows = slots * block
    mine = rows // mp
    near = 2 * mine
    tokens, t_width = teacher_in.shape
    used = s_qkv.shape[2]
    wide = 256
    nb = 2
    span = nb * block
    steps = slots // nb
    core = lambda x: swap(x, 1, mp)
    across = lambda x: swap(x, 2, mp)

    order = jnp.stack([me, me ^ 2, me ^ 1, me ^ 3]).astype(jnp.int32)
    mask_row = lax.dynamic_index_in_dim(keep_mask, home, 0, keepdims=False)
    seg_row = lax.dynamic_index_in_dim(segment_ids, home, 0, keepdims=False)
    rank, scalars, inverse = layout(mask_row, seg_row, order, home, steps, span)

    t_w2 = across(t_out)
    s_w2 = across(s_out)
    s_f1 = (s_fc1, core(s_fc1))
    s_f2 = (s_fc2, core(s_fc2))
    biases = core(jnp.concatenate([t_fc1_bias, s_fc1_bias]))

    x4 = student_in.reshape(slots, mp, piece, width)
    by_piece = lambda w: pl.BlockSpec((mine, w), lambda k, sc: (k, 0))
    turned = pl.BlockSpec((used, mine), lambda k, sc: (0, k))
    x_stud, a_stud, sq, sk, sv, skt, svt = call(
        functools.partial(student_qkv_kernel, block), "student_qkv", (mp,),
        [
            pl.BlockSpec((slots, 1, piece, width), lambda k, sc: (0, sc[ORD + k], 0, 0)),
            whole((1, width)), whole((1, width)), whole(s_qkv.shape), whole(s_qv_bias.shape),
        ],
        [by_piece(width)] * 2 + [by_piece(wide)] * 3 + [turned] * 2,
        [sds((rows, width), BF)] * 2 + [sds((rows, wide), BF)] * 3 + [sds((used, rows), BF)] * 2,
        (x4, row(s_norm1_gain), row(s_norm1_shift), s_qkv, s_qv_bias),
        flops=2 * rows * width * 3 * wide, scalars=scalars,
    )
    heads = used // HD
    by_rows = lambda w: pl.BlockSpec((near, w), lambda j: (j, 0))
    by_lanes = lambda h: pl.BlockSpec((h, near), lambda j: (0, j))
    ctx, mixed, logs = call(
        functools.partial(student_attend_kernel, used), "student_attend", (rows // near,),
        [by_rows(wide), whole((rows, wide)), whole((used, rows))],
        [by_rows(used), by_lanes(used), by_lanes(8)],
        [sds((rows, used), BF), sds((used, rows), F32), sds((8, rows), F32)],
        (sq, sk, svt),
        flops=heads * rows * rows * wide * 4,
    )

    ctx, teacher_rows, t_w2, s_w2, s_f1, s_f2, biases, s_out_late = lax.optimization_barrier(
        (ctx, teacher_in, t_w2, s_w2, s_f1, s_f2, biases, s_out)
    )
    t_b1 = (row(t_fc1_bias), row(biases[: t_fc1_bias.shape[0]]))
    s_b1 = (row(s_fc1_bias), row(biases[t_fc1_bias.shape[0] :]))
    s_c0 = ctx[:near]
    s_c1 = core(ctx[near:])
    s_c2 = across(s_c0)
    s_w1 = core(s_out_late)
    s_w3 = core(s_w2)

    cols = t_qkv.shape[2]
    tk, tv = call(
        teacher_kv_kernel, "teacher_kv", (tokens // 512,),
        [
            pl.BlockSpec((512, t_width), lambda j, sc: (j, 0)), whole((1, t_width)), whole((1, t_width)),
            whole(t_qkv.shape), whole(t_qv_bias.shape),
        ],
        [pl.BlockSpec((512, 2 * cols), lambda j, sc: (j, 0)), pl.BlockSpec((cols, 512), lambda j, sc: (0, j))],
        [sds((tokens, 2 * cols), BF), sds((cols, tokens), BF)],
        (teacher_rows, row(t_norm1_gain), row(t_norm1_shift), t_qkv, t_qv_bias),
        flops=2 * tokens * t_width * 2 * cols, scalars=scalars,
    )
    tk, teacher_rows, s_c1, s_w1, s_w3, t_fc1_late, t_out_late = lax.optimization_barrier(
        (tk, teacher_rows, s_c1, s_w1, s_w3, t_fc1, t_out)
    )
    s_c3 = across(s_c1)
    t_f1 = (t_fc1, core(t_fc1_late))
    t_w1 = core(t_out_late)
    by_slot = lambda w: pl.BlockSpec((mp, nb, piece, w), lambda j, sc: (0, j, 0, 0))
    x_kept, tq = call(
        functools.partial(teacher_q_kernel, slots, block, span), "teacher_q", (steps,),
        [
            whole(teacher_in.shape), whole(rank.shape), whole((1, t_width)), whole((1, t_width)),
            whole(t_qkv.shape), whole(t_qv_bias.shape),
        ],
        [by_slot(t_width), by_slot(2 * cols)],
        [sds((mp, slots, piece, t_width), BF), sds((mp, slots, piece, 2 * cols), BF)],
        (teacher_rows, rank, row(t_norm1_gain), row(t_norm1_shift), t_qkv, t_qv_bias),
        scratch=[pltpu.VMEM((span, t_width), F32)],
        flops=2 * rows * t_width * (cols + 512), scalars=scalars,
    )
    half_slot = lambda w: pl.BlockSpec((mp, slots // 2, piece, w), lambda j: (0, j, 0, 0))
    t_ctx = call(
        teacher_attend_kernel, "teacher_attend", (2,),
        [half_slot(2 * cols), whole((tokens, 2 * cols)), whole((cols, tokens))],
        half_slot(cols),
        sds((mp, slots, piece, cols), BF),
        (tq, tk, tv),
        flops=(cols // HD) * rows * tokens * (512 + 256),
    ).reshape(rows, cols)

    t_ctx, s_c2, s_c3, t_f1, t_w1, t_fc2_late = lax.optimization_barrier((t_ctx, s_c2, s_c3, t_f1, t_w1, t_fc2))
    t_f2 = (t_fc2, core(t_fc2_late))
    t_w3 = core(t_w2)
    t_c0 = t_ctx[:near]
    t_c2 = across(t_c0)
    t_c1 = core(t_ctx[near:])
    t_c3 = across(t_c1)
    s_send, s_own, sent, a2, act, slope = forward(
        "both", "student_forward", near, (s_c0, s_c1, s_c2, s_c3), (s_out, s_w1, s_w2, s_w3), x_stud,
        row(s_out_bias), row(s_norm2_gain), row(s_norm2_shift), s_f1, s_b1, s_f2, row(s_fc2_bias), s_fc1.shape[1],
    )
    s_send, t_c2, t_c3, t_f2, t_w3 = lax.optimization_barrier((s_send, t_c2, t_c3, t_f2, t_w3))
    s_recv = across(s_send)
    t_args = (
        (t_ctx, t_c1, t_c2, t_c3), (t_out, t_w1, t_w2, t_w3), x_kept.reshape(rows, t_width), row(t_out_bias),
        row(t_norm2_gain), row(t_norm2_shift), t_f1, t_b1, t_f2, row(t_fc2_bias),
    )
    t_send = forward("send", "teacher_forward_far", mine, *t_args, 512)
    s_recv, t_args, t_send = lax.optimization_barrier((s_recv, t_args, t_send))
    t_recv = across(t_send)
    t_own = forward("own", "teacher_forward_own", mine, *t_args, 512)
    out_rows = (s_own + s_recv.astype(F32)).astype(BF)

    owners = lax.dynamic_index_in_dim(block_owner, home, 0, keepdims=False)
    capacity = (slots + homes - 1) // homes
    labels = jnp.arange(homes, dtype=jnp.int32)
    hits = (owners[:, None] == labels[None, :]).astype(jnp.int32)
    earlier = (jnp.arange(slots)[:, None] > jnp.arange(slots)[None, :]).astype(jnp.int32)
    order_in = jnp.sum(earlier * (owners[:, None] == owners[None, :]).astype(jnp.int32), axis=1)
    spot = jnp.where(owners >= 0, owners * capacity + order_in, homes * capacity)
    spots = jnp.arange(homes * capacity, dtype=jnp.int32)
    leaving = jnp.sum(
        jnp.where(spots[:, None] == spot[None, :], jnp.arange(slots, dtype=jnp.int32)[None, :], 0), axis=1
    )
    per_source = jnp.sum((block_owner == home).astype(jnp.int32), axis=1)
    ahead = (labels[:, None] > labels[None, :]).astype(jnp.int32)
    before = jnp.sum(ahead * per_source[None, :], axis=1)
    lane = jnp.arange(capacity, dtype=jnp.int32)
    target_slot = jnp.where(lane[None, :] < per_source[:, None], before[:, None] + lane[None, :], OWN).reshape(-1)
    chosen = jnp.sum(
        jnp.where(jnp.arange(OWN, dtype=jnp.int32)[:, None] == target_slot[None, :], spots[None, :], 0), axis=1
    )

    def pick(name, blocks, places):
        shape = (places.shape[0],) + blocks.shape[1:]
        return call(
            pick_kernel, name, (1,), [whole(blocks.shape)], whole(shape), sds(shape, blocks.dtype), (blocks,),
            scalars=places,
        )

    out_after, t_own = lax.optimization_barrier((out_rows, t_own))
    outbound = pick("pick_out", out_after.reshape(slots, piece, width), leaving)
    t_own, t_recv, outbound = lax.optimization_barrier((t_own, t_recv, outbound))
    inbound = lax.all_to_all(outbound, "dp", split_axis=0, concat_axis=0, tiled=True)

    d_guess, d_out, loss_row, head_b_row, fc2_b_row = call(
        functools.partial(head_kernel, block, piece), "head", (1,),
        [
            whole((mine, t_width)), whole((mine, t_width)), whole((mine, width)), whole((width, t_width)),
            whole((1, t_width)), pl.BlockSpec(memory_space=pltpu.SMEM),
        ],
        [whole((mine, t_width)), whole((mine, width)), whole((1, t_width)), whole((1, t_width)), whole((1, width))],
        [sds((mine, t_width), BF), sds((mine, width), BF), sds((1, t_width), F32), sds((1, t_width), F32), sds((1, width), F32)],
        (t_own, t_recv, out_rows, head_weight, row(head_bias), inverse),
        flops=4 * mine * width * t_width, scalars=scalars,
    )
    d_out_far = across(d_out)

    half_cols, quarter = t_width // 2, t_width // 4
    head_keep, head_send = call(
        head_grad_kernel, "head_grad", (1,),
        [
            whole((mine, width)),
            pl.BlockSpec((mine, half_cols), lambda j, sc: (0, sc[ORD] & 1)),
            pl.BlockSpec((mine, half_cols), lambda j, sc: (0, 1 - (sc[ORD] & 1))),
        ],
        [whole((width, half_cols))] * 2,
        [sds((width, half_cols), F32), sds((width, half_cols), BF)],
        (out_rows, d_guess, d_guess), scalars=scalars,
    )
    head_recv = core(head_send)
    own_quarter = pl.BlockSpec((width, quarter), lambda j, sc: (0, sc[ORD] >> 1))
    far_quarter = pl.BlockSpec((width, quarter), lambda j, sc: (0, 1 - (sc[ORD] >> 1)))
    head_keep, head_send = call(
        head_add_kernel, "head_add", (1,),
        [own_quarter, own_quarter, far_quarter, far_quarter],
        [whole((width, quarter))] * 2,
        [sds((width, quarter), F32), sds((width, quarter), BF)],
        (head_keep, head_recv, head_keep, head_recv), scalars=scalars,
    )
    d_out_far, head_send, inbound = lax.optimization_barrier((d_out_far, head_send, inbound))
    head_recv = across(head_send)

    hidden = s_fc1.shape[1]
    cut = lambda i: pl.BlockSpec((near, hidden), lambda *_: (0, i))
    square, turned_square, line = whole((width, hidden)), whole((hidden, width)), whole((1, hidden))
    tall, short_rows = whole((near, width)), whole((mine, width))
    d_scratch = [pltpu.VMEM((near, width), BF)]
    g1_send, g2_send, b1_send, da2_part = call(
        feed_far_kernel, "feed_back_far", (1,),
        [short_rows, short_rows, cut(1), cut(1), tall, square, turned_square],
        [square, turned_square, line, tall],
        [sds((width, hidden), BF), sds((hidden, width), BF), sds((1, hidden), F32), sds((near, width), F32)],
        (d_out, d_out_far, act, slope, a2, s_f1[1], s_f2[1]),
        scratch=d_scratch,
    )
    da2_part, g1_send, g2_send, head_recv = lax.optimization_barrier((da2_part, g1_send, g2_send, head_recv))
    g1_recv, g2_recv = core(g1_send), core(g2_send)
    dpre, b1_own, da2_own, da2_send = call(
        feed_own_kernel, "feed_back_own", (1,),
        [short_rows, short_rows, cut(0), square, turned_square, tall],
        [whole((near, hidden)), line, tall, tall],
        [sds((near, hidden), BF), sds((1, hidden), F32), sds((near, width), F32), sds((near, width), BF)],
        (d_out, d_out_far, slope, s_f1[0], s_f2[0], da2_part),
        scratch=d_scratch,
    )
    g1_recv, g2_recv, dpre, da2_send = lax.optimization_barrier((g1_recv, g2_recv, dpre, da2_send))
    da2_far = across(da2_send)

    bits = log2(homes)
    x_first = list(range(bits))
    z_first = x_first[1:] + x_first[:1]

    def partner(value, bit):
        return lax.ppermute(value, "dp", [(i, i ^ (1 << bit)) for i in range(homes)])

    def go(name, *bundles):
        advance(name, bundles, partner, scalars)

    half = width // 2
    a_width = hidden + quarter
    keep_a, send_a, keep_b, send_b = call(
        functools.partial(feed_grad_kernel, x_first[0], z_first[0]), "feed_back_grad", (1,),
        [
            short_rows, short_rows, cut(0), tall, whole((near, hidden)), square, turned_square,
            whole((width, quarter)), whole((width, quarter)),
        ],
        [whole((half, a_width))] * 2 + [whole((half, width))] * 2,
        [sds((half, a_width), BF)] * 2 + [sds((half, width), BF)] * 2,
        (d_out, d_out_far, act, a2, dpre, g1_recv, g2_recv, head_keep, head_recv),
        scratch=d_scratch, scalars=scalars,
    )
    one = Bundle(x_first, keep_a, partner(send_a, x_first[0]), ((0, hidden, F32), (hidden, a_width, BF)))
    two = Bundle(z_first, keep_b, partner(send_b, z_first[0]), ((0, width, F32),))

    da2_far, one.flight, two.flight = lax.optimization_barrier((da2_far, one.flight, two.flight))
    d_sent, sums2 = norm_back(
        "norm2_back", da2_own, da2_far, (d_out, d_out_far), sent, row(s_norm2_gain), BF
    )
    d_core = core(d_sent)
    d_core, one.flight, two.flight = lax.optimization_barrier((d_core, one.flight, two.flight))
    ds = (d_sent, d_core)
    for extra in range(bits - 2):
        go("sum_b%d" % extra, one, two)

    def back(name, picked, with_out):
        size = HD * len(picked)
        outs = [sds((rows, 3 * size), BF), sds((2, size), F32)] + [sds((used, width), F32)] * with_out
        return call(
            functools.partial(student_back_kernel, used, picked, with_out), name, (2,),
            [tall] * 2
            + [
                whole((used, width)), by_lanes(used), by_lanes(8), by_rows(wide), whole((rows, wide)),
                whole((rows, wide)), whole((used, rows)),
            ],
            [whole(o.shape) for o in outs], outs,
            (*ds, s_out, mixed, logs, sq, sk, sv, skt),
            scratch=[pltpu.VMEM((near, width), BF), pltpu.VMEM((near, wide), F32)]
            + [pltpu.VMEM((rows, wide), F32)] * 2 + [pltpu.VMEM((1, size), F32)]
            + [pltpu.VMEM((used, width), F32)] * with_out,
            flops=len(picked) * rows * rows * wide * 9,
        )

    def project(name, bit, d, more):
        size = d.shape[1] + sum(m.shape[0] for m in more)
        specs = [whole(d.shape), whole(a_stud.shape)] + [whole(m.shape) for m in more]
        keep, send = call(
            functools.partial(project_grad_kernel, bit, bool(more)), name, (1,), specs,
            [whole((size // 2, width))] * 2, [sds((size // 2, width), BF)] * 2,
            (d, a_stud, *more), scalars=scalars,
        )
        return keep, partner(send, bit)

    pair, odd = tuple(range(heads - 1)), (heads - 1,)
    d_pair, pair_sums = back("student_back_pair", pair, False)
    d_pair, one.flight, two.flight = lax.optimization_barrier((d_pair, one.flight, two.flight))
    go("sum_c", one, two)
    student_out = pick("pick_in", inbound, chosen)
    whole_width = ((0, width, BF),)
    three = Bundle(x_first, *project("project_pair", x_first[0], d_pair, ()), whole_width)
    tied = lax.optimization_barrier((*ds, three.flight[0], d_pair))
    ds, d_pair = tied[:2], tied[3]
    three.flight = (tied[2], three.flight[1])
    d_odd, odd_sums, g_out = back("student_back_odd", odd, True)
    d_odd, one.flight, two.flight, three.flight = lax.optimization_barrier(
        (d_odd, one.flight, two.flight, three.flight)
    )
    go("sum_d", one, two, three)
    four = Bundle(z_first, *project("project_odd", z_first[0], d_odd, (g_out,)), whole_width)
    mixed_size = HD * (heads - 1)
    w_turn = jnp.transpose(s_qkv, (0, 2, 1))
    w_pair = w_turn[:, :mixed_size].reshape(3 * mixed_size, width)
    w_odd = w_turn[:, mixed_size:].reshape(3 * HD, width)
    at = lambda w: pl.BlockSpec((near, w), lambda j: (1 - j, 0))
    da1_near, da1_send = call(
        input_grad_kernel, "input_grad", (2,),
        [at(3 * mixed_size), at(3 * HD), whole(w_pair.shape), whole(w_odd.shape)],
        [tall, tall], [sds((near, width), F32), sds((near, width), BF)],
        (d_pair, d_odd, w_pair, w_odd),
    )
    da1_recv = core(da1_send)
    da1_recv, one.flight, two.flight, three.flight, four.flight = lax.optimization_barrier(
        (da1_recv, one.flight, two.flight, three.flight, four.flight)
    )
    da1_own = da1_near[:mine] + da1_recv[:mine].astype(F32)
    da1_far = across((da1_near[mine:] + da1_recv[mine:].astype(F32)).astype(BF))
    go("sum_e", one, two, three, four)
    for extra in range(bits - 3):
        go("sum_f%d" % extra, one, two, three, four)
    grad_in, sums1 = norm_back("norm1_back", da1_own, da1_far, (d_sent,), x_stud, row(s_norm1_gain), F32)

    fit = lambda v: jnp.pad(v, ((0, 0), (0, width - v.shape[1])))
    loss_fit = jnp.sum(loss_row.reshape(-1, t_width // 4), axis=0, keepdims=True)
    early = jnp.concatenate(
        [sums2, fc2_b_row, head_b_row[:, :width], fit(head_b_row[:, width:]), fit(loss_fit), b1_send], axis=0
    )
    qv = fit(jnp.concatenate([pair_sums, odd_sums], axis=1))
    short = jnp.concatenate([sums1[:2], early], axis=0)
    short_own = jnp.concatenate([short[:9], b1_own], axis=0) + core(short)
    short_sum = short_own[:9] + across(short_own[:9])
    vec = jnp.concatenate([short_sum, short_own[9:], qv, jnp.zeros((4, width), F32)], axis=0)
    for bit in range(bits):
        vec = vec + partner(vec, bit)

    go("sum_g", one, two, three, four)
    turn = 0
    while three.result is None or four.result is None:
        go("sum_h%d" % turn, *[b for b in (three, four) if b.result is None])
        turn += 1
    while one.result is None:
        go("sum_last%d" % turn, one, two)
        turn += 1

    g1_all, head_all = one.result
    head_cross, head_core = across(head_all), core(head_all)
    piece_spec = whole((width, quarter))
    grad_head = call(
        place_kernel, "place_head", (mp,), [piece_spec] * 4,
        pl.BlockSpec((width, quarter), lambda k, sc: (0, 2 * (sc[ORD + k] & 1) + (sc[ORD + k] >> 1))),
        sds((width, t_width), F32),
        (head_all, head_cross, head_core, core(head_cross)), scalars=scalars,
    )
    low_pair, low_odd = three.result[0], four.result[0]
    qkv_turned = jnp.concatenate(
        [low_pair.reshape(3, mixed_size, width), low_odd[: 3 * HD].reshape(3, HD, width)], axis=1
    )
    return (
        jnp.sum(vec[8]),
        student_out,
        grad_in.reshape(slots, piece, width),
        vec[0],
        vec[1],
        jnp.transpose(qkv_turned, (0, 2, 1)).astype(F32),
        vec[10:12, :used],
        low_odd[3 * HD :].astype(F32),
        vec[4],
        vec[2],
        vec[3],
        g1_all,
        vec[9],
        two.result[0],
        vec[5],
        grad_head,
        jnp.concatenate([vec[6], vec[7, : t_width - width]]),
    )


def solution(mesh):
    rep = P()
    in_specs = (
        P("dp", None), rep, rep, rep, P("dp", None, None), rep, rep, P(None, None, "mp"), P(None, "mp"),
        P("mp", None), rep, rep, rep, P(None, "mp"), P("mp"), P("mp", None), rep, rep, rep,
        P(None, None, "mp"), P(None, "mp"), P("mp", None), rep, rep, rep, P(None, "mp"), P("mp"),
        P("mp", None), rep, rep, rep,
    )
    out_specs = (
        rep, P("dp", "mp", None), P("dp", "mp", None), rep, rep, P(None, None, "mp"), P(None, "mp"),
        P("mp", None), rep, rep, rep, P(None, "mp"), P("mp"), P("mp", None), rep, rep, rep,
    )
    return jax.shard_map(body, mesh=mesh, in_specs=in_specs, out_specs=out_specs, check_vma=False)
```

```python
import functools

import jax
import jax.numpy as jnp
from jax import lax
from jax.experimental import pallas as pl
from jax.experimental.pallas import tpu as pltpu
from jax.sharding import PartitionSpec as P

HD = 64
OWN = 8
CLIPS = 8
EPS = 1e-05
BIG = -1e30
F32 = jnp.float32
BF = jnp.bfloat16
LIMIT = 24 * 2**20
COST = 1

ORD, CUM, END, HOME, LOW = 0, 4, 12, 20, 21


def dot_nn(a, b):
    return lax.dot_general(a, b, (((1,), (0,)), ((), ())), preferred_element_type=F32)


def dot_nt(a, b):
    return lax.dot_general(a, b, (((1,), (1,)), ((), ())), preferred_element_type=F32)


def dot_tn(a, b):
    return lax.dot_general(a, b, (((0,), (0,)), ((), ())), preferred_element_type=F32)


def unit(values):
    mean = jnp.mean(values, axis=-1, keepdims=True)
    centred = values - mean
    spread = jnp.mean(centred * centred, axis=-1, keepdims=True)
    inverse = lax.rsqrt(spread + EPS)
    return centred * inverse, inverse


def norm_low(values, gain_ref, shift_ref):
    u, _ = unit(values)
    return (u * gain_ref[...].astype(F32) + shift_ref[...].astype(F32)).astype(BF)


def log2(size):
    return size.bit_length() - 1


def whole(shape):
    return pl.BlockSpec(shape, lambda *_: (0,) * len(shape))


def call(kernel, name, grid, in_specs, out_specs, out_shape, args, scratch=(), flops=0, scalars=None, limit=LIMIT, far=()):
    moved = sum(a.size * a.dtype.itemsize for a in args)
    moved += sum(s.size * jnp.dtype(s.dtype).itemsize for s in jax.tree.leaves(out_shape))
    if far:
        out_shape = [pltpu.HBM(o.shape, o.dtype) if i in far else o for i, o in enumerate(out_shape)]
    params = pltpu.CompilerParams(
        dimension_semantics=("arbitrary",) * len(grid), vmem_limit_bytes=limit
    )
    cost = pl.CostEstimate(flops=int(flops) // COST, bytes_accessed=int(moved) // COST, transcendentals=0)
    lead = 0 if scalars is None else 1
    spec = pltpu.PrefetchScalarGridSpec(
        num_scalar_prefetch=lead,
        grid=grid,
        in_specs=in_specs,
        out_specs=out_specs,
        scratch_shapes=list(scratch),
    )
    run = pl.pallas_call(
        kernel,
        grid_spec=spec,
        out_shape=out_shape,
        compiler_params=params,
        cost_estimate=cost,
        name=name,
    )
    return run(*([scalars] if lead else []), *args)


def sds(shape, dtype):
    return jax.ShapeDtypeStruct(shape, dtype)


def group_of(index, sc, base):
    group = jnp.zeros(index.shape, jnp.int32)
    for c in range(CLIPS):
        group = group + (index >= sc[base + c]).astype(jnp.int32)
    return group


def teacher_kv_kernel(sc, x_ref, g_ref, s_ref, w_ref, b_ref, k_ref, v_ref):
    rows = x_ref.shape[0]
    a = norm_low(x_ref[...].astype(F32), g_ref, s_ref)
    token = pl.program_id(0) * rows + lax.broadcasted_iota(jnp.int32, (rows, 1), 0)
    lane = lax.broadcasted_iota(jnp.int32, (rows, 128), 1)
    hot = jnp.where(lane == group_of(token, sc, END), 1.0, 0.0).astype(BF)
    k = (dot_nn(a, w_ref[1]).astype(BF).astype(F32) * (HD**-0.5)).astype(BF)
    for p in range(k.shape[1] // 128):
        k_ref[:, 256 * p : 256 * p + 128] = k[:, 128 * p : 128 * (p + 1)]
        k_ref[:, 256 * p + 128 : 256 * (p + 1)] = hot
    v_ref[...] = (dot_nn(a, w_ref[2]) + b_ref[1:2, :].astype(F32)).T.astype(BF)


def teacher_q_kernel(slots, block, step, sc, x_ref, rank_ref, g_ref, s_ref, w_ref, b_ref, xk_ref, q_ref, acc):
    j = pl.program_id(0)
    pieces, nb, piece, width = xk_ref.shape
    rows = pieces * nb * piece

    line = lax.broadcasted_iota(jnp.int32, (rows, 1), 0)
    part = line >> log2(nb * piece)
    inner = line & (nb * piece - 1)
    order = jnp.zeros((rows, 1), jnp.int32)
    for p in range(pieces):
        order = jnp.where(part == p, sc[ORD + p], order)
    slot = (j * nb + (inner >> log2(piece))) * block + order * piece + (inner & (piece - 1))
    group = group_of(slot, sc, CUM)
    acc[...] = jnp.zeros_like(acc)

    def one(t, _):
        hit = jnp.where(slot == rank_ref[pl.ds(t, 1), :], 1.0, 0.0).astype(BF)
        acc[...] += dot_nn(hit, x_ref[pl.ds(pl.multiple_of(t * step, step), step), :])
        return 0

    steps = slots // nb
    lax.fori_loop(sc[LOW + j], sc[LOW + steps + j], one, 0)
    kept = acc[...]
    xk_ref[...] = kept.astype(BF).reshape(xk_ref.shape)
    a = norm_low(kept, g_ref, s_ref)
    q = (dot_nn(a, w_ref[0]) + b_ref[0:1, :].astype(F32)).astype(BF)
    lane = lax.broadcasted_iota(jnp.int32, (rows, 128), 1)
    other = (lane != group) & (lane <= CLIPS)
    mask = jnp.where(other, BIG, 0.0).astype(BF)
    pairs = q.shape[1] // 128
    out = []
    for p in range(pairs):
        out += [q[:, 128 * p : 128 * (p + 1)], mask]
    q_ref[...] = jnp.concatenate(out, axis=1).reshape(q_ref.shape)


def softmax_mix(keys, query, values):
    scores = dot_nt(keys, query)
    top = jnp.max(scores, axis=0, keepdims=True)
    e = jnp.exp(scores - top)
    mass = jnp.sum(e, axis=0, keepdims=True)
    return dot_nn(values, e.astype(BF)) * (1.0 / mass), top + jnp.log(mass)


def teacher_attend_kernel(q_ref, k_ref, v_ref, ctx_ref):
    pieces, nb, piece, both = q_ref.shape
    rows = pieces * nb * piece
    q = q_ref[...].reshape(rows, both)
    lane = lax.broadcasted_iota(jnp.int32, (rows, 256), 1)
    mixed = []
    for p in range(both // 256):
        part = q[:, 256 * p : 256 * (p + 1)].astype(F32)
        for h in range(2):
            mine = ((lane >> 6) == h) | (lane >= 128)
            query = jnp.where(mine, part, 0.0).astype(BF)
            at = HD * (2 * p + h)
            mixed.append(softmax_mix(k_ref[:, 256 * p : 256 * (p + 1)], query, v_ref[at : at + HD, :])[0])
    ctx_ref[...] = jnp.concatenate(mixed, axis=0).T.astype(BF).reshape(ctx_ref.shape)


def student_qkv_kernel(block, sc, x_ref, g_ref, s_ref, w_ref, b_ref, xo_ref, a_ref, q_ref, k_ref, v_ref, kt_ref, vt_ref):
    slots, _, piece, width = x_ref.shape
    rows = slots * piece
    used, wide = w_ref.shape[1], q_ref.shape[1]
    x = x_ref[...].reshape(rows, width)
    xo_ref[...] = x
    a = norm_low(x.astype(F32), g_ref, s_ref)
    a_ref[...] = a
    line = lax.broadcasted_iota(jnp.int32, (rows, 1), 0)
    lane = lax.broadcasted_iota(jnp.int32, (rows, wide - used), 1)
    slot = (line >> log2(piece)) * block + sc[ORD + pl.program_id(0)] * piece + (line & (piece - 1))
    same = lane == group_of(slot, sc, CUM)
    q_ref[:, :used] = (dot_nt(a, w_ref[0]) + b_ref[0:1, :].astype(F32)).astype(BF)
    q_ref[:, used:] = jnp.where(same | (lane > CLIPS), 0.0, BIG).astype(BF)
    k = dot_nt(a, w_ref[1]).astype(BF).astype(F32) * (HD**-0.5)
    k_ref[:, :used] = k.astype(BF)
    k_ref[:, used:] = jnp.where(same, 1.0, 0.0).astype(BF)
    kt_ref[...] = k.T.astype(BF)
    v = dot_nt(a, w_ref[2]) + b_ref[1:2, :].astype(F32)
    v_ref[:, :used] = v.astype(BF)
    v_ref[:, used:] = jnp.zeros((rows, wide - used), BF)
    vt_ref[...] = v.T.astype(BF)


def student_attend_kernel(used, q_ref, k_ref, vt_ref, ctx_ref, mixed_ref, log_ref):
    q = q_ref[...].astype(F32)
    rows, wide = q.shape
    lane = lax.broadcasted_iota(jnp.int32, (rows, wide), 1)
    mixed, logs = [], []
    for h in range(used // HD):
        query = jnp.where(((lane >> 6) == h) | (lane >= used), q, 0.0).astype(BF)
        part, log = softmax_mix(k_ref[...], query, vt_ref[HD * h : HD * (h + 1), :])
        mixed.append(part)
        logs.append(log)
    total = jnp.concatenate(mixed, axis=0)
    mixed_ref[...] = total
    ctx_ref[...] = total.T.astype(BF)
    log_ref[...] = jnp.concatenate(logs + [jnp.zeros((8 - len(logs), rows), F32)], axis=0)


def student_back_kernel(used, picked, with_out, p0, p1, w_ref, mixed_ref, log_ref, q_ref, k_ref, v_ref, kt_ref, *rest):
    if with_out:
        out_ref, sums_ref, w_grad_ref, ds, da, dk, dv, dqs, dw = rest
    else:
        out_ref, sums_ref, ds, da, dk, dv, dqs = rest
    j = pl.program_id(0)
    steps = pl.num_programs(0)
    lo, size = HD * picked[0], HD * len(picked)
    rows, wide = q_ref.shape

    @pl.when(j == 0)
    def _():
        dk[...] = jnp.zeros_like(dk)
        dv[...] = jnp.zeros_like(dv)
        dqs[...] = jnp.zeros_like(dqs)
        ds[...] = p0[...]
        if with_out:
            dw[...] = jnp.zeros_like(dw)

    @pl.when(j == 1)
    def _():
        ds[...] = p1[...]

    grad = ds[...]
    da[:, :used] = dot_nt(grad, w_ref[...])
    da[:, used:] = jnp.zeros((rows, wide - used), F32)
    low = da[...].astype(BF).astype(F32)
    mixed = mixed_ref[...]
    turned = dot_nt(w_ref[lo : lo + size, :], grad).astype(BF).astype(F32)
    product = turned * mixed[lo : lo + size, :]
    if with_out:
        dw[...] += dot_nn(mixed.astype(BF), grad)
    lane = lax.broadcasted_iota(jnp.int32, (rows, wide), 1)
    q = q_ref[...].astype(F32)
    grads_q = []
    for i, h in enumerate(picked):
        mine = (lane >> 6) == h
        query = jnp.where(mine | (lane >= used), q, 0.0).astype(BF)
        outer = jnp.where(mine, low, 0.0).astype(BF)
        delta = jnp.sum(product[HD * i : HD * (i + 1), :], axis=0, keepdims=True)
        pt = jnp.exp(dot_nt(k_ref[...], query) - log_ref[h : h + 1, :])
        dst = (pt * (dot_nt(v_ref[...], outer) - delta)).astype(BF)
        dv[...] += dot_nn(pt.astype(BF), outer)
        dk[...] += dot_nn(dst, query)
        grads_q.append(dot_nn(kt_ref[HD * h : HD * (h + 1), :], dst))
    dq = jnp.concatenate(grads_q, axis=0).T.astype(BF)
    out_ref[pl.ds(pl.multiple_of(j * rows, rows), rows), 0:size] = dq
    dqs[...] += jnp.sum(dq.astype(F32), axis=0, keepdims=True)

    @pl.when(j == steps - 1)
    def _():
        out_ref[:, size : 2 * size] = (dk[:, lo : lo + size] * (HD**-0.5)).astype(BF)
        dv_low = dv[:, lo : lo + size].astype(BF)
        out_ref[:, 2 * size : 3 * size] = dv_low
        sums_ref[...] = jnp.concatenate(
            [dqs[...], jnp.sum(dv_low.astype(F32), axis=0, keepdims=True)], axis=0
        )
        if with_out:
            w_grad_ref[...] = dw[...]


def gelu_both(pre):
    phi = 0.5 * (1.0 + lax.erf(pre * 0.7071067811865476))
    return pre * phi, phi + pre * (0.3989422804014327 * jnp.exp(-0.5 * pre * pre))


def flipped(ref):
    half = ref.shape[0] // 2
    return jnp.concatenate([ref[half:], ref[:half]], axis=0)


def forward_kernel(
    mode, half_steps,
    c0, c1, c2, c3, w0, w1, w2, w3, x_ref, ob_ref, g_ref, s_ref,
    f1a, f1b, b1a, b1b, f2a, f2b, b2_ref, *rest,
):
    both = mode == "both"
    if both:
        send_ref, own_ref, sent_ref, a2_ref, act_ref, slope_ref, a2, acc, base = rest
    elif mode == "own":
        own_ref, a2, acc, base = rest
    else:
        send_ref, a2, acc = rest
    j = pl.program_id(0)
    rows = x_ref.shape[0]

    @pl.when(j == 0)
    def _():
        far = (flipped(c2), flipped(c3)) if both else (c2[...], c3[...])
        parts = [
            dot_nn(c0[...], w0[...]),
            dot_nn(c1[...], w1[...]),
            dot_nn(far[0], w2[...]),
            dot_nn(far[1], w3[...]),
        ]
        if not both:
            parts = [p.astype(BF).astype(F32) for p in parts]
        resid = x_ref[...].astype(F32) + (parts[0] + parts[1] + parts[2] + parts[3])
        resid = resid + ob_ref[...].astype(F32)
        if both:
            low = resid.astype(BF)
            sent_ref[...] = low
            resid = low.astype(F32)
        a2[...] = norm_low(resid, g_ref, s_ref)
        if both:
            a2_ref[...] = a2[...]
            base[...] = resid[: rows // 2] + b2_ref[...].astype(F32)
        elif mode == "own":
            base[...] = resid + b2_ref[...].astype(F32)
        acc[...] = jnp.zeros_like(acc)

    def half(f1, b1, f2):
        pre = dot_nn(a2[...], f1[...]) + b1[...].astype(F32)
        if both:
            act, slope = gelu_both(pre)
            slope_ref[...] = slope.astype(BF)
        else:
            act = pre * (0.5 * (1.0 + lax.erf(pre * 0.7071067811865476)))
        act = act.astype(BF)
        if both:
            act_ref[...] = act
        acc[...] += dot_nn(act, f2[...])

    @pl.when(j < half_steps)
    def _():
        half(f1a, b1a, f2a)

    @pl.when(j >= half_steps)
    def _():
        half(f1b, b1b, f2b)

    @pl.when(j == 2 * half_steps - 1)
    def _():
        if both:
            own_ref[...] = acc[: rows // 2] + base[...]
            send_ref[...] = acc[rows // 2 :].astype(BF)
        elif mode == "own":
            own_ref[...] = acc[...] + base[...]
        else:
            send_ref[...] = acc[...].astype(BF)


def forward(mode, name, rows, ctx, w_out, x, out_b, gain, shift, f1, b1, f2, b2, chunk):
    width = x.shape[1]
    heads_wide, hidden = w_out[0].shape[0], f1[0].shape[1]
    n = hidden // chunk
    both = mode == "both"
    near_at = 1 if mode == "send" else 0
    far_at = 1 if mode == "own" else 0
    first = lambda j: jnp.minimum(j, n - 1)
    second = lambda j: jnp.maximum(j - n, 0)
    at = lambda i, w: pl.BlockSpec((rows, w), lambda j: (i, 0))
    specs = [at(near_at, heads_wide)] * 2 + [at(far_at, heads_wide)] * 2
    specs += [whole(w.shape) for w in w_out]
    specs += [at(near_at, width)] + [whole((1, width))] * 3
    specs += [pl.BlockSpec((width, chunk), lambda j, f=f: (0, f(j))) for f in (first, second)]
    specs += [pl.BlockSpec((1, chunk), lambda j, f=f: (0, f(j))) for f in (first, second)]
    specs += [pl.BlockSpec((chunk, width), lambda j, f=f: (f(j), 0)) for f in (first, second)]
    specs += [whole((1, width))]
    half = rows // 2
    scratch = [pltpu.VMEM((rows, width), BF), pltpu.VMEM((rows, width), F32)]
    if both:
        outs = [sds((half, width), BF), sds((half, width), F32)] + [sds((rows, width), BF)] * 2
        outs += [sds((rows, 2 * hidden), BF)] * 2
        out_specs = [whole((half, width))] * 2 + [whole((rows, width))] * 2
        out_specs += [pl.BlockSpec((rows, chunk), lambda j: (0, j))] * 2
        scratch += [pltpu.VMEM((half, width), F32)]
    elif mode == "own":
        outs, out_specs = sds((rows, width), F32), whole((rows, width))
        scratch += [pltpu.VMEM((rows, width), F32)]
    else:
        outs, out_specs = sds((rows, width), BF), whole((rows, width))
    return call(
        functools.partial(forward_kernel, mode, n), name, (2 * n,), specs, out_specs, outs,
        (*ctx, *w_out, x, out_b, gain, shift, *f1, *b1, *f2, b2),
        scratch=scratch,
        flops=2 * rows * width * (4 * heads_wide + 4 * hidden), far=(2, 3, 4, 5) if both else (),
    )


def head_kernel(block, piece, sc, own_ref, recv_ref, out_ref, w_ref, b_ref, inv_ref, dg_ref, do_ref, loss_ref, hb_ref, ob_ref):
    rows, width = own_ref.shape
    target = (own_ref[...] + recv_ref[...].astype(F32)).astype(BF).astype(F32)
    line = lax.broadcasted_iota(jnp.int32, (rows, 1), 0)
    slot = (line >> log2(piece)) * block + sc[ORD] * piece + (line & (piece - 1))
    live = slot < sc[CUM + CLIPS - 1]
    group = group_of(slot, sc, CUM)
    weight = jnp.zeros((rows, 1), F32)
    for c in range(CLIPS):
        weight = jnp.where(group == c, inv_ref[0, c], weight)
    weight = jnp.where(live, weight, 0.0)
    target = jnp.where(live, target, 0.0)
    miss = dot_nn(out_ref[...], w_ref[...]) + b_ref[...].astype(F32) - target
    dg = (weight * miss).astype(BF)
    dg_ref[...] = dg
    loss_ref[...] = 0.5 * jnp.sum(weight * miss * miss, axis=0, keepdims=True)
    hb_ref[...] = jnp.sum(dg.astype(F32), axis=0, keepdims=True)
    do = dot_nt(dg, w_ref[...]).astype(BF)
    do_ref[...] = do
    ob_ref[...] = jnp.sum(do.astype(F32), axis=0, keepdims=True)


def head_grad_kernel(sc, out_ref, own_ref, other_ref, keep_ref, send_ref):
    keep_ref[...] = dot_tn(out_ref[...], own_ref[...])
    send_ref[...] = dot_tn(out_ref[...], other_ref[...]).astype(BF)


def head_add_kernel(sc, keep_a, recv_a, keep_b, recv_b, keep_ref, send_ref):
    keep_ref[...] = keep_a[...] + recv_a[...].astype(F32)
    send_ref[...] = (keep_b[...] + recv_b[...].astype(F32)).astype(BF)


def feed_far_kernel(d0, d1, act_ref, slope_ref, a2_ref, f1, f2, g1_ref, g2_ref, gb_ref, acc_ref, d):
    half = d0.shape[0]
    d[:half] = d0[...]
    d[half:] = d1[...]
    grad = d[...]
    dpre = (dot_nt(grad, f2[...]) * slope_ref[...].astype(F32)).astype(BF)
    gb_ref[...] = jnp.sum(dpre.astype(F32), axis=0, keepdims=True)
    acc_ref[...] = dot_nt(dpre, f1[...])
    g2_ref[...] = dot_tn(act_ref[...], grad).astype(BF)
    g1_ref[...] = dot_tn(a2_ref[...], dpre).astype(BF)


def feed_own_kernel(d0, d1, slope_ref, f1, f2, before, dpre_ref, gb_ref, own_ref, send_ref, d):
    half = d0.shape[0]
    d[:half] = d0[...]
    d[half:] = d1[...]
    dpre = (dot_nt(d[...], f2[...]) * slope_ref[...].astype(F32)).astype(BF)
    dpre_ref[...] = dpre
    gb_ref[...] = jnp.sum(dpre.astype(F32), axis=0, keepdims=True)
    part = dot_nt(dpre, f1[...]) + before[...]
    own_ref[...] = part
    send_ref[:half] = part[half:].astype(BF)
    send_ref[half:] = part[:half].astype(BF)


def keep_and_send(value, mark, keep_ref, send_ref):
    half = value.shape[0] // 2
    top, bottom = value[:half], value[half:]
    first = mark == 0
    keep_ref[...] = jnp.where(first, top, bottom).astype(keep_ref.dtype)
    send_ref[...] = jnp.where(first, bottom, top).astype(send_ref.dtype)


def feed_grad_kernel(bit_a, bit_b, sc, d0, d1, act_ref, a2_ref, dpre_ref, r1, r2, hk, hr,
                     keep_a, send_a, keep_b, send_b, d):
    half = d0.shape[0]
    d[:half] = d0[...]
    d[half:] = d1[...]
    g1 = dot_tn(a2_ref[...], dpre_ref[...]) + r1[...].astype(F32)
    head = hk[...] + hr[...].astype(F32)
    keep_and_send(jnp.concatenate([g1, head], axis=1), (sc[HOME] >> bit_a) & 1, keep_a, send_a)
    g2 = dot_tn(act_ref[...], d[...]) + r2[...].astype(F32)
    keep_and_send(g2, (sc[HOME] >> bit_b) & 1, keep_b, send_b)


def project_grad_kernel(bit, more, sc, d_ref, a_ref, *rest):
    value = dot_tn(d_ref[...], a_ref[...])
    if more:
        value = jnp.concatenate([value, rest[0][...]], axis=0)
    keep_and_send(value, (sc[HOME] >> bit) & 1, rest[-2], rest[-1])


def short_kernel(sums_ref, fc2_ref, hb_ref, loss_ref, b1s_ref, b1_ref, *rest):
    own_ref, send_ref = rest[-2:]
    width = own_ref.shape[1]
    for out in (own_ref, send_ref):
        out[...] = jnp.zeros(out.shape, F32)
        out[2:5, :] = sums_ref[...]
        out[5:6, :] = fc2_ref[...]
        out[6:7, :] = hb_ref[:, :width]
        left = hb_ref.shape[1] - width
        out[7:8, :left] = hb_ref[:, width:]
        loss = loss_ref[:, :left]
        for i in range(1, loss_ref.shape[1] // left):
            loss += loss_ref[:, left * i : left * (i + 1)]
        out[8:9, :left] = loss
    own_ref[9:10, :] = b1_ref[...]
    send_ref[9:10, :] = b1s_ref[...]
    at = 0
    for ref in rest[:-2]:
        own_ref[10:12, at : at + ref.shape[1]] = ref[...]
        at += ref.shape[1]


def input_grad_kernel(da_ref, db_ref, wa_ref, wb_ref, near_ref, send_ref):
    value = dot_nn(da_ref[...], wa_ref[...]) + dot_nn(db_ref[...], wb_ref[...])

    @pl.when(pl.program_id(0) == 0)
    def _():
        send_ref[...] = value.astype(BF)

    @pl.when(pl.program_id(0) == 1)
    def _():
        near_ref[...] = value


def stage_kernel(ops, sc, *refs):
    ins, outs = refs[: 2 * len(ops)], refs[2 * len(ops) :]
    at = 0
    for i, (kind, bit, parts) in enumerate(ops):
        a, b = ins[2 * i][...].astype(F32), ins[2 * i + 1][...].astype(F32)
        mark = (sc[HOME] >> bit) & 1
        if kind == "split":
            keep_and_send(a + b, mark, outs[at], outs[at + 1])
            at += 2
        elif kind == "add":
            outs[at][...] = (a + b).astype(BF)
            at += 1
        else:
            rows = a.shape[0]
            for lo, hi, dtype in parts:
                outs[at][:rows] = jnp.where(mark == 0, a[:, lo:hi], b[:, lo:hi]).astype(dtype)
                outs[at][rows:] = jnp.where(mark == 0, b[:, lo:hi], a[:, lo:hi]).astype(dtype)
                at += 1


def stage(name, ops, pairs, scalars):
    shapes = []
    for (kind, bit, parts), (a, b) in zip(ops, pairs):
        rows, width = a.shape
        if kind == "split":
            shapes.append([sds((rows // 2, width), BF)] * 2)
        elif kind == "add":
            shapes.append([sds((rows, width), BF)])
        else:
            shapes.append([sds((2 * rows, hi - lo), dtype) for lo, hi, dtype in parts])
    sizes = [a.shape[0] for a, _ in pairs] + [s.shape[0] for group in shapes for s in group]
    if all(size % 16 == 0 for size in sizes):
        flat = [x for pair in pairs for x in pair]
        outs = [s for group in shapes for s in group]
        found = call(
            functools.partial(stage_kernel, ops), name, (1,), [whole(x.shape) for x in flat],
            [whole(s.shape) for s in outs], outs, flat, scalars=scalars,
        )
    else:
        found = []
        for (kind, bit, parts), (a, b) in zip(ops, pairs):
            first = ((scalars[HOME] >> bit) & 1) == 0
            if kind == "join":
                for lo, hi, dtype in parts:
                    a1, b1 = a[:, lo:hi].astype(dtype), b[:, lo:hi].astype(dtype)
                    found.append(
                        jnp.where(first, jnp.concatenate([a1, b1], 0), jnp.concatenate([b1, a1], 0))
                    )
                continue
            total = (a.astype(F32) + b.astype(F32)).astype(BF)
            if kind == "add":
                found.append(total)
            else:
                half = total.shape[0] // 2
                found.append(jnp.where(first, total[:half], total[half:]))
                found.append(jnp.where(first, total[half:], total[:half]))
    result, at = [], 0
    for group in shapes:
        result.append(found[at : at + len(group)])
        at += len(group)
    return result


class Bundle:
    def __init__(self, bits, keep, recv, parts):
        self.bits, self.step, self.phase, self.parts = bits, 0, "split", parts
        self.flight = (keep, recv)
        self.result = None

    def op(self):
        if self.phase == "split":
            last = self.step == len(self.bits) - 1
            return ("add", 0, None) if last else ("split", self.bits[self.step + 1], None)
        width = self.flight[0].shape[1]
        parts = self.parts if self.step == 0 else ((0, width, BF),)
        return ("join", self.bits[self.step], parts)


def advance(name, bundles, partner, scalars):
    ops = [b.op() for b in bundles]
    done = stage(name, ops, [b.flight for b in bundles], scalars)
    for b, (kind, bit, _), got in zip(bundles, ops, done):
        if kind == "split":
            b.step += 1
            b.flight = (got[0], partner(got[1], bit))
        elif kind == "add":
            b.phase = "join"
            b.flight = (got[0], partner(got[0], b.bits[b.step]))
        elif b.step == 0:
            b.flight, b.result = None, got
        else:
            b.step -= 1
            b.flight = (got[0], partner(got[0], b.bits[b.step]))


def pick_kernel(places, in_ref, out_ref):
    for i in range(out_ref.shape[0]):
        out_ref[i] = in_ref[places[i]]


def place_kernel(sc, h0, h1, h2, h3, out_ref):
    for i, ref in enumerate((h0, h1, h2, h3)):

        @pl.when(pl.program_id(0) == i)
        def _(ref=ref):
            out_ref[...] = ref[...].astype(F32)


def norm_back_kernel(count, own_ref, recv_ref, *rest):
    base_refs, (x_ref, g_ref, dx_ref, sums_ref) = rest[:count], rest[count:]
    rows = own_ref.shape[0]
    mine = rows // count
    d = own_ref[...].astype(F32) + recv_ref[...].astype(F32)
    u, inverse = unit(x_ref[...].astype(F32))
    e = g_ref[...].astype(F32) * d
    mean_e = jnp.mean(e, axis=-1, keepdims=True)
    mean_eu = jnp.mean(e * u, axis=-1, keepdims=True)
    change = (e - mean_e - u * mean_eu) * inverse
    for i, base in enumerate(base_refs):
        at = slice(mine * i, mine * (i + 1))
        dx_ref[at] = (base[...].astype(F32) + change[at]).astype(dx_ref.dtype)
    sums_ref[...] = jnp.concatenate(
        [
            jnp.sum((d * u)[:mine], axis=0, keepdims=True),
            jnp.sum(d[:mine], axis=0, keepdims=True),
            jnp.sum(dx_ref[:mine].astype(F32), axis=0, keepdims=True),
        ],
        axis=0,
    )


def norm_back(name, own, recv, bases, x, gain, dtype):
    rows, width = own.shape
    block = pl.BlockSpec((rows, width), lambda *_: (0, 0))
    piece = pl.BlockSpec((rows // len(bases), width), lambda *_: (0, 0))
    return call(
        functools.partial(norm_back_kernel, len(bases)), name, (1,),
        [block] * 2 + [piece] * len(bases) + [block, whole((1, width))],
        [block, whole((3, width))],
        [sds((rows, width), dtype), sds((3, width), F32)],
        (own, recv, *bases, x, gain),
    )


def swap(x, bit, count):
    return lax.ppermute(x, "mp", [(i, i ^ bit) for i in range(count)])


def row(vector):
    return vector.reshape(1, -1)


def layout(mask_row, seg_row, order, home, steps, span):
    tokens = mask_row.shape[0]
    grid = mask_row.reshape(tokens // 128, 128).astype(BF)
    upper = (jnp.arange(128)[:, None] <= jnp.arange(128)[None, :]).astype(BF)
    within = jnp.dot(grid, upper, preferred_element_type=F32)
    lines = tokens // 128
    lower = (jnp.arange(lines)[:, None] > jnp.arange(lines)[None, :]).astype(BF)
    ahead = jnp.dot(lower, within[:, 127:].astype(BF), preferred_element_type=F32)
    count = (within + ahead).astype(jnp.int32).reshape(tokens)
    rank = jnp.where(mask_row == 1, count - 1, -1)
    labels = jnp.arange(CLIPS, dtype=jnp.int32)
    upto = (seg_row[None, :] <= labels[:, None]).astype(jnp.int32)
    ends = jnp.sum(upto, axis=1)
    cum = jnp.sum(upto * mask_row[None, :], axis=1)
    edge = jnp.arange(steps, dtype=jnp.int32) * span
    low = jnp.sum((count[None, :] <= edge[:, None]).astype(jnp.int32), axis=1)
    high = jnp.sum((count[None, :] < edge[:, None] + span).astype(jnp.int32), axis=1)
    low = low // span
    high = jnp.minimum(high, tokens - 1) // span + 1
    each = cum - jnp.concatenate([jnp.zeros((1,), jnp.int32), cum[:-1]])
    inverse = 1.0 / jnp.maximum(each, 1).astype(F32)
    scalars = jnp.concatenate([order, cum, ends, home[None].astype(jnp.int32), low, high])
    return rank.reshape(tokens // span, span), scalars, inverse.reshape(1, CLIPS)


def body(
    teacher_in, segment_ids, keep_mask, block_owner, student_in,
    t_norm1_gain, t_norm1_shift, t_qkv, t_qv_bias, t_out, t_out_bias,
    t_norm2_gain, t_norm2_shift, t_fc1, t_fc1_bias, t_fc2, t_fc2_bias,
    s_norm1_gain, s_norm1_shift, s_qkv, s_qv_bias, s_out, s_out_bias,
    s_norm2_gain, s_norm2_shift, s_fc1, s_fc1_bias, s_fc2, s_fc2_bias,
    head_weight, head_bias,
):
    mp = lax.axis_size("mp")
    me = lax.axis_index("mp")
    homes = lax.axis_size("dp")
    home = lax.axis_index("dp")
    slots, block, width = student_in.shape
    piece = block // mp
    rows = slots * block
    mine = rows // mp
    near = 2 * mine
    tokens, t_width = teacher_in.shape
    used = s_qkv.shape[2]
    wide = 256
    nb = 2
    span = nb * block
    steps = slots // nb
    core = lambda x: swap(x, 1, mp)
    across = lambda x: swap(x, 2, mp)

    order = jnp.stack([me, me ^ 2, me ^ 1, me ^ 3]).astype(jnp.int32)
    mask_row = lax.dynamic_index_in_dim(keep_mask, home, 0, keepdims=False)
    seg_row = lax.dynamic_index_in_dim(segment_ids, home, 0, keepdims=False)
    rank, scalars, inverse = layout(mask_row, seg_row, order, home, steps, span)

    t_w2 = across(t_out)
    s_w2 = across(s_out)
    s_f1 = (s_fc1, core(s_fc1))
    s_f2 = (s_fc2, core(s_fc2))
    biases = core(jnp.concatenate([t_fc1_bias, s_fc1_bias]))

    x4 = pltpu.with_memory_space_constraint(student_in.reshape(slots, mp, piece, width), pltpu.HBM)
    w_turn = jnp.transpose(s_qkv, (0, 2, 1))
    by_piece = lambda w: pl.BlockSpec((mine, w), lambda k, sc: (k, 0))
    turned = pl.BlockSpec((used, mine), lambda k, sc: (0, k))
    x_stud, a_stud, sq, sk, sv, skt, svt = call(
        functools.partial(student_qkv_kernel, block), "student_qkv", (mp,),
        [
            pl.BlockSpec((slots, 1, piece, width), lambda k, sc: (0, sc[ORD + k], 0, 0)),
            whole((1, width)), whole((1, width)), whole(w_turn.shape), whole(s_qv_bias.shape),
        ],
        [by_piece(width)] * 2 + [by_piece(wide)] * 3 + [turned] * 2,
        [sds((rows, width), BF)] * 2 + [sds((rows, wide), BF)] * 3 + [sds((used, rows), BF)] * 2,
        (x4, row(s_norm1_gain), row(s_norm1_shift), w_turn, s_qv_bias),
        flops=2 * rows * width * 3 * wide, scalars=scalars, far=(0, 1, 4, 5),
    )
    heads = used // HD
    by_rows = lambda w: pl.BlockSpec((near, w), lambda j: (j, 0))
    by_lanes = lambda h: pl.BlockSpec((h, near), lambda j: (0, j))
    ctx, mixed, logs = call(
        functools.partial(student_attend_kernel, used), "student_attend", (rows // near,),
        [by_rows(wide), whole((rows, wide)), whole((used, rows))],
        [by_rows(used), by_lanes(used), by_lanes(8)],
        [sds((rows, used), BF), sds((used, rows), F32), sds((8, rows), F32)],
        (sq, sk, svt),
        flops=heads * rows * rows * wide * 4, far=(1, 2),
    )

    ctx, teacher_rows, t_w2, s_w2, s_f1, s_f2, biases, s_out_late = lax.optimization_barrier(
        (ctx, teacher_in, t_w2, s_w2, s_f1, s_f2, biases, s_out)
    )
    t_b1 = (row(t_fc1_bias), row(biases[: t_fc1_bias.shape[0]]))
    s_b1 = (row(s_fc1_bias), row(biases[t_fc1_bias.shape[0] :]))
    s_c0 = ctx[:near]
    s_c1 = core(ctx[near:])
    s_c2 = across(s_c0)
    s_w1 = core(s_out_late)
    s_w3 = core(s_w2)

    cols = t_qkv.shape[2]
    tk, tv = call(
        teacher_kv_kernel, "teacher_kv", (tokens // 512,),
        [
            pl.BlockSpec((512, t_width), lambda j, sc: (j, 0)), whole((1, t_width)), whole((1, t_width)),
            whole(t_qkv.shape), whole(t_qv_bias.shape),
        ],
        [pl.BlockSpec((512, 2 * cols), lambda j, sc: (j, 0)), pl.BlockSpec((cols, 512), lambda j, sc: (0, j))],
        [sds((tokens, 2 * cols), BF), sds((cols, tokens), BF)],
        (teacher_rows, row(t_norm1_gain), row(t_norm1_shift), t_qkv, t_qv_bias),
        flops=2 * tokens * t_width * 2 * cols, scalars=scalars,
    )
    tk, teacher_rows, s_c1, s_w1, s_w3, t_fc1_late, t_out_late = lax.optimization_barrier(
        (tk, teacher_rows, s_c1, s_w1, s_w3, t_fc1, t_out)
    )
    s_c3 = across(s_c1)
    t_f1 = (t_fc1, core(t_fc1_late))
    t_w1 = core(t_out_late)
    by_slot = lambda w: pl.BlockSpec((mp, nb, piece, w), lambda j, sc: (0, j, 0, 0))
    x_kept, tq = call(
        functools.partial(teacher_q_kernel, slots, block, span), "teacher_q", (steps,),
        [
            whole(teacher_in.shape), whole(rank.shape), whole((1, t_width)), whole((1, t_width)),
            whole(t_qkv.shape), whole(t_qv_bias.shape),
        ],
        [by_slot(t_width), by_slot(2 * cols)],
        [sds((mp, slots, piece, t_width), BF), sds((mp, slots, piece, 2 * cols), BF)],
        (teacher_rows, rank, row(t_norm1_gain), row(t_norm1_shift), t_qkv, t_qv_bias),
        scratch=[pltpu.VMEM((span, t_width), F32)],
        flops=2 * rows * t_width * (cols + 512), scalars=scalars,
    )
    half_slot = lambda w: pl.BlockSpec((mp, slots // 2, piece, w), lambda j: (0, j, 0, 0))
    t_ctx = call(
        teacher_attend_kernel, "teacher_attend", (2,),
        [half_slot(2 * cols), whole((tokens, 2 * cols)), whole((cols, tokens))],
        half_slot(cols),
        sds((mp, slots, piece, cols), BF),
        (tq, tk, tv),
        flops=(cols // HD) * rows * tokens * (512 + 256),
    ).reshape(rows, cols)

    t_ctx, s_c2, s_c3, t_f1, t_w1, t_fc2_late = lax.optimization_barrier((t_ctx, s_c2, s_c3, t_f1, t_w1, t_fc2))
    t_f2 = (t_fc2, core(t_fc2_late))
    t_w3 = core(t_w2)
    t_c0 = t_ctx[:near]
    t_c2 = across(t_c0)
    t_c1 = core(t_ctx[near:])
    t_c3 = across(t_c1)
    s_send, s_own, sent, a2, act, slope = forward(
        "both", "student_forward", near, (s_c0, s_c1, s_c2, s_c3), (s_out, s_w1, s_w2, s_w3), x_stud,
        row(s_out_bias), row(s_norm2_gain), row(s_norm2_shift), s_f1, s_b1, s_f2, row(s_fc2_bias), s_fc1.shape[1],
    )
    s_send, t_c2, t_c3, t_f2, t_w3 = lax.optimization_barrier((s_send, t_c2, t_c3, t_f2, t_w3))
    s_recv = across(s_send)
    t_args = (
        (t_ctx, t_c1, t_c2, t_c3), (t_out, t_w1, t_w2, t_w3), x_kept.reshape(rows, t_width), row(t_out_bias),
        row(t_norm2_gain), row(t_norm2_shift), t_f1, t_b1, t_f2, row(t_fc2_bias),
    )
    t_send = forward("send", "teacher_forward_far", mine, *t_args, 512)
    s_recv, t_args, t_send = lax.optimization_barrier((s_recv, t_args, t_send))
    t_recv = across(t_send)
    t_own = forward("own", "teacher_forward_own", mine, *t_args, 512)
    out_rows = (s_own + s_recv.astype(F32)).astype(BF)

    owners = lax.dynamic_index_in_dim(block_owner, home, 0, keepdims=False)
    capacity = (slots + homes - 1) // homes
    labels = jnp.arange(homes, dtype=jnp.int32)
    hits = (owners[:, None] == labels[None, :]).astype(jnp.int32)
    earlier = (jnp.arange(slots)[:, None] > jnp.arange(slots)[None, :]).astype(jnp.int32)
    order_in = jnp.sum(earlier * (owners[:, None] == owners[None, :]).astype(jnp.int32), axis=1)
    spot = jnp.where(owners >= 0, owners * capacity + order_in, homes * capacity)
    spots = jnp.arange(homes * capacity, dtype=jnp.int32)
    leaving = jnp.sum(
        jnp.where(spots[:, None] == spot[None, :], jnp.arange(slots, dtype=jnp.int32)[None, :], 0), axis=1
    )
    per_source = jnp.sum((block_owner == home).astype(jnp.int32), axis=1)
    ahead = (labels[:, None] > labels[None, :]).astype(jnp.int32)
    before = jnp.sum(ahead * per_source[None, :], axis=1)
    lane = jnp.arange(capacity, dtype=jnp.int32)
    target_slot = jnp.where(lane[None, :] < per_source[:, None], before[:, None] + lane[None, :], OWN).reshape(-1)
    chosen = jnp.sum(
        jnp.where(jnp.arange(OWN, dtype=jnp.int32)[:, None] == target_slot[None, :], spots[None, :], 0), axis=1
    )

    def pick(name, blocks, places):
        shape = (places.shape[0],) + blocks.shape[1:]
        return call(
            pick_kernel, name, (1,), [whole(blocks.shape)], whole(shape), sds(shape, blocks.dtype), (blocks,),
            scalars=places,
        )

    out_after, t_own = lax.optimization_barrier((out_rows, t_own))
    outbound = pick("pick_out", out_after.reshape(slots, piece, width), leaving)
    t_own, t_recv, outbound = lax.optimization_barrier((t_own, t_recv, outbound))
    inbound = lax.all_to_all(outbound, "dp", split_axis=0, concat_axis=0, tiled=True)

    d_guess, d_out, loss_row, head_b_row, fc2_b_row = call(
        functools.partial(head_kernel, block, piece), "head", (1,),
        [
            whole((mine, t_width)), whole((mine, t_width)), whole((mine, width)), whole((width, t_width)),
            whole((1, t_width)), pl.BlockSpec(memory_space=pltpu.SMEM),
        ],
        [whole((mine, t_width)), whole((mine, width)), whole((1, t_width)), whole((1, t_width)), whole((1, width))],
        [sds((mine, t_width), BF), sds((mine, width), BF), sds((1, t_width), F32), sds((1, t_width), F32), sds((1, width), F32)],
        (t_own, t_recv, out_rows, head_weight, row(head_bias), inverse),
        flops=4 * mine * width * t_width, scalars=scalars,
    )
    d_out_far = across(d_out)

    half_cols, quarter = t_width // 2, t_width // 4
    head_keep, head_send = call(
        head_grad_kernel, "head_grad", (1,),
        [
            whole((mine, width)),
            pl.BlockSpec((mine, half_cols), lambda j, sc: (0, sc[ORD] & 1)),
            pl.BlockSpec((mine, half_cols), lambda j, sc: (0, 1 - (sc[ORD] & 1))),
        ],
        [whole((width, half_cols))] * 2,
        [sds((width, half_cols), F32), sds((width, half_cols), BF)],
        (out_rows, d_guess, d_guess), scalars=scalars,
    )
    head_recv = core(head_send)
    own_quarter = pl.BlockSpec((width, quarter), lambda j, sc: (0, sc[ORD] >> 1))
    far_quarter = pl.BlockSpec((width, quarter), lambda j, sc: (0, 1 - (sc[ORD] >> 1)))
    head_keep, head_send = call(
        head_add_kernel, "head_add", (1,),
        [own_quarter, own_quarter, far_quarter, far_quarter],
        [whole((width, quarter))] * 2,
        [sds((width, quarter), F32), sds((width, quarter), BF)],
        (head_keep, head_recv, head_keep, head_recv), scalars=scalars, far=(0,),
    )
    d_out_far, head_send, inbound = lax.optimization_barrier((d_out_far, head_send, inbound))
    head_recv = across(head_send)

    hidden = s_fc1.shape[1]
    cut = lambda i: pl.BlockSpec((near, hidden), lambda *_: (0, i))
    square, turned_square, line = whole((width, hidden)), whole((hidden, width)), whole((1, hidden))
    tall, short_rows = whole((near, width)), whole((mine, width))
    d_scratch = [pltpu.VMEM((near, width), BF)]
    g1_send, g2_send, b1_send, da2_part = call(
        feed_far_kernel, "feed_back_far", (1,),
        [short_rows, short_rows, cut(1), cut(1), tall, square, turned_square],
        [square, turned_square, line, tall],
        [sds((width, hidden), BF), sds((hidden, width), BF), sds((1, hidden), F32), sds((near, width), F32)],
        (d_out, d_out_far, act, slope, a2, s_f1[1], s_f2[1]),
        scratch=d_scratch,
    )
    da2_part, g1_send, g2_send, head_recv = lax.optimization_barrier((da2_part, g1_send, g2_send, head_recv))
    g1_recv, g2_recv = core(g1_send), core(g2_send)
    dpre, b1_own, da2_own, da2_send = call(
        feed_own_kernel, "feed_back_own", (1,),
        [short_rows, short_rows, cut(0), square, turned_square, tall],
        [whole((near, hidden)), line, tall, tall],
        [sds((near, hidden), BF), sds((1, hidden), F32), sds((near, width), F32), sds((near, width), BF)],
        (d_out, d_out_far, slope, s_f1[0], s_f2[0], da2_part),
        scratch=d_scratch,
    )
    g1_recv, g2_recv, dpre, da2_send = lax.optimization_barrier((g1_recv, g2_recv, dpre, da2_send))
    da2_far = across(da2_send)

    bits = log2(homes)
    x_first = list(range(bits))
    z_first = x_first[1:] + x_first[:1]

    def partner(value, bit):
        return lax.ppermute(value, "dp", [(i, i ^ (1 << bit)) for i in range(homes)])

    def go(name, *bundles):
        advance(name, bundles, partner, scalars)

    half = width // 2
    a_width = hidden + quarter
    keep_a, send_a, keep_b, send_b = call(
        functools.partial(feed_grad_kernel, x_first[0], z_first[0]), "feed_back_grad", (1,),
        [
            short_rows, short_rows, cut(0), tall, whole((near, hidden)), square, turned_square,
            whole((width, quarter)), whole((width, quarter)),
        ],
        [whole((half, a_width))] * 2 + [whole((half, width))] * 2,
        [sds((half, a_width), BF)] * 2 + [sds((half, width), BF)] * 2,
        (d_out, d_out_far, act, a2, dpre, g1_recv, g2_recv, head_keep, head_recv),
        scratch=d_scratch, scalars=scalars,
    )
    one = Bundle(x_first, keep_a, partner(send_a, x_first[0]), ((0, hidden, F32), (hidden, a_width, BF)))
    two = Bundle(z_first, keep_b, partner(send_b, z_first[0]), ((0, width, F32),))

    inbound, keep_a = lax.optimization_barrier((inbound, keep_a))
    one.flight = (keep_a, one.flight[1])
    student_out = pick("pick_in", inbound, chosen)
    da2_far, student_out, one.flight, two.flight = lax.optimization_barrier(
        (da2_far, student_out, one.flight, two.flight)
    )
    d_sent, sums2 = norm_back(
        "norm2_back", da2_own, da2_far, (d_out, d_out_far), sent, row(s_norm2_gain), BF
    )
    d_core = core(d_sent)
    d_core, one.flight, two.flight = lax.optimization_barrier((d_core, one.flight, two.flight))
    ds = (d_sent, d_core)
    for extra in range(bits - 2):
        go("sum_b%d" % extra, one, two)

    def back(name, picked, with_out):
        size = HD * len(picked)
        outs = [sds((rows, 3 * size), BF), sds((2, size), F32)] + [sds((used, width), F32)] * with_out
        return call(
            functools.partial(student_back_kernel, used, picked, with_out), name, (2,),
            [tall] * 2
            + [
                whole((used, width)), by_lanes(used), by_lanes(8), by_rows(wide), whole((rows, wide)),
                whole((rows, wide)), whole((used, rows)),
            ],
            [whole(o.shape) for o in outs], outs,
            (*ds, s_out, mixed, logs, sq, sk, sv, skt),
            scratch=[pltpu.VMEM((near, width), BF), pltpu.VMEM((near, wide), F32)]
            + [pltpu.VMEM((rows, wide), F32)] * 2 + [pltpu.VMEM((1, size), F32)]
            + [pltpu.VMEM((used, width), F32)] * with_out,
            flops=len(picked) * rows * rows * wide * 9,
        )

    def project(name, bit, d, more):
        size = d.shape[1] + sum(m.shape[0] for m in more)
        specs = [whole(d.shape), whole(a_stud.shape)] + [whole(m.shape) for m in more]
        keep, send = call(
            functools.partial(project_grad_kernel, bit, bool(more)), name, (1,), specs,
            [whole((size // 2, width))] * 2, [sds((size // 2, width), BF)] * 2,
            (d, a_stud, *more), scalars=scalars,
        )
        return keep, partner(send, bit)

    pair, odd = tuple(range(heads - 1)), (heads - 1,)
    d_pair, pair_sums = back("student_back_pair", pair, False)
    d_pair, one.flight, two.flight = lax.optimization_barrier((d_pair, one.flight, two.flight))
    go("sum_c", one, two)
    whole_width = ((0, width, BF),)
    three = Bundle(x_first, *project("project_pair", x_first[0], d_pair, ()), whole_width)
    tied = lax.optimization_barrier((*ds, three.flight[0], d_pair))
    ds, d_pair = tied[:2], tied[3]
    three.flight = (tied[2], three.flight[1])
    d_odd, odd_sums, g_out = back("student_back_odd", odd, True)
    d_odd, one.flight, two.flight, three.flight = lax.optimization_barrier(
        (d_odd, one.flight, two.flight, three.flight)
    )
    go("sum_d", one, two, three)
    four = Bundle(x_first, *project("project_odd", x_first[0], d_odd, (g_out,)), whole_width)
    mixed_size = HD * (heads - 1)
    w_pair = w_turn[:, :mixed_size].reshape(3 * mixed_size, width)
    w_odd = w_turn[:, mixed_size:].reshape(3 * HD, width)
    at = lambda w: pl.BlockSpec((near, w), lambda j: (1 - j, 0))
    da1_near, da1_send = call(
        input_grad_kernel, "input_grad", (2,),
        [at(3 * mixed_size), at(3 * HD), whole(w_pair.shape), whole(w_odd.shape)],
        [tall, tall], [sds((near, width), F32), sds((near, width), BF)],
        (d_pair, d_odd, w_pair, w_odd),
    )
    da1_recv = core(da1_send)
    da1_recv, one.flight, two.flight, three.flight, four.flight = lax.optimization_barrier(
        (da1_recv, one.flight, two.flight, three.flight, four.flight)
    )
    da1_own = da1_near[:mine] + da1_recv[:mine].astype(F32)
    da1_far = across((da1_near[mine:] + da1_recv[mine:].astype(F32)).astype(BF))
    go("sum_e", one, two, three, four)
    for extra in range(bits - 3):
        go("sum_f%d" % extra, one, two, three, four)
    short_in = (sums2, fc2_b_row, head_b_row, loss_row, b1_send, b1_own, pair_sums, odd_sums)
    short_early = call(
        short_kernel, "short", (1,), [whole(v.shape) for v in short_in],
        [whole((16, width))] * 2, [sds((16, width), F32)] * 2, short_in,
    )
    grad_in, sums1 = norm_back("norm1_back", da1_own, da1_far, (d_sent,), x_stud, row(s_norm1_gain), F32)

    norm_rows = jnp.concatenate([sums1[:2], jnp.zeros((14, width), F32)], axis=0)
    vec = short_early[0] + norm_rows + core(short_early[1] + norm_rows)
    home_rows = (jnp.arange(16) < 9)[:, None]
    vec = jnp.where(home_rows, vec + across(vec), vec)
    for bit in range(bits):
        vec = vec + partner(vec, bit)

    go("sum_g", one, two, three, four)
    turn = 0
    while three.result is None or four.result is None:
        go("sum_h%d" % turn, *[b for b in (three, four) if b.result is None])
        turn += 1
    while one.result is None:
        go("sum_last%d" % turn, one, two)
        turn += 1

    g1_all, head_all = one.result
    head_cross, head_core = across(head_all), core(head_all)
    piece_spec = whole((width, quarter))
    grad_head = call(
        place_kernel, "place_head", (mp,), [piece_spec] * 4,
        pl.BlockSpec((width, quarter), lambda k, sc: (0, 2 * (sc[ORD + k] & 1) + (sc[ORD + k] >> 1))),
        sds((width, t_width), F32),
        (head_all, head_cross, head_core, core(head_cross)), scalars=scalars,
    )
    low_pair, low_odd = three.result[0], four.result[0]
    qkv_turned = jnp.concatenate(
        [low_pair.reshape(3, mixed_size, width), low_odd[: 3 * HD].reshape(3, HD, width)], axis=1
    )
    return (
        jnp.sum(vec[8]),
        student_out,
        grad_in.reshape(slots, piece, width),
        vec[0],
        vec[1],
        jnp.transpose(qkv_turned, (0, 2, 1)).astype(F32),
        vec[10:12, :used],
        low_odd[3 * HD :].astype(F32),
        vec[4],
        vec[2],
        vec[3],
        g1_all,
        vec[9],
        two.result[0],
        vec[5],
        grad_head,
        jnp.concatenate([vec[6], vec[7, : t_width - width]]),
    )


def solution(mesh):
    rep = P()
    in_specs = (
        P("dp", None), rep, rep, rep, P("dp", None, None), rep, rep, P(None, None, "mp"), P(None, "mp"),
        P("mp", None), rep, rep, rep, P(None, "mp"), P("mp"), P("mp", None), rep, rep, rep,
        P(None, None, "mp"), P(None, "mp"), P("mp", None), rep, rep, rep, P(None, "mp"), P("mp"),
        P("mp", None), rep, rep, rep,
    )
    out_specs = (
        rep, P("dp", "mp", None), P("dp", "mp", None), rep, rep, P(None, None, "mp"), P(None, "mp"),
        P("mp", None), rep, rep, rep, P(None, "mp"), P("mp"), P("mp", None), rep, rep, rep,
    )
    return jax.shard_map(body, mesh=mesh, in_specs=in_specs, out_specs=out_specs, check_vma=False)
```

```python
import functools

import jax
import jax.numpy as jnp
from jax import lax
from jax.experimental import pallas as pl
from jax.experimental.pallas import tpu as pltpu
from jax.sharding import PartitionSpec as P

HD = 64
OWN = 8
CLIPS = 8
EPS = 1e-05
BIG = -1e30
F32 = jnp.float32
BF = jnp.bfloat16
LIMIT = 24 * 2**20
COST = 1

ORD, CUM, END, HOME, LOW = 0, 4, 12, 20, 21


def dot_nn(a, b):
    return lax.dot_general(a, b, (((1,), (0,)), ((), ())), preferred_element_type=F32)


def dot_nt(a, b):
    return lax.dot_general(a, b, (((1,), (1,)), ((), ())), preferred_element_type=F32)


def dot_tn(a, b):
    return lax.dot_general(a, b, (((0,), (0,)), ((), ())), preferred_element_type=F32)


def unit(values):
    mean = jnp.mean(values, axis=-1, keepdims=True)
    centred = values - mean
    spread = jnp.mean(centred * centred, axis=-1, keepdims=True)
    inverse = lax.rsqrt(spread + EPS)
    return centred * inverse, inverse


def norm_low(values, gain_ref, shift_ref):
    u, _ = unit(values)
    return (u * gain_ref[...].astype(F32) + shift_ref[...].astype(F32)).astype(BF)


def log2(size):
    return size.bit_length() - 1


def whole(shape):
    return pl.BlockSpec(shape, lambda *_: (0,) * len(shape))


def call(kernel, name, grid, in_specs, out_specs, out_shape, args, scratch=(), flops=0, scalars=None, limit=LIMIT, far=()):
    moved = sum(a.size * a.dtype.itemsize for a in args)
    moved += sum(s.size * jnp.dtype(s.dtype).itemsize for s in jax.tree.leaves(out_shape))
    if far:
        if isinstance(out_shape, list):
            out_shape = [pltpu.HBM(o.shape, o.dtype) if i in far else o for i, o in enumerate(out_shape)]
        else:
            out_shape = pltpu.HBM(out_shape.shape, out_shape.dtype)
    params = pltpu.CompilerParams(
        dimension_semantics=("arbitrary",) * len(grid), vmem_limit_bytes=limit
    )
    cost = pl.CostEstimate(flops=int(flops) // COST, bytes_accessed=int(moved) // COST, transcendentals=0)
    lead = 0 if scalars is None else 1
    spec = pltpu.PrefetchScalarGridSpec(
        num_scalar_prefetch=lead,
        grid=grid,
        in_specs=in_specs,
        out_specs=out_specs,
        scratch_shapes=list(scratch),
    )
    run = pl.pallas_call(
        kernel,
        grid_spec=spec,
        out_shape=out_shape,
        compiler_params=params,
        cost_estimate=cost,
        name=name,
    )
    return run(*([scalars] if lead else []), *args)


def sds(shape, dtype):
    return jax.ShapeDtypeStruct(shape, dtype)


def group_of(index, sc, base):
    group = jnp.zeros(index.shape, jnp.int32)
    for c in range(CLIPS):
        group = group + (index >= sc[base + c]).astype(jnp.int32)
    return group


def teacher_kv_kernel(sc, x_ref, g_ref, s_ref, w_ref, b_ref, k_ref, v_ref):
    rows = x_ref.shape[0]
    a = norm_low(x_ref[...].astype(F32), g_ref, s_ref)
    token = pl.program_id(0) * rows + lax.broadcasted_iota(jnp.int32, (rows, 1), 0)
    lane = lax.broadcasted_iota(jnp.int32, (rows, 128), 1)
    hot = jnp.where(lane == group_of(token, sc, END), 1.0, 0.0).astype(BF)
    k = (dot_nn(a, w_ref[1]).astype(BF).astype(F32) * (HD**-0.5)).astype(BF)
    for p in range(k.shape[1] // 128):
        k_ref[:, 256 * p : 256 * p + 128] = k[:, 128 * p : 128 * (p + 1)]
        k_ref[:, 256 * p + 128 : 256 * (p + 1)] = hot
    v_ref[...] = (dot_nn(a, w_ref[2]) + b_ref[1:2, :].astype(F32)).T.astype(BF)


def teacher_q_kernel(slots, block, step, sc, x_ref, rank_ref, g_ref, s_ref, w_ref, b_ref, xk_ref, q_ref, acc):
    j = pl.program_id(0)
    pieces, nb, piece, width = xk_ref.shape
    rows = pieces * nb * piece

    line = lax.broadcasted_iota(jnp.int32, (rows, 1), 0)
    part = line >> log2(nb * piece)
    inner = line & (nb * piece - 1)
    order = jnp.zeros((rows, 1), jnp.int32)
    for p in range(pieces):
        order = jnp.where(part == p, sc[ORD + p], order)
    slot = (j * nb + (inner >> log2(piece))) * block + order * piece + (inner & (piece - 1))
    group = group_of(slot, sc, CUM)
    acc[...] = jnp.zeros_like(acc)

    def one(t, _):
        hit = jnp.where(slot == rank_ref[pl.ds(t, 1), :], 1.0, 0.0).astype(BF)
        acc[...] += dot_nn(hit, x_ref[pl.ds(pl.multiple_of(t * step, step), step), :])
        return 0

    steps = slots // nb
    lax.fori_loop(sc[LOW + j], sc[LOW + steps + j], one, 0)
    kept = acc[...]
    xk_ref[...] = kept.astype(BF).reshape(xk_ref.shape)
    a = norm_low(kept, g_ref, s_ref)
    q = (dot_nn(a, w_ref[0]) + b_ref[0:1, :].astype(F32)).astype(BF)
    lane = lax.broadcasted_iota(jnp.int32, (rows, 128), 1)
    other = (lane != group) & (lane <= CLIPS)
    mask = jnp.where(other, BIG, 0.0).astype(BF)
    pairs = q.shape[1] // 128
    out = []
    for p in range(pairs):
        out += [q[:, 128 * p : 128 * (p + 1)], mask]
    q_ref[...] = jnp.concatenate(out, axis=1).reshape(q_ref.shape)


def softmax_mix(keys, query, values):
    scores = dot_nt(keys, query)
    top = jnp.max(scores, axis=0, keepdims=True)
    e = jnp.exp(scores - top)
    mass = jnp.sum(e, axis=0, keepdims=True)
    return dot_nn(values, e.astype(BF)) * (1.0 / mass), top + jnp.log(mass)


def teacher_attend_kernel(q_ref, k_ref, v_ref, ctx_ref):
    pieces, nb, piece, both = q_ref.shape
    rows = pieces * nb * piece
    part = q_ref[...].reshape(rows, both).astype(F32)
    lane = lax.broadcasted_iota(jnp.int32, (rows, both), 1)
    mixed = []
    for h in range(2):
        query = jnp.where(((lane >> 6) == h) | (lane >= 128), part, 0.0).astype(BF)
        mixed.append(softmax_mix(k_ref[...], query, v_ref[HD * h : HD * (h + 1), :])[0])
    ctx_ref[...] = jnp.concatenate(mixed, axis=0).T.astype(BF).reshape(ctx_ref.shape)


def student_qkv_kernel(block, sc, x_ref, g_ref, s_ref, w_ref, b_ref, xo_ref, a_ref, q_ref, k_ref, v_ref, kt_ref, vt_ref):
    slots, _, piece, width = x_ref.shape
    rows = slots * piece
    used, wide = w_ref.shape[1], q_ref.shape[1]
    x = x_ref[...].reshape(rows, width)
    xo_ref[...] = x
    a = norm_low(x.astype(F32), g_ref, s_ref)
    a_ref[...] = a
    line = lax.broadcasted_iota(jnp.int32, (rows, 1), 0)
    lane = lax.broadcasted_iota(jnp.int32, (rows, wide - used), 1)
    slot = (line >> log2(piece)) * block + sc[ORD + pl.program_id(0)] * piece + (line & (piece - 1))
    same = lane == group_of(slot, sc, CUM)
    q_ref[:, :used] = (dot_nt(a, w_ref[0]) + b_ref[0:1, :].astype(F32)).astype(BF)
    q_ref[:, used:] = jnp.where(same | (lane > CLIPS), 0.0, BIG).astype(BF)
    k = dot_nt(a, w_ref[1]).astype(BF).astype(F32) * (HD**-0.5)
    k_ref[:, :used] = k.astype(BF)
    k_ref[:, used:] = jnp.where(same, 1.0, 0.0).astype(BF)
    kt_ref[...] = k.T.astype(BF)
    v = dot_nt(a, w_ref[2]) + b_ref[1:2, :].astype(F32)
    v_ref[:, :used] = v.astype(BF)
    v_ref[:, used:] = jnp.zeros((rows, wide - used), BF)
    vt_ref[...] = v.T.astype(BF)


def student_attend_kernel(used, q_ref, k_ref, vt_ref, ctx_ref, mixed_ref, log_ref):
    q = q_ref[...].astype(F32)
    rows, wide = q.shape
    lane = lax.broadcasted_iota(jnp.int32, (rows, wide), 1)
    mixed, logs = [], []
    for h in range(used // HD):
        query = jnp.where(((lane >> 6) == h) | (lane >= used), q, 0.0).astype(BF)
        part, log = softmax_mix(k_ref[...], query, vt_ref[HD * h : HD * (h + 1), :])
        mixed.append(part)
        logs.append(log)
    total = jnp.concatenate(mixed, axis=0)
    mixed_ref[...] = total
    ctx_ref[...] = total.T.astype(BF)
    log_ref[...] = jnp.concatenate(logs + [jnp.zeros((8 - len(logs), rows), F32)], axis=0)


def student_probs_kernel(used, q_ref, k_ref, log_ref, out_ref):
    rows, wide = q_ref.shape
    lane = lax.broadcasted_iota(jnp.int32, (rows, wide), 1)
    h = pl.program_id(0)
    query = jnp.where(((lane >> 6) == h) | (lane >= used), q_ref[...].astype(F32), 0.0).astype(BF)
    out_ref[0] = jnp.exp(dot_nt(k_ref[...], query) - log_ref[pl.ds(h, 1), :]).astype(BF)


def student_back_kernel(used, picked, with_out, p0, p1, w_ref, mixed_ref, probs_ref, q_ref, v_ref, kt_ref, *rest):
    if with_out:
        out_ref, sums_ref, w_grad_ref, ds, da, dk, dv, dqs, dw = rest
    else:
        out_ref, sums_ref, ds, da, dk, dv, dqs = rest
    j = pl.program_id(0)
    steps = pl.num_programs(0)
    lo, size = HD * picked[0], HD * len(picked)
    rows, wide = q_ref.shape

    @pl.when(j == 0)
    def _():
        dk[...] = jnp.zeros_like(dk)
        dv[...] = jnp.zeros_like(dv)
        dqs[...] = jnp.zeros_like(dqs)
        ds[...] = p0[...]
        if with_out:
            dw[...] = jnp.zeros_like(dw)

    @pl.when(j == 1)
    def _():
        ds[...] = p1[...]

    grad = ds[...]
    da[:, :used] = dot_nt(grad, w_ref[...])
    da[:, used:] = jnp.zeros((rows, wide - used), F32)
    low = da[...].astype(BF).astype(F32)
    mixed = mixed_ref[...]
    turned = dot_nt(w_ref[lo : lo + size, :], grad).astype(BF).astype(F32)
    product = turned * mixed[lo : lo + size, :]
    if with_out:
        dw[...] += dot_nn(mixed.astype(BF), grad)
    lane = lax.broadcasted_iota(jnp.int32, (rows, wide), 1)
    q = q_ref[...].astype(F32)
    grads_q = []
    for i, h in enumerate(picked):
        mine = (lane >> 6) == h
        query = jnp.where(mine | (lane >= used), q, 0.0).astype(BF)
        outer = jnp.where(mine, low, 0.0).astype(BF)
        delta = jnp.sum(product[HD * i : HD * (i + 1), :], axis=0, keepdims=True)
        pt = probs_ref[i]
        dst = (pt.astype(F32) * (dot_nt(v_ref[...], outer) - delta)).astype(BF)
        dv[...] += dot_nn(pt, outer)
        dk[...] += dot_nn(dst, query)
        grads_q.append(dot_nn(kt_ref[HD * h : HD * (h + 1), :], dst))
    dq = jnp.concatenate(grads_q, axis=0).T.astype(BF)
    out_ref[pl.ds(pl.multiple_of(j * rows, rows), rows), 0:size] = dq
    dqs[...] += jnp.sum(dq.astype(F32), axis=0, keepdims=True)

    @pl.when(j == steps - 1)
    def _():
        out_ref[:, size : 2 * size] = (dk[:, lo : lo + size] * (HD**-0.5)).astype(BF)
        dv_low = dv[:, lo : lo + size].astype(BF)
        out_ref[:, 2 * size : 3 * size] = dv_low
        sums_ref[...] = jnp.concatenate(
            [dqs[...], jnp.sum(dv_low.astype(F32), axis=0, keepdims=True)], axis=0
        )
        if with_out:
            w_grad_ref[...] = dw[...]


def gelu_both(pre):
    phi = 0.5 * (1.0 + lax.erf(pre * 0.7071067811865476))
    return pre * phi, phi + pre * (0.3989422804014327 * jnp.exp(-0.5 * pre * pre))


def flipped(ref):
    half = ref.shape[0] // 2
    return jnp.concatenate([ref[half:], ref[:half]], axis=0)


def forward_kernel(
    mode, half_steps,
    *refs,
):
    both = mode == "both"
    count = 4 if both else 8
    ctx, (w0, w1, w2, w3, x_ref, ob_ref, g_ref, s_ref), refs = refs[:count], refs[count : count + 8], refs[count + 8 :]
    (f1a, f1b, b1a, b1b, f2a, f2b, b2_ref), rest = refs[:7], refs[7:]
    if both:
        send_ref, own_ref, sent_ref, a2_ref, act_ref, slope_ref, a2, acc, base = rest
    elif mode == "own":
        own_ref, a2, acc, base = rest
    else:
        send_ref, a2, acc = rest
    j = pl.program_id(0)
    rows = x_ref.shape[0]

    @pl.when(j == 0)
    def _():
        if both:
            found = [ctx[0][...], ctx[1][...], flipped(ctx[2]), flipped(ctx[3])]
        else:
            found = [jnp.concatenate([ctx[i][...], ctx[4 + i][...]], axis=1) for i in range(4)]
        parts = [dot_nn(c, w[...]) for c, w in zip(found, (w0, w1, w2, w3))]
        if not both:
            parts = [p.astype(BF).astype(F32) for p in parts]
        resid = x_ref[...].astype(F32) + (parts[0] + parts[1] + parts[2] + parts[3])
        resid = resid + ob_ref[...].astype(F32)
        if both:
            low = resid.astype(BF)
            sent_ref[...] = low
            resid = low.astype(F32)
        a2[...] = norm_low(resid, g_ref, s_ref)
        if both:
            a2_ref[...] = a2[...]
            base[...] = resid[: rows // 2] + b2_ref[...].astype(F32)
        elif mode == "own":
            base[...] = resid + b2_ref[...].astype(F32)
        acc[...] = jnp.zeros_like(acc)

    def half(f1, b1, f2):
        pre = dot_nn(a2[...], f1[...]) + b1[...].astype(F32)
        if both:
            act, slope = gelu_both(pre)
            slope_ref[...] = slope.astype(BF)
        else:
            act = pre * (0.5 * (1.0 + lax.erf(pre * 0.7071067811865476)))
        act = act.astype(BF)
        if both:
            act_ref[...] = act
        acc[...] += dot_nn(act, f2[...])

    @pl.when(j < half_steps)
    def _():
        half(f1a, b1a, f2a)

    @pl.when(j >= half_steps)
    def _():
        half(f1b, b1b, f2b)

    @pl.when(j == 2 * half_steps - 1)
    def _():
        if both:
            own_ref[...] = acc[: rows // 2] + base[...]
            send_ref[...] = acc[rows // 2 :].astype(BF)
        elif mode == "own":
            own_ref[...] = acc[...] + base[...]
        else:
            send_ref[...] = acc[...].astype(BF)


def forward(mode, name, rows, ctx, w_out, x, out_b, gain, shift, f1, b1, f2, b2, chunk):
    width = x.shape[1]
    heads_wide, hidden = w_out[0].shape[0], f1[0].shape[1]
    n = hidden // chunk
    both = mode == "both"
    near_at = 1 if mode == "send" else 0
    far_at = 1 if mode == "own" else 0
    first = lambda j: jnp.minimum(j, n - 1)
    second = lambda j: jnp.maximum(j - n, 0)
    at = lambda i, w: pl.BlockSpec((rows, w), lambda j: (i, 0))
    c_wide = ctx[0].shape[1]
    specs = ([at(near_at, c_wide)] * 2 + [at(far_at, c_wide)] * 2) * (len(ctx) // 4)
    specs += [whole(w.shape) for w in w_out]
    specs += [at(near_at, width)] + [whole((1, width))] * 3
    specs += [pl.BlockSpec((width, chunk), lambda j, f=f: (0, f(j))) for f in (first, second)]
    specs += [pl.BlockSpec((1, chunk), lambda j, f=f: (0, f(j))) for f in (first, second)]
    specs += [pl.BlockSpec((chunk, width), lambda j, f=f: (f(j), 0)) for f in (first, second)]
    specs += [whole((1, width))]
    half = rows // 2
    scratch = [pltpu.VMEM((rows, width), BF), pltpu.VMEM((rows, width), F32)]
    if both:
        outs = [sds((half, width), BF), sds((half, width), F32)] + [sds((rows, width), BF)] * 2
        outs += [sds((rows, 2 * hidden), BF)] * 2
        out_specs = [whole((half, width))] * 2 + [whole((rows, width))] * 2
        out_specs += [pl.BlockSpec((rows, chunk), lambda j: (0, j))] * 2
        scratch += [pltpu.VMEM((half, width), F32)]
    elif mode == "own":
        outs, out_specs = sds((rows, width), F32), whole((rows, width))
        scratch += [pltpu.VMEM((rows, width), F32)]
    else:
        outs, out_specs = sds((rows, width), BF), whole((rows, width))
    return call(
        functools.partial(forward_kernel, mode, n), name, (2 * n,), specs, out_specs, outs,
        (*ctx, *w_out, x, out_b, gain, shift, *f1, *b1, *f2, b2),
        scratch=scratch,
        flops=2 * rows * width * (4 * heads_wide + 4 * hidden), far=(2, 3, 4, 5) if both else (0,) if mode == "own" else (),
    )


def head_kernel(block, piece, sc, own_ref, recv_ref, out_ref, w_ref, b_ref, inv_ref, dg_ref, do_ref, loss_ref, hb_ref, ob_ref):
    rows, width = own_ref.shape
    target = (own_ref[...] + recv_ref[...].astype(F32)).astype(BF).astype(F32)
    line = lax.broadcasted_iota(jnp.int32, (rows, 1), 0)
    slot = (line >> log2(piece)) * block + sc[ORD] * piece + (line & (piece - 1))
    live = slot < sc[CUM + CLIPS - 1]
    group = group_of(slot, sc, CUM)
    weight = jnp.zeros((rows, 1), F32)
    for c in range(CLIPS):
        weight = jnp.where(group == c, inv_ref[0, c], weight)
    weight = jnp.where(live, weight, 0.0)
    target = jnp.where(live, target, 0.0)
    miss = dot_nn(out_ref[...], w_ref[...]) + b_ref[...].astype(F32) - target
    dg = (weight * miss).astype(BF)
    dg_ref[...] = dg
    loss_ref[...] = 0.5 * jnp.sum(weight * miss * miss, axis=0, keepdims=True)
    hb_ref[...] = jnp.sum(dg.astype(F32), axis=0, keepdims=True)
    do = dot_nt(dg, w_ref[...]).astype(BF)
    do_ref[...] = do
    ob_ref[...] = jnp.sum(do.astype(F32), axis=0, keepdims=True)


def head_grad_kernel(sc, out_ref, own_ref, other_ref, keep_ref, send_ref):
    keep_ref[...] = dot_tn(out_ref[...], own_ref[...])
    send_ref[...] = dot_tn(out_ref[...], other_ref[...]).astype(BF)


def head_add_kernel(sc, keep_a, recv_a, keep_b, recv_b, keep_ref, send_ref):
    keep_ref[...] = keep_a[...] + recv_a[...].astype(F32)
    send_ref[...] = (keep_b[...] + recv_b[...].astype(F32)).astype(BF)


def feed_far_kernel(d0, d1, act_ref, slope_ref, a2_ref, f1, f2, g1_ref, g2_ref, gb_ref, acc_ref, d):
    half = d0.shape[0]
    d[:half] = d0[...]
    d[half:] = d1[...]
    grad = d[...]
    dpre = (dot_nt(grad, f2[...]) * slope_ref[...].astype(F32)).astype(BF)
    gb_ref[...] = jnp.sum(dpre.astype(F32), axis=0, keepdims=True)
    acc_ref[...] = dot_nt(dpre, f1[...])
    g2_ref[...] = dot_tn(act_ref[...], grad).astype(BF)
    g1_ref[...] = dot_tn(a2_ref[...], dpre).astype(BF)


def feed_own_kernel(d0, d1, slope_ref, f1, f2, before, dpre_ref, gb_ref, own_ref, send_ref, d):
    half = d0.shape[0]
    d[:half] = d0[...]
    d[half:] = d1[...]
    dpre = (dot_nt(d[...], f2[...]) * slope_ref[...].astype(F32)).astype(BF)
    dpre_ref[...] = dpre
    gb_ref[...] = jnp.sum(dpre.astype(F32), axis=0, keepdims=True)
    part = dot_nt(dpre, f1[...]) + before[...]
    own_ref[...] = part
    send_ref[:half] = part[half:].astype(BF)
    send_ref[half:] = part[:half].astype(BF)


def keep_and_send(value, mark, keep_ref, send_ref):
    half = value.shape[0] // 2
    top, bottom = value[:half], value[half:]
    first = mark == 0
    keep_ref[...] = jnp.where(first, top, bottom).astype(keep_ref.dtype)
    send_ref[...] = jnp.where(first, bottom, top).astype(send_ref.dtype)


def feed_grad_kernel(bit_a, bit_b, sc, d0, d1, act_ref, a2_ref, dpre_ref, r1, r2, hk, hr,
                     keep_a, send_a, keep_b, send_b, d):
    half = d0.shape[0]
    d[:half] = d0[...]
    d[half:] = d1[...]
    g1 = dot_tn(a2_ref[...], dpre_ref[...]) + r1[...].astype(F32)
    head = hk[...] + hr[...].astype(F32)
    keep_and_send(jnp.concatenate([g1, head], axis=1), (sc[HOME] >> bit_a) & 1, keep_a, send_a)
    g2 = dot_tn(act_ref[...], d[...]) + r2[...].astype(F32)
    keep_and_send(g2, (sc[HOME] >> bit_b) & 1, keep_b, send_b)


def project_grad_kernel(bit, more, sc, d_ref, a_ref, *rest):
    value = dot_tn(d_ref[...], a_ref[...])
    if more:
        value = jnp.concatenate([value, rest[0][...]], axis=0)
    keep_and_send(value, (sc[HOME] >> bit) & 1, rest[-2], rest[-1])


def short_kernel(sums_ref, fc2_ref, hb_ref, loss_ref, b1s_ref, b1_ref, *rest):
    own_ref, send_ref = rest[-2:]
    width = own_ref.shape[1]
    for out in (own_ref, send_ref):
        out[...] = jnp.zeros(out.shape, F32)
        out[2:5, :] = sums_ref[...]
        out[5:6, :] = fc2_ref[...]
        out[6:7, :] = hb_ref[:, :width]
        left = hb_ref.shape[1] - width
        out[7:8, :left] = hb_ref[:, width:]
        loss = loss_ref[:, :left]
        for i in range(1, loss_ref.shape[1] // left):
            loss += loss_ref[:, left * i : left * (i + 1)]
        out[8:9, :left] = loss
    own_ref[9:10, :] = b1_ref[...]
    send_ref[9:10, :] = b1s_ref[...]
    at = 0
    for ref in rest[:-2]:
        own_ref[10:12, at : at + ref.shape[1]] = ref[...]
        at += ref.shape[1]


def input_grad_kernel(da_ref, db_ref, wa_ref, wb_ref, near_ref, send_ref):
    value = dot_nn(da_ref[...], wa_ref[...]) + dot_nn(db_ref[...], wb_ref[...])

    @pl.when(pl.program_id(0) == 0)
    def _():
        send_ref[...] = value.astype(BF)

    @pl.when(pl.program_id(0) == 1)
    def _():
        near_ref[...] = value


def stage_kernel(ops, sc, *refs):
    ins, outs = refs[: 2 * len(ops)], refs[2 * len(ops) :]
    at = 0
    for i, (kind, bit, parts) in enumerate(ops):
        a, b = ins[2 * i][...].astype(F32), ins[2 * i + 1][...].astype(F32)
        mark = (sc[HOME] >> bit) & 1
        if kind == "split":
            keep_and_send(a + b, mark, outs[at], outs[at + 1])
            at += 2
        elif kind == "add":
            outs[at][...] = (a + b).astype(BF)
            at += 1
        else:
            rows = a.shape[0]
            for lo, hi, dtype in parts:
                outs[at][:rows] = jnp.where(mark == 0, a[:, lo:hi], b[:, lo:hi]).astype(dtype)
                outs[at][rows:] = jnp.where(mark == 0, b[:, lo:hi], a[:, lo:hi]).astype(dtype)
                at += 1


def stage(name, ops, pairs, scalars):
    shapes = []
    for (kind, bit, parts), (a, b) in zip(ops, pairs):
        rows, width = a.shape
        if kind == "split":
            shapes.append([sds((rows // 2, width), BF)] * 2)
        elif kind == "add":
            shapes.append([sds((rows, width), BF)])
        else:
            shapes.append([sds((2 * rows, hi - lo), dtype) for lo, hi, dtype in parts])
    sizes = [a.shape[0] for a, _ in pairs] + [s.shape[0] for group in shapes for s in group]
    if all(size % 16 == 0 for size in sizes):
        flat = [x for pair in pairs for x in pair]
        outs = [s for group in shapes for s in group]
        found = call(
            functools.partial(stage_kernel, ops), name, (1,), [whole(x.shape) for x in flat],
            [whole(s.shape) for s in outs], outs, flat, scalars=scalars,
        )
    else:
        found = []
        for (kind, bit, parts), (a, b) in zip(ops, pairs):
            first = ((scalars[HOME] >> bit) & 1) == 0
            if kind == "join":
                for lo, hi, dtype in parts:
                    a1, b1 = a[:, lo:hi].astype(dtype), b[:, lo:hi].astype(dtype)
                    found.append(
                        jnp.where(first, jnp.concatenate([a1, b1], 0), jnp.concatenate([b1, a1], 0))
                    )
                continue
            total = (a.astype(F32) + b.astype(F32)).astype(BF)
            if kind == "add":
                found.append(total)
            else:
                half = total.shape[0] // 2
                found.append(jnp.where(first, total[:half], total[half:]))
                found.append(jnp.where(first, total[half:], total[:half]))
    result, at = [], 0
    for group in shapes:
        result.append(found[at : at + len(group)])
        at += len(group)
    return result


class Bundle:
    def __init__(self, bits, keep, recv, parts):
        self.bits, self.step, self.phase, self.parts = bits, 0, "split", parts
        self.flight = (keep, recv)
        self.result = None

    def op(self):
        if self.phase == "split":
            last = self.step == len(self.bits) - 1
            return ("add", 0, None) if last else ("split", self.bits[self.step + 1], None)
        width = self.flight[0].shape[1]
        parts = self.parts if self.step == 0 else ((0, width, BF),)
        return ("join", self.bits[self.step], parts)


def advance(name, bundles, partner, scalars):
    ops = [b.op() for b in bundles]
    done = stage(name, ops, [b.flight for b in bundles], scalars)
    for b, (kind, bit, _), got in zip(bundles, ops, done):
        if kind == "split":
            b.step += 1
            b.flight = (got[0], partner(got[1], bit))
        elif kind == "add":
            b.phase = "join"
            b.flight = (got[0], partner(got[0], b.bits[b.step]))
        elif b.step == 0:
            b.flight, b.result = None, got
        else:
            b.step -= 1
            b.flight = (got[0], partner(got[0], b.bits[b.step]))


def spread_kernel(came, going, shift, base, sc, in_ref, *refs):
    refs = list(refs)
    recv_ref = None if came is None else refs.pop(0)
    n = refs[0].shape[0] if going is not None else in_ref.shape[0]
    bit_in = 0 if came is None else (sc[base] >> (came - shift)) & 1

    def entry(i):
        if came is None:
            return in_ref[sc[i]]
        side = (i & ((1 << came) - 1)) | ((i >> (came + 1)) << came)
        return jnp.where(((i >> came) & 1) == bit_in, in_ref[i], recv_ref[side])

    if going is None:
        kept_ref, out_ref = refs[1], refs[0]
        for i in range(n):
            kept_ref[i] = entry(i)
        for i in range(out_ref.shape[0]):
            out_ref[i] = kept_ref[sc[i]]
        return
    keep_ref, send_ref = refs
    bit_out = (sc[base] >> (going - shift)) & 1
    for i in range(n):
        keep_ref[i] = entry(i)
    for j in range(send_ref.shape[0]):
        low = (j & ((1 << going) - 1)) | ((j >> going) << (going + 1))
        send_ref[j] = jnp.where(bit_out == 0, keep_ref[low | (1 << going)], keep_ref[low])


def place_kernel(sc, h0, h1, h2, h3, out_ref):
    for i, ref in enumerate((h0, h1, h2, h3)):

        @pl.when(pl.program_id(0) == i)
        def _(ref=ref):
            out_ref[...] = ref[...].astype(F32)


def norm_back_kernel(count, own_ref, recv_ref, *rest):
    base_refs, (x_ref, g_ref, dx_ref, sums_ref) = rest[:count], rest[count:]
    rows = own_ref.shape[0]
    mine = rows // count
    d = own_ref[...].astype(F32) + recv_ref[...].astype(F32)
    u, inverse = unit(x_ref[...].astype(F32))
    e = g_ref[...].astype(F32) * d
    mean_e = jnp.mean(e, axis=-1, keepdims=True)
    mean_eu = jnp.mean(e * u, axis=-1, keepdims=True)
    change = (e - mean_e - u * mean_eu) * inverse
    for i, base in enumerate(base_refs):
        at = slice(mine * i, mine * (i + 1))
        dx_ref[at] = (base[...].astype(F32) + change[at]).astype(dx_ref.dtype)
    sums_ref[...] = jnp.concatenate(
        [
            jnp.sum((d * u)[:mine], axis=0, keepdims=True),
            jnp.sum(d[:mine], axis=0, keepdims=True),
            jnp.sum(dx_ref[:mine].astype(F32), axis=0, keepdims=True),
        ],
        axis=0,
    )


def norm_back(name, own, recv, bases, x, gain, dtype):
    rows, width = own.shape
    block = pl.BlockSpec((rows, width), lambda *_: (0, 0))
    piece = pl.BlockSpec((rows // len(bases), width), lambda *_: (0, 0))
    return call(
        functools.partial(norm_back_kernel, len(bases)), name, (1,),
        [block] * 2 + [piece] * len(bases) + [block, whole((1, width))],
        [block, whole((3, width))],
        [sds((rows, width), dtype), sds((3, width), F32)],
        (own, recv, *bases, x, gain),
    )


def hbm(x):
    return pltpu.with_memory_space_constraint(x, pltpu.HBM)


def swap(x, bit, count):
    return lax.ppermute(x, "mp", [(i, i ^ bit) for i in range(count)])


def row(vector):
    return vector.reshape(1, -1)


def layout(mask_row, seg_row, order, home, steps, span):
    tokens = mask_row.shape[0]
    grid = mask_row.reshape(tokens // 128, 128).astype(BF)
    upper = (jnp.arange(128)[:, None] <= jnp.arange(128)[None, :]).astype(BF)
    within = jnp.dot(grid, upper, preferred_element_type=F32)
    lines = tokens // 128
    lower = (jnp.arange(lines)[:, None] > jnp.arange(lines)[None, :]).astype(BF)
    ahead = jnp.dot(lower, within[:, 127:].astype(BF), preferred_element_type=F32)
    count = (within + ahead).astype(jnp.int32).reshape(tokens)
    rank = jnp.where(mask_row == 1, count - 1, -1)
    labels = jnp.arange(CLIPS, dtype=jnp.int32)
    upto = (seg_row[None, :] <= labels[:, None]).astype(jnp.int32)
    ends = jnp.sum(upto, axis=1)
    cum = jnp.sum(upto * mask_row[None, :], axis=1)
    edge = jnp.arange(steps, dtype=jnp.int32) * span
    low = jnp.sum((count[None, :] <= edge[:, None]).astype(jnp.int32), axis=1)
    high = jnp.sum((count[None, :] < edge[:, None] + span).astype(jnp.int32), axis=1)
    low = low // span
    high = jnp.minimum(high, tokens - 1) // span + 1
    each = cum - jnp.concatenate([jnp.zeros((1,), jnp.int32), cum[:-1]])
    inverse = 1.0 / jnp.maximum(each, 1).astype(F32)
    first = jnp.concatenate([order, cum, ends, home[None].astype(jnp.int32)])
    scalars = jnp.concatenate([first, low, high])
    return rank.reshape(tokens // span, span), first, scalars, inverse.reshape(1, CLIPS)


def body(
    teacher_in, segment_ids, keep_mask, block_owner, student_in,
    t_norm1_gain, t_norm1_shift, t_qkv, t_qv_bias, t_out, t_out_bias,
    t_norm2_gain, t_norm2_shift, t_fc1, t_fc1_bias, t_fc2, t_fc2_bias,
    s_norm1_gain, s_norm1_shift, s_qkv, s_qv_bias, s_out, s_out_bias,
    s_norm2_gain, s_norm2_shift, s_fc1, s_fc1_bias, s_fc2, s_fc2_bias,
    head_weight, head_bias,
):
    mp = lax.axis_size("mp")
    me = lax.axis_index("mp")
    homes = lax.axis_size("dp")
    home = lax.axis_index("dp")
    slots, block, width = student_in.shape
    piece = block // mp
    rows = slots * block
    mine = rows // mp
    near = 2 * mine
    tokens, t_width = teacher_in.shape
    used = s_qkv.shape[2]
    wide = 256
    nb = 2
    span = nb * block
    steps = slots // nb
    core = lambda x: swap(x, 1, mp)
    across = lambda x: swap(x, 2, mp)

    order = jnp.stack([me, me ^ 2, me ^ 1, me ^ 3]).astype(jnp.int32)
    mask_row = lax.dynamic_index_in_dim(keep_mask, home, 0, keepdims=False)
    seg_row = lax.dynamic_index_in_dim(segment_ids, home, 0, keepdims=False)
    rank, first_scalars, scalars, inverse = layout(mask_row, seg_row, order, home, steps, span)

    t_w2 = across(t_out)
    s_w2 = across(s_out)
    s_f1 = (s_fc1, core(s_fc1))
    s_f2 = (s_fc2, core(s_fc2))
    biases = core(jnp.concatenate([t_fc1_bias, s_fc1_bias]))

    x4 = hbm(student_in.reshape(slots, mp, piece, width))
    w_turn = jnp.transpose(s_qkv, (0, 2, 1))
    by_piece = lambda w: pl.BlockSpec((mine, w), lambda k, sc: (k, 0))
    turned = pl.BlockSpec((used, mine), lambda k, sc: (0, k))
    x_stud, a_stud, sq, sk, sv, skt, svt = call(
        functools.partial(student_qkv_kernel, block), "student_qkv", (mp,),
        [
            pl.BlockSpec((slots, 1, piece, width), lambda k, sc: (0, sc[ORD + k], 0, 0)),
            whole((1, width)), whole((1, width)), whole(w_turn.shape), whole(s_qv_bias.shape),
        ],
        [by_piece(width)] * 2 + [by_piece(wide)] * 3 + [turned] * 2,
        [sds((rows, width), BF)] * 2 + [sds((rows, wide), BF)] * 3 + [sds((used, rows), BF)] * 2,
        (x4, row(s_norm1_gain), row(s_norm1_shift), w_turn, s_qv_bias),
        flops=2 * rows * width * 3 * wide, scalars=first_scalars, far=(0, 1, 4, 5),
    )
    heads = used // HD
    by_rows = lambda w: pl.BlockSpec((near, w), lambda j: (j, 0))
    by_lanes = lambda h: pl.BlockSpec((h, near), lambda j: (0, j))
    ctx, mixed, logs = call(
        functools.partial(student_attend_kernel, used), "student_attend", (rows // near,),
        [by_rows(wide), whole((rows, wide)), whole((used, rows))],
        [by_rows(used), by_lanes(used), by_lanes(8)],
        [sds((rows, used), BF), sds((used, rows), F32), sds((8, rows), F32)],
        (sq, sk, svt),
        flops=heads * rows * rows * wide * 4, far=(1, 2),
    )

    ctx, teacher_rows, t_w2, s_w2, s_f1, s_f2, biases, s_out_late = lax.optimization_barrier(
        (ctx, teacher_in, t_w2, s_w2, s_f1, s_f2, biases, s_out)
    )
    t_b1 = (row(t_fc1_bias), row(biases[: t_fc1_bias.shape[0]]))
    s_b1 = (row(s_fc1_bias), row(biases[t_fc1_bias.shape[0] :]))
    s_c0 = ctx[:near]
    s_c1 = core(ctx[near:])
    s_c2 = across(s_c0)
    s_w1 = core(s_out_late)
    s_w3 = core(s_w2)

    cols = t_qkv.shape[2]
    tk, tv = call(
        teacher_kv_kernel, "teacher_kv", (tokens // 512,),
        [
            pl.BlockSpec((512, t_width), lambda j, sc: (j, 0)), whole((1, t_width)), whole((1, t_width)),
            whole(t_qkv.shape), whole(t_qv_bias.shape),
        ],
        [pl.BlockSpec((512, 2 * cols), lambda j, sc: (j, 0)), pl.BlockSpec((cols, 512), lambda j, sc: (0, j))],
        [sds((tokens, 2 * cols), BF), sds((cols, tokens), BF)],
        (teacher_rows, row(t_norm1_gain), row(t_norm1_shift), t_qkv, t_qv_bias),
        flops=2 * tokens * t_width * 2 * cols, scalars=scalars, far=(0, 1),
    )
    tk, teacher_rows, s_c1, s_w1, s_w3, t_fc1_late, t_out_late = lax.optimization_barrier(
        (tk, teacher_rows, s_c1, s_w1, s_w3, t_fc1, t_out)
    )
    s_c3 = across(s_c1)
    t_f1 = (t_fc1, core(t_fc1_late))
    t_w1 = core(t_out_late)
    by_slot = lambda w: pl.BlockSpec((mp, nb, piece, w), lambda j, sc: (0, j, 0, 0))
    x_kept, tq = call(
        functools.partial(teacher_q_kernel, slots, block, span), "teacher_q", (steps,),
        [
            whole(teacher_in.shape), whole(rank.shape), whole((1, t_width)), whole((1, t_width)),
            whole(t_qkv.shape), whole(t_qv_bias.shape),
        ],
        [by_slot(t_width), by_slot(2 * cols)],
        [sds((mp, slots, piece, t_width), BF), sds((mp, slots, piece, 2 * cols), BF)],
        (hbm(teacher_rows), rank, row(t_norm1_gain), row(t_norm1_shift), hbm(t_qkv), t_qv_bias),
        scratch=[pltpu.VMEM((span, t_width), F32)],
        flops=2 * rows * t_width * (cols + 512), scalars=scalars,
    )
    def attend(name, p, query):
        half_slot = lambda w, lane: pl.BlockSpec((mp, slots // 2, piece, w), lambda j: (0, j, 0, lane))
        return call(
            teacher_attend_kernel, name, (2,),
            [
                half_slot(256, p), pl.BlockSpec((tokens, 256), lambda j: (0, p)),
                pl.BlockSpec((128, tokens), lambda j: (p, 0)),
            ],
            half_slot(128, 0),
            sds((mp, slots, piece, 128), BF),
            (query, tk, tv),
            flops=2 * rows * tokens * (512 + 256),
        ).reshape(rows, 128)

    t_ctx = []
    for p in range(cols // 128):
        mixed_pair = attend("teacher_attend%d" % p, p, tq)
        if p == 0:
            mixed_pair, tq, s_c2, s_c3 = lax.optimization_barrier((mixed_pair, tq, s_c2, s_c3))
        else:
            t_ctx[0], mixed_pair, t_f1, t_w1, t_fc2_late = lax.optimization_barrier(
                (t_ctx[0], mixed_pair, t_f1, t_w1, t_fc2)
            )
        t_ctx.append([mixed_pair, core(mixed_pair[near:]), across(mixed_pair)])
    t_f2 = (t_fc2, core(t_fc2_late))
    t_w3 = core(t_w2)

    s_send, s_own, sent, a2, act, slope = forward(
        "both", "student_forward", near, (s_c0, s_c1, s_c2, s_c3), (s_out, s_w1, s_w2, s_w3), x_stud,
        row(s_out_bias), row(s_norm2_gain), row(s_norm2_shift), s_f1, s_b1, s_f2, row(s_fc2_bias), s_fc1.shape[1],
    )
    s_send, t_ctx, t_f2, t_w3 = lax.optimization_barrier((s_send, t_ctx, t_f2, t_w3))
    t_ctx = [x for own, from_core, from_chip in t_ctx for x in (own, from_core, from_chip, core(from_chip[near:]))]
    s_recv = across(s_send)
    t_args = (
        t_ctx, (t_out, t_w1, t_w2, t_w3), x_kept.reshape(rows, t_width), row(t_out_bias),
        row(t_norm2_gain), row(t_norm2_shift), t_f1, t_b1, t_f2, row(t_fc2_bias),
    )
    t_send = forward("send", "teacher_forward_far", mine, *t_args, 512)
    s_recv, t_args, t_send = lax.optimization_barrier((s_recv, t_args, t_send))
    t_recv = across(t_send)
    out_rows = (s_own + s_recv.astype(F32)).astype(BF)

    owners = lax.dynamic_index_in_dim(block_owner, home, 0, keepdims=False)
    capacity = (slots + homes - 1) // homes
    labels = jnp.arange(homes, dtype=jnp.int32)
    hits = (owners[:, None] == labels[None, :]).astype(jnp.int32)
    earlier = (jnp.arange(slots)[:, None] > jnp.arange(slots)[None, :]).astype(jnp.int32)
    order_in = jnp.sum(earlier * (owners[:, None] == owners[None, :]).astype(jnp.int32), axis=1)
    spot = jnp.where(owners >= 0, owners * capacity + order_in, homes * capacity)
    spots = jnp.arange(homes * capacity, dtype=jnp.int32)
    leaving = jnp.sum(
        jnp.where(spots[:, None] == spot[None, :], jnp.arange(slots, dtype=jnp.int32)[None, :], 0), axis=1
    )
    per_source = jnp.sum((block_owner == home).astype(jnp.int32), axis=1)
    ahead = (labels[:, None] > labels[None, :]).astype(jnp.int32)
    before = jnp.sum(ahead * per_source[None, :], axis=1)
    lane = jnp.arange(capacity, dtype=jnp.int32)
    target_slot = jnp.where(lane[None, :] < per_source[:, None], before[:, None] + lane[None, :], OWN).reshape(-1)
    chosen = jnp.sum(
        jnp.where(jnp.arange(OWN, dtype=jnp.int32)[:, None] == target_slot[None, :], spots[None, :], 0), axis=1
    )

    bits = log2(homes)

    def partner(value, bit):
        return lax.ppermute(value, "dp", [(i, i ^ (1 << bit)) for i in range(homes)])

    entries, shift = homes * capacity, log2(capacity)
    entry_shape = (entries, piece, width)
    leaving_sc = jnp.concatenate([leaving, home[None].astype(jnp.int32)])
    home_sc = home[None].astype(jnp.int32)

    def spread(name, came, going, blocks, came_in, places):
        ins = [blocks] if came_in is None else [blocks, came_in]
        base = places.shape[0] - 1
        lift = lambda bit: None if bit is None else bit + shift
        if going is None:
            outs = [sds((OWN, piece, width), BF)]
            scratch = [pltpu.VMEM(entry_shape, BF)]
        else:
            outs = [sds(entry_shape, BF), sds((entries // 2, piece, width), BF)]
            scratch = []
        return call(
            functools.partial(spread_kernel, lift(came), lift(going), shift, base), name, (1,),
            [whole(x.shape) for x in ins], [whole(o.shape) for o in outs], outs, ins, scratch=scratch, scalars=places,
        )

    turns = [bits - 1] + list(range(bits - 1))
    kept, sending = spread("spread0", None, turns[0], out_rows.reshape(slots, piece, width), None, leaving_sc)
    t_args, kept = lax.optimization_barrier((t_args, kept))
    travel = partner(sending, turns[0])
    t_own = forward("own", "teacher_forward_own", mine, *t_args, 512)
    t_own, t_recv, travel = lax.optimization_barrier((t_own, t_recv, travel))
    kept, sending = spread("spread1", turns[0], turns[1], kept, travel, home_sc)
    t_own, kept = lax.optimization_barrier((t_own, kept))
    travel = partner(sending, turns[1])

    d_guess, d_out, loss_row, head_b_row, fc2_b_row = call(
        functools.partial(head_kernel, block, piece), "head", (1,),
        [
            whole((mine, t_width)), whole((mine, t_width)), whole((mine, width)), whole((width, t_width)),
            whole((1, t_width)), pl.BlockSpec(memory_space=pltpu.SMEM),
        ],
        [whole((mine, t_width)), whole((mine, width)), whole((1, t_width)), whole((1, t_width)), whole((1, width))],
        [sds((mine, t_width), BF), sds((mine, width), BF), sds((1, t_width), F32), sds((1, t_width), F32), sds((1, width), F32)],
        (t_own, t_recv, out_rows, hbm(head_weight), row(head_bias), inverse),
        flops=4 * mine * width * t_width, scalars=scalars,
    )
    d_out_far = across(d_out)

    half_cols, quarter = t_width // 2, t_width // 4
    head_keep, head_send = call(
        head_grad_kernel, "head_grad", (1,),
        [
            whole((mine, width)),
            pl.BlockSpec((mine, half_cols), lambda j, sc: (0, sc[ORD] & 1)),
            pl.BlockSpec((mine, half_cols), lambda j, sc: (0, 1 - (sc[ORD] & 1))),
        ],
        [whole((width, half_cols))] * 2,
        [sds((width, half_cols), F32), sds((width, half_cols), BF)],
        (out_rows, d_guess, d_guess), scalars=scalars,
    )
    head_recv = core(head_send)
    own_quarter = pl.BlockSpec((width, quarter), lambda j, sc: (0, sc[ORD] >> 1))
    far_quarter = pl.BlockSpec((width, quarter), lambda j, sc: (0, 1 - (sc[ORD] >> 1)))
    head_keep, head_send = call(
        head_add_kernel, "head_add", (1,),
        [own_quarter, own_quarter, far_quarter, far_quarter],
        [whole((width, quarter))] * 2,
        [sds((width, quarter), F32), sds((width, quarter), BF)],
        (head_keep, head_recv, head_keep, head_recv), scalars=scalars, far=(0,),
    )
    head_send, travel = lax.optimization_barrier((head_send, travel))
    for turn in range(2, bits):
        kept, sending = spread("spread%d" % turn, turns[turn - 1], turns[turn], kept, travel, home_sc)
        travel = partner(sending, turns[turn])
    d_out_far, head_send, kept = lax.optimization_barrier((d_out_far, head_send, kept))
    head_recv = across(head_send)

    hidden = s_fc1.shape[1]
    cut = lambda i: pl.BlockSpec((near, hidden), lambda *_: (0, i))
    square, turned_square, line = whole((width, hidden)), whole((hidden, width)), whole((1, hidden))
    tall, short_rows = whole((near, width)), whole((mine, width))
    d_scratch = [pltpu.VMEM((near, width), BF)]
    g1_send, g2_send, b1_send, da2_part = call(
        feed_far_kernel, "feed_back_far", (1,),
        [short_rows, short_rows, cut(1), cut(1), tall, square, turned_square],
        [square, turned_square, line, tall],
        [sds((width, hidden), BF), sds((hidden, width), BF), sds((1, hidden), F32), sds((near, width), F32)],
        (d_out, d_out_far, *map(hbm, (act, slope, a2, s_f1[1], s_f2[1]))),
        scratch=d_scratch,
    )
    da2_part, g1_send, g2_send, head_recv = lax.optimization_barrier((da2_part, g1_send, g2_send, head_recv))
    g1_recv, g2_recv = core(g1_send), core(g2_send)
    dpre, b1_own, da2_own, da2_send = call(
        feed_own_kernel, "feed_back_own", (1,),
        [short_rows, short_rows, cut(0), square, turned_square, tall],
        [whole((near, hidden)), line, tall, tall],
        [sds((near, hidden), BF), sds((1, hidden), F32), sds((near, width), F32), sds((near, width), BF)],
        (d_out, d_out_far, *map(hbm, (slope, s_f1[0], s_f2[0])), da2_part),
        scratch=d_scratch,
    )
    g1_recv, g2_recv, dpre, da2_send = lax.optimization_barrier((g1_recv, g2_recv, dpre, da2_send))
    da2_far = across(da2_send)

    x_first = list(range(bits))
    z_first = x_first[1:] + x_first[:1]

    def go(name, *bundles):
        advance(name, bundles, partner, scalars)

    half = width // 2
    a_width = hidden + quarter
    keep_a, send_a, keep_b, send_b = call(
        functools.partial(feed_grad_kernel, x_first[0], z_first[0]), "feed_back_grad", (1,),
        [
            short_rows, short_rows, cut(0), tall, whole((near, hidden)), square, turned_square,
            whole((width, quarter)), whole((width, quarter)),
        ],
        [whole((half, a_width))] * 2 + [whole((half, width))] * 2,
        [sds((half, a_width), BF)] * 2 + [sds((half, width), BF)] * 2,
        (d_out, d_out_far, hbm(act), hbm(a2), dpre, g1_recv, g2_recv, head_keep, head_recv),
        scratch=d_scratch, scalars=scalars,
    )
    one = Bundle(x_first, keep_a, partner(send_a, x_first[0]), ((0, hidden, F32), (hidden, a_width, BF)))
    two = Bundle(z_first, keep_b, partner(send_b, z_first[0]), ((0, width, F32),))

    q_late, keep_a = lax.optimization_barrier((sq, keep_a))
    one.flight = (keep_a, one.flight[1])
    probs = call(
        functools.partial(student_probs_kernel, used), "student_probs", (heads, rows // near),
        [
            pl.BlockSpec((near, wide), lambda h, j: (j, 0)), whole((rows, wide)),
            pl.BlockSpec((8, near), lambda h, j: (0, j)),
        ],
        [pl.BlockSpec((1, rows, near), lambda h, j: (h, 0, j))],
        [sds((heads, rows, rows), BF)],
        (q_late, sk, logs),
        flops=heads * rows * rows * wide * 2, far=(0,),
    )[0]
    da2_far, travel, probs, one.flight, two.flight = lax.optimization_barrier(
        (da2_far, travel, probs, one.flight, two.flight)
    )
    d_sent, sums2 = norm_back(
        "norm2_back", da2_own, da2_far, (d_out, d_out_far), sent, row(s_norm2_gain), BF
    )
    d_core = core(d_sent)
    d_core, one.flight, two.flight = lax.optimization_barrier((d_core, one.flight, two.flight))
    ds = (d_sent, d_core)
    for extra in range(bits - 2):
        go("sum_b%d" % extra, one, two)

    def back(name, picked, with_out):
        size = HD * len(picked)
        outs = [sds((rows, 3 * size), BF), sds((2, size), F32)] + [sds((used, width), F32)] * with_out
        return call(
            functools.partial(student_back_kernel, used, picked, with_out), name, (2,),
            [tall] * 2
            + [
                whole((used, width)), by_lanes(used),
                pl.BlockSpec((len(picked), rows, near), lambda j: (picked[0] // len(picked), 0, j)), by_rows(wide),
                whole((rows, wide)), whole((used, rows)),
            ],
            [whole(o.shape) for o in outs], outs,
            (*ds, s_out, mixed, probs, sq, sv, skt),
            scratch=[pltpu.VMEM((near, width), BF), pltpu.VMEM((near, wide), F32)]
            + [pltpu.VMEM((rows, wide), F32)] * 2 + [pltpu.VMEM((1, size), F32)]
            + [pltpu.VMEM((used, width), F32)] * with_out,
            flops=len(picked) * rows * rows * wide * 7, limit=36 * 2**20,
        )

    def project(name, bit, d, more):
        size = d.shape[1] + sum(m.shape[0] for m in more)
        specs = [whole(d.shape), whole(a_stud.shape)] + [whole(m.shape) for m in more]
        keep, send = call(
            functools.partial(project_grad_kernel, bit, bool(more)), name, (1,), specs,
            [whole((size // 2, width))] * 2, [sds((size // 2, width), BF)] * 2,
            (d, a_stud, *more), scalars=scalars,
        )
        return keep, partner(send, bit)

    pair, odd = tuple(range(heads - 1)), (heads - 1,)
    d_pair, pair_sums = back("student_back_pair", pair, False)
    d_pair, one.flight, two.flight = lax.optimization_barrier((d_pair, one.flight, two.flight))
    chosen_sc = jnp.concatenate([chosen, home_sc])
    student_out = spread("spread_end", turns[-1], None, kept, travel, chosen_sc)[0]
    go("sum_c", one, two)
    whole_width = ((0, width, BF),)
    three = Bundle(x_first, *project("project_pair", x_first[0], d_pair, ()), whole_width)
    tied = lax.optimization_barrier((*ds, three.flight[0], d_pair))
    ds, d_pair = tied[:2], tied[3]
    three.flight = (tied[2], three.flight[1])
    d_odd, odd_sums, g_out = back("student_back_odd", odd, True)
    d_odd, one.flight, two.flight, three.flight = lax.optimization_barrier(
        (d_odd, one.flight, two.flight, three.flight)
    )
    go("sum_d", one, two, three)
    four = Bundle(x_first, *project("project_odd", x_first[0], d_odd, (g_out,)), whole_width)
    mixed_size = HD * (heads - 1)
    w_pair = w_turn[:, :mixed_size].reshape(3 * mixed_size, width)
    w_odd = w_turn[:, mixed_size:].reshape(3 * HD, width)
    at = lambda w: pl.BlockSpec((near, w), lambda j: (1 - j, 0))
    da1_near, da1_send = call(
        input_grad_kernel, "input_grad", (2,),
        [at(3 * mixed_size), at(3 * HD), whole(w_pair.shape), whole(w_odd.shape)],
        [tall, tall], [sds((near, width), F32), sds((near, width), BF)],
        (d_pair, d_odd, w_pair, w_odd),
    )
    da1_recv = core(da1_send)
    da1_recv, one.flight, two.flight, three.flight, four.flight = lax.optimization_barrier(
        (da1_recv, one.flight, two.flight, three.flight, four.flight)
    )
    da1_own = da1_near[:mine] + da1_recv[:mine].astype(F32)
    da1_far = across((da1_near[mine:] + da1_recv[mine:].astype(F32)).astype(BF))
    go("sum_e", one, two, three, four)
    for extra in range(bits - 3):
        go("sum_f%d" % extra, one, two, three, four)
    short_in = (sums2, fc2_b_row, head_b_row, loss_row, b1_send, b1_own, pair_sums, odd_sums)
    short_early = call(
        short_kernel, "short", (1,), [whole(v.shape) for v in short_in],
        [whole((16, width))] * 2, [sds((16, width), F32)] * 2, short_in,
    )
    grad_in, sums1 = norm_back("norm1_back", da1_own, da1_far, (d_sent,), x_stud, row(s_norm1_gain), F32)

    def tie(held, *bundles):
        kept, held = lax.optimization_barrier(([b.flight[0] for b in bundles], held))
        for b, first in zip(bundles, kept):
            b.flight = (first, b.flight[1])
        return held

    norm_rows = jnp.concatenate([sums1[:2], jnp.zeros((14, width), F32)], axis=0)
    vec = short_early[0] + norm_rows + core(short_early[1] + norm_rows)
    home_rows = (jnp.arange(16) < 9)[:, None]
    vec = tie(vec, three)
    go("sum_g", one, two, three, four)
    vec = jnp.where(home_rows, vec + across(vec), vec)
    turn = 0
    while three.result is None or four.result is None or one.result is None:
        left = [b for b in (three, four) if b.result is None]
        if turn <= bits and left:
            vec = tie(vec, left[0])
        if turn < bits:
            moved_vec = partner(vec, turn)
        if turn % 2 and one.result is None:
            left = left + [one, two]
        go("sum_h%d" % turn, *left)
        if turn < bits:
            vec = vec + moved_vec
        turn += 1
    for bit in range(turn, bits):
        vec = vec + partner(vec, bit)

    g1_all, head_all = one.result
    head_cross, head_core = across(head_all), core(head_all)
    piece_spec = whole((width, quarter))
    grad_head = call(
        place_kernel, "place_head", (mp,), [piece_spec] * 4,
        pl.BlockSpec((width, quarter), lambda k, sc: (0, 2 * (sc[ORD + k] & 1) + (sc[ORD + k] >> 1))),
        sds((width, t_width), F32),
        (head_all, head_cross, head_core, core(head_cross)), scalars=scalars,
    )
    low_pair, low_odd = three.result[0], four.result[0]
    qkv_turned = jnp.concatenate(
        [low_pair.reshape(3, mixed_size, width), low_odd[: 3 * HD].reshape(3, HD, width)], axis=1
    )
    return (
        jnp.sum(vec[8]),
        student_out,
        grad_in.reshape(slots, piece, width),
        vec[0],
        vec[1],
        jnp.transpose(qkv_turned, (0, 2, 1)).astype(F32),
        vec[10:12, :used],
        low_odd[3 * HD :].astype(F32),
        vec[4],
        vec[2],
        vec[3],
        g1_all,
        vec[9],
        two.result[0],
        vec[5],
        grad_head,
        jnp.concatenate([vec[6], vec[7, : t_width - width]]),
    )


def solution(mesh):
    rep = P()
    in_specs = (
        P("dp", None), rep, rep, rep, P("dp", None, None), rep, rep, P(None, None, "mp"), P(None, "mp"),
        P("mp", None), rep, rep, rep, P(None, "mp"), P("mp"), P("mp", None), rep, rep, rep,
        P(None, None, "mp"), P(None, "mp"), P("mp", None), rep, rep, rep, P(None, "mp"), P("mp"),
        P("mp", None), rep, rep, rep,
    )
    out_specs = (
        rep, P("dp", "mp", None), P("dp", "mp", None), rep, rep, P(None, None, "mp"), P(None, "mp"),
        P("mp", None), rep, rep, rep, P(None, "mp"), P("mp"), P("mp", None), rep, rep, rep,
    )
    return jax.shard_map(body, mesh=mesh, in_specs=in_specs, out_specs=out_specs, check_vma=False)
```

```python
import functools

import jax
import jax.numpy as jnp
from jax import lax
from jax.experimental import pallas as pl
from jax.experimental.pallas import tpu as pltpu
from jax.sharding import PartitionSpec as P

HD = 64
OWN = 8
CLIPS = 8
EPS = 1e-05
BIG = -1e30
F32 = jnp.float32
BF = jnp.bfloat16
LIMIT = 24 * 2**20
COST = 1

ORD, CUM, END, HOME, LOW = 0, 4, 12, 20, 21


def dot_nn(a, b):
    return lax.dot_general(a, b, (((1,), (0,)), ((), ())), preferred_element_type=F32)


def dot_nt(a, b):
    return lax.dot_general(a, b, (((1,), (1,)), ((), ())), preferred_element_type=F32)


def dot_tn(a, b):
    return lax.dot_general(a, b, (((0,), (0,)), ((), ())), preferred_element_type=F32)


def unit(values):
    mean = jnp.mean(values, axis=-1, keepdims=True)
    centred = values - mean
    spread = jnp.mean(centred * centred, axis=-1, keepdims=True)
    inverse = lax.rsqrt(spread + EPS)
    return centred * inverse, inverse


def norm_low(values, gain_ref, shift_ref):
    u, _ = unit(values)
    return (u * gain_ref[...].astype(F32) + shift_ref[...].astype(F32)).astype(BF)


def log2(size):
    return size.bit_length() - 1


def whole(shape):
    return pl.BlockSpec(shape, lambda *_: (0,) * len(shape))


def call(kernel, name, grid, in_specs, out_specs, out_shape, args, scratch=(), flops=0, scalars=None, limit=LIMIT, far=()):
    moved = sum(a.size * a.dtype.itemsize for a in args)
    moved += sum(s.size * jnp.dtype(s.dtype).itemsize for s in jax.tree.leaves(out_shape))
    if far:
        if isinstance(out_shape, list):
            out_shape = [pltpu.HBM(o.shape, o.dtype) if i in far else o for i, o in enumerate(out_shape)]
        else:
            out_shape = pltpu.HBM(out_shape.shape, out_shape.dtype)
    params = pltpu.CompilerParams(
        dimension_semantics=("arbitrary",) * len(grid), vmem_limit_bytes=limit
    )
    cost = pl.CostEstimate(flops=int(flops) // COST, bytes_accessed=int(moved) // COST, transcendentals=0)
    lead = 0 if scalars is None else 1
    spec = pltpu.PrefetchScalarGridSpec(
        num_scalar_prefetch=lead,
        grid=grid,
        in_specs=in_specs,
        out_specs=out_specs,
        scratch_shapes=list(scratch),
    )
    run = pl.pallas_call(
        kernel,
        grid_spec=spec,
        out_shape=out_shape,
        compiler_params=params,
        cost_estimate=cost,
        name=name,
    )
    return run(*([scalars] if lead else []), *args)


def sds(shape, dtype):
    return jax.ShapeDtypeStruct(shape, dtype)


def group_of(index, sc, base):
    group = jnp.zeros(index.shape, jnp.int32)
    for c in range(CLIPS):
        group = group + (index >= sc[base + c]).astype(jnp.int32)
    return group


def teacher_kv_kernel(sc, x_ref, g_ref, s_ref, w_ref, b_ref, k_ref, v_ref):
    rows = x_ref.shape[0]
    a = norm_low(x_ref[...].astype(F32), g_ref, s_ref)
    token = pl.program_id(0) * rows + lax.broadcasted_iota(jnp.int32, (rows, 1), 0)
    lane = lax.broadcasted_iota(jnp.int32, (rows, 128), 1)
    hot = jnp.where(lane == group_of(token, sc, END), 1.0, 0.0).astype(BF)
    k = (dot_nn(a, w_ref[1]).astype(BF).astype(F32) * (HD**-0.5)).astype(BF)
    for p in range(k.shape[1] // 128):
        k_ref[:, 256 * p : 256 * p + 128] = k[:, 128 * p : 128 * (p + 1)]
        k_ref[:, 256 * p + 128 : 256 * (p + 1)] = hot
    v_ref[...] = (dot_nn(a, w_ref[2]) + b_ref[1:2, :].astype(F32)).T.astype(BF)


def teacher_q_kernel(slots, block, step, sc, x_ref, rank_ref, g_ref, s_ref, w_ref, b_ref, xk_ref, q_ref, acc):
    j = pl.program_id(0)
    pieces, nb, piece, width = xk_ref.shape
    rows = pieces * nb * piece

    line = lax.broadcasted_iota(jnp.int32, (rows, 1), 0)
    part = line >> log2(nb * piece)
    inner = line & (nb * piece - 1)
    order = jnp.zeros((rows, 1), jnp.int32)
    for p in range(pieces):
        order = jnp.where(part == p, sc[ORD + p], order)
    slot = (j * nb + (inner >> log2(piece))) * block + order * piece + (inner & (piece - 1))
    group = group_of(slot, sc, CUM)
    acc[...] = jnp.zeros_like(acc)

    def one(t, _):
        hit = jnp.where(slot == rank_ref[pl.ds(t, 1), :], 1.0, 0.0).astype(BF)
        acc[...] += dot_nn(hit, x_ref[pl.ds(pl.multiple_of(t * step, step), step), :])
        return 0

    steps = slots // nb
    lax.fori_loop(sc[LOW + j], sc[LOW + steps + j], one, 0)
    kept = acc[...]
    xk_ref[...] = kept.astype(BF).reshape(xk_ref.shape)
    a = norm_low(kept, g_ref, s_ref)
    q = (dot_nn(a, w_ref[0]) + b_ref[0:1, :].astype(F32)).astype(BF)
    lane = lax.broadcasted_iota(jnp.int32, (rows, 128), 1)
    other = (lane != group) & (lane <= CLIPS)
    mask = jnp.where(other, BIG, 0.0).astype(BF)
    pairs = q.shape[1] // 128
    out = []
    for p in range(pairs):
        out += [q[:, 128 * p : 128 * (p + 1)], mask]
    q_ref[...] = jnp.concatenate(out, axis=1).reshape(q_ref.shape)


def softmax_mix(keys, query, values):
    scores = dot_nt(keys, query)
    top = jnp.max(scores, axis=0, keepdims=True)
    e = jnp.exp(scores - top)
    mass = jnp.sum(e, axis=0, keepdims=True)
    return dot_nn(values, e.astype(BF)) * (1.0 / mass), top + jnp.log(mass)


def teacher_attend_kernel(q_ref, k_ref, v_ref, ctx_ref):
    pieces, nb, piece, both = q_ref.shape
    rows = pieces * nb * piece
    part = q_ref[...].reshape(rows, both).astype(F32)
    lane = lax.broadcasted_iota(jnp.int32, (rows, both), 1)
    mixed = []
    for h in range(2):
        query = jnp.where(((lane >> 6) == h) | (lane >= 128), part, 0.0).astype(BF)
        mixed.append(softmax_mix(k_ref[...], query, v_ref[HD * h : HD * (h + 1), :])[0])
    ctx_ref[...] = jnp.concatenate(mixed, axis=0).T.astype(BF).reshape(ctx_ref.shape)


def student_qkv_kernel(block, sc, x_ref, g_ref, s_ref, w_ref, b_ref, xo_ref, a_ref, q_ref, k_ref, v_ref, kt_ref, vt_ref):
    slots, _, piece, width = x_ref.shape
    rows = slots * piece
    used, wide = w_ref.shape[1], q_ref.shape[1]
    x = x_ref[...].reshape(rows, width)
    xo_ref[...] = x
    a = norm_low(x.astype(F32), g_ref, s_ref)
    a_ref[...] = a
    line = lax.broadcasted_iota(jnp.int32, (rows, 1), 0)
    lane = lax.broadcasted_iota(jnp.int32, (rows, wide - used), 1)
    slot = (line >> log2(piece)) * block + sc[ORD + pl.program_id(0)] * piece + (line & (piece - 1))
    same = lane == group_of(slot, sc, CUM)
    q_ref[:, :used] = (dot_nt(a, w_ref[0]) + b_ref[0:1, :].astype(F32)).astype(BF)
    q_ref[:, used:] = jnp.where(same | (lane > CLIPS), 0.0, BIG).astype(BF)
    k = dot_nt(a, w_ref[1]).astype(BF).astype(F32) * (HD**-0.5)
    k_ref[:, :used] = k.astype(BF)
    k_ref[:, used:] = jnp.where(same, 1.0, 0.0).astype(BF)
    kt_ref[...] = k.T.astype(BF)
    v = dot_nt(a, w_ref[2]) + b_ref[1:2, :].astype(F32)
    v_ref[:, :used] = v.astype(BF)
    v_ref[:, used:] = jnp.zeros((rows, wide - used), BF)
    vt_ref[...] = v.T.astype(BF)


def student_attend_kernel(used, q_ref, k_ref, vt_ref, ctx_ref, mixed_ref, log_ref):
    q = q_ref[...].astype(F32)
    rows, wide = q.shape
    lane = lax.broadcasted_iota(jnp.int32, (rows, wide), 1)
    mixed, logs = [], []
    for h in range(used // HD):
        query = jnp.where(((lane >> 6) == h) | (lane >= used), q, 0.0).astype(BF)
        part, log = softmax_mix(k_ref[...], query, vt_ref[HD * h : HD * (h + 1), :])
        mixed.append(part)
        logs.append(log)
    total = jnp.concatenate(mixed, axis=0)
    mixed_ref[...] = total
    ctx_ref[...] = total.T.astype(BF)
    log_ref[...] = jnp.concatenate(logs + [jnp.zeros((8 - len(logs), rows), F32)], axis=0)


def student_probs_kernel(used, q_ref, k_ref, log_ref, out_ref):
    rows, wide = q_ref.shape
    lane = lax.broadcasted_iota(jnp.int32, (rows, wide), 1)
    h = pl.program_id(0)
    query = jnp.where(((lane >> 6) == h) | (lane >= used), q_ref[...].astype(F32), 0.0).astype(BF)
    out_ref[0] = jnp.exp(dot_nt(k_ref[...], query) - log_ref[pl.ds(h, 1), :]).astype(BF)


def student_back_kernel(used, picked, with_out, p0, p1, w_ref, mixed_ref, probs_ref, q_ref, v_ref, kt_ref, *rest):
    if with_out:
        out_ref, sums_ref, w_grad_ref, ds, da, dk, dv, dqs, dw = rest
    else:
        out_ref, sums_ref, ds, da, dk, dv, dqs = rest
    j = pl.program_id(0)
    steps = pl.num_programs(0)
    lo, size = HD * picked[0], HD * len(picked)
    rows, wide = q_ref.shape

    @pl.when(j == 0)
    def _():
        dk[...] = jnp.zeros_like(dk)
        dv[...] = jnp.zeros_like(dv)
        dqs[...] = jnp.zeros_like(dqs)
        ds[...] = p0[...]
        if with_out:
            dw[...] = jnp.zeros_like(dw)

    @pl.when(j == 1)
    def _():
        ds[...] = p1[...]

    grad = ds[...]
    da[:, :used] = dot_nt(grad, w_ref[...])
    da[:, used:] = jnp.zeros((rows, wide - used), F32)
    low = da[...].astype(BF).astype(F32)
    mixed = mixed_ref[...]
    turned = dot_nt(w_ref[lo : lo + size, :], grad).astype(BF).astype(F32)
    product = turned * mixed[lo : lo + size, :]
    if with_out:
        dw[...] += dot_nn(mixed.astype(BF), grad)
    lane = lax.broadcasted_iota(jnp.int32, (rows, wide), 1)
    q = q_ref[...].astype(F32)
    grads_q = []
    for i, h in enumerate(picked):
        mine = (lane >> 6) == h
        query = jnp.where(mine | (lane >= used), q, 0.0).astype(BF)
        outer = jnp.where(mine, low, 0.0).astype(BF)
        delta = jnp.sum(product[HD * i : HD * (i + 1), :], axis=0, keepdims=True)
        pt = probs_ref[i]
        dst = (pt.astype(F32) * (dot_nt(v_ref[...], outer) - delta)).astype(BF)
        dv[...] += dot_nn(pt, outer)
        dk[...] += dot_nn(dst, query)
        grads_q.append(dot_nn(kt_ref[HD * h : HD * (h + 1), :], dst))
    dq = jnp.concatenate(grads_q, axis=0).T.astype(BF)
    out_ref[pl.ds(pl.multiple_of(j * rows, rows), rows), 0:size] = dq
    dqs[...] += jnp.sum(dq.astype(F32), axis=0, keepdims=True)

    @pl.when(j == steps - 1)
    def _():
        out_ref[:, size : 2 * size] = (dk[:, lo : lo + size] * (HD**-0.5)).astype(BF)
        dv_low = dv[:, lo : lo + size].astype(BF)
        out_ref[:, 2 * size : 3 * size] = dv_low
        sums_ref[...] = jnp.concatenate(
            [dqs[...], jnp.sum(dv_low.astype(F32), axis=0, keepdims=True)], axis=0
        )
        if with_out:
            w_grad_ref[...] = dw[...]


def gelu_both(pre):
    phi = 0.5 * (1.0 + lax.erf(pre * 0.7071067811865476))
    return pre * phi, phi + pre * (0.3989422804014327 * jnp.exp(-0.5 * pre * pre))


def flipped(ref):
    half = ref.shape[0] // 2
    return jnp.concatenate([ref[half:], ref[:half]], axis=0)


def forward_kernel(
    mode, half_steps,
    *refs,
):
    both = mode == "both"
    count = 4 if both else 8
    ctx, (w0, w1, w2, w3, x_ref, ob_ref, g_ref, s_ref), refs = refs[:count], refs[count : count + 8], refs[count + 8 :]
    (f1a, f1b, b1a, b1b, f2a, f2b, b2_ref), rest = refs[:7], refs[7:]
    if both:
        send_ref, own_ref, sent_ref, a2_ref, act_ref, slope_ref, a2, acc, base = rest
    elif mode == "own":
        own_ref, a2, acc, base = rest
    else:
        send_ref, a2, acc = rest
    j = pl.program_id(0)
    rows = x_ref.shape[0]

    @pl.when(j == 0)
    def _():
        if both:
            found = [ctx[0][...], ctx[1][...], flipped(ctx[2]), flipped(ctx[3])]
        else:
            found = [jnp.concatenate([ctx[i][...], ctx[4 + i][...]], axis=1) for i in range(4)]
        parts = [dot_nn(c, w[...]) for c, w in zip(found, (w0, w1, w2, w3))]
        if not both:
            parts = [p.astype(BF).astype(F32) for p in parts]
        resid = x_ref[...].astype(F32) + (parts[0] + parts[1] + parts[2] + parts[3])
        resid = resid + ob_ref[...].astype(F32)
        if both:
            low = resid.astype(BF)
            sent_ref[...] = low
            resid = low.astype(F32)
        a2[...] = norm_low(resid, g_ref, s_ref)
        if both:
            a2_ref[...] = a2[...]
            base[...] = resid[: rows // 2] + b2_ref[...].astype(F32)
        elif mode == "own":
            base[...] = resid + b2_ref[...].astype(F32)
        acc[...] = jnp.zeros_like(acc)

    def half(f1, b1, f2):
        pre = dot_nn(a2[...], f1[...]) + b1[...].astype(F32)
        if both:
            act, slope = gelu_both(pre)
            slope_ref[...] = slope.astype(BF)
        else:
            act = pre * (0.5 * (1.0 + lax.erf(pre * 0.7071067811865476)))
        act = act.astype(BF)
        if both:
            act_ref[...] = act
        acc[...] += dot_nn(act, f2[...])

    @pl.when(j < half_steps)
    def _():
        half(f1a, b1a, f2a)

    @pl.when(j >= half_steps)
    def _():
        half(f1b, b1b, f2b)

    @pl.when(j == 2 * half_steps - 1)
    def _():
        if both:
            own_ref[...] = acc[: rows // 2] + base[...]
            send_ref[...] = acc[rows // 2 :].astype(BF)
        elif mode == "own":
            own_ref[...] = acc[...] + base[...]
        else:
            send_ref[...] = acc[...].astype(BF)


def forward(mode, name, rows, ctx, w_out, x, out_b, gain, shift, f1, b1, f2, b2, chunk):
    width = x.shape[1]
    heads_wide, hidden = w_out[0].shape[0], f1[0].shape[1]
    n = hidden // chunk
    both = mode == "both"
    near_at = 1 if mode == "send" else 0
    far_at = 1 if mode == "own" else 0
    first = lambda j: jnp.minimum(j, n - 1)
    second = lambda j: jnp.maximum(j - n, 0)
    at = lambda i, w: pl.BlockSpec((rows, w), lambda j: (i, 0))
    c_wide = ctx[0].shape[1]
    specs = ([at(near_at, c_wide)] * 2 + [at(far_at, c_wide)] * 2) * (len(ctx) // 4)
    specs += [whole(w.shape) for w in w_out]
    specs += [at(near_at, width)] + [whole((1, width))] * 3
    specs += [pl.BlockSpec((width, chunk), lambda j, f=f: (0, f(j))) for f in (first, second)]
    specs += [pl.BlockSpec((1, chunk), lambda j, f=f: (0, f(j))) for f in (first, second)]
    specs += [pl.BlockSpec((chunk, width), lambda j, f=f: (f(j), 0)) for f in (first, second)]
    specs += [whole((1, width))]
    half = rows // 2
    scratch = [pltpu.VMEM((rows, width), BF), pltpu.VMEM((rows, width), F32)]
    if both:
        outs = [sds((half, width), BF), sds((half, width), F32)] + [sds((rows, width), BF)] * 2
        outs += [sds((rows, 2 * hidden), BF)] * 2
        out_specs = [whole((half, width))] * 2 + [whole((rows, width))] * 2
        out_specs += [pl.BlockSpec((rows, chunk), lambda j: (0, j))] * 2
        scratch += [pltpu.VMEM((half, width), F32)]
    elif mode == "own":
        outs, out_specs = sds((rows, width), F32), whole((rows, width))
        scratch += [pltpu.VMEM((rows, width), F32)]
    else:
        outs, out_specs = sds((rows, width), BF), whole((rows, width))
    return call(
        functools.partial(forward_kernel, mode, n), name, (2 * n,), specs, out_specs, outs,
        (*ctx, *w_out, x, out_b, gain, shift, *f1, *b1, *f2, b2),
        scratch=scratch,
        flops=2 * rows * width * (4 * heads_wide + 4 * hidden), far=(2, 3, 4, 5) if both else (0,) if mode == "own" else (),
    )


def head_kernel(block, piece, sc, own_ref, recv_ref, out_ref, w_ref, b_ref, inv_ref, dg_ref, do_ref, loss_ref, hb_ref, ob_ref):
    rows, width = own_ref.shape
    target = (own_ref[...] + recv_ref[...].astype(F32)).astype(BF).astype(F32)
    line = lax.broadcasted_iota(jnp.int32, (rows, 1), 0)
    slot = (line >> log2(piece)) * block + sc[ORD] * piece + (line & (piece - 1))
    live = slot < sc[CUM + CLIPS - 1]
    group = group_of(slot, sc, CUM)
    weight = jnp.zeros((rows, 1), F32)
    for c in range(CLIPS):
        weight = jnp.where(group == c, inv_ref[0, c], weight)
    weight = jnp.where(live, weight, 0.0)
    target = jnp.where(live, target, 0.0)
    miss = dot_nn(out_ref[...], w_ref[...]) + b_ref[...].astype(F32) - target
    dg = (weight * miss).astype(BF)
    dg_ref[...] = dg
    loss_ref[...] = 0.5 * jnp.sum(weight * miss * miss, axis=0, keepdims=True)
    hb_ref[...] = jnp.sum(dg.astype(F32), axis=0, keepdims=True)
    do = dot_nt(dg, w_ref[...]).astype(BF)
    do_ref[...] = do
    ob_ref[...] = jnp.sum(do.astype(F32), axis=0, keepdims=True)


def head_grad_kernel(sc, out_ref, own_ref, other_ref, keep_ref, send_ref):
    keep_ref[...] = dot_tn(out_ref[...], own_ref[...])
    send_ref[...] = dot_tn(out_ref[...], other_ref[...]).astype(BF)


def head_add_kernel(sc, keep_a, recv_a, keep_b, recv_b, keep_ref, send_ref):
    keep_ref[...] = keep_a[...] + recv_a[...].astype(F32)
    send_ref[...] = (keep_b[...] + recv_b[...].astype(F32)).astype(BF)


def feed_far_kernel(d0, d1, act_ref, slope_ref, a2_ref, f1, f2, g1_ref, g2_ref, gb_ref, acc_ref, d):
    half = d0.shape[0]
    d[:half] = d0[...]
    d[half:] = d1[...]
    grad = d[...]
    dpre = (dot_nt(grad, f2[...]) * slope_ref[...].astype(F32)).astype(BF)
    gb_ref[...] = jnp.sum(dpre.astype(F32), axis=0, keepdims=True)
    acc_ref[...] = dot_nt(dpre, f1[...])
    g2_ref[...] = dot_tn(act_ref[...], grad).astype(BF)
    g1_ref[...] = dot_tn(a2_ref[...], dpre).astype(BF)


def feed_own_kernel(d0, d1, slope_ref, f1, f2, before, dpre_ref, gb_ref, own_ref, send_ref, d):
    half = d0.shape[0]
    d[:half] = d0[...]
    d[half:] = d1[...]
    dpre = (dot_nt(d[...], f2[...]) * slope_ref[...].astype(F32)).astype(BF)
    dpre_ref[...] = dpre
    gb_ref[...] = jnp.sum(dpre.astype(F32), axis=0, keepdims=True)
    part = dot_nt(dpre, f1[...]) + before[...]
    own_ref[...] = part
    send_ref[:half] = part[half:].astype(BF)
    send_ref[half:] = part[:half].astype(BF)


def keep_and_send(value, mark, keep_ref, send_ref):
    half = value.shape[0] // 2
    top, bottom = value[:half], value[half:]
    first = mark == 0
    keep_ref[...] = jnp.where(first, top, bottom).astype(keep_ref.dtype)
    send_ref[...] = jnp.where(first, bottom, top).astype(send_ref.dtype)


def feed_grad_kernel(bit_a, bit_b, sc, d0, d1, act_ref, a2_ref, dpre_ref, r1, r2, hk, hr,
                     keep_a, send_a, keep_b, send_b, d):
    half = d0.shape[0]
    d[:half] = d0[...]
    d[half:] = d1[...]
    g1 = dot_tn(a2_ref[...], dpre_ref[...]) + r1[...].astype(F32)
    head = hk[...] + hr[...].astype(F32)
    keep_and_send(jnp.concatenate([g1, head], axis=1), (sc[HOME] >> bit_a) & 1, keep_a, send_a)
    g2 = dot_tn(act_ref[...], d[...]) + r2[...].astype(F32)
    keep_and_send(g2, (sc[HOME] >> bit_b) & 1, keep_b, send_b)


def project_grad_kernel(bit, more, sc, d_ref, a_ref, *rest):
    value = dot_tn(d_ref[...], a_ref[...])
    if more:
        value = jnp.concatenate([value, rest[0][...]], axis=0)
    keep_and_send(value, (sc[HOME] >> bit) & 1, rest[-2], rest[-1])


def short_kernel(sums_ref, fc2_ref, hb_ref, loss_ref, b1s_ref, b1_ref, *rest):
    own_ref, send_ref = rest[-2:]
    width = own_ref.shape[1]
    for out in (own_ref, send_ref):
        out[...] = jnp.zeros(out.shape, F32)
        out[2:5, :] = sums_ref[...]
        out[5:6, :] = fc2_ref[...]
        out[6:7, :] = hb_ref[:, :width]
        left = hb_ref.shape[1] - width
        out[7:8, :left] = hb_ref[:, width:]
        loss = loss_ref[:, :left]
        for i in range(1, loss_ref.shape[1] // left):
            loss += loss_ref[:, left * i : left * (i + 1)]
        out[8:9, :left] = loss
    own_ref[9:10, :] = b1_ref[...]
    send_ref[9:10, :] = b1s_ref[...]
    at = 0
    for ref in rest[:-2]:
        own_ref[10:12, at : at + ref.shape[1]] = ref[...]
        at += ref.shape[1]


def input_grad_kernel(da_ref, db_ref, wa_ref, wb_ref, near_ref, send_ref):
    value = dot_nn(da_ref[...], wa_ref[...]) + dot_nn(db_ref[...], wb_ref[...])

    @pl.when(pl.program_id(0) == 0)
    def _():
        send_ref[...] = value.astype(BF)

    @pl.when(pl.program_id(0) == 1)
    def _():
        near_ref[...] = value


def stage_kernel(ops, sc, *refs):
    ins, outs = refs[: 2 * len(ops)], refs[2 * len(ops) :]
    at = 0
    for i, (kind, bit, parts) in enumerate(ops):
        a, b = ins[2 * i][...].astype(F32), ins[2 * i + 1][...].astype(F32)
        mark = (sc[HOME] >> bit) & 1
        if kind == "split":
            keep_and_send(a + b, mark, outs[at], outs[at + 1])
            at += 2
        elif kind == "add":
            outs[at][...] = (a + b).astype(BF)
            at += 1
        else:
            rows = a.shape[0]
            for lo, hi, dtype in parts:
                outs[at][:rows] = jnp.where(mark == 0, a[:, lo:hi], b[:, lo:hi]).astype(dtype)
                outs[at][rows:] = jnp.where(mark == 0, b[:, lo:hi], a[:, lo:hi]).astype(dtype)
                at += 1


def stage(name, ops, pairs, scalars):
    shapes = []
    for (kind, bit, parts), (a, b) in zip(ops, pairs):
        rows, width = a.shape
        if kind == "split":
            shapes.append([sds((rows // 2, width), BF)] * 2)
        elif kind == "add":
            shapes.append([sds((rows, width), BF)])
        else:
            shapes.append([sds((2 * rows, hi - lo), dtype) for lo, hi, dtype in parts])
    sizes = [a.shape[0] for a, _ in pairs] + [s.shape[0] for group in shapes for s in group]
    if all(size % 16 == 0 for size in sizes):
        flat = [x for pair in pairs for x in pair]
        outs = [s for group in shapes for s in group]
        found = call(
            functools.partial(stage_kernel, ops), name, (1,), [whole(x.shape) for x in flat],
            [whole(s.shape) for s in outs], outs, flat, scalars=scalars,
        )
    else:
        found = []
        for (kind, bit, parts), (a, b) in zip(ops, pairs):
            first = ((scalars[HOME] >> bit) & 1) == 0
            if kind == "join":
                for lo, hi, dtype in parts:
                    a1, b1 = a[:, lo:hi].astype(dtype), b[:, lo:hi].astype(dtype)
                    found.append(
                        jnp.where(first, jnp.concatenate([a1, b1], 0), jnp.concatenate([b1, a1], 0))
                    )
                continue
            total = (a.astype(F32) + b.astype(F32)).astype(BF)
            if kind == "add":
                found.append(total)
            else:
                half = total.shape[0] // 2
                found.append(jnp.where(first, total[:half], total[half:]))
                found.append(jnp.where(first, total[half:], total[:half]))
    result, at = [], 0
    for group in shapes:
        result.append(found[at : at + len(group)])
        at += len(group)
    return result


class Bundle:
    def __init__(self, bits, keep, recv, parts):
        self.bits, self.step, self.phase, self.parts = bits, 0, "split", parts
        self.flight = (keep, recv)
        self.result = None

    def op(self):
        if self.phase == "split":
            last = self.step == len(self.bits) - 1
            return ("add", 0, None) if last else ("split", self.bits[self.step + 1], None)
        width = self.flight[0].shape[1]
        parts = self.parts if self.step == 0 else ((0, width, BF),)
        return ("join", self.bits[self.step], parts)


def advance(name, bundles, partner, scalars):
    ops = [b.op() for b in bundles]
    done = stage(name, ops, [b.flight for b in bundles], scalars)
    for b, (kind, bit, _), got in zip(bundles, ops, done):
        if kind == "split":
            b.step += 1
            b.flight = (got[0], partner(got[1], bit))
        elif kind == "add":
            b.phase = "join"
            b.flight = (got[0], partner(got[0], b.bits[b.step]))
        elif b.step == 0:
            b.flight, b.result = None, got
        else:
            b.step -= 1
            b.flight = (got[0], partner(got[0], b.bits[b.step]))


def spread_kernel(came, going, shift, base, sc, in_ref, *refs):
    refs = list(refs)
    recv_ref = None if came is None else refs.pop(0)
    n = refs[0].shape[0] if going is not None else in_ref.shape[0]
    bit_in = 0 if came is None else (sc[base] >> (came - shift)) & 1

    def entry(i):
        if came is None:
            return in_ref[sc[i]]
        side = (i & ((1 << came) - 1)) | ((i >> (came + 1)) << came)
        return jnp.where(((i >> came) & 1) == bit_in, in_ref[i], recv_ref[side])

    if going is None:
        kept_ref, out_ref = refs[1], refs[0]
        for i in range(n):
            kept_ref[i] = entry(i)
        for i in range(out_ref.shape[0]):
            out_ref[i] = kept_ref[sc[i]]
        return
    keep_ref, send_ref = refs
    bit_out = (sc[base] >> (going - shift)) & 1
    for i in range(n):
        keep_ref[i] = entry(i)
    for j in range(send_ref.shape[0]):
        low = (j & ((1 << going) - 1)) | ((j >> going) << (going + 1))
        send_ref[j] = jnp.where(bit_out == 0, keep_ref[low | (1 << going)], keep_ref[low])


def place_kernel(sc, h0, h1, h2, h3, out_ref):
    for i, ref in enumerate((h0, h1, h2, h3)):

        @pl.when(pl.program_id(0) == i)
        def _(ref=ref):
            out_ref[...] = ref[...].astype(F32)


def norm_back_kernel(count, own_ref, recv_ref, *rest):
    base_refs, (x_ref, g_ref, dx_ref, sums_ref) = rest[:count], rest[count:]
    rows = own_ref.shape[0]
    mine = rows // count
    d = own_ref[...].astype(F32) + recv_ref[...].astype(F32)
    u, inverse = unit(x_ref[...].astype(F32))
    e = g_ref[...].astype(F32) * d
    mean_e = jnp.mean(e, axis=-1, keepdims=True)
    mean_eu = jnp.mean(e * u, axis=-1, keepdims=True)
    change = (e - mean_e - u * mean_eu) * inverse
    for i, base in enumerate(base_refs):
        at = slice(mine * i, mine * (i + 1))
        dx_ref[at] = (base[...].astype(F32) + change[at]).astype(dx_ref.dtype)
    sums_ref[...] = jnp.concatenate(
        [
            jnp.sum((d * u)[:mine], axis=0, keepdims=True),
            jnp.sum(d[:mine], axis=0, keepdims=True),
            jnp.sum(dx_ref[:mine].astype(F32), axis=0, keepdims=True),
        ],
        axis=0,
    )


def norm_back(name, own, recv, bases, x, gain, dtype):
    rows, width = own.shape
    block = pl.BlockSpec((rows, width), lambda *_: (0, 0))
    piece = pl.BlockSpec((rows // len(bases), width), lambda *_: (0, 0))
    return call(
        functools.partial(norm_back_kernel, len(bases)), name, (1,),
        [block] * 2 + [piece] * len(bases) + [block, whole((1, width))],
        [block, whole((3, width))],
        [sds((rows, width), dtype), sds((3, width), F32)],
        (own, recv, *bases, x, gain),
    )


def hbm(x):
    return pltpu.with_memory_space_constraint(x, pltpu.HBM)


def swap(x, bit, count):
    return lax.ppermute(x, "mp", [(i, i ^ bit) for i in range(count)])


def row(vector):
    return vector.reshape(1, -1)


def layout(mask_row, seg_row, order, home, steps, span):
    tokens = mask_row.shape[0]
    grid = mask_row.reshape(tokens // 128, 128).astype(BF)
    upper = (jnp.arange(128)[:, None] <= jnp.arange(128)[None, :]).astype(BF)
    within = jnp.dot(grid, upper, preferred_element_type=F32)
    lines = tokens // 128
    lower = (jnp.arange(lines)[:, None] > jnp.arange(lines)[None, :]).astype(BF)
    ahead = jnp.dot(lower, within[:, 127:].astype(BF), preferred_element_type=F32)
    count = (within + ahead).astype(jnp.int32).reshape(tokens)
    rank = jnp.where(mask_row == 1, count - 1, -1)
    labels = jnp.arange(CLIPS, dtype=jnp.int32)
    upto = (seg_row[None, :] <= labels[:, None]).astype(jnp.int32)
    ends = jnp.sum(upto, axis=1)
    cum = jnp.sum(upto * mask_row[None, :], axis=1)
    edge = jnp.arange(steps, dtype=jnp.int32) * span
    low = jnp.sum((count[None, :] <= edge[:, None]).astype(jnp.int32), axis=1)
    high = jnp.sum((count[None, :] < edge[:, None] + span).astype(jnp.int32), axis=1)
    low = low // span
    high = jnp.minimum(high, tokens - 1) // span + 1
    each = cum - jnp.concatenate([jnp.zeros((1,), jnp.int32), cum[:-1]])
    inverse = 1.0 / jnp.maximum(each, 1).astype(F32)
    first = jnp.concatenate([order, cum, ends, home[None].astype(jnp.int32)])
    scalars = jnp.concatenate([first, low, high])
    return rank.reshape(tokens // span, span), first, scalars, inverse.reshape(1, CLIPS)


def body(
    teacher_in, segment_ids, keep_mask, block_owner, student_in,
    t_norm1_gain, t_norm1_shift, t_qkv, t_qv_bias, t_out, t_out_bias,
    t_norm2_gain, t_norm2_shift, t_fc1, t_fc1_bias, t_fc2, t_fc2_bias,
    s_norm1_gain, s_norm1_shift, s_qkv, s_qv_bias, s_out, s_out_bias,
    s_norm2_gain, s_norm2_shift, s_fc1, s_fc1_bias, s_fc2, s_fc2_bias,
    head_weight, head_bias,
):
    mp = lax.axis_size("mp")
    me = lax.axis_index("mp")
    homes = lax.axis_size("dp")
    home = lax.axis_index("dp")
    slots, block, width = student_in.shape
    piece = block // mp
    rows = slots * block
    mine = rows // mp
    near = 2 * mine
    tokens, t_width = teacher_in.shape
    used = s_qkv.shape[2]
    wide = 256
    nb = 2
    span = nb * block
    steps = slots // nb
    core = lambda x: swap(x, 1, mp)
    across = lambda x: swap(x, 2, mp)

    order = jnp.stack([me, me ^ 2, me ^ 1, me ^ 3]).astype(jnp.int32)
    mask_row = lax.dynamic_index_in_dim(keep_mask, home, 0, keepdims=False)
    seg_row = lax.dynamic_index_in_dim(segment_ids, home, 0, keepdims=False)
    rank, first_scalars, scalars, inverse = layout(mask_row, seg_row, order, home, steps, span)

    t_w2 = across(t_out)
    s_w2 = across(s_out)
    s_f1 = (s_fc1, core(s_fc1))
    s_f2 = (s_fc2, core(s_fc2))
    biases = core(jnp.concatenate([t_fc1_bias, s_fc1_bias]))

    x4 = hbm(student_in.reshape(slots, mp, piece, width))
    w_turn = jnp.transpose(s_qkv, (0, 2, 1))
    by_piece = lambda w: pl.BlockSpec((mine, w), lambda k, sc: (k, 0))
    turned = pl.BlockSpec((used, mine), lambda k, sc: (0, k))
    x_stud, a_stud, sq, sk, sv, skt, svt = call(
        functools.partial(student_qkv_kernel, block), "student_qkv", (mp,),
        [
            pl.BlockSpec((slots, 1, piece, width), lambda k, sc: (0, sc[ORD + k], 0, 0)),
            whole((1, width)), whole((1, width)), whole(w_turn.shape), whole(s_qv_bias.shape),
        ],
        [by_piece(width)] * 2 + [by_piece(wide)] * 3 + [turned] * 2,
        [sds((rows, width), BF)] * 2 + [sds((rows, wide), BF)] * 3 + [sds((used, rows), BF)] * 2,
        (x4, row(s_norm1_gain), row(s_norm1_shift), hbm(w_turn), s_qv_bias),
        flops=2 * rows * width * 3 * wide, scalars=first_scalars, far=(0, 1, 4, 5),
    )
    heads = used // HD
    by_rows = lambda w: pl.BlockSpec((near, w), lambda j: (j, 0))
    by_lanes = lambda h: pl.BlockSpec((h, near), lambda j: (0, j))
    ctx, mixed, logs = call(
        functools.partial(student_attend_kernel, used), "student_attend", (rows // near,),
        [by_rows(wide), whole((rows, wide)), whole((used, rows))],
        [by_rows(used), by_lanes(used), by_lanes(8)],
        [sds((rows, used), BF), sds((used, rows), F32), sds((8, rows), F32)],
        (sq, sk, svt),
        flops=heads * rows * rows * wide * 4, far=(1, 2),
    )

    ctx, teacher_rows, t_w2, s_w2, s_f1, s_f2, biases, s_out_late = lax.optimization_barrier(
        (ctx, teacher_in, t_w2, s_w2, s_f1, s_f2, biases, s_out)
    )
    t_b1 = (row(t_fc1_bias), row(biases[: t_fc1_bias.shape[0]]))
    s_b1 = (row(s_fc1_bias), row(biases[t_fc1_bias.shape[0] :]))
    s_c0 = ctx[:near]
    s_c1 = core(ctx[near:])
    s_c2 = across(s_c0)
    s_w1 = core(s_out_late)
    s_w3 = core(s_w2)

    cols = t_qkv.shape[2]
    tk, tv = call(
        teacher_kv_kernel, "teacher_kv", (tokens // 512,),
        [
            pl.BlockSpec((512, t_width), lambda j, sc: (j, 0)), whole((1, t_width)), whole((1, t_width)),
            whole(t_qkv.shape), whole(t_qv_bias.shape),
        ],
        [pl.BlockSpec((512, 2 * cols), lambda j, sc: (j, 0)), pl.BlockSpec((cols, 512), lambda j, sc: (0, j))],
        [sds((tokens, 2 * cols), BF), sds((cols, tokens), BF)],
        (hbm(teacher_rows), row(t_norm1_gain), row(t_norm1_shift), hbm(t_qkv), t_qv_bias),
        flops=2 * tokens * t_width * 2 * cols, scalars=scalars, far=(0, 1),
    )
    tk, teacher_rows, s_c1, s_w1, s_w3, t_fc1_late, t_out_late = lax.optimization_barrier(
        (tk, teacher_rows, s_c1, s_w1, s_w3, t_fc1, t_out)
    )
    s_c3 = across(s_c1)
    t_f1 = (t_fc1, core(t_fc1_late))
    t_w1 = core(t_out_late)
    by_slot = lambda w: pl.BlockSpec((mp, nb, piece, w), lambda j, sc: (0, j, 0, 0))
    x_kept, tq = call(
        functools.partial(teacher_q_kernel, slots, block, span), "teacher_q", (steps,),
        [
            whole(teacher_in.shape), whole(rank.shape), whole((1, t_width)), whole((1, t_width)),
            whole(t_qkv.shape), whole(t_qv_bias.shape),
        ],
        [by_slot(t_width), by_slot(2 * cols)],
        [sds((mp, slots, piece, t_width), BF), sds((mp, slots, piece, 2 * cols), BF)],
        (hbm(teacher_rows), rank, row(t_norm1_gain), row(t_norm1_shift), hbm(t_qkv), t_qv_bias),
        scratch=[pltpu.VMEM((span, t_width), F32)],
        flops=2 * rows * t_width * (cols + 512), scalars=scalars,
    )
    def attend(name, p, query):
        half_slot = lambda w, lane: pl.BlockSpec((mp, slots // 2, piece, w), lambda j: (0, j, 0, lane))
        return call(
            teacher_attend_kernel, name, (2,),
            [
                half_slot(256, p), pl.BlockSpec((tokens, 256), lambda j: (0, p)),
                pl.BlockSpec((128, tokens), lambda j: (p, 0)),
            ],
            half_slot(128, 0),
            sds((mp, slots, piece, 128), BF),
            (query, tk, tv),
            flops=2 * rows * tokens * (512 + 256),
        ).reshape(rows, 128)

    t_ctx = []
    for p in range(cols // 128):
        mixed_pair = attend("teacher_attend%d" % p, p, tq)
        if p == 0:
            mixed_pair, tq, s_c2, s_c3 = lax.optimization_barrier((mixed_pair, tq, s_c2, s_c3))
        else:
            t_ctx[0], mixed_pair, t_f1, t_w1, t_fc2_late = lax.optimization_barrier(
                (t_ctx[0], mixed_pair, t_f1, t_w1, t_fc2)
            )
        t_ctx.append([mixed_pair, core(mixed_pair[near:]), across(mixed_pair)])
    t_f2 = (t_fc2, core(t_fc2_late))
    t_w3 = core(t_w2)

    s_send, s_own, sent, a2, act, slope = forward(
        "both", "student_forward", near, (s_c0, s_c1, s_c2, s_c3), (s_out, s_w1, s_w2, s_w3), x_stud,
        row(s_out_bias), row(s_norm2_gain), row(s_norm2_shift), s_f1, s_b1, s_f2, row(s_fc2_bias), s_fc1.shape[1],
    )
    s_send, t_ctx, t_f2, t_w3 = lax.optimization_barrier((s_send, t_ctx, t_f2, t_w3))
    t_ctx = [x for own, from_core, from_chip in t_ctx for x in (own, from_core, from_chip, core(from_chip[near:]))]
    s_recv = across(s_send)
    t_args = (
        t_ctx, (t_out, t_w1, t_w2, t_w3), x_kept.reshape(rows, t_width), row(t_out_bias),
        row(t_norm2_gain), row(t_norm2_shift), t_f1, t_b1, t_f2, row(t_fc2_bias),
    )
    t_send = forward("send", "teacher_forward_far", mine, *t_args, 512)
    s_recv, t_args, t_send = lax.optimization_barrier((s_recv, t_args, t_send))
    t_recv = across(t_send)
    out_rows = (s_own + s_recv.astype(F32)).astype(BF)

    owners = lax.dynamic_index_in_dim(block_owner, home, 0, keepdims=False)
    capacity = (slots + homes - 1) // homes
    labels = jnp.arange(homes, dtype=jnp.int32)
    hits = (owners[:, None] == labels[None, :]).astype(jnp.int32)
    earlier = (jnp.arange(slots)[:, None] > jnp.arange(slots)[None, :]).astype(jnp.int32)
    order_in = jnp.sum(earlier * (owners[:, None] == owners[None, :]).astype(jnp.int32), axis=1)
    spot = jnp.where(owners >= 0, owners * capacity + order_in, homes * capacity)
    spots = jnp.arange(homes * capacity, dtype=jnp.int32)
    leaving = jnp.sum(
        jnp.where(spots[:, None] == spot[None, :], jnp.arange(slots, dtype=jnp.int32)[None, :], 0), axis=1
    )
    per_source = jnp.sum((block_owner == home).astype(jnp.int32), axis=1)
    ahead = (labels[:, None] > labels[None, :]).astype(jnp.int32)
    before = jnp.sum(ahead * per_source[None, :], axis=1)
    lane = jnp.arange(capacity, dtype=jnp.int32)
    target_slot = jnp.where(lane[None, :] < per_source[:, None], before[:, None] + lane[None, :], OWN).reshape(-1)
    chosen = jnp.sum(
        jnp.where(jnp.arange(OWN, dtype=jnp.int32)[:, None] == target_slot[None, :], spots[None, :], 0), axis=1
    )

    bits = log2(homes)

    def partner(value, bit):
        return lax.ppermute(value, "dp", [(i, i ^ (1 << bit)) for i in range(homes)])

    entries, shift = homes * capacity, log2(capacity)
    entry_shape = (entries, piece, width)
    leaving_sc = jnp.concatenate([leaving, home[None].astype(jnp.int32)])
    home_sc = home[None].astype(jnp.int32)

    def spread(name, came, going, blocks, came_in, places):
        ins = [blocks] if came_in is None else [blocks, came_in]
        base = places.shape[0] - 1
        lift = lambda bit: None if bit is None else bit + shift
        if going is None:
            outs = [sds((OWN, piece, width), BF)]
            scratch = [pltpu.VMEM(entry_shape, BF)]
        else:
            outs = [sds(entry_shape, BF), sds((entries // 2, piece, width), BF)]
            scratch = []
        return call(
            functools.partial(spread_kernel, lift(came), lift(going), shift, base), name, (1,),
            [whole(x.shape) for x in ins], [whole(o.shape) for o in outs], outs, ins, scratch=scratch, scalars=places,
        )

    turns = [1, 0] + list(range(2, bits))
    kept, sending = spread("spread0", None, turns[0], out_rows.reshape(slots, piece, width), None, leaving_sc)
    t_args, kept = lax.optimization_barrier((t_args, kept))
    travel = partner(sending, turns[0])
    t_own = forward("own", "teacher_forward_own", mine, *t_args, 512)
    t_own, t_recv, travel = lax.optimization_barrier((t_own, t_recv, travel))
    kept, sending = spread("spread1", turns[0], turns[1], kept, travel, home_sc)
    t_own, kept = lax.optimization_barrier((t_own, kept))
    travel = partner(sending, turns[1])

    d_guess, d_out, loss_row, head_b_row, fc2_b_row = call(
        functools.partial(head_kernel, block, piece), "head", (1,),
        [
            whole((mine, t_width)), whole((mine, t_width)), whole((mine, width)), whole((width, t_width)),
            whole((1, t_width)), pl.BlockSpec(memory_space=pltpu.SMEM),
        ],
        [whole((mine, t_width)), whole((mine, width)), whole((1, t_width)), whole((1, t_width)), whole((1, width))],
        [sds((mine, t_width), BF), sds((mine, width), BF), sds((1, t_width), F32), sds((1, t_width), F32), sds((1, width), F32)],
        (t_own, t_recv, out_rows, hbm(head_weight), row(head_bias), inverse),
        flops=4 * mine * width * t_width, scalars=scalars,
    )
    d_out_far = across(d_out)

    half_cols, quarter = t_width // 2, t_width // 4
    head_keep, head_send = call(
        head_grad_kernel, "head_grad", (1,),
        [
            whole((mine, width)),
            pl.BlockSpec((mine, half_cols), lambda j, sc: (0, sc[ORD] & 1)),
            pl.BlockSpec((mine, half_cols), lambda j, sc: (0, 1 - (sc[ORD] & 1))),
        ],
        [whole((width, half_cols))] * 2,
        [sds((width, half_cols), F32), sds((width, half_cols), BF)],
        (out_rows, d_guess, d_guess), scalars=scalars,
    )
    head_recv = core(head_send)
    own_quarter = pl.BlockSpec((width, quarter), lambda j, sc: (0, sc[ORD] >> 1))
    far_quarter = pl.BlockSpec((width, quarter), lambda j, sc: (0, 1 - (sc[ORD] >> 1)))
    head_keep, head_send = call(
        head_add_kernel, "head_add", (1,),
        [own_quarter, own_quarter, far_quarter, far_quarter],
        [whole((width, quarter))] * 2,
        [sds((width, quarter), F32), sds((width, quarter), BF)],
        (head_keep, head_recv, head_keep, head_recv), scalars=scalars, far=(0,),
    )
    d_out_far, head_send, travel = lax.optimization_barrier((d_out_far, head_send, travel))
    for turn in range(2, bits):
        kept, sending = spread("spread%d" % turn, turns[turn - 1], turns[turn], kept, travel, home_sc)
        travel = partner(sending, turns[turn])
    head_recv = across(head_send)

    hidden = s_fc1.shape[1]
    cut = lambda i: pl.BlockSpec((near, hidden), lambda *_: (0, i))
    square, turned_square, line = whole((width, hidden)), whole((hidden, width)), whole((1, hidden))
    tall, short_rows = whole((near, width)), whole((mine, width))
    d_scratch = [pltpu.VMEM((near, width), BF)]
    g1_send, g2_send, b1_send, da2_part = call(
        feed_far_kernel, "feed_back_far", (1,),
        [short_rows, short_rows, cut(1), cut(1), tall, square, turned_square],
        [square, turned_square, line, tall],
        [sds((width, hidden), BF), sds((hidden, width), BF), sds((1, hidden), F32), sds((near, width), F32)],
        (d_out, d_out_far, *map(hbm, (act, slope, a2, s_f1[1], s_f2[1]))),
        scratch=d_scratch,
    )
    da2_part, g1_send, g2_send, head_recv = lax.optimization_barrier((da2_part, g1_send, g2_send, head_recv))
    g1_recv, g2_recv = core(g1_send), core(g2_send)
    dpre, b1_own, da2_own, da2_send = call(
        feed_own_kernel, "feed_back_own", (1,),
        [short_rows, short_rows, cut(0), square, turned_square, tall],
        [whole((near, hidden)), line, tall, tall],
        [sds((near, hidden), BF), sds((1, hidden), F32), sds((near, width), F32), sds((near, width), BF)],
        (d_out, d_out_far, *map(hbm, (slope, s_f1[0], s_f2[0])), da2_part),
        scratch=d_scratch,
    )
    g1_recv, g2_recv, dpre, da2_send = lax.optimization_barrier((g1_recv, g2_recv, dpre, da2_send))
    da2_far = across(da2_send)

    x_first = list(range(bits))
    z_first = x_first[1:] + x_first[:1]

    def go(name, *bundles):
        advance(name, bundles, partner, scalars)

    half = width // 2
    a_width = hidden + quarter
    keep_a, send_a, keep_b, send_b = call(
        functools.partial(feed_grad_kernel, x_first[0], z_first[0]), "feed_back_grad", (1,),
        [
            short_rows, short_rows, cut(0), tall, whole((near, hidden)), square, turned_square,
            whole((width, quarter)), whole((width, quarter)),
        ],
        [whole((half, a_width))] * 2 + [whole((half, width))] * 2,
        [sds((half, a_width), BF)] * 2 + [sds((half, width), BF)] * 2,
        (d_out, d_out_far, hbm(act), hbm(a2), dpre, g1_recv, g2_recv, head_keep, head_recv),
        scratch=d_scratch, scalars=scalars,
    )
    one = Bundle(x_first, keep_a, partner(send_a, x_first[0]), ((0, hidden, F32), (hidden, a_width, BF)))
    two = Bundle(z_first, keep_b, partner(send_b, z_first[0]), ((0, width, F32),))

    q_late, keep_a = lax.optimization_barrier((sq, keep_a))
    one.flight = (keep_a, one.flight[1])
    probs = call(
        functools.partial(student_probs_kernel, used), "student_probs", (heads, rows // near),
        [
            pl.BlockSpec((near, wide), lambda h, j: (j, 0)), whole((rows, wide)),
            pl.BlockSpec((8, near), lambda h, j: (0, j)),
        ],
        [pl.BlockSpec((1, rows, near), lambda h, j: (h, 0, j))],
        [sds((heads, rows, rows), BF)],
        (q_late, sk, logs),
        flops=heads * rows * rows * wide * 2, far=(0,),
    )[0]
    da2_far, travel, probs, one.flight, two.flight = lax.optimization_barrier(
        (da2_far, travel, probs, one.flight, two.flight)
    )
    d_sent, sums2 = norm_back(
        "norm2_back", da2_own, da2_far, (d_out, d_out_far), sent, row(s_norm2_gain), BF
    )
    d_core = core(d_sent)
    d_core, one.flight, two.flight = lax.optimization_barrier((d_core, one.flight, two.flight))
    ds = (d_sent, d_core)
    for extra in range(bits - 2):
        go("sum_b%d" % extra, one, two)

    def back(name, picked, with_out):
        size = HD * len(picked)
        outs = [sds((rows, 3 * size), BF), sds((2, size), F32)] + [sds((used, width), F32)] * with_out
        return call(
            functools.partial(student_back_kernel, used, picked, with_out), name, (2,),
            [tall] * 2
            + [
                whole((used, width)), by_lanes(used),
                pl.BlockSpec((len(picked), rows, near), lambda j: (picked[0] // len(picked), 0, j)), by_rows(wide),
                whole((rows, wide)), whole((used, rows)),
            ],
            [whole(o.shape) for o in outs], outs,
            (*ds, s_out, mixed, probs, sq, sv, skt),
            scratch=[pltpu.VMEM((near, width), BF), pltpu.VMEM((near, wide), F32)]
            + [pltpu.VMEM((rows, wide), F32)] * 2 + [pltpu.VMEM((1, size), F32)]
            + [pltpu.VMEM((used, width), F32)] * with_out,
            flops=len(picked) * rows * rows * wide * 7, limit=36 * 2**20,
        )

    def project(name, bit, d, more):
        size = d.shape[1] + sum(m.shape[0] for m in more)
        specs = [whole(d.shape), whole(a_stud.shape)] + [whole(m.shape) for m in more]
        keep, send = call(
            functools.partial(project_grad_kernel, bit, bool(more)), name, (1,), specs,
            [whole((size // 2, width))] * 2, [sds((size // 2, width), BF)] * 2,
            (d, a_stud, *more), scalars=scalars,
        )
        return keep, partner(send, bit)

    pair, odd = tuple(range(heads - 1)), (heads - 1,)
    d_pair, pair_sums = back("student_back_pair", pair, False)
    d_pair, one.flight, two.flight = lax.optimization_barrier((d_pair, one.flight, two.flight))
    chosen_sc = jnp.concatenate([chosen, home_sc])
    student_out = spread("spread_end", turns[-1], None, kept, travel, chosen_sc)[0]
    go("sum_c", one, two)
    whole_width = ((0, width, BF),)
    three = Bundle(x_first, *project("project_pair", x_first[0], d_pair, ()), whole_width)
    tied = lax.optimization_barrier((*ds, three.flight[0], d_pair))
    ds, d_pair = tied[:2], tied[3]
    three.flight = (tied[2], three.flight[1])
    d_odd, odd_sums, g_out = back("student_back_odd", odd, True)
    d_odd, one.flight, two.flight, three.flight = lax.optimization_barrier(
        (d_odd, one.flight, two.flight, three.flight)
    )
    go("sum_d", one, two, three)
    four = Bundle(x_first, *project("project_odd", x_first[0], d_odd, (g_out,)), whole_width)
    mixed_size = HD * (heads - 1)
    w_pair = w_turn[:, :mixed_size].reshape(3 * mixed_size, width)
    w_odd = w_turn[:, mixed_size:].reshape(3 * HD, width)
    at = lambda w: pl.BlockSpec((near, w), lambda j: (1 - j, 0))
    da1_near, da1_send = call(
        input_grad_kernel, "input_grad", (2,),
        [at(3 * mixed_size), at(3 * HD), whole(w_pair.shape), whole(w_odd.shape)],
        [tall, tall], [sds((near, width), F32), sds((near, width), BF)],
        (d_pair, d_odd, w_pair, w_odd),
    )
    da1_recv = core(da1_send)
    da1_own = da1_near[:mine] + da1_recv[:mine].astype(F32)
    da1_far = across((da1_near[mine:] + da1_recv[mine:].astype(F32)).astype(BF))
    go("sum_e", one, two, three, four)
    for extra in range(bits - 3):
        go("sum_f%d" % extra, one, two, three, four)
    short_in = (sums2, fc2_b_row, head_b_row, loss_row, b1_send, b1_own, pair_sums, odd_sums)
    short_early = call(
        short_kernel, "short", (1,), [whole(v.shape) for v in short_in],
        [whole((16, width))] * 2, [sds((16, width), F32)] * 2, short_in,
    )
    grad_in, sums1 = norm_back("norm1_back", da1_own, da1_far, (d_sent,), x_stud, row(s_norm1_gain), F32)

    def tie(held, *bundles):
        kept, held = lax.optimization_barrier(([b.flight[0] for b in bundles], held))
        for b, first in zip(bundles, kept):
            b.flight = (first, b.flight[1])
        return held

    norm_rows = jnp.concatenate([sums1[:2], jnp.zeros((14, width), F32)], axis=0)
    vec = short_early[0] + norm_rows + core(short_early[1] + norm_rows)
    home_rows = (jnp.arange(16) < 9)[:, None]
    vec = tie(vec, three)
    go("sum_g", one, two, three, four)
    vec = jnp.where(home_rows, vec + across(vec), vec)
    turn = 0
    while three.result is None or four.result is None or one.result is None:
        left = [b for b in (three, four) if b.result is None]
        if turn <= bits and left:
            vec = tie(vec, left[0])
        if turn < bits:
            moved_vec = partner(vec, turn)
        go("sum_h%d" % turn, *left)
        if turn % 2 and one.result is None:
            flying = [b for b in left if b.result is None]
            if flying:
                tie(flying[0].flight[0], one, two)
            go("sum_last%d" % turn, one, two)
        if turn < bits:
            vec = vec + moved_vec
        turn += 1
    for bit in range(turn, bits):
        vec = vec + partner(vec, bit)

    g1_all, head_all = one.result
    head_cross, head_core = across(head_all), core(head_all)
    piece_spec = whole((width, quarter))
    grad_head = call(
        place_kernel, "place_head", (mp,), [piece_spec] * 4,
        pl.BlockSpec((width, quarter), lambda k, sc: (0, 2 * (sc[ORD + k] & 1) + (sc[ORD + k] >> 1))),
        sds((width, t_width), F32),
        (head_all, head_cross, head_core, core(head_cross)), scalars=scalars,
    )
    low_pair, low_odd = three.result[0], four.result[0]
    qkv_turned = jnp.concatenate(
        [low_pair.reshape(3, mixed_size, width), low_odd[: 3 * HD].reshape(3, HD, width)], axis=1
    )
    return (
        jnp.sum(vec[8]),
        student_out,
        grad_in.reshape(slots, piece, width),
        vec[0],
        vec[1],
        jnp.transpose(qkv_turned, (0, 2, 1)).astype(F32),
        vec[10:12, :used],
        low_odd[3 * HD :].astype(F32),
        vec[4],
        vec[2],
        vec[3],
        g1_all,
        vec[9],
        two.result[0],
        vec[5],
        grad_head,
        jnp.concatenate([vec[6], vec[7, : t_width - width]]),
    )


def solution(mesh):
    rep = P()
    in_specs = (
        P("dp", None), rep, rep, rep, P("dp", None, None), rep, rep, P(None, None, "mp"), P(None, "mp"),
        P("mp", None), rep, rep, rep, P(None, "mp"), P("mp"), P("mp", None), rep, rep, rep,
        P(None, None, "mp"), P(None, "mp"), P("mp", None), rep, rep, rep, P(None, "mp"), P("mp"),
        P("mp", None), rep, rep, rep,
    )
    out_specs = (
        rep, P("dp", "mp", None), P("dp", "mp", None), rep, rep, P(None, None, "mp"), P(None, "mp"),
        P("mp", None), rep, rep, rep, P(None, "mp"), P("mp"), P("mp", None), rep, rep, rep,
    )
    return jax.shard_map(body, mesh=mesh, in_specs=in_specs, out_specs=out_specs, check_vma=False)
```

```python
import functools

import jax
import jax.numpy as jnp
from jax import lax
from jax.experimental import pallas as pl
from jax.experimental.pallas import tpu as pltpu
from jax.sharding import PartitionSpec as P

HD = 64
OWN = 8
CLIPS = 8
EPS = 1e-05
BIG = -1e30
F32 = jnp.float32
BF = jnp.bfloat16
LIMIT = 24 * 2**20
COST = 4

ORD, CUM, END, HOME, LOW = 0, 4, 12, 20, 21


def dot_nn(a, b):
    return lax.dot_general(a, b, (((1,), (0,)), ((), ())), preferred_element_type=F32)


def dot_nt(a, b):
    return lax.dot_general(a, b, (((1,), (1,)), ((), ())), preferred_element_type=F32)


def dot_tn(a, b):
    return lax.dot_general(a, b, (((0,), (0,)), ((), ())), preferred_element_type=F32)


def unit(values):
    mean = jnp.mean(values, axis=-1, keepdims=True)
    centred = values - mean
    spread = jnp.mean(centred * centred, axis=-1, keepdims=True)
    inverse = lax.rsqrt(spread + EPS)
    return centred * inverse, inverse


def norm_low(values, gain_ref, shift_ref):
    u, _ = unit(values)
    return (u * gain_ref[...].astype(F32) + shift_ref[...].astype(F32)).astype(BF)


def log2(size):
    return size.bit_length() - 1


def whole(shape):
    return pl.BlockSpec(shape, lambda *_: (0,) * len(shape))


def call(kernel, name, grid, in_specs, out_specs, out_shape, args, scratch=(), flops=0, scalars=None, limit=LIMIT, far=()):
    moved = sum(a.size * a.dtype.itemsize for a in args)
    moved += sum(s.size * jnp.dtype(s.dtype).itemsize for s in jax.tree.leaves(out_shape))
    if far:
        if isinstance(out_shape, list):
            out_shape = [pltpu.HBM(o.shape, o.dtype) if i in far else o for i, o in enumerate(out_shape)]
        else:
            out_shape = pltpu.HBM(out_shape.shape, out_shape.dtype)
    params = pltpu.CompilerParams(
        dimension_semantics=("arbitrary",) * len(grid), vmem_limit_bytes=limit
    )
    cost = pl.CostEstimate(flops=int(flops) // COST, bytes_accessed=int(moved) // COST, transcendentals=0)
    lead = 0 if scalars is None else 1
    spec = pltpu.PrefetchScalarGridSpec(
        num_scalar_prefetch=lead,
        grid=grid,
        in_specs=in_specs,
        out_specs=out_specs,
        scratch_shapes=list(scratch),
    )
    run = pl.pallas_call(
        kernel,
        grid_spec=spec,
        out_shape=out_shape,
        compiler_params=params,
        cost_estimate=cost,
        name=name,
    )
    return run(*([scalars] if lead else []), *args)


def sds(shape, dtype):
    return jax.ShapeDtypeStruct(shape, dtype)


def group_of(index, sc, base):
    group = jnp.zeros(index.shape, jnp.int32)
    for c in range(CLIPS):
        group = group + (index >= sc[base + c]).astype(jnp.int32)
    return group


def teacher_kv_kernel(sc, x_ref, g_ref, s_ref, w_ref, b_ref, k_ref, v_ref):
    rows = x_ref.shape[0]
    a = norm_low(x_ref[...].astype(F32), g_ref, s_ref)
    token = pl.program_id(0) * rows + lax.broadcasted_iota(jnp.int32, (rows, 1), 0)
    lane = lax.broadcasted_iota(jnp.int32, (rows, 128), 1)
    hot = jnp.where(lane == group_of(token, sc, END), 1.0, 0.0).astype(BF)
    k = (dot_nn(a, w_ref[1]).astype(BF).astype(F32) * (HD**-0.5)).astype(BF)
    for p in range(k.shape[1] // 128):
        k_ref[:, 256 * p : 256 * p + 128] = k[:, 128 * p : 128 * (p + 1)]
        k_ref[:, 256 * p + 128 : 256 * (p + 1)] = hot
    v_ref[...] = (dot_nn(a, w_ref[2]) + b_ref[1:2, :].astype(F32)).T.astype(BF)


def teacher_q_kernel(slots, block, step, sc, x_ref, rank_ref, g_ref, s_ref, w_ref, b_ref, xk_ref, q_ref, acc):
    j = pl.program_id(0)
    pieces, nb, piece, width = xk_ref.shape
    rows = pieces * nb * piece

    line = lax.broadcasted_iota(jnp.int32, (rows, 1), 0)
    part = line >> log2(nb * piece)
    inner = line & (nb * piece - 1)
    order = jnp.zeros((rows, 1), jnp.int32)
    for p in range(pieces):
        order = jnp.where(part == p, sc[ORD + p], order)
    slot = (j * nb + (inner >> log2(piece))) * block + order * piece + (inner & (piece - 1))
    group = group_of(slot, sc, CUM)
    acc[...] = jnp.zeros_like(acc)

    def one(t, _):
        hit = jnp.where(slot == rank_ref[pl.ds(t, 1), :], 1.0, 0.0).astype(BF)
        acc[...] += dot_nn(hit, x_ref[pl.ds(pl.multiple_of(t * step, step), step), :])
        return 0

    steps = slots // nb
    lax.fori_loop(sc[LOW + j], sc[LOW + steps + j], one, 0)
    kept = acc[...]
    xk_ref[...] = kept.astype(BF).reshape(xk_ref.shape)
    a = norm_low(kept, g_ref, s_ref)
    q = (dot_nn(a, w_ref[0]) + b_ref[0:1, :].astype(F32)).astype(BF)
    lane = lax.broadcasted_iota(jnp.int32, (rows, 128), 1)
    other = (lane != group) & (lane <= CLIPS)
    mask = jnp.where(other, BIG, 0.0).astype(BF)
    pairs = q.shape[1] // 128
    out = []
    for p in range(pairs):
        out += [q[:, 128 * p : 128 * (p + 1)], mask]
    q_ref[...] = jnp.concatenate(out, axis=1).reshape(q_ref.shape)


def softmax_mix(keys, query, values):
    scores = dot_nt(keys, query)
    top = jnp.max(scores, axis=0, keepdims=True)
    e = jnp.exp(scores - top)
    mass = jnp.sum(e, axis=0, keepdims=True)
    return dot_nn(values, e.astype(BF)) * (1.0 / mass), top + jnp.log(mass)


def teacher_attend_kernel(q_ref, k_ref, v_ref, ctx_ref):
    pieces, nb, piece, both = q_ref.shape
    rows = pieces * nb * piece
    part = q_ref[...].reshape(rows, both).astype(F32)
    lane = lax.broadcasted_iota(jnp.int32, (rows, both), 1)
    mixed = []
    for h in range(2):
        query = jnp.where(((lane >> 6) == h) | (lane >= 128), part, 0.0).astype(BF)
        mixed.append(softmax_mix(k_ref[...], query, v_ref[HD * h : HD * (h + 1), :])[0])
    ctx_ref[...] = jnp.concatenate(mixed, axis=0).T.astype(BF).reshape(ctx_ref.shape)


def student_qkv_kernel(block, sc, x_ref, g_ref, s_ref, w_ref, b_ref, xo_ref, a_ref, q_ref, k_ref, v_ref, kt_ref, vt_ref):
    slots, _, piece, width = x_ref.shape
    rows = slots * piece
    used, wide = w_ref.shape[1], q_ref.shape[1]
    x = x_ref[...].reshape(rows, width)
    xo_ref[...] = x
    a = norm_low(x.astype(F32), g_ref, s_ref)
    a_ref[...] = a
    line = lax.broadcasted_iota(jnp.int32, (rows, 1), 0)
    lane = lax.broadcasted_iota(jnp.int32, (rows, wide - used), 1)
    slot = (line >> log2(piece)) * block + sc[ORD + pl.program_id(0)] * piece + (line & (piece - 1))
    same = lane == group_of(slot, sc, CUM)
    q_ref[:, :used] = (dot_nt(a, w_ref[0]) + b_ref[0:1, :].astype(F32)).astype(BF)
    q_ref[:, used:] = jnp.where(same | (lane > CLIPS), 0.0, BIG).astype(BF)
    k = dot_nt(a, w_ref[1]).astype(BF).astype(F32) * (HD**-0.5)
    k_ref[:, :used] = k.astype(BF)
    k_ref[:, used:] = jnp.where(same, 1.0, 0.0).astype(BF)
    kt_ref[...] = k.T.astype(BF)
    v = dot_nt(a, w_ref[2]) + b_ref[1:2, :].astype(F32)
    v_ref[:, :used] = v.astype(BF)
    v_ref[:, used:] = jnp.zeros((rows, wide - used), BF)
    vt_ref[...] = v.T.astype(BF)


def student_attend_kernel(used, q_ref, k_ref, vt_ref, ctx_ref, mixed_ref, log_ref):
    q = q_ref[...].astype(F32)
    rows, wide = q.shape
    lane = lax.broadcasted_iota(jnp.int32, (rows, wide), 1)
    mixed, logs = [], []
    for h in range(used // HD):
        query = jnp.where(((lane >> 6) == h) | (lane >= used), q, 0.0).astype(BF)
        part, log = softmax_mix(k_ref[...], query, vt_ref[HD * h : HD * (h + 1), :])
        mixed.append(part)
        logs.append(log)
    total = jnp.concatenate(mixed, axis=0)
    mixed_ref[...] = total
    ctx_ref[...] = total.T.astype(BF)
    log_ref[...] = jnp.concatenate(logs + [jnp.zeros((8 - len(logs), rows), F32)], axis=0)


def student_probs_kernel(used, q_ref, k_ref, log_ref, out_ref):
    rows, wide = q_ref.shape
    lane = lax.broadcasted_iota(jnp.int32, (rows, wide), 1)
    h = pl.program_id(0)
    query = jnp.where(((lane >> 6) == h) | (lane >= used), q_ref[...].astype(F32), 0.0).astype(BF)
    out_ref[0] = jnp.exp(dot_nt(k_ref[...], query) - log_ref[pl.ds(h, 1), :]).astype(BF)


def student_back_kernel(used, picked, with_out, p0, p1, w_ref, mixed_ref, probs_ref, q_ref, v_ref, kt_ref, *rest):
    if with_out:
        out_ref, sums_ref, w_grad_ref, ds, da, dk, dv, dqs, dw = rest
    else:
        out_ref, sums_ref, ds, da, dk, dv, dqs = rest
    j = pl.program_id(0)
    steps = pl.num_programs(0)
    lo, size = HD * picked[0], HD * len(picked)
    rows, wide = q_ref.shape

    @pl.when(j == 0)
    def _():
        dk[...] = jnp.zeros_like(dk)
        dv[...] = jnp.zeros_like(dv)
        dqs[...] = jnp.zeros_like(dqs)
        ds[...] = p0[...]
        if with_out:
            dw[...] = jnp.zeros_like(dw)

    @pl.when(j == 1)
    def _():
        ds[...] = p1[...]

    grad = ds[...]
    da[:, :used] = dot_nt(grad, w_ref[...])
    da[:, used:] = jnp.zeros((rows, wide - used), F32)
    low = da[...].astype(BF).astype(F32)
    mixed = mixed_ref[...]
    turned = dot_nt(w_ref[lo : lo + size, :], grad).astype(BF).astype(F32)
    product = turned * mixed[lo : lo + size, :]
    if with_out:
        dw[...] += dot_nn(mixed.astype(BF), grad)
    lane = lax.broadcasted_iota(jnp.int32, (rows, wide), 1)
    q = q_ref[...].astype(F32)
    grads_q = []
    for i, h in enumerate(picked):
        mine = (lane >> 6) == h
        query = jnp.where(mine | (lane >= used), q, 0.0).astype(BF)
        outer = jnp.where(mine, low, 0.0).astype(BF)
        delta = jnp.sum(product[HD * i : HD * (i + 1), :], axis=0, keepdims=True)
        pt = probs_ref[i]
        dst = (pt.astype(F32) * (dot_nt(v_ref[...], outer) - delta)).astype(BF)
        dv[...] += dot_nn(pt, outer)
        dk[...] += dot_nn(dst, query)
        grads_q.append(dot_nn(kt_ref[HD * h : HD * (h + 1), :], dst))
    dq = jnp.concatenate(grads_q, axis=0).T.astype(BF)
    out_ref[pl.ds(pl.multiple_of(j * rows, rows), rows), 0:size] = dq
    dqs[...] += jnp.sum(dq.astype(F32), axis=0, keepdims=True)

    @pl.when(j == steps - 1)
    def _():
        out_ref[:, size : 2 * size] = (dk[:, lo : lo + size] * (HD**-0.5)).astype(BF)
        dv_low = dv[:, lo : lo + size].astype(BF)
        out_ref[:, 2 * size : 3 * size] = dv_low
        sums_ref[...] = jnp.concatenate(
            [dqs[...], jnp.sum(dv_low.astype(F32), axis=0, keepdims=True)], axis=0
        )
        if with_out:
            w_grad_ref[...] = dw[...]


def gelu_both(pre):
    phi = 0.5 * (1.0 + lax.erf(pre * 0.7071067811865476))
    return pre * phi, phi + pre * (0.3989422804014327 * jnp.exp(-0.5 * pre * pre))


def flipped(ref):
    half = ref.shape[0] // 2
    return jnp.concatenate([ref[half:], ref[:half]], axis=0)


def forward_kernel(
    mode, half_steps,
    *refs,
):
    both = mode == "both"
    count = 4 if both else 8
    ctx, (w0, w1, w2, w3, x_ref, ob_ref, g_ref, s_ref), refs = refs[:count], refs[count : count + 8], refs[count + 8 :]
    (f1a, f1b, b1a, b1b, f2a, f2b, b2_ref), rest = refs[:7], refs[7:]
    if both:
        send_ref, own_ref, sent_ref, a2_ref, act_ref, slope_ref, a2, acc, base = rest
    elif mode == "own":
        own_ref, a2, acc, base = rest
    else:
        send_ref, a2, acc = rest
    j = pl.program_id(0)
    rows = x_ref.shape[0]

    @pl.when(j == 0)
    def _():
        if both:
            found = [ctx[0][...], ctx[1][...], flipped(ctx[2]), flipped(ctx[3])]
        else:
            found = [jnp.concatenate([ctx[i][...], ctx[4 + i][...]], axis=1) for i in range(4)]
        parts = [dot_nn(c, w[...]) for c, w in zip(found, (w0, w1, w2, w3))]
        if not both:
            parts = [p.astype(BF).astype(F32) for p in parts]
        resid = x_ref[...].astype(F32) + (parts[0] + parts[1] + parts[2] + parts[3])
        resid = resid + ob_ref[...].astype(F32)
        if both:
            low = resid.astype(BF)
            sent_ref[...] = low
            resid = low.astype(F32)
        a2[...] = norm_low(resid, g_ref, s_ref)
        if both:
            a2_ref[...] = a2[...]
            base[...] = resid[: rows // 2] + b2_ref[...].astype(F32)
        elif mode == "own":
            base[...] = resid + b2_ref[...].astype(F32)
        acc[...] = jnp.zeros_like(acc)

    def half(f1, b1, f2):
        pre = dot_nn(a2[...], f1[...]) + b1[...].astype(F32)
        if both:
            act, slope = gelu_both(pre)
            slope_ref[...] = slope.astype(BF)
        else:
            act = pre * (0.5 * (1.0 + lax.erf(pre * 0.7071067811865476)))
        act = act.astype(BF)
        if both:
            act_ref[...] = act
        acc[...] += dot_nn(act, f2[...])

    @pl.when(j < half_steps)
    def _():
        half(f1a, b1a, f2a)

    @pl.when(j >= half_steps)
    def _():
        half(f1b, b1b, f2b)

    @pl.when(j == 2 * half_steps - 1)
    def _():
        if both:
            own_ref[...] = acc[: rows // 2] + base[...]
            send_ref[...] = acc[rows // 2 :].astype(BF)
        elif mode == "own":
            own_ref[...] = acc[...] + base[...]
        else:
            send_ref[...] = acc[...].astype(BF)


def forward(mode, name, rows, ctx, w_out, x, out_b, gain, shift, f1, b1, f2, b2, chunk):
    width = x.shape[1]
    heads_wide, hidden = w_out[0].shape[0], f1[0].shape[1]
    n = hidden // chunk
    both = mode == "both"
    near_at = 1 if mode == "send" else 0
    far_at = 1 if mode == "own" else 0
    first = lambda j: jnp.minimum(j, n - 1)
    second = lambda j: jnp.maximum(j - n, 0)
    at = lambda i, w: pl.BlockSpec((rows, w), lambda j: (i, 0))
    c_wide = ctx[0].shape[1]
    specs = ([at(near_at, c_wide)] * 2 + [at(far_at, c_wide)] * 2) * (len(ctx) // 4)
    specs += [whole(w.shape) for w in w_out]
    specs += [at(near_at, width)] + [whole((1, width))] * 3
    specs += [pl.BlockSpec((width, chunk), lambda j, f=f: (0, f(j))) for f in (first, second)]
    specs += [pl.BlockSpec((1, chunk), lambda j, f=f: (0, f(j))) for f in (first, second)]
    specs += [pl.BlockSpec((chunk, width), lambda j, f=f: (f(j), 0)) for f in (first, second)]
    specs += [whole((1, width))]
    half = rows // 2
    scratch = [pltpu.VMEM((rows, width), BF), pltpu.VMEM((rows, width), F32)]
    if both:
        outs = [sds((half, width), BF), sds((half, width), F32)] + [sds((rows, width), BF)] * 2
        outs += [sds((rows, 2 * hidden), BF)] * 2
        out_specs = [whole((half, width))] * 2 + [whole((rows, width))] * 2
        out_specs += [pl.BlockSpec((rows, chunk), lambda j: (0, j))] * 2
        scratch += [pltpu.VMEM((half, width), F32)]
    elif mode == "own":
        outs, out_specs = sds((rows, width), F32), whole((rows, width))
        scratch += [pltpu.VMEM((rows, width), F32)]
    else:
        outs, out_specs = sds((rows, width), BF), whole((rows, width))
    return call(
        functools.partial(forward_kernel, mode, n), name, (2 * n,), specs, out_specs, outs,
        (*ctx, *w_out, x, out_b, gain, shift, *f1, *b1, *f2, b2),
        scratch=scratch,
        flops=2 * rows * width * (4 * heads_wide + 4 * hidden), far=(2, 3, 4, 5) if both else (0,) if mode == "own" else (),
    )


def head_kernel(block, piece, sc, own_ref, recv_ref, out_ref, w_ref, b_ref, inv_ref, dg_ref, do_ref, loss_ref, hb_ref, ob_ref):
    rows, width = own_ref.shape
    target = (own_ref[...] + recv_ref[...].astype(F32)).astype(BF).astype(F32)
    line = lax.broadcasted_iota(jnp.int32, (rows, 1), 0)
    slot = (line >> log2(piece)) * block + sc[ORD] * piece + (line & (piece - 1))
    live = slot < sc[CUM + CLIPS - 1]
    group = group_of(slot, sc, CUM)
    weight = jnp.zeros((rows, 1), F32)
    for c in range(CLIPS):
        weight = jnp.where(group == c, inv_ref[0, c], weight)
    weight = jnp.where(live, weight, 0.0)
    target = jnp.where(live, target, 0.0)
    miss = dot_nn(out_ref[...], w_ref[...]) + b_ref[...].astype(F32) - target
    dg = (weight * miss).astype(BF)
    dg_ref[...] = dg
    loss_ref[...] = 0.5 * jnp.sum(weight * miss * miss, axis=0, keepdims=True)
    hb_ref[...] = jnp.sum(dg.astype(F32), axis=0, keepdims=True)
    do = dot_nt(dg, w_ref[...]).astype(BF)
    do_ref[...] = do
    ob_ref[...] = jnp.sum(do.astype(F32), axis=0, keepdims=True)


def head_grad_kernel(sc, out_ref, own_ref, other_ref, keep_ref, send_ref):
    keep_ref[...] = dot_tn(out_ref[...], own_ref[...])
    send_ref[...] = dot_tn(out_ref[...], other_ref[...]).astype(BF)


def head_add_kernel(sc, keep_a, recv_a, keep_b, recv_b, keep_ref, send_ref):
    keep_ref[...] = keep_a[...] + recv_a[...].astype(F32)
    send_ref[...] = (keep_b[...] + recv_b[...].astype(F32)).astype(BF)


def feed_far_kernel(d0, d1, act_ref, slope_ref, a2_ref, f1, f2, g1_ref, g2_ref, gb_ref, acc_ref, d):
    half = d0.shape[0]
    d[:half] = d0[...]
    d[half:] = d1[...]
    grad = d[...]
    dpre = (dot_nt(grad, f2[...]) * slope_ref[...].astype(F32)).astype(BF)
    gb_ref[...] = jnp.sum(dpre.astype(F32), axis=0, keepdims=True)
    acc_ref[...] = dot_nt(dpre, f1[...])
    g2_ref[...] = dot_tn(act_ref[...], grad).astype(BF)
    g1_ref[...] = dot_tn(a2_ref[...], dpre).astype(BF)


def feed_own_kernel(d0, d1, slope_ref, f1, f2, before, dpre_ref, gb_ref, own_ref, send_ref, d):
    half = d0.shape[0]
    d[:half] = d0[...]
    d[half:] = d1[...]
    dpre = (dot_nt(d[...], f2[...]) * slope_ref[...].astype(F32)).astype(BF)
    dpre_ref[...] = dpre
    gb_ref[...] = jnp.sum(dpre.astype(F32), axis=0, keepdims=True)
    part = dot_nt(dpre, f1[...]) + before[...]
    own_ref[...] = part
    send_ref[:half] = part[half:].astype(BF)
    send_ref[half:] = part[:half].astype(BF)


def keep_and_send(value, mark, keep_ref, send_ref):
    half = value.shape[0] // 2
    top, bottom = value[:half], value[half:]
    first = mark == 0
    keep_ref[...] = jnp.where(first, top, bottom).astype(keep_ref.dtype)
    send_ref[...] = jnp.where(first, bottom, top).astype(send_ref.dtype)


def feed_grad_kernel(bit_a, bit_b, sc, d0, d1, act_ref, a2_ref, dpre_ref, r1, r2, hk, hr,
                     keep_a, send_a, keep_b, send_b, d):
    half = d0.shape[0]
    d[:half] = d0[...]
    d[half:] = d1[...]
    g1 = dot_tn(a2_ref[...], dpre_ref[...]) + r1[...].astype(F32)
    head = hk[...] + hr[...].astype(F32)
    keep_and_send(jnp.concatenate([g1, head], axis=1), (sc[HOME] >> bit_a) & 1, keep_a, send_a)
    g2 = dot_tn(act_ref[...], d[...]) + r2[...].astype(F32)
    keep_and_send(g2, (sc[HOME] >> bit_b) & 1, keep_b, send_b)


def project_grad_kernel(bit, more, sc, d_ref, a_ref, *rest):
    value = dot_tn(d_ref[...], a_ref[...])
    if more:
        value = jnp.concatenate([value, rest[0][...]], axis=0)
    keep_and_send(value, (sc[HOME] >> bit) & 1, rest[-2], rest[-1])


def short_kernel(sums_ref, fc2_ref, hb_ref, loss_ref, b1s_ref, b1_ref, *rest):
    own_ref, send_ref = rest[-2:]
    width = own_ref.shape[1]
    for out in (own_ref, send_ref):
        out[...] = jnp.zeros(out.shape, F32)
        out[2:5, :] = sums_ref[...]
        out[5:6, :] = fc2_ref[...]
        out[6:7, :] = hb_ref[:, :width]
        left = hb_ref.shape[1] - width
        out[7:8, :left] = hb_ref[:, width:]
        loss = loss_ref[:, :left]
        for i in range(1, loss_ref.shape[1] // left):
            loss += loss_ref[:, left * i : left * (i + 1)]
        out[8:9, :left] = loss
    own_ref[9:10, :] = b1_ref[...]
    send_ref[9:10, :] = b1s_ref[...]
    at = 0
    for ref in rest[:-2]:
        own_ref[10:12, at : at + ref.shape[1]] = ref[...]
        at += ref.shape[1]


def input_grad_kernel(da_ref, db_ref, wa_ref, wb_ref, near_ref, send_ref):
    value = dot_nn(da_ref[...], wa_ref[...]) + dot_nn(db_ref[...], wb_ref[...])

    @pl.when(pl.program_id(0) == 0)
    def _():
        send_ref[...] = value.astype(BF)

    @pl.when(pl.program_id(0) == 1)
    def _():
        near_ref[...] = value


def stage_kernel(ops, sc, *refs):
    ins, outs = refs[: 2 * len(ops)], refs[2 * len(ops) :]
    at = 0
    for i, (kind, bit, parts) in enumerate(ops):
        a, b = ins[2 * i][...].astype(F32), ins[2 * i + 1][...].astype(F32)
        mark = (sc[HOME] >> bit) & 1
        if kind == "split":
            keep_and_send(a + b, mark, outs[at], outs[at + 1])
            at += 2
        elif kind == "add":
            outs[at][...] = (a + b).astype(BF)
            at += 1
        else:
            rows = a.shape[0]
            for lo, hi, dtype in parts:
                outs[at][:rows] = jnp.where(mark == 0, a[:, lo:hi], b[:, lo:hi]).astype(dtype)
                outs[at][rows:] = jnp.where(mark == 0, b[:, lo:hi], a[:, lo:hi]).astype(dtype)
                at += 1


def stage(name, ops, pairs, scalars):
    shapes = []
    for (kind, bit, parts), (a, b) in zip(ops, pairs):
        rows, width = a.shape
        if kind == "split":
            shapes.append([sds((rows // 2, width), BF)] * 2)
        elif kind == "add":
            shapes.append([sds((rows, width), BF)])
        else:
            shapes.append([sds((2 * rows, hi - lo), dtype) for lo, hi, dtype in parts])
    sizes = [a.shape[0] for a, _ in pairs] + [s.shape[0] for group in shapes for s in group]
    if all(size % 16 == 0 for size in sizes):
        flat = [x for pair in pairs for x in pair]
        outs = [s for group in shapes for s in group]
        found = call(
            functools.partial(stage_kernel, ops), name, (1,), [whole(x.shape) for x in flat],
            [whole(s.shape) for s in outs], outs, flat, scalars=scalars,
        )
    else:
        found = []
        for (kind, bit, parts), (a, b) in zip(ops, pairs):
            first = ((scalars[HOME] >> bit) & 1) == 0
            if kind == "join":
                for lo, hi, dtype in parts:
                    a1, b1 = a[:, lo:hi].astype(dtype), b[:, lo:hi].astype(dtype)
                    found.append(
                        jnp.where(first, jnp.concatenate([a1, b1], 0), jnp.concatenate([b1, a1], 0))
                    )
                continue
            total = (a.astype(F32) + b.astype(F32)).astype(BF)
            if kind == "add":
                found.append(total)
            else:
                half = total.shape[0] // 2
                found.append(jnp.where(first, total[:half], total[half:]))
                found.append(jnp.where(first, total[half:], total[:half]))
    result, at = [], 0
    for group in shapes:
        result.append(found[at : at + len(group)])
        at += len(group)
    return result


class Bundle:
    def __init__(self, bits, keep, recv, parts):
        self.bits, self.step, self.phase, self.parts = bits, 0, "split", parts
        self.flight = (keep, recv)
        self.result = None

    def op(self):
        if self.phase == "split":
            last = self.step == len(self.bits) - 1
            return ("add", 0, None) if last else ("split", self.bits[self.step + 1], None)
        width = self.flight[0].shape[1]
        parts = self.parts if self.step == 0 else ((0, width, BF),)
        return ("join", self.bits[self.step], parts)


def advance(name, bundles, partner, scalars):
    ops = [b.op() for b in bundles]
    done = stage(name, ops, [b.flight for b in bundles], scalars)
    for b, (kind, bit, _), got in zip(bundles, ops, done):
        if kind == "split":
            b.step += 1
            b.flight = (got[0], partner(got[1], bit))
        elif kind == "add":
            b.phase = "join"
            b.flight = (got[0], partner(got[0], b.bits[b.step]))
        elif b.step == 0:
            b.flight, b.result = None, got
        else:
            b.step -= 1
            b.flight = (got[0], partner(got[0], b.bits[b.step]))


def spread_kernel(came, going, shift, base, sc, in_ref, *refs):
    refs = list(refs)
    recv_ref = None if came is None else refs.pop(0)
    n = refs[0].shape[0] if going is not None else in_ref.shape[0]
    bit_in = 0 if came is None else (sc[base] >> (came - shift)) & 1

    def entry(i):
        if came is None:
            return in_ref[sc[i]]
        side = (i & ((1 << came) - 1)) | ((i >> (came + 1)) << came)
        return jnp.where(((i >> came) & 1) == bit_in, in_ref[i], recv_ref[side])

    if going is None:
        kept_ref, out_ref = refs[1], refs[0]
        for i in range(n):
            kept_ref[i] = entry(i)
        for i in range(out_ref.shape[0]):
            out_ref[i] = kept_ref[sc[i]]
        return
    keep_ref, send_ref = refs
    bit_out = (sc[base] >> (going - shift)) & 1
    for i in range(n):
        keep_ref[i] = entry(i)
    for j in range(send_ref.shape[0]):
        low = (j & ((1 << going) - 1)) | ((j >> going) << (going + 1))
        send_ref[j] = jnp.where(bit_out == 0, keep_ref[low | (1 << going)], keep_ref[low])


def place_kernel(sc, h0, h1, h2, h3, out_ref):
    for i, ref in enumerate((h0, h1, h2, h3)):

        @pl.when(pl.program_id(0) == i)
        def _(ref=ref):
            out_ref[...] = ref[...].astype(F32)


def norm_back_kernel(count, own_ref, recv_ref, *rest):
    base_refs, (x_ref, g_ref, dx_ref, sums_ref) = rest[:count], rest[count:]
    rows = own_ref.shape[0]
    mine = rows // count
    d = own_ref[...].astype(F32) + recv_ref[...].astype(F32)
    u, inverse = unit(x_ref[...].astype(F32))
    e = g_ref[...].astype(F32) * d
    mean_e = jnp.mean(e, axis=-1, keepdims=True)
    mean_eu = jnp.mean(e * u, axis=-1, keepdims=True)
    change = (e - mean_e - u * mean_eu) * inverse
    for i, base in enumerate(base_refs):
        at = slice(mine * i, mine * (i + 1))
        dx_ref[at] = (base[...].astype(F32) + change[at]).astype(dx_ref.dtype)
    sums_ref[...] = jnp.concatenate(
        [
            jnp.sum((d * u)[:mine], axis=0, keepdims=True),
            jnp.sum(d[:mine], axis=0, keepdims=True),
            jnp.sum(dx_ref[:mine].astype(F32), axis=0, keepdims=True),
        ],
        axis=0,
    )


def norm_back(name, own, recv, bases, x, gain, dtype):
    rows, width = own.shape
    block = pl.BlockSpec((rows, width), lambda *_: (0, 0))
    piece = pl.BlockSpec((rows // len(bases), width), lambda *_: (0, 0))
    return call(
        functools.partial(norm_back_kernel, len(bases)), name, (1,),
        [block] * 2 + [piece] * len(bases) + [block, whole((1, width))],
        [block, whole((3, width))],
        [sds((rows, width), dtype), sds((3, width), F32)],
        (own, recv, *bases, x, gain),
    )


def hbm(x):
    return pltpu.with_memory_space_constraint(x, pltpu.HBM)


def swap(x, bit, count):
    return lax.ppermute(x, "mp", [(i, i ^ bit) for i in range(count)])


def row(vector):
    return vector.reshape(1, -1)


def layout(mask_row, seg_row, order, home, steps, span):
    tokens = mask_row.shape[0]
    grid = mask_row.reshape(tokens // 128, 128).astype(BF)
    upper = (jnp.arange(128)[:, None] <= jnp.arange(128)[None, :]).astype(BF)
    within = jnp.dot(grid, upper, preferred_element_type=F32)
    lines = tokens // 128
    lower = (jnp.arange(lines)[:, None] > jnp.arange(lines)[None, :]).astype(BF)
    ahead = jnp.dot(lower, within[:, 127:].astype(BF), preferred_element_type=F32)
    count = (within + ahead).astype(jnp.int32).reshape(tokens)
    rank = jnp.where(mask_row == 1, count - 1, -1)
    labels = jnp.arange(CLIPS, dtype=jnp.int32)
    upto = (seg_row[None, :] <= labels[:, None]).astype(jnp.int32)
    ends = jnp.sum(upto, axis=1)
    cum = jnp.sum(upto * mask_row[None, :], axis=1)
    edge = jnp.arange(steps, dtype=jnp.int32) * span
    low = jnp.sum((count[None, :] <= edge[:, None]).astype(jnp.int32), axis=1)
    high = jnp.sum((count[None, :] < edge[:, None] + span).astype(jnp.int32), axis=1)
    low = low // span
    high = jnp.minimum(high, tokens - 1) // span + 1
    each = cum - jnp.concatenate([jnp.zeros((1,), jnp.int32), cum[:-1]])
    inverse = 1.0 / jnp.maximum(each, 1).astype(F32)
    first = jnp.concatenate([order, cum, ends, home[None].astype(jnp.int32)])
    scalars = jnp.concatenate([first, low, high])
    return rank.reshape(tokens // span, span), first, scalars, inverse.reshape(1, CLIPS)


def body(
    teacher_in, segment_ids, keep_mask, block_owner, student_in,
    t_norm1_gain, t_norm1_shift, t_qkv, t_qv_bias, t_out, t_out_bias,
    t_norm2_gain, t_norm2_shift, t_fc1, t_fc1_bias, t_fc2, t_fc2_bias,
    s_norm1_gain, s_norm1_shift, s_qkv, s_qv_bias, s_out, s_out_bias,
    s_norm2_gain, s_norm2_shift, s_fc1, s_fc1_bias, s_fc2, s_fc2_bias,
    head_weight, head_bias,
):
    mp = lax.axis_size("mp")
    me = lax.axis_index("mp")
    homes = lax.axis_size("dp")
    home = lax.axis_index("dp")
    slots, block, width = student_in.shape
    piece = block // mp
    rows = slots * block
    mine = rows // mp
    near = 2 * mine
    tokens, t_width = teacher_in.shape
    used = s_qkv.shape[2]
    wide = 256
    nb = 2
    span = nb * block
    steps = slots // nb
    core = lambda x: swap(x, 1, mp)
    across = lambda x: swap(x, 2, mp)

    order = jnp.stack([me, me ^ 2, me ^ 1, me ^ 3]).astype(jnp.int32)
    mask_row = lax.dynamic_index_in_dim(keep_mask, home, 0, keepdims=False)
    seg_row = lax.dynamic_index_in_dim(segment_ids, home, 0, keepdims=False)
    rank, first_scalars, scalars, inverse = layout(mask_row, seg_row, order, home, steps, span)

    t_w2 = across(t_out)
    s_w2 = across(s_out)
    s_f1 = (s_fc1, core(s_fc1))
    s_f2 = (s_fc2, core(s_fc2))
    biases = core(jnp.concatenate([t_fc1_bias, s_fc1_bias]))

    x4 = hbm(student_in.reshape(slots, mp, piece, width))
    w_turn = jnp.transpose(s_qkv, (0, 2, 1))
    by_piece = lambda w: pl.BlockSpec((mine, w), lambda k, sc: (k, 0))
    turned = pl.BlockSpec((used, mine), lambda k, sc: (0, k))
    x_stud, a_stud, sq, sk, sv, skt, svt = call(
        functools.partial(student_qkv_kernel, block), "student_qkv", (mp,),
        [
            pl.BlockSpec((slots, 1, piece, width), lambda k, sc: (0, sc[ORD + k], 0, 0)),
            whole((1, width)), whole((1, width)), whole(w_turn.shape), whole(s_qv_bias.shape),
        ],
        [by_piece(width)] * 2 + [by_piece(wide)] * 3 + [turned] * 2,
        [sds((rows, width), BF)] * 2 + [sds((rows, wide), BF)] * 3 + [sds((used, rows), BF)] * 2,
        (x4, row(s_norm1_gain), row(s_norm1_shift), hbm(w_turn), s_qv_bias),
        flops=2 * rows * width * 3 * wide, scalars=first_scalars, far=(0, 1, 4, 5),
    )
    heads = used // HD
    by_rows = lambda w: pl.BlockSpec((near, w), lambda j: (j, 0))
    by_lanes = lambda h: pl.BlockSpec((h, near), lambda j: (0, j))
    ctx, mixed, logs = call(
        functools.partial(student_attend_kernel, used), "student_attend", (rows // near,),
        [by_rows(wide), whole((rows, wide)), whole((used, rows))],
        [by_rows(used), by_lanes(used), by_lanes(8)],
        [sds((rows, used), BF), sds((used, rows), F32), sds((8, rows), F32)],
        (sq, sk, svt),
        flops=heads * rows * rows * wide * 4, far=(1, 2),
    )

    ctx, teacher_rows, t_w2, s_w2, s_f1, s_f2, biases, s_out_late = lax.optimization_barrier(
        (ctx, teacher_in, t_w2, s_w2, s_f1, s_f2, biases, s_out)
    )
    t_b1 = (row(t_fc1_bias), row(biases[: t_fc1_bias.shape[0]]))
    s_b1 = (row(s_fc1_bias), row(biases[t_fc1_bias.shape[0] :]))
    s_c0 = ctx[:near]
    s_c1 = core(ctx[near:])
    s_c2 = across(s_c0)
    s_w1 = core(s_out_late)
    s_w3 = core(s_w2)

    cols = t_qkv.shape[2]
    tk, tv = call(
        teacher_kv_kernel, "teacher_kv", (tokens // 512,),
        [
            pl.BlockSpec((512, t_width), lambda j, sc: (j, 0)), whole((1, t_width)), whole((1, t_width)),
            whole(t_qkv.shape), whole(t_qv_bias.shape),
        ],
        [pl.BlockSpec((512, 2 * cols), lambda j, sc: (j, 0)), pl.BlockSpec((cols, 512), lambda j, sc: (0, j))],
        [sds((tokens, 2 * cols), BF), sds((cols, tokens), BF)],
        (hbm(teacher_rows), row(t_norm1_gain), row(t_norm1_shift), hbm(t_qkv), t_qv_bias),
        flops=2 * tokens * t_width * 2 * cols, scalars=scalars, far=(0, 1),
    )
    tk, teacher_rows, s_c1, s_w1, s_w3, t_fc1_late, t_out_late = lax.optimization_barrier(
        (tk, teacher_rows, s_c1, s_w1, s_w3, t_fc1, t_out)
    )
    s_c3 = across(s_c1)
    t_f1 = (t_fc1, core(t_fc1_late))
    t_w1 = core(t_out_late)
    by_slot = lambda w: pl.BlockSpec((mp, nb, piece, w), lambda j, sc: (0, j, 0, 0))
    x_kept, tq = call(
        functools.partial(teacher_q_kernel, slots, block, span), "teacher_q", (steps,),
        [
            whole(teacher_in.shape), whole(rank.shape), whole((1, t_width)), whole((1, t_width)),
            whole(t_qkv.shape), whole(t_qv_bias.shape),
        ],
        [by_slot(t_width), by_slot(2 * cols)],
        [sds((mp, slots, piece, t_width), BF), sds((mp, slots, piece, 2 * cols), BF)],
        (hbm(teacher_rows), rank, row(t_norm1_gain), row(t_norm1_shift), hbm(t_qkv), t_qv_bias),
        scratch=[pltpu.VMEM((span, t_width), F32)],
        flops=2 * rows * t_width * (cols + 512), scalars=scalars,
    )
    def attend(name, p, query):
        half_slot = lambda w, lane: pl.BlockSpec((mp, slots // 2, piece, w), lambda j: (0, j, 0, lane))
        return call(
            teacher_attend_kernel, name, (2,),
            [
                half_slot(256, p), pl.BlockSpec((tokens, 256), lambda j: (0, p)),
                pl.BlockSpec((128, tokens), lambda j: (p, 0)),
            ],
            half_slot(128, 0),
            sds((mp, slots, piece, 128), BF),
            (query, tk, tv),
            flops=2 * rows * tokens * (512 + 256),
        ).reshape(rows, 128)

    t_ctx = []
    for p in range(cols // 128):
        mixed_pair = attend("teacher_attend%d" % p, p, tq)
        if p == 0:
            mixed_pair, tq, s_c2, s_c3 = lax.optimization_barrier((mixed_pair, tq, s_c2, s_c3))
        else:
            t_ctx[0], mixed_pair, t_f1, t_w1, t_fc2_late = lax.optimization_barrier(
                (t_ctx[0], mixed_pair, t_f1, t_w1, t_fc2)
            )
        t_ctx.append([mixed_pair, core(mixed_pair[near:]), across(mixed_pair)])
    t_f2 = (t_fc2, core(t_fc2_late))
    t_w3 = core(t_w2)

    s_send, s_own, sent, a2, act, slope = forward(
        "both", "student_forward", near, (s_c0, s_c1, s_c2, s_c3), (s_out, s_w1, s_w2, s_w3), x_stud,
        row(s_out_bias), row(s_norm2_gain), row(s_norm2_shift), s_f1, s_b1, s_f2, row(s_fc2_bias), s_fc1.shape[1],
    )
    s_send, t_ctx, t_f2, t_w3 = lax.optimization_barrier((s_send, t_ctx, t_f2, t_w3))
    t_ctx = [x for own, from_core, from_chip in t_ctx for x in (own, from_core, from_chip, core(from_chip[near:]))]
    s_recv = across(s_send)
    t_args = (
        t_ctx, (t_out, t_w1, t_w2, t_w3), x_kept.reshape(rows, t_width), row(t_out_bias),
        row(t_norm2_gain), row(t_norm2_shift), t_f1, t_b1, t_f2, row(t_fc2_bias),
    )
    t_send = forward("send", "teacher_forward_far", mine, *t_args, 512)
    s_recv, t_args, t_send = lax.optimization_barrier((s_recv, t_args, t_send))
    t_recv = across(t_send)
    out_rows = (s_own + s_recv.astype(F32)).astype(BF)

    owners = lax.dynamic_index_in_dim(block_owner, home, 0, keepdims=False)
    capacity = (slots + homes - 1) // homes
    labels = jnp.arange(homes, dtype=jnp.int32)
    hits = (owners[:, None] == labels[None, :]).astype(jnp.int32)
    earlier = (jnp.arange(slots)[:, None] > jnp.arange(slots)[None, :]).astype(jnp.int32)
    order_in = jnp.sum(earlier * (owners[:, None] == owners[None, :]).astype(jnp.int32), axis=1)
    spot = jnp.where(owners >= 0, owners * capacity + order_in, homes * capacity)
    spots = jnp.arange(homes * capacity, dtype=jnp.int32)
    leaving = jnp.sum(
        jnp.where(spots[:, None] == spot[None, :], jnp.arange(slots, dtype=jnp.int32)[None, :], 0), axis=1
    )
    per_source = jnp.sum((block_owner == home).astype(jnp.int32), axis=1)
    ahead = (labels[:, None] > labels[None, :]).astype(jnp.int32)
    before = jnp.sum(ahead * per_source[None, :], axis=1)
    lane = jnp.arange(capacity, dtype=jnp.int32)
    target_slot = jnp.where(lane[None, :] < per_source[:, None], before[:, None] + lane[None, :], OWN).reshape(-1)
    chosen = jnp.sum(
        jnp.where(jnp.arange(OWN, dtype=jnp.int32)[:, None] == target_slot[None, :], spots[None, :], 0), axis=1
    )

    bits = log2(homes)

    def partner(value, bit):
        return lax.ppermute(value, "dp", [(i, i ^ (1 << bit)) for i in range(homes)])

    entries, shift = homes * capacity, log2(capacity)
    entry_shape = (entries, piece, width)
    leaving_sc = jnp.concatenate([leaving, home[None].astype(jnp.int32)])
    home_sc = home[None].astype(jnp.int32)

    def spread(name, came, going, blocks, came_in, places):
        ins = [blocks] if came_in is None else [blocks, came_in]
        base = places.shape[0] - 1
        lift = lambda bit: None if bit is None else bit + shift
        if going is None:
            outs = [sds((OWN, piece, width), BF)]
            scratch = [pltpu.VMEM(entry_shape, BF)]
        else:
            outs = [sds(entry_shape, BF), sds((entries // 2, piece, width), BF)]
            scratch = []
        return call(
            functools.partial(spread_kernel, lift(came), lift(going), shift, base), name, (1,),
            [whole(x.shape) for x in ins], [whole(o.shape) for o in outs], outs, ins, scratch=scratch, scalars=places,
        )

    turns = [1, 0] + list(range(2, bits))
    kept, sending = spread("spread0", None, turns[0], out_rows.reshape(slots, piece, width), None, leaving_sc)
    t_args, kept = lax.optimization_barrier((t_args, kept))
    travel = partner(sending, turns[0])
    t_own = forward("own", "teacher_forward_own", mine, *t_args, 512)
    t_own, t_recv, travel = lax.optimization_barrier((t_own, t_recv, travel))
    kept, sending = spread("spread1", turns[0], turns[1], kept, travel, home_sc)
    t_own, kept = lax.optimization_barrier((t_own, kept))
    travel = partner(sending, turns[1])

    d_guess, d_out, loss_row, head_b_row, fc2_b_row = call(
        functools.partial(head_kernel, block, piece), "head", (1,),
        [
            whole((mine, t_width)), whole((mine, t_width)), whole((mine, width)), whole((width, t_width)),
            whole((1, t_width)), pl.BlockSpec(memory_space=pltpu.SMEM),
        ],
        [whole((mine, t_width)), whole((mine, width)), whole((1, t_width)), whole((1, t_width)), whole((1, width))],
        [sds((mine, t_width), BF), sds((mine, width), BF), sds((1, t_width), F32), sds((1, t_width), F32), sds((1, width), F32)],
        (t_own, t_recv, out_rows, hbm(head_weight), row(head_bias), inverse),
        flops=4 * mine * width * t_width, scalars=scalars,
    )
    d_out_far = across(d_out)

    half_cols, quarter = t_width // 2, t_width // 4
    head_keep, head_send = call(
        head_grad_kernel, "head_grad", (1,),
        [
            whole((mine, width)),
            pl.BlockSpec((mine, half_cols), lambda j, sc: (0, sc[ORD] & 1)),
            pl.BlockSpec((mine, half_cols), lambda j, sc: (0, 1 - (sc[ORD] & 1))),
        ],
        [whole((width, half_cols))] * 2,
        [sds((width, half_cols), F32), sds((width, half_cols), BF)],
        (out_rows, d_guess, d_guess), scalars=scalars,
    )
    head_recv = core(head_send)
    own_quarter = pl.BlockSpec((width, quarter), lambda j, sc: (0, sc[ORD] >> 1))
    far_quarter = pl.BlockSpec((width, quarter), lambda j, sc: (0, 1 - (sc[ORD] >> 1)))
    head_keep, head_send = call(
        head_add_kernel, "head_add", (1,),
        [own_quarter, own_quarter, far_quarter, far_quarter],
        [whole((width, quarter))] * 2,
        [sds((width, quarter), F32), sds((width, quarter), BF)],
        (head_keep, head_recv, head_keep, head_recv), scalars=scalars, far=(0,),
    )
    d_out_far, head_send, travel = lax.optimization_barrier((d_out_far, head_send, travel))
    for turn in range(2, bits):
        kept, sending = spread("spread%d" % turn, turns[turn - 1], turns[turn], kept, travel, home_sc)
        travel = partner(sending, turns[turn])
    head_recv = across(head_send)

    hidden = s_fc1.shape[1]
    cut = lambda i: pl.BlockSpec((near, hidden), lambda *_: (0, i))
    square, turned_square, line = whole((width, hidden)), whole((hidden, width)), whole((1, hidden))
    tall, short_rows = whole((near, width)), whole((mine, width))
    d_scratch = [pltpu.VMEM((near, width), BF)]
    g1_send, g2_send, b1_send, da2_part = call(
        feed_far_kernel, "feed_back_far", (1,),
        [short_rows, short_rows, cut(1), cut(1), tall, square, turned_square],
        [square, turned_square, line, tall],
        [sds((width, hidden), BF), sds((hidden, width), BF), sds((1, hidden), F32), sds((near, width), F32)],
        (d_out, d_out_far, *map(hbm, (act, slope, a2, s_f1[1], s_f2[1]))),
        scratch=d_scratch,
    )
    da2_part, g1_send, g2_send, head_recv = lax.optimization_barrier((da2_part, g1_send, g2_send, head_recv))
    g1_recv, g2_recv = core(g1_send), core(g2_send)
    dpre, b1_own, da2_own, da2_send = call(
        feed_own_kernel, "feed_back_own", (1,),
        [short_rows, short_rows, cut(0), square, turned_square, tall],
        [whole((near, hidden)), line, tall, tall],
        [sds((near, hidden), BF), sds((1, hidden), F32), sds((near, width), F32), sds((near, width), BF)],
        (d_out, d_out_far, *map(hbm, (slope, s_f1[0], s_f2[0])), da2_part),
        scratch=d_scratch,
    )
    g1_recv, g2_recv, dpre, da2_send = lax.optimization_barrier((g1_recv, g2_recv, dpre, da2_send))
    da2_far = across(da2_send)

    x_first = list(range(bits))
    z_first = x_first[1:] + x_first[:1]

    def go(name, *bundles):
        advance(name, bundles, partner, scalars)

    half = width // 2
    a_width = hidden + quarter
    keep_a, send_a, keep_b, send_b = call(
        functools.partial(feed_grad_kernel, x_first[0], z_first[0]), "feed_back_grad", (1,),
        [
            short_rows, short_rows, cut(0), tall, whole((near, hidden)), square, turned_square,
            whole((width, quarter)), whole((width, quarter)),
        ],
        [whole((half, a_width))] * 2 + [whole((half, width))] * 2,
        [sds((half, a_width), BF)] * 2 + [sds((half, width), BF)] * 2,
        (d_out, d_out_far, hbm(act), hbm(a2), dpre, g1_recv, g2_recv, head_keep, head_recv),
        scratch=d_scratch, scalars=scalars,
    )
    one = Bundle(x_first, keep_a, partner(send_a, x_first[0]), ((0, hidden, F32), (hidden, a_width, BF)))
    two = Bundle(z_first, keep_b, partner(send_b, z_first[0]), ((0, width, F32),))

    q_late, keep_a = lax.optimization_barrier((sq, keep_a))
    one.flight = (keep_a, one.flight[1])
    probs = call(
        functools.partial(student_probs_kernel, used), "student_probs", (heads, rows // near),
        [
            pl.BlockSpec((near, wide), lambda h, j: (j, 0)), whole((rows, wide)),
            pl.BlockSpec((8, near), lambda h, j: (0, j)),
        ],
        [pl.BlockSpec((1, rows, near), lambda h, j: (h, 0, j))],
        [sds((heads, rows, rows), BF)],
        (q_late, sk, logs),
        flops=heads * rows * rows * wide * 2, far=(0,),
    )[0]
    da2_far, travel, probs, one.flight, two.flight = lax.optimization_barrier(
        (da2_far, travel, probs, one.flight, two.flight)
    )
    d_sent, sums2 = norm_back(
        "norm2_back", da2_own, da2_far, (d_out, d_out_far), sent, row(s_norm2_gain), BF
    )
    d_core = core(d_sent)
    d_core, one.flight, two.flight = lax.optimization_barrier((d_core, one.flight, two.flight))
    ds = (d_sent, d_core)
    for extra in range(bits - 2):
        go("sum_b%d" % extra, one, two)

    def back(name, picked, with_out):
        size = HD * len(picked)
        outs = [sds((rows, 3 * size), BF), sds((2, size), F32)] + [sds((used, width), F32)] * with_out
        return call(
            functools.partial(student_back_kernel, used, picked, with_out), name, (2,),
            [tall] * 2
            + [
                whole((used, width)), by_lanes(used),
                pl.BlockSpec((len(picked), rows, near), lambda j: (picked[0] // len(picked), 0, j)), by_rows(wide),
                whole((rows, wide)), whole((used, rows)),
            ],
            [whole(o.shape) for o in outs], outs,
            (*ds, s_out, mixed, probs, sq, sv, skt),
            scratch=[pltpu.VMEM((near, width), BF), pltpu.VMEM((near, wide), F32)]
            + [pltpu.VMEM((rows, wide), F32)] * 2 + [pltpu.VMEM((1, size), F32)]
            + [pltpu.VMEM((used, width), F32)] * with_out,
            flops=len(picked) * rows * rows * wide * 7, limit=36 * 2**20,
        )

    def project(name, bit, d, more):
        size = d.shape[1] + sum(m.shape[0] for m in more)
        specs = [whole(d.shape), whole(a_stud.shape)] + [whole(m.shape) for m in more]
        keep, send = call(
            functools.partial(project_grad_kernel, bit, bool(more)), name, (1,), specs,
            [whole((size // 2, width))] * 2, [sds((size // 2, width), BF)] * 2,
            (d, a_stud, *more), scalars=scalars,
        )
        return keep, partner(send, bit)

    pair, odd = tuple(range(heads - 1)), (heads - 1,)
    d_pair, pair_sums = back("student_back_pair", pair, False)
    d_pair, one.flight, two.flight = lax.optimization_barrier((d_pair, one.flight, two.flight))
    chosen_sc = jnp.concatenate([chosen, home_sc])
    student_out = spread("spread_end", turns[-1], None, kept, travel, chosen_sc)[0]
    go("sum_c", one, two)
    whole_width = ((0, width, BF),)
    three = Bundle(x_first, *project("project_pair", x_first[0], d_pair, ()), whole_width)
    tied = lax.optimization_barrier((*ds, three.flight[0], d_pair))
    ds, d_pair = tied[:2], tied[3]
    three.flight = (tied[2], three.flight[1])
    d_odd, odd_sums, g_out = back("student_back_odd", odd, True)
    d_odd, one.flight, two.flight, three.flight = lax.optimization_barrier(
        (d_odd, one.flight, two.flight, three.flight)
    )
    go("sum_d", one, two, three)
    four = Bundle(x_first, *project("project_odd", x_first[0], d_odd, (g_out,)), whole_width)
    mixed_size = HD * (heads - 1)
    w_pair = w_turn[:, :mixed_size].reshape(3 * mixed_size, width)
    w_odd = w_turn[:, mixed_size:].reshape(3 * HD, width)
    at = lambda w: pl.BlockSpec((near, w), lambda j: (1 - j, 0))
    da1_near, da1_send = call(
        input_grad_kernel, "input_grad", (2,),
        [at(3 * mixed_size), at(3 * HD), whole(w_pair.shape), whole(w_odd.shape)],
        [tall, tall], [sds((near, width), F32), sds((near, width), BF)],
        (d_pair, d_odd, w_pair, w_odd),
    )
    da1_recv = core(da1_send)
    da1_own = da1_near[:mine] + da1_recv[:mine].astype(F32)
    da1_far = across((da1_near[mine:] + da1_recv[mine:].astype(F32)).astype(BF))
    go("sum_e", one, two, three, four)
    for extra in range(bits - 3):
        go("sum_f%d" % extra, one, two, three, four)
    short_in = (sums2, fc2_b_row, head_b_row, loss_row, b1_send, b1_own, pair_sums, odd_sums)
    short_early = call(
        short_kernel, "short", (1,), [whole(v.shape) for v in short_in],
        [whole((16, width))] * 2, [sds((16, width), F32)] * 2, short_in,
    )
    grad_in, sums1 = norm_back("norm1_back", da1_own, da1_far, (d_sent,), x_stud, row(s_norm1_gain), F32)

    def tie(held, *bundles):
        kept, held = lax.optimization_barrier(([b.flight[0] for b in bundles], held))
        for b, first in zip(bundles, kept):
            b.flight = (first, b.flight[1])
        return held

    norm_rows = jnp.concatenate([sums1[:2], jnp.zeros((14, width), F32)], axis=0)
    vec = short_early[0] + norm_rows + core(short_early[1] + norm_rows)
    home_rows = (jnp.arange(16) < 9)[:, None]
    vec = tie(vec, three)
    go("sum_g", one, two, three, four)
    vec = jnp.where(home_rows, vec + across(vec), vec)
    turn = 0
    while three.result is None or four.result is None or one.result is None:
        left = [b for b in (three, four) if b.result is None]
        if turn <= bits and left:
            vec = tie(vec, left[0])
        if turn < bits:
            moved_vec = partner(vec, turn)
        go("sum_h%d" % turn, *left)
        if turn % 2 and one.result is None:
            flying = [b for b in left if b.result is None]
            if flying:
                tie(flying[0].flight[0], one, two)
            go("sum_last%d" % turn, one, two)
        if turn < bits:
            vec = vec + moved_vec
        turn += 1
    for bit in range(turn, bits):
        vec = vec + partner(vec, bit)

    g1_all, head_all = one.result
    head_cross, head_core = across(head_all), core(head_all)
    piece_spec = whole((width, quarter))
    grad_head = call(
        place_kernel, "place_head", (mp,), [piece_spec] * 4,
        pl.BlockSpec((width, quarter), lambda k, sc: (0, 2 * (sc[ORD + k] & 1) + (sc[ORD + k] >> 1))),
        sds((width, t_width), F32),
        (head_all, head_cross, head_core, core(head_cross)), scalars=scalars,
    )
    low_pair, low_odd = three.result[0], four.result[0]
    qkv_turned = jnp.concatenate(
        [low_pair.reshape(3, mixed_size, width), low_odd[: 3 * HD].reshape(3, HD, width)], axis=1
    )
    return (
        jnp.sum(vec[8]),
        student_out,
        grad_in.reshape(slots, piece, width),
        vec[0],
        vec[1],
        jnp.transpose(qkv_turned, (0, 2, 1)).astype(F32),
        vec[10:12, :used],
        low_odd[3 * HD :].astype(F32),
        vec[4],
        vec[2],
        vec[3],
        g1_all,
        vec[9],
        two.result[0],
        vec[5],
        grad_head,
        jnp.concatenate([vec[6], vec[7, : t_width - width]]),
    )


def solution(mesh):
    rep = P()
    in_specs = (
        P("dp", None), rep, rep, rep, P("dp", None, None), rep, rep, P(None, None, "mp"), P(None, "mp"),
        P("mp", None), rep, rep, rep, P(None, "mp"), P("mp"), P("mp", None), rep, rep, rep,
        P(None, None, "mp"), P(None, "mp"), P("mp", None), rep, rep, rep, P(None, "mp"), P("mp"),
        P("mp", None), rep, rep, rep,
    )
    out_specs = (
        rep, P("dp", "mp", None), P("dp", "mp", None), rep, rep, P(None, None, "mp"), P(None, "mp"),
        P("mp", None), rep, rep, rep, P(None, "mp"), P("mp"), P("mp", None), rep, rep, rep,
    )
    return jax.shard_map(body, mesh=mesh, in_specs=in_specs, out_specs=out_specs, check_vma=False)
```

```python
import functools

import jax
import jax.numpy as jnp
from jax import lax
from jax.experimental import pallas as pl
from jax.experimental.pallas import tpu as pltpu
from jax.sharding import PartitionSpec as P

HD = 64
OWN = 8
CLIPS = 8
EPS = 1e-05
BIG = -1e30
F32 = jnp.float32
BF = jnp.bfloat16
LIMIT = 24 * 2**20
COST = 4

ORD, CUM, END, HOME, LOW = 0, 4, 12, 20, 21


def dot_nn(a, b):
    return lax.dot_general(a, b, (((1,), (0,)), ((), ())), preferred_element_type=F32)


def dot_nt(a, b):
    return lax.dot_general(a, b, (((1,), (1,)), ((), ())), preferred_element_type=F32)


def dot_tn(a, b):
    return lax.dot_general(a, b, (((0,), (0,)), ((), ())), preferred_element_type=F32)


def unit(values):
    mean = jnp.mean(values, axis=-1, keepdims=True)
    centred = values - mean
    spread = jnp.mean(centred * centred, axis=-1, keepdims=True)
    inverse = lax.rsqrt(spread + EPS)
    return centred * inverse, inverse


def norm_low(values, gain_ref, shift_ref):
    u, _ = unit(values)
    return (u * gain_ref[...].astype(F32) + shift_ref[...].astype(F32)).astype(BF)


def log2(size):
    return size.bit_length() - 1


def whole(shape):
    return pl.BlockSpec(shape, lambda *_: (0,) * len(shape))


def call(kernel, name, grid, in_specs, out_specs, out_shape, args, scratch=(), flops=0, scalars=None, limit=LIMIT, far=()):
    moved = sum(a.size * a.dtype.itemsize for a in args)
    moved += sum(s.size * jnp.dtype(s.dtype).itemsize for s in jax.tree.leaves(out_shape))
    if far:
        if isinstance(out_shape, list):
            out_shape = [pltpu.HBM(o.shape, o.dtype) if i in far else o for i, o in enumerate(out_shape)]
        else:
            out_shape = pltpu.HBM(out_shape.shape, out_shape.dtype)
    params = pltpu.CompilerParams(
        dimension_semantics=("arbitrary",) * len(grid), vmem_limit_bytes=limit
    )
    cost = pl.CostEstimate(flops=int(flops) // COST, bytes_accessed=int(moved) // COST, transcendentals=0)
    lead = 0 if scalars is None else 1
    spec = pltpu.PrefetchScalarGridSpec(
        num_scalar_prefetch=lead,
        grid=grid,
        in_specs=in_specs,
        out_specs=out_specs,
        scratch_shapes=list(scratch),
    )
    run = pl.pallas_call(
        kernel,
        grid_spec=spec,
        out_shape=out_shape,
        compiler_params=params,
        cost_estimate=cost,
        name=name,
    )
    return run(*([scalars] if lead else []), *args)


def sds(shape, dtype):
    return jax.ShapeDtypeStruct(shape, dtype)


def group_of(index, sc, base):
    group = jnp.zeros(index.shape, jnp.int32)
    for c in range(CLIPS):
        group = group + (index >= sc[base + c]).astype(jnp.int32)
    return group


def teacher_kv_kernel(sc, x_ref, g_ref, s_ref, w_ref, b_ref, k_ref, v_ref):
    rows = x_ref.shape[0]
    a = norm_low(x_ref[...].astype(F32), g_ref, s_ref)
    token = pl.program_id(0) * rows + lax.broadcasted_iota(jnp.int32, (rows, 1), 0)
    lane = lax.broadcasted_iota(jnp.int32, (rows, 128), 1)
    hot = jnp.where(lane == group_of(token, sc, END), 1.0, 0.0).astype(BF)
    k = (dot_nn(a, w_ref[1]).astype(BF).astype(F32) * (HD**-0.5)).astype(BF)
    for p in range(k.shape[1] // 128):
        k_ref[:, 256 * p : 256 * p + 128] = k[:, 128 * p : 128 * (p + 1)]
        k_ref[:, 256 * p + 128 : 256 * (p + 1)] = hot
    v_ref[...] = (dot_nn(a, w_ref[2]) + b_ref[1:2, :].astype(F32)).T.astype(BF)


def teacher_q_kernel(slots, block, step, sc, x_ref, rank_ref, g_ref, s_ref, w_ref, b_ref, xk_ref, q_ref, acc):
    j = pl.program_id(0)
    pieces, nb, piece, width = xk_ref.shape
    rows = pieces * nb * piece

    line = lax.broadcasted_iota(jnp.int32, (rows, 1), 0)
    part = line >> log2(nb * piece)
    inner = line & (nb * piece - 1)
    order = jnp.zeros((rows, 1), jnp.int32)
    for p in range(pieces):
        order = jnp.where(part == p, sc[ORD + p], order)
    slot = (j * nb + (inner >> log2(piece))) * block + order * piece + (inner & (piece - 1))
    group = group_of(slot, sc, CUM)
    acc[...] = jnp.zeros_like(acc)

    def one(t, _):
        hit = jnp.where(slot == rank_ref[pl.ds(t, 1), :], 1.0, 0.0).astype(BF)
        acc[...] += dot_nn(hit, x_ref[pl.ds(pl.multiple_of(t * step, step), step), :])
        return 0

    steps = slots // nb
    lax.fori_loop(sc[LOW + j], sc[LOW + steps + j], one, 0)
    kept = acc[...]
    xk_ref[...] = kept.astype(BF).reshape(xk_ref.shape)
    a = norm_low(kept, g_ref, s_ref)
    q = (dot_nn(a, w_ref[0]) + b_ref[0:1, :].astype(F32)).astype(BF)
    lane = lax.broadcasted_iota(jnp.int32, (rows, 128), 1)
    other = (lane != group) & (lane <= CLIPS)
    mask = jnp.where(other, BIG, 0.0).astype(BF)
    pairs = q.shape[1] // 128
    out = []
    for p in range(pairs):
        out += [q[:, 128 * p : 128 * (p + 1)], mask]
    q_ref[...] = jnp.concatenate(out, axis=1).reshape(q_ref.shape)


def softmax_mix(keys, query, values):
    scores = dot_nt(keys, query)
    top = jnp.max(scores, axis=0, keepdims=True)
    e = jnp.exp(scores - top)
    mass = jnp.sum(e, axis=0, keepdims=True)
    return dot_nn(values, e.astype(BF)) * (1.0 / mass), top + jnp.log(mass)


def teacher_attend_kernel(q_ref, k_ref, v_ref, ctx_ref):
    pieces, nb, piece, both = q_ref.shape
    rows = pieces * nb * piece
    part = q_ref[...].reshape(rows, both).astype(F32)
    lane = lax.broadcasted_iota(jnp.int32, (rows, both), 1)
    mixed = []
    for h in range(2):
        query = jnp.where(((lane >> 6) == h) | (lane >= 128), part, 0.0).astype(BF)
        mixed.append(softmax_mix(k_ref[...], query, v_ref[HD * h : HD * (h + 1), :])[0])
    ctx_ref[...] = jnp.concatenate(mixed, axis=0).T.astype(BF).reshape(ctx_ref.shape)


def student_qkv_kernel(block, sc, x_ref, g_ref, s_ref, w_ref, b_ref, xo_ref, a_ref, q_ref, k_ref, v_ref, kt_ref, vt_ref):
    slots, _, piece, width = x_ref.shape
    rows = slots * piece
    used, wide = w_ref.shape[1], q_ref.shape[1]
    x = x_ref[...].reshape(rows, width)
    xo_ref[...] = x
    a = norm_low(x.astype(F32), g_ref, s_ref)
    a_ref[...] = a
    line = lax.broadcasted_iota(jnp.int32, (rows, 1), 0)
    lane = lax.broadcasted_iota(jnp.int32, (rows, wide - used), 1)
    slot = (line >> log2(piece)) * block + sc[ORD + pl.program_id(0)] * piece + (line & (piece - 1))
    same = lane == group_of(slot, sc, CUM)
    q_ref[:, :used] = (dot_nt(a, w_ref[0]) + b_ref[0:1, :].astype(F32)).astype(BF)
    q_ref[:, used:] = jnp.where(same | (lane > CLIPS), 0.0, BIG).astype(BF)
    k = dot_nt(a, w_ref[1]).astype(BF).astype(F32) * (HD**-0.5)
    k_ref[:, :used] = k.astype(BF)
    k_ref[:, used:] = jnp.where(same, 1.0, 0.0).astype(BF)
    kt_ref[...] = k.T.astype(BF)
    v = dot_nt(a, w_ref[2]) + b_ref[1:2, :].astype(F32)
    v_ref[:, :used] = v.astype(BF)
    v_ref[:, used:] = jnp.zeros((rows, wide - used), BF)
    vt_ref[...] = v.T.astype(BF)


def student_attend_kernel(used, q_ref, k_ref, vt_ref, ctx_ref, mixed_ref, log_ref):
    q = q_ref[...].astype(F32)
    rows, wide = q.shape
    lane = lax.broadcasted_iota(jnp.int32, (rows, wide), 1)
    mixed, logs = [], []
    for h in range(used // HD):
        query = jnp.where(((lane >> 6) == h) | (lane >= used), q, 0.0).astype(BF)
        part, log = softmax_mix(k_ref[...], query, vt_ref[HD * h : HD * (h + 1), :])
        mixed.append(part)
        logs.append(log)
    total = jnp.concatenate(mixed, axis=0)
    mixed_ref[...] = total
    ctx_ref[...] = total.T.astype(BF)
    log_ref[...] = jnp.concatenate(logs + [jnp.zeros((8 - len(logs), rows), F32)], axis=0)


def student_probs_kernel(used, q_ref, k_ref, log_ref, out_ref):
    rows, wide = q_ref.shape
    lane = lax.broadcasted_iota(jnp.int32, (rows, wide), 1)
    h = pl.program_id(0)
    query = jnp.where(((lane >> 6) == h) | (lane >= used), q_ref[...].astype(F32), 0.0).astype(BF)
    out_ref[0] = jnp.exp(dot_nt(k_ref[...], query) - log_ref[pl.ds(h, 1), :]).astype(BF)


def student_back_kernel(used, picked, with_out, p0, p1, w_ref, mixed_ref, probs_ref, q_ref, v_ref, kt_ref, *rest):
    if with_out:
        out_ref, sums_ref, w_grad_ref, ds, da, dk, dv, dqs, dw = rest
    else:
        out_ref, sums_ref, ds, da, dk, dv, dqs = rest
    j = pl.program_id(0)
    steps = pl.num_programs(0)
    lo, size = HD * picked[0], HD * len(picked)
    rows, wide = q_ref.shape

    @pl.when(j == 0)
    def _():
        dk[...] = jnp.zeros_like(dk)
        dv[...] = jnp.zeros_like(dv)
        dqs[...] = jnp.zeros_like(dqs)
        ds[...] = p0[...]
        if with_out:
            dw[...] = jnp.zeros_like(dw)

    @pl.when(j == 1)
    def _():
        ds[...] = p1[...]

    grad = ds[...]
    da[:, :used] = dot_nt(grad, w_ref[...])
    da[:, used:] = jnp.zeros((rows, wide - used), F32)
    low = da[...].astype(BF).astype(F32)
    mixed = mixed_ref[...]
    turned = dot_nt(w_ref[lo : lo + size, :], grad).astype(BF).astype(F32)
    product = turned * mixed[lo : lo + size, :]
    if with_out:
        dw[...] += dot_nn(mixed.astype(BF), grad)
    lane = lax.broadcasted_iota(jnp.int32, (rows, wide), 1)
    q = q_ref[...].astype(F32)
    grads_q = []
    for i, h in enumerate(picked):
        mine = (lane >> 6) == h
        query = jnp.where(mine | (lane >= used), q, 0.0).astype(BF)
        outer = jnp.where(mine, low, 0.0).astype(BF)
        delta = jnp.sum(product[HD * i : HD * (i + 1), :], axis=0, keepdims=True)
        pt = probs_ref[i]
        dst = (pt.astype(F32) * (dot_nt(v_ref[...], outer) - delta)).astype(BF)
        dv[...] += dot_nn(pt, outer)
        dk[...] += dot_nn(dst, query)
        grads_q.append(dot_nn(kt_ref[HD * h : HD * (h + 1), :], dst))
    dq = jnp.concatenate(grads_q, axis=0).T.astype(BF)
    out_ref[pl.ds(pl.multiple_of(j * rows, rows), rows), 0:size] = dq
    dqs[...] += jnp.sum(dq.astype(F32), axis=0, keepdims=True)

    @pl.when(j == steps - 1)
    def _():
        out_ref[:, size : 2 * size] = (dk[:, lo : lo + size] * (HD**-0.5)).astype(BF)
        dv_low = dv[:, lo : lo + size].astype(BF)
        out_ref[:, 2 * size : 3 * size] = dv_low
        sums_ref[...] = jnp.concatenate(
            [dqs[...], jnp.sum(dv_low.astype(F32), axis=0, keepdims=True)], axis=0
        )
        if with_out:
            w_grad_ref[...] = dw[...]


def gelu_both(pre):
    phi = 0.5 * (1.0 + lax.erf(pre * 0.7071067811865476))
    return pre * phi, phi + pre * (0.3989422804014327 * jnp.exp(-0.5 * pre * pre))


def flipped(ref):
    half = ref.shape[0] // 2
    return jnp.concatenate([ref[half:], ref[:half]], axis=0)


def forward_kernel(
    mode, half_steps,
    *refs,
):
    both = mode == "both"
    count = 4 if both else 8
    ctx, (w0, w1, w2, w3, x_ref, ob_ref, g_ref, s_ref), refs = refs[:count], refs[count : count + 8], refs[count + 8 :]
    (f1a, f1b, b1a, b1b, f2a, f2b, b2_ref), rest = refs[:7], refs[7:]
    if both:
        send_ref, own_ref, sent_ref, a2_ref, act_ref, slope_ref, a2, acc, base = rest
    elif mode == "own":
        own_ref, a2, acc, base = rest
    else:
        send_ref, a2, acc = rest
    j = pl.program_id(0)
    rows = x_ref.shape[0]

    @pl.when(j == 0)
    def _():
        if both:
            found = [ctx[0][...], ctx[1][...], flipped(ctx[2]), flipped(ctx[3])]
        else:
            found = [jnp.concatenate([ctx[i][...], ctx[4 + i][...]], axis=1) for i in range(4)]
        parts = [dot_nn(c, w[...]) for c, w in zip(found, (w0, w1, w2, w3))]
        if not both:
            parts = [p.astype(BF).astype(F32) for p in parts]
        resid = x_ref[...].astype(F32) + (parts[0] + parts[1] + parts[2] + parts[3])
        resid = resid + ob_ref[...].astype(F32)
        if both:
            low = resid.astype(BF)
            sent_ref[...] = low
            resid = low.astype(F32)
        a2[...] = norm_low(resid, g_ref, s_ref)
        if both:
            a2_ref[...] = a2[...]
            base[...] = resid[: rows // 2] + b2_ref[...].astype(F32)
        elif mode == "own":
            base[...] = resid + b2_ref[...].astype(F32)
        acc[...] = jnp.zeros_like(acc)

    def half(f1, b1, f2):
        pre = dot_nn(a2[...], f1[...]) + b1[...].astype(F32)
        if both:
            act, slope = gelu_both(pre)
            slope_ref[...] = slope.astype(BF)
        else:
            act = pre * (0.5 * (1.0 + lax.erf(pre * 0.7071067811865476)))
        act = act.astype(BF)
        if both:
            act_ref[...] = act
        acc[...] += dot_nn(act, f2[...])

    @pl.when(j < half_steps)
    def _():
        half(f1a, b1a, f2a)

    @pl.when(j >= half_steps)
    def _():
        half(f1b, b1b, f2b)

    @pl.when(j == 2 * half_steps - 1)
    def _():
        if both:
            own_ref[...] = acc[: rows // 2] + base[...]
            send_ref[...] = acc[rows // 2 :].astype(BF)
        elif mode == "own":
            own_ref[...] = acc[...] + base[...]
        else:
            send_ref[...] = acc[...].astype(BF)


def forward(mode, name, rows, ctx, w_out, x, out_b, gain, shift, f1, b1, f2, b2, chunk):
    width = x.shape[1]
    heads_wide, hidden = w_out[0].shape[0], f1[0].shape[1]
    n = hidden // chunk
    both = mode == "both"
    near_at = 1 if mode == "send" else 0
    far_at = 1 if mode == "own" else 0
    first = lambda j: jnp.minimum(j, n - 1)
    second = lambda j: jnp.maximum(j - n, 0)
    at = lambda i, w: pl.BlockSpec((rows, w), lambda j: (i, 0))
    c_wide = ctx[0].shape[1]
    specs = ([at(near_at, c_wide)] * 2 + [at(far_at, c_wide)] * 2) * (len(ctx) // 4)
    specs += [whole(w.shape) for w in w_out]
    specs += [at(near_at, width)] + [whole((1, width))] * 3
    specs += [pl.BlockSpec((width, chunk), lambda j, f=f: (0, f(j))) for f in (first, second)]
    specs += [pl.BlockSpec((1, chunk), lambda j, f=f: (0, f(j))) for f in (first, second)]
    specs += [pl.BlockSpec((chunk, width), lambda j, f=f: (f(j), 0)) for f in (first, second)]
    specs += [whole((1, width))]
    half = rows // 2
    scratch = [pltpu.VMEM((rows, width), BF), pltpu.VMEM((rows, width), F32)]
    if both:
        outs = [sds((half, width), BF), sds((half, width), F32)] + [sds((rows, width), BF)] * 2
        outs += [sds((rows, 2 * hidden), BF)] * 2
        out_specs = [whole((half, width))] * 2 + [whole((rows, width))] * 2
        out_specs += [pl.BlockSpec((rows, chunk), lambda j: (0, j))] * 2
        scratch += [pltpu.VMEM((half, width), F32)]
    elif mode == "own":
        outs, out_specs = sds((rows, width), F32), whole((rows, width))
        scratch += [pltpu.VMEM((rows, width), F32)]
    else:
        outs, out_specs = sds((rows, width), BF), whole((rows, width))
    return call(
        functools.partial(forward_kernel, mode, n), name, (2 * n,), specs, out_specs, outs,
        (*ctx, *w_out, x, out_b, gain, shift, *f1, *b1, *f2, b2),
        scratch=scratch,
        flops=2 * rows * width * (4 * heads_wide + 4 * hidden), far=(2, 3, 4, 5) if both else (0,) if mode == "own" else (),
    )


def head_kernel(block, piece, sc, own_ref, recv_ref, out_ref, w_ref, b_ref, inv_ref, dg_ref, do_ref, loss_ref, hb_ref, ob_ref):
    rows, width = own_ref.shape
    target = (own_ref[...] + recv_ref[...].astype(F32)).astype(BF).astype(F32)
    line = lax.broadcasted_iota(jnp.int32, (rows, 1), 0)
    slot = (line >> log2(piece)) * block + sc[ORD] * piece + (line & (piece - 1))
    live = slot < sc[CUM + CLIPS - 1]
    group = group_of(slot, sc, CUM)
    weight = jnp.zeros((rows, 1), F32)
    for c in range(CLIPS):
        weight = jnp.where(group == c, inv_ref[0, c], weight)
    weight = jnp.where(live, weight, 0.0)
    target = jnp.where(live, target, 0.0)
    miss = dot_nn(out_ref[...], w_ref[...]) + b_ref[...].astype(F32) - target
    dg = (weight * miss).astype(BF)
    dg_ref[...] = dg
    loss_ref[...] = 0.5 * jnp.sum(weight * miss * miss, axis=0, keepdims=True)
    hb_ref[...] = jnp.sum(dg.astype(F32), axis=0, keepdims=True)
    do = dot_nt(dg, w_ref[...]).astype(BF)
    do_ref[...] = do
    ob_ref[...] = jnp.sum(do.astype(F32), axis=0, keepdims=True)


def head_grad_kernel(sc, out_ref, own_ref, other_ref, keep_ref, send_ref):
    keep_ref[...] = dot_tn(out_ref[...], own_ref[...])
    send_ref[...] = dot_tn(out_ref[...], other_ref[...]).astype(BF)


def head_add_kernel(sc, keep_a, recv_a, keep_b, recv_b, keep_ref, send_ref):
    keep_ref[...] = keep_a[...] + recv_a[...].astype(F32)
    send_ref[...] = (keep_b[...] + recv_b[...].astype(F32)).astype(BF)


def feed_far_kernel(d0, d1, act_ref, slope_ref, a2_ref, f1, f2, g1_ref, g2_ref, gb_ref, acc_ref, d):
    half = d0.shape[0]
    d[:half] = d0[...]
    d[half:] = d1[...]
    grad = d[...]
    dpre = (dot_nt(grad, f2[...]) * slope_ref[...].astype(F32)).astype(BF)
    gb_ref[...] = jnp.sum(dpre.astype(F32), axis=0, keepdims=True)
    acc_ref[...] = dot_nt(dpre, f1[...])
    g2_ref[...] = dot_tn(act_ref[...], grad).astype(BF)
    g1_ref[...] = dot_tn(a2_ref[...], dpre).astype(BF)


def feed_own_kernel(d0, d1, slope_ref, f1, f2, before, dpre_ref, gb_ref, own_ref, send_ref, d):
    half = d0.shape[0]
    d[:half] = d0[...]
    d[half:] = d1[...]
    dpre = (dot_nt(d[...], f2[...]) * slope_ref[...].astype(F32)).astype(BF)
    dpre_ref[...] = dpre
    gb_ref[...] = jnp.sum(dpre.astype(F32), axis=0, keepdims=True)
    part = dot_nt(dpre, f1[...]) + before[...]
    own_ref[...] = part
    send_ref[:half] = part[half:].astype(BF)
    send_ref[half:] = part[:half].astype(BF)


def keep_and_send(value, mark, keep_ref, send_ref):
    half = value.shape[0] // 2
    top, bottom = value[:half], value[half:]
    first = mark == 0
    keep_ref[...] = jnp.where(first, top, bottom).astype(keep_ref.dtype)
    send_ref[...] = jnp.where(first, bottom, top).astype(send_ref.dtype)


def feed_grad_kernel(bit_a, bit_b, sc, d0, d1, act_ref, a2_ref, dpre_ref, r1, r2, hk, hr,
                     keep_a, send_a, keep_b, send_b, d):
    half = d0.shape[0]
    d[:half] = d0[...]
    d[half:] = d1[...]
    g1 = dot_tn(a2_ref[...], dpre_ref[...]) + r1[...].astype(F32)
    head = hk[...] + hr[...].astype(F32)
    keep_and_send(jnp.concatenate([g1, head], axis=1), (sc[HOME] >> bit_a) & 1, keep_a, send_a)
    g2 = dot_tn(act_ref[...], d[...]) + r2[...].astype(F32)
    keep_and_send(g2, (sc[HOME] >> bit_b) & 1, keep_b, send_b)


def project_grad_kernel(bit, more, sc, d_ref, a_ref, *rest):
    value = dot_tn(d_ref[...], a_ref[...])
    if more:
        value = jnp.concatenate([value, rest[0][...]], axis=0)
    keep_and_send(value, (sc[HOME] >> bit) & 1, rest[-2], rest[-1])


def short_kernel(sums_ref, fc2_ref, hb_ref, loss_ref, b1s_ref, b1_ref, *rest):
    own_ref, send_ref = rest[-2:]
    width = own_ref.shape[1]
    for out in (own_ref, send_ref):
        out[...] = jnp.zeros(out.shape, F32)
        out[2:5, :] = sums_ref[...]
        out[5:6, :] = fc2_ref[...]
        out[6:7, :] = hb_ref[:, :width]
        left = hb_ref.shape[1] - width
        out[7:8, :left] = hb_ref[:, width:]
        loss = loss_ref[:, :left]
        for i in range(1, loss_ref.shape[1] // left):
            loss += loss_ref[:, left * i : left * (i + 1)]
        out[8:9, :left] = loss
    own_ref[9:10, :] = b1_ref[...]
    send_ref[9:10, :] = b1s_ref[...]
    at = 0
    for ref in rest[:-2]:
        own_ref[10:12, at : at + ref.shape[1]] = ref[...]
        at += ref.shape[1]


def input_grad_kernel(da_ref, db_ref, wa_ref, wb_ref, near_ref, send_ref):
    value = dot_nn(da_ref[...], wa_ref[...]) + dot_nn(db_ref[...], wb_ref[...])

    @pl.when(pl.program_id(0) == 0)
    def _():
        send_ref[...] = value.astype(BF)

    @pl.when(pl.program_id(0) == 1)
    def _():
        near_ref[...] = value


def stage_kernel(ops, sc, *refs):
    ins, outs = refs[: 2 * len(ops)], refs[2 * len(ops) :]
    at = 0
    for i, (kind, bit, parts) in enumerate(ops):
        a, b = ins[2 * i][...].astype(F32), ins[2 * i + 1][...].astype(F32)
        mark = (sc[HOME] >> bit) & 1
        if kind == "split":
            keep_and_send(a + b, mark, outs[at], outs[at + 1])
            at += 2
        elif kind == "add":
            outs[at][...] = (a + b).astype(BF)
            at += 1
        else:
            rows = a.shape[0]
            for lo, hi, dtype in parts:
                outs[at][:rows] = jnp.where(mark == 0, a[:, lo:hi], b[:, lo:hi]).astype(dtype)
                outs[at][rows:] = jnp.where(mark == 0, b[:, lo:hi], a[:, lo:hi]).astype(dtype)
                at += 1


def stage(name, ops, pairs, scalars):
    shapes = []
    for (kind, bit, parts), (a, b) in zip(ops, pairs):
        rows, width = a.shape
        if kind == "split":
            shapes.append([sds((rows // 2, width), BF)] * 2)
        elif kind == "add":
            shapes.append([sds((rows, width), BF)])
        else:
            shapes.append([sds((2 * rows, hi - lo), dtype) for lo, hi, dtype in parts])
    sizes = [a.shape[0] for a, _ in pairs] + [s.shape[0] for group in shapes for s in group]
    if all(size % 16 == 0 for size in sizes):
        flat = [x for pair in pairs for x in pair]
        outs = [s for group in shapes for s in group]
        found = call(
            functools.partial(stage_kernel, ops), name, (1,), [whole(x.shape) for x in flat],
            [whole(s.shape) for s in outs], outs, flat, scalars=scalars,
        )
    else:
        found = []
        for (kind, bit, parts), (a, b) in zip(ops, pairs):
            first = ((scalars[HOME] >> bit) & 1) == 0
            if kind == "join":
                for lo, hi, dtype in parts:
                    a1, b1 = a[:, lo:hi].astype(dtype), b[:, lo:hi].astype(dtype)
                    found.append(
                        jnp.where(first, jnp.concatenate([a1, b1], 0), jnp.concatenate([b1, a1], 0))
                    )
                continue
            total = (a.astype(F32) + b.astype(F32)).astype(BF)
            if kind == "add":
                found.append(total)
            else:
                half = total.shape[0] // 2
                found.append(jnp.where(first, total[:half], total[half:]))
                found.append(jnp.where(first, total[half:], total[:half]))
    result, at = [], 0
    for group in shapes:
        result.append(found[at : at + len(group)])
        at += len(group)
    return result


class Bundle:
    def __init__(self, bits, keep, recv, parts):
        self.bits, self.step, self.phase, self.parts = bits, 0, "split", parts
        self.flight = (keep, recv)
        self.result = None

    def op(self):
        if self.phase == "split":
            last = self.step == len(self.bits) - 1
            return ("add", 0, None) if last else ("split", self.bits[self.step + 1], None)
        width = self.flight[0].shape[1]
        parts = self.parts if self.step == 0 else ((0, width, BF),)
        return ("join", self.bits[self.step], parts)


def advance(name, bundles, partner, scalars):
    ops = [b.op() for b in bundles]
    done = stage(name, ops, [b.flight for b in bundles], scalars)
    for b, (kind, bit, _), got in zip(bundles, ops, done):
        if kind == "split":
            b.step += 1
            b.flight = (got[0], partner(got[1], bit))
        elif kind == "add":
            b.phase = "join"
            b.flight = (got[0], partner(got[0], b.bits[b.step]))
        elif b.step == 0:
            b.flight, b.result = None, got
        else:
            b.step -= 1
            b.flight = (got[0], partner(got[0], b.bits[b.step]))


def spread_kernel(came, going, shift, base, sc, in_ref, *refs):
    refs = list(refs)
    recv_ref = None if came is None else refs.pop(0)
    n = refs[0].shape[0] if going is not None else in_ref.shape[0]
    bit_in = 0 if came is None else (sc[base] >> (came - shift)) & 1

    def entry(i):
        if came is None:
            return in_ref[sc[i]]
        side = (i & ((1 << came) - 1)) | ((i >> (came + 1)) << came)
        return jnp.where(((i >> came) & 1) == bit_in, in_ref[i], recv_ref[side])

    if going is None:
        kept_ref, out_ref = refs[1], refs[0]
        for i in range(n):
            kept_ref[i] = entry(i)
        for i in range(out_ref.shape[0]):
            out_ref[i] = kept_ref[sc[i]]
        return
    keep_ref, send_ref = refs
    bit_out = (sc[base] >> (going - shift)) & 1
    for i in range(n):
        keep_ref[i] = entry(i)
    for j in range(send_ref.shape[0]):
        low = (j & ((1 << going) - 1)) | ((j >> going) << (going + 1))
        send_ref[j] = jnp.where(bit_out == 0, keep_ref[low | (1 << going)], keep_ref[low])


def place_kernel(sc, h0, h1, h2, h3, out_ref):
    for i, ref in enumerate((h0, h1, h2, h3)):

        @pl.when(pl.program_id(0) == i)
        def _(ref=ref):
            out_ref[...] = ref[...].astype(F32)


def norm_back_kernel(count, own_ref, recv_ref, *rest):
    base_refs, (x_ref, g_ref, dx_ref, sums_ref) = rest[:count], rest[count:]
    rows = own_ref.shape[0]
    mine = rows // count
    d = own_ref[...].astype(F32) + recv_ref[...].astype(F32)
    u, inverse = unit(x_ref[...].astype(F32))
    e = g_ref[...].astype(F32) * d
    mean_e = jnp.mean(e, axis=-1, keepdims=True)
    mean_eu = jnp.mean(e * u, axis=-1, keepdims=True)
    change = (e - mean_e - u * mean_eu) * inverse
    for i, base in enumerate(base_refs):
        at = slice(mine * i, mine * (i + 1))
        dx_ref[at] = (base[...].astype(F32) + change[at]).astype(dx_ref.dtype)
    sums_ref[...] = jnp.concatenate(
        [
            jnp.sum((d * u)[:mine], axis=0, keepdims=True),
            jnp.sum(d[:mine], axis=0, keepdims=True),
            jnp.sum(dx_ref[:mine].astype(F32), axis=0, keepdims=True),
        ],
        axis=0,
    )


def norm_back(name, own, recv, bases, x, gain, dtype):
    rows, width = own.shape
    block = pl.BlockSpec((rows, width), lambda *_: (0, 0))
    piece = pl.BlockSpec((rows // len(bases), width), lambda *_: (0, 0))
    return call(
        functools.partial(norm_back_kernel, len(bases)), name, (1,),
        [block] * 2 + [piece] * len(bases) + [block, whole((1, width))],
        [block, whole((3, width))],
        [sds((rows, width), dtype), sds((3, width), F32)],
        (own, recv, *bases, x, gain),
    )


def hbm(x):
    return pltpu.with_memory_space_constraint(x, pltpu.HBM)


def swap(x, bit, count):
    return lax.ppermute(x, "mp", [(i, i ^ bit) for i in range(count)])


def row(vector):
    return vector.reshape(1, -1)


def layout(mask_row, seg_row, order, home, steps, span):
    tokens = mask_row.shape[0]
    grid = mask_row.reshape(tokens // 128, 128).astype(BF)
    upper = (jnp.arange(128)[:, None] <= jnp.arange(128)[None, :]).astype(BF)
    within = jnp.dot(grid, upper, preferred_element_type=F32)
    lines = tokens // 128
    lower = (jnp.arange(lines)[:, None] > jnp.arange(lines)[None, :]).astype(BF)
    ahead = jnp.dot(lower, within[:, 127:].astype(BF), preferred_element_type=F32)
    count = (within + ahead).astype(jnp.int32).reshape(tokens)
    rank = jnp.where(mask_row == 1, count - 1, -1)
    labels = jnp.arange(CLIPS, dtype=jnp.int32)
    upto = (seg_row[None, :] <= labels[:, None]).astype(jnp.int32)
    ends = jnp.sum(upto, axis=1)
    cum = jnp.sum(upto * mask_row[None, :], axis=1)
    edge = jnp.arange(steps, dtype=jnp.int32) * span
    low = jnp.sum((count[None, :] <= edge[:, None]).astype(jnp.int32), axis=1)
    high = jnp.sum((count[None, :] < edge[:, None] + span).astype(jnp.int32), axis=1)
    low = low // span
    high = jnp.minimum(high, tokens - 1) // span + 1
    each = cum - jnp.concatenate([jnp.zeros((1,), jnp.int32), cum[:-1]])
    inverse = 1.0 / jnp.maximum(each, 1).astype(F32)
    first = jnp.concatenate([order, cum, ends, home[None].astype(jnp.int32)])
    scalars = jnp.concatenate([first, low, high])
    return rank.reshape(tokens // span, span), first, scalars, inverse.reshape(1, CLIPS)


def body(
    teacher_in, segment_ids, keep_mask, block_owner, student_in,
    t_norm1_gain, t_norm1_shift, t_qkv, t_qv_bias, t_out, t_out_bias,
    t_norm2_gain, t_norm2_shift, t_fc1, t_fc1_bias, t_fc2, t_fc2_bias,
    s_norm1_gain, s_norm1_shift, s_qkv, s_qv_bias, s_out, s_out_bias,
    s_norm2_gain, s_norm2_shift, s_fc1, s_fc1_bias, s_fc2, s_fc2_bias,
    head_weight, head_bias,
):
    mp = lax.axis_size("mp")
    me = lax.axis_index("mp")
    homes = lax.axis_size("dp")
    home = lax.axis_index("dp")
    slots, block, width = student_in.shape
    piece = block // mp
    rows = slots * block
    mine = rows // mp
    near = 2 * mine
    tokens, t_width = teacher_in.shape
    used = s_qkv.shape[2]
    wide = 256
    nb = 2
    span = nb * block
    steps = slots // nb
    core = lambda x: swap(x, 1, mp)
    across = lambda x: swap(x, 2, mp)

    order = jnp.stack([me, me ^ 2, me ^ 1, me ^ 3]).astype(jnp.int32)
    mask_row = lax.dynamic_index_in_dim(keep_mask, home, 0, keepdims=False)
    seg_row = lax.dynamic_index_in_dim(segment_ids, home, 0, keepdims=False)
    rank, first_scalars, scalars, inverse = layout(mask_row, seg_row, order, home, steps, span)

    t_w2 = across(t_out)
    s_w2 = across(s_out)
    s_f1 = (s_fc1, core(s_fc1))
    s_f2 = (s_fc2, core(s_fc2))
    biases = core(jnp.concatenate([t_fc1_bias, s_fc1_bias]))

    x4 = hbm(student_in.reshape(slots, mp, piece, width))
    w_turn = jnp.transpose(s_qkv, (0, 2, 1))
    by_piece = lambda w: pl.BlockSpec((mine, w), lambda k, sc: (k, 0))
    turned = pl.BlockSpec((used, mine), lambda k, sc: (0, k))
    x_stud, a_stud, sq, sk, sv, skt, svt = call(
        functools.partial(student_qkv_kernel, block), "student_qkv", (mp,),
        [
            pl.BlockSpec((slots, 1, piece, width), lambda k, sc: (0, sc[ORD + k], 0, 0)),
            whole((1, width)), whole((1, width)), whole(w_turn.shape), whole(s_qv_bias.shape),
        ],
        [by_piece(width)] * 2 + [by_piece(wide)] * 3 + [turned] * 2,
        [sds((rows, width), BF)] * 2 + [sds((rows, wide), BF)] * 3 + [sds((used, rows), BF)] * 2,
        (x4, row(s_norm1_gain), row(s_norm1_shift), hbm(w_turn), s_qv_bias),
        flops=2 * rows * width * 3 * wide, scalars=first_scalars, far=(0, 1, 4, 5),
    )
    heads = used // HD
    by_rows = lambda w: pl.BlockSpec((near, w), lambda j: (j, 0))
    by_lanes = lambda h: pl.BlockSpec((h, near), lambda j: (0, j))
    ctx, mixed, logs = call(
        functools.partial(student_attend_kernel, used), "student_attend", (rows // near,),
        [by_rows(wide), whole((rows, wide)), whole((used, rows))],
        [by_rows(used), by_lanes(used), by_lanes(8)],
        [sds((rows, used), BF), sds((used, rows), F32), sds((8, rows), F32)],
        (sq, sk, svt),
        flops=heads * rows * rows * wide * 4, far=(1, 2),
    )

    ctx, teacher_rows, t_w2, s_w2, s_f1, s_f2, biases, s_out_late = lax.optimization_barrier(
        (ctx, teacher_in, t_w2, s_w2, s_f1, s_f2, biases, s_out)
    )
    t_b1 = (row(t_fc1_bias), row(biases[: t_fc1_bias.shape[0]]))
    s_b1 = (row(s_fc1_bias), row(biases[t_fc1_bias.shape[0] :]))
    s_c0 = ctx[:near]
    s_c1 = core(ctx[near:])
    s_c2 = across(s_c0)
    s_w1 = core(s_out_late)
    s_w3 = core(s_w2)

    cols = t_qkv.shape[2]
    tk, tv = call(
        teacher_kv_kernel, "teacher_kv", (tokens // 512,),
        [
            pl.BlockSpec((512, t_width), lambda j, sc: (j, 0)), whole((1, t_width)), whole((1, t_width)),
            whole(t_qkv.shape), whole(t_qv_bias.shape),
        ],
        [pl.BlockSpec((512, 2 * cols), lambda j, sc: (j, 0)), pl.BlockSpec((cols, 512), lambda j, sc: (0, j))],
        [sds((tokens, 2 * cols), BF), sds((cols, tokens), BF)],
        (hbm(teacher_rows), row(t_norm1_gain), row(t_norm1_shift), hbm(t_qkv), t_qv_bias),
        flops=2 * tokens * t_width * 2 * cols, scalars=scalars, far=(0, 1),
    )
    tk, teacher_rows, s_c1, s_w1, s_w3, t_fc1_late, t_out_late = lax.optimization_barrier(
        (tk, teacher_rows, s_c1, s_w1, s_w3, t_fc1, t_out)
    )
    s_c3 = across(s_c1)
    t_f1 = (t_fc1, core(t_fc1_late))
    t_w1 = core(t_out_late)
    by_slot = lambda w: pl.BlockSpec((mp, nb, piece, w), lambda j, sc: (0, j, 0, 0))
    x_kept, tq = call(
        functools.partial(teacher_q_kernel, slots, block, span), "teacher_q", (steps,),
        [
            whole(teacher_in.shape), whole(rank.shape), whole((1, t_width)), whole((1, t_width)),
            whole(t_qkv.shape), whole(t_qv_bias.shape),
        ],
        [by_slot(t_width), by_slot(2 * cols)],
        [sds((mp, slots, piece, t_width), BF), sds((mp, slots, piece, 2 * cols), BF)],
        (hbm(teacher_rows), rank, row(t_norm1_gain), row(t_norm1_shift), hbm(t_qkv), t_qv_bias),
        scratch=[pltpu.VMEM((span, t_width), F32)],
        flops=2 * rows * t_width * (cols + 512), scalars=scalars,
    )
    def attend(name, p, query):
        half_slot = lambda w, lane: pl.BlockSpec((mp, slots // 2, piece, w), lambda j: (0, j, 0, lane))
        return call(
            teacher_attend_kernel, name, (2,),
            [
                half_slot(256, p), pl.BlockSpec((tokens, 256), lambda j: (0, p)),
                pl.BlockSpec((128, tokens), lambda j: (p, 0)),
            ],
            half_slot(128, 0),
            sds((mp, slots, piece, 128), BF),
            (query, tk, tv),
            flops=2 * rows * tokens * (512 + 256),
        ).reshape(rows, 128)

    t_ctx = []
    for p in range(cols // 128):
        mixed_pair = attend("teacher_attend%d" % p, p, tq)
        if p == 0:
            mixed_pair, tq, s_c2, s_c3 = lax.optimization_barrier((mixed_pair, tq, s_c2, s_c3))
        else:
            t_ctx[0], mixed_pair, t_f1, t_w1, t_fc2_late = lax.optimization_barrier(
                (t_ctx[0], mixed_pair, t_f1, t_w1, t_fc2)
            )
        t_ctx.append([mixed_pair, core(mixed_pair[near:]), across(mixed_pair)])
    t_f2 = (t_fc2, core(t_fc2_late))
    t_w3 = core(t_w2)

    s_send, s_own, sent, a2, act, slope = forward(
        "both", "student_forward", near, (s_c0, s_c1, s_c2, s_c3), (s_out, s_w1, s_w2, s_w3), x_stud,
        row(s_out_bias), row(s_norm2_gain), row(s_norm2_shift), s_f1, s_b1, s_f2, row(s_fc2_bias), s_fc1.shape[1],
    )
    s_send, t_ctx, t_f2, t_w3 = lax.optimization_barrier((s_send, t_ctx, t_f2, t_w3))
    t_ctx = [x for own, from_core, from_chip in t_ctx for x in (own, from_core, from_chip, core(from_chip[near:]))]
    s_recv = across(s_send)
    t_args = (
        t_ctx, (t_out, t_w1, t_w2, t_w3), x_kept.reshape(rows, t_width), row(t_out_bias),
        row(t_norm2_gain), row(t_norm2_shift), t_f1, t_b1, t_f2, row(t_fc2_bias),
    )
    t_send = forward("send", "teacher_forward_far", mine, *t_args, 512)
    s_recv, t_args, t_send = lax.optimization_barrier((s_recv, t_args, t_send))
    t_recv = across(t_send)
    out_rows = (s_own + s_recv.astype(F32)).astype(BF)

    owners = lax.dynamic_index_in_dim(block_owner, home, 0, keepdims=False)
    capacity = (slots + homes - 1) // homes
    labels = jnp.arange(homes, dtype=jnp.int32)
    hits = (owners[:, None] == labels[None, :]).astype(jnp.int32)
    earlier = (jnp.arange(slots)[:, None] > jnp.arange(slots)[None, :]).astype(jnp.int32)
    order_in = jnp.sum(earlier * (owners[:, None] == owners[None, :]).astype(jnp.int32), axis=1)
    spot = jnp.where(owners >= 0, owners * capacity + order_in, homes * capacity)
    spots = jnp.arange(homes * capacity, dtype=jnp.int32)
    leaving = jnp.sum(
        jnp.where(spots[:, None] == spot[None, :], jnp.arange(slots, dtype=jnp.int32)[None, :], 0), axis=1
    )
    per_source = jnp.sum((block_owner == home).astype(jnp.int32), axis=1)
    ahead = (labels[:, None] > labels[None, :]).astype(jnp.int32)
    before = jnp.sum(ahead * per_source[None, :], axis=1)
    lane = jnp.arange(capacity, dtype=jnp.int32)
    target_slot = jnp.where(lane[None, :] < per_source[:, None], before[:, None] + lane[None, :], OWN).reshape(-1)
    chosen = jnp.sum(
        jnp.where(jnp.arange(OWN, dtype=jnp.int32)[:, None] == target_slot[None, :], spots[None, :], 0), axis=1
    )

    bits = log2(homes)

    def partner(value, bit):
        return lax.ppermute(value, "dp", [(i, i ^ (1 << bit)) for i in range(homes)])

    entries, shift = homes * capacity, log2(capacity)
    entry_shape = (entries, piece, width)
    leaving_sc = jnp.concatenate([leaving, home[None].astype(jnp.int32)])
    home_sc = home[None].astype(jnp.int32)

    def spread(name, came, going, blocks, came_in, places):
        ins = [blocks] if came_in is None else [blocks, came_in]
        base = places.shape[0] - 1
        lift = lambda bit: None if bit is None else bit + shift
        if going is None:
            outs = [sds((OWN, piece, width), BF)]
            scratch = [pltpu.VMEM(entry_shape, BF)]
        else:
            outs = [sds(entry_shape, BF), sds((entries // 2, piece, width), BF)]
            scratch = []
        return call(
            functools.partial(spread_kernel, lift(came), lift(going), shift, base), name, (1,),
            [whole(x.shape) for x in ins], [whole(o.shape) for o in outs], outs, ins, scratch=scratch, scalars=places,
        )

    turns = [0] + list(range(bits - 1, 0, -1))
    kept, sending = spread("spread0", None, turns[0], out_rows.reshape(slots, piece, width), None, leaving_sc)
    t_args, kept = lax.optimization_barrier((t_args, kept))
    travel = partner(sending, turns[0])
    t_own = forward("own", "teacher_forward_own", mine, *t_args, 512)
    t_own, t_recv, travel = lax.optimization_barrier((t_own, t_recv, travel))
    kept, sending = spread("spread1", turns[0], turns[1], kept, travel, home_sc)
    t_own, kept = lax.optimization_barrier((t_own, kept))
    travel = partner(sending, turns[1])

    d_guess, d_out, loss_row, head_b_row, fc2_b_row = call(
        functools.partial(head_kernel, block, piece), "head", (1,),
        [
            whole((mine, t_width)), whole((mine, t_width)), whole((mine, width)), whole((width, t_width)),
            whole((1, t_width)), pl.BlockSpec(memory_space=pltpu.SMEM),
        ],
        [whole((mine, t_width)), whole((mine, width)), whole((1, t_width)), whole((1, t_width)), whole((1, width))],
        [sds((mine, t_width), BF), sds((mine, width), BF), sds((1, t_width), F32), sds((1, t_width), F32), sds((1, width), F32)],
        (t_own, t_recv, out_rows, hbm(head_weight), row(head_bias), inverse),
        flops=4 * mine * width * t_width, scalars=scalars,
    )
    d_out_far = across(d_out)

    half_cols, quarter = t_width // 2, t_width // 4
    head_keep, head_send = call(
        head_grad_kernel, "head_grad", (1,),
        [
            whole((mine, width)),
            pl.BlockSpec((mine, half_cols), lambda j, sc: (0, sc[ORD] & 1)),
            pl.BlockSpec((mine, half_cols), lambda j, sc: (0, 1 - (sc[ORD] & 1))),
        ],
        [whole((width, half_cols))] * 2,
        [sds((width, half_cols), F32), sds((width, half_cols), BF)],
        (out_rows, d_guess, d_guess), scalars=scalars,
    )
    head_recv = core(head_send)
    own_quarter = pl.BlockSpec((width, quarter), lambda j, sc: (0, sc[ORD] >> 1))
    far_quarter = pl.BlockSpec((width, quarter), lambda j, sc: (0, 1 - (sc[ORD] >> 1)))
    head_keep, head_send = call(
        head_add_kernel, "head_add", (1,),
        [own_quarter, own_quarter, far_quarter, far_quarter],
        [whole((width, quarter))] * 2,
        [sds((width, quarter), F32), sds((width, quarter), BF)],
        (head_keep, head_recv, head_keep, head_recv), scalars=scalars, far=(0,),
    )
    d_out_far, head_send = lax.optimization_barrier((d_out_far, head_send))
    head_recv = across(head_send)

    hidden = s_fc1.shape[1]
    cut = lambda i: pl.BlockSpec((near, hidden), lambda *_: (0, i))
    square, turned_square, line = whole((width, hidden)), whole((hidden, width)), whole((1, hidden))
    tall, short_rows = whole((near, width)), whole((mine, width))
    d_scratch = [pltpu.VMEM((near, width), BF)]
    g1_send, g2_send, b1_send, da2_part = call(
        feed_far_kernel, "feed_back_far", (1,),
        [short_rows, short_rows, cut(1), cut(1), tall, square, turned_square],
        [square, turned_square, line, tall],
        [sds((width, hidden), BF), sds((hidden, width), BF), sds((1, hidden), F32), sds((near, width), F32)],
        (d_out, d_out_far, *map(hbm, (act, slope, a2, s_f1[1], s_f2[1]))),
        scratch=d_scratch,
    )
    da2_part, g1_send, g2_send, head_recv, travel = lax.optimization_barrier(
        (da2_part, g1_send, g2_send, head_recv, travel)
    )
    for turn in range(2, bits):
        kept, sending = spread("spread%d" % turn, turns[turn - 1], turns[turn], kept, travel, home_sc)
        travel = partner(sending, turns[turn])
    g1_recv, g2_recv = core(g1_send), core(g2_send)
    dpre, b1_own, da2_own, da2_send = call(
        feed_own_kernel, "feed_back_own", (1,),
        [short_rows, short_rows, cut(0), square, turned_square, tall],
        [whole((near, hidden)), line, tall, tall],
        [sds((near, hidden), BF), sds((1, hidden), F32), sds((near, width), F32), sds((near, width), BF)],
        (d_out, d_out_far, *map(hbm, (slope, s_f1[0], s_f2[0])), da2_part),
        scratch=d_scratch,
    )
    g1_recv, g2_recv, dpre, da2_send = lax.optimization_barrier((g1_recv, g2_recv, dpre, da2_send))
    da2_far = across(da2_send)

    x_first = list(range(bits))
    z_first = x_first[1:] + x_first[:1]

    def go(name, *bundles):
        advance(name, bundles, partner, scalars)

    half = width // 2
    a_width = hidden + quarter
    keep_a, send_a, keep_b, send_b = call(
        functools.partial(feed_grad_kernel, x_first[0], z_first[0]), "feed_back_grad", (1,),
        [
            short_rows, short_rows, cut(0), tall, whole((near, hidden)), square, turned_square,
            whole((width, quarter)), whole((width, quarter)),
        ],
        [whole((half, a_width))] * 2 + [whole((half, width))] * 2,
        [sds((half, a_width), BF)] * 2 + [sds((half, width), BF)] * 2,
        (d_out, d_out_far, hbm(act), hbm(a2), dpre, g1_recv, g2_recv, head_keep, head_recv),
        scratch=d_scratch, scalars=scalars,
    )
    one = Bundle(x_first, keep_a, partner(send_a, x_first[0]), ((0, hidden, F32), (hidden, a_width, BF)))
    two = Bundle(z_first, keep_b, partner(send_b, z_first[0]), ((0, width, F32),))

    q_late, keep_a = lax.optimization_barrier((sq, keep_a))
    one.flight = (keep_a, one.flight[1])
    probs = call(
        functools.partial(student_probs_kernel, used), "student_probs", (heads, rows // near),
        [
            pl.BlockSpec((near, wide), lambda h, j: (j, 0)), whole((rows, wide)),
            pl.BlockSpec((8, near), lambda h, j: (0, j)),
        ],
        [pl.BlockSpec((1, rows, near), lambda h, j: (h, 0, j))],
        [sds((heads, rows, rows), BF)],
        (q_late, sk, logs),
        flops=heads * rows * rows * wide * 2, far=(0,),
    )[0]
    da2_far, travel, probs, one.flight, two.flight = lax.optimization_barrier(
        (da2_far, travel, probs, one.flight, two.flight)
    )
    d_sent, sums2 = norm_back(
        "norm2_back", da2_own, da2_far, (d_out, d_out_far), sent, row(s_norm2_gain), BF
    )
    d_core = core(d_sent)
    d_core, one.flight, two.flight = lax.optimization_barrier((d_core, one.flight, two.flight))
    ds = (d_sent, d_core)
    for extra in range(bits - 2):
        go("sum_b%d" % extra, one, two)

    def back(name, picked, with_out):
        size = HD * len(picked)
        outs = [sds((rows, 3 * size), BF), sds((2, size), F32)] + [sds((used, width), F32)] * with_out
        return call(
            functools.partial(student_back_kernel, used, picked, with_out), name, (2,),
            [tall] * 2
            + [
                whole((used, width)), by_lanes(used),
                pl.BlockSpec((len(picked), rows, near), lambda j: (picked[0] // len(picked), 0, j)), by_rows(wide),
                whole((rows, wide)), whole((used, rows)),
            ],
            [whole(o.shape) for o in outs], outs,
            (*ds, s_out, mixed, probs, sq, sv, skt),
            scratch=[pltpu.VMEM((near, width), BF), pltpu.VMEM((near, wide), F32)]
            + [pltpu.VMEM((rows, wide), F32)] * 2 + [pltpu.VMEM((1, size), F32)]
            + [pltpu.VMEM((used, width), F32)] * with_out,
            flops=len(picked) * rows * rows * wide * 7, limit=36 * 2**20,
        )

    def project(name, bit, d, more):
        size = d.shape[1] + sum(m.shape[0] for m in more)
        specs = [whole(d.shape), whole(a_stud.shape)] + [whole(m.shape) for m in more]
        keep, send = call(
            functools.partial(project_grad_kernel, bit, bool(more)), name, (1,), specs,
            [whole((size // 2, width))] * 2, [sds((size // 2, width), BF)] * 2,
            (d, a_stud, *more), scalars=scalars,
        )
        return keep, partner(send, bit)

    pair, odd = tuple(range(heads - 1)), (heads - 1,)
    d_pair, pair_sums = back("student_back_pair", pair, False)
    d_pair, one.flight, two.flight = lax.optimization_barrier((d_pair, one.flight, two.flight))
    chosen_sc = jnp.concatenate([chosen, home_sc])
    student_out = spread("spread_end", turns[-1], None, kept, travel, chosen_sc)[0]
    go("sum_c", one, two)
    whole_width = ((0, width, BF),)
    three = Bundle(x_first, *project("project_pair", x_first[0], d_pair, ()), whole_width)
    tied = lax.optimization_barrier((*ds, three.flight[0], d_pair))
    ds, d_pair = tied[:2], tied[3]
    three.flight = (tied[2], three.flight[1])
    d_odd, odd_sums, g_out = back("student_back_odd", odd, True)
    d_odd, one.flight, two.flight, three.flight = lax.optimization_barrier(
        (d_odd, one.flight, two.flight, three.flight)
    )
    go("sum_d", one, two, three)
    four = Bundle(x_first, *project("project_odd", x_first[0], d_odd, (g_out,)), whole_width)
    mixed_size = HD * (heads - 1)
    w_pair = w_turn[:, :mixed_size].reshape(3 * mixed_size, width)
    w_odd = w_turn[:, mixed_size:].reshape(3 * HD, width)
    at = lambda w: pl.BlockSpec((near, w), lambda j: (1 - j, 0))
    da1_near, da1_send = call(
        input_grad_kernel, "input_grad", (2,),
        [at(3 * mixed_size), at(3 * HD), whole(w_pair.shape), whole(w_odd.shape)],
        [tall, tall], [sds((near, width), F32), sds((near, width), BF)],
        (d_pair, d_odd, w_pair, w_odd),
    )
    da1_recv = core(da1_send)
    da1_own = da1_near[:mine] + da1_recv[:mine].astype(F32)
    da1_far = across((da1_near[mine:] + da1_recv[mine:].astype(F32)).astype(BF))
    go("sum_e", one, two, three, four)
    for extra in range(bits - 3):
        go("sum_f%d" % extra, one, two, three, four)
    short_in = (sums2, fc2_b_row, head_b_row, loss_row, b1_send, b1_own, pair_sums, odd_sums)
    short_early = call(
        short_kernel, "short", (1,), [whole(v.shape) for v in short_in],
        [whole((16, width))] * 2, [sds((16, width), F32)] * 2, short_in,
    )
    grad_in, sums1 = norm_back("norm1_back", da1_own, da1_far, (d_sent,), x_stud, row(s_norm1_gain), F32)

    def tie(held, *bundles):
        kept, held = lax.optimization_barrier(([b.flight[0] for b in bundles], held))
        for b, first in zip(bundles, kept):
            b.flight = (first, b.flight[1])
        return held

    norm_rows = jnp.concatenate([sums1[:2], jnp.zeros((14, width), F32)], axis=0)
    vec = short_early[0] + norm_rows + core(short_early[1] + norm_rows)
    home_rows = (jnp.arange(16) < 9)[:, None]
    vec = tie(vec, three)
    go("sum_g", one, two, three, four)
    vec = jnp.where(home_rows, vec + across(vec), vec)
    turn = 0
    while three.result is None or four.result is None or one.result is None:
        left = [b for b in (three, four) if b.result is None]
        if turn <= bits and left:
            vec = tie(vec, left[0])
        if turn < bits:
            moved_vec = partner(vec, turn)
        go("sum_h%d" % turn, *left)
        if turn % 2 and one.result is None:
            flying = [b for b in left if b.result is None]
            if flying:
                tie(flying[0].flight[0], one, two)
            go("sum_last%d" % turn, one, two)
        if turn < bits:
            vec = vec + moved_vec
        turn += 1
    for bit in range(turn, bits):
        vec = vec + partner(vec, bit)

    g1_all, head_all = one.result
    head_cross, head_core = across(head_all), core(head_all)
    piece_spec = whole((width, quarter))
    grad_head = call(
        place_kernel, "place_head", (mp,), [piece_spec] * 4,
        pl.BlockSpec((width, quarter), lambda k, sc: (0, 2 * (sc[ORD + k] & 1) + (sc[ORD + k] >> 1))),
        sds((width, t_width), F32),
        (head_all, head_cross, head_core, core(head_cross)), scalars=scalars,
    )
    low_pair, low_odd = three.result[0], four.result[0]
    qkv_turned = jnp.concatenate(
        [low_pair.reshape(3, mixed_size, width), low_odd[: 3 * HD].reshape(3, HD, width)], axis=1
    )
    return (
        jnp.sum(vec[8]),
        student_out,
        grad_in.reshape(slots, piece, width),
        vec[0],
        vec[1],
        jnp.transpose(qkv_turned, (0, 2, 1)).astype(F32),
        vec[10:12, :used],
        low_odd[3 * HD :].astype(F32),
        vec[4],
        vec[2],
        vec[3],
        g1_all,
        vec[9],
        two.result[0],
        vec[5],
        grad_head,
        jnp.concatenate([vec[6], vec[7, : t_width - width]]),
    )


def solution(mesh):
    rep = P()
    in_specs = (
        P("dp", None), rep, rep, rep, P("dp", None, None), rep, rep, P(None, None, "mp"), P(None, "mp"),
        P("mp", None), rep, rep, rep, P(None, "mp"), P("mp"), P("mp", None), rep, rep, rep,
        P(None, None, "mp"), P(None, "mp"), P("mp", None), rep, rep, rep, P(None, "mp"), P("mp"),
        P("mp", None), rep, rep, rep,
    )
    out_specs = (
        rep, P("dp", "mp", None), P("dp", "mp", None), rep, rep, P(None, None, "mp"), P(None, "mp"),
        P("mp", None), rep, rep, rep, P(None, "mp"), P("mp"), P("mp", None), rep, rep, rep,
    )
    return jax.shard_map(body, mesh=mesh, in_specs=in_specs, out_specs=out_specs, check_vma=False)
```
